32 devices in a mesh: gx: 8 (over z, core), gy: 4 (over y, x).
Axes of the slice: x: 2, y: 2, z: 4, core: 2. Of those that a mesh axis runs over, the one named last changes fastest.
Arguments:
- pressure0: float32 [4, 128, 512], P(None, 'gx', 'gy'), may hold values from -6 to 6
- saturation0: float32 [4, 128, 512], P(None, 'gx', 'gy'), may hold values from 0.1 to 0.9
- trans_x: float32 [4, 128, 512], P(None, 'gx', 'gy'), may hold values from 0.1 to 2
- trans_y: float32 [4, 128, 512], P(None, 'gx', 'gy'), may hold values from 0.1 to 2
- trans_z: float32 [3, 128, 512], P(None, 'gx', 'gy'), may hold values from 0.05 to 1
- pore_volume: float32 [4, 128, 512], P(None, 'gx', 'gy'), may hold values from 0.5 to 2
- upwind: int32 [4, 128, 512], P(None, 'gx', 'gy'), may hold values from 0 to 63
- well_cell: int32 [8, 4, 64], P('gx', 'gy'), may hold values from 0 to 8191
- well_rate: float32 [8, 4, 64], P('gx', 'gy'), may hold values from -8 to 8
- plan: int32 [2, 8, 4, 64], P(None, 'gx', 'gy'), may hold values from 0 to 2
- observed: float32 [2, 2, 8, 4, 64], P(None, None, 'gx', 'gy'), may hold values from -6 to 6
Outputs:
- grad_x: float32 [4, 128, 512], P(None, 'gx', 'gy')
- grad_y: float32 [4, 128, 512], P(None, 'gx', 'gy')
- grad_z: float32 [3, 128, 512], P(None, 'gx', 'gy')
The draws below stay inside these ranges and needn't reach their ends.
Inputs may be any that keep to these rules, and one draw needn't show every extreme that they name: `upwind`: bit 3 n + d of an entry is 1 where the cell itself is upstream of its forward face along x, y or layers (d = 0, 1, 2) in step n, 0 where the next cell is. `well_cell`: a cell of the well's own tile, numbered layer by layer, then row, then column. `plan`: 0 shut, 1 half rate, 2 full rate.
All inputs are finite; a program needn't handle non-finite values.
Results may differ from the reference program's by a relative error of at most 0.0001.
Values sent between devices are 32-bit elements; how exact they have to be, the bound alone decides.
No kernel may reach another device: no remote copies, remote signals or barrier semaphores. Data moves between devices by JAX's collectives and lax.ppermute only.
A program may use at most 64 MiB of HBM per device.

```python
import math
import jax
import jax.numpy as jnp
from jax import lax

LAYERS = 4
CX = 16
CY = 128
STEPS = 2
WELL_DEV = 64
NX = 128
NY = 512
TILES_X = 8
TILES_Y = 4


def set_ends(values, rng, low, largest):
    index_at = [jax.random.randint(jax.random.fold_in(rng, axis), (), 0, length) for axis, length in enumerate(values.shape)]
    main_axis = values.shape.index(max(values.shape))
    beside = index_at[:main_axis] + [(index_at[main_axis] + 1) % values.shape[main_axis]] + index_at[main_axis + 1:]
    return values.at[tuple(index_at)].set(low).at[tuple(beside)].set(largest)


def block_scale(stream_key, dims, cuts, smallest, top_value):
    factor_of = 1.0
    for dim, shards_of in cuts:
        draws = jax.random.uniform(jax.random.fold_in(jax.random.fold_in(stream_key, 6), dim), (shards_of,), jnp.float32, smallest / len(cuts), top_value / len(cuts))
        factor_of = factor_of * jnp.repeat(jnp.exp(draws), dims[dim] // shards_of).reshape((-1,) + (1,) * (len(dims) - 1 - dim))
    return factor_of


def noise(stream_key, dims, spread, reach, shards=(), held_as=jnp.bfloat16):
    values = spread * jax.random.normal(stream_key, dims, jnp.float32)
    if shards:
        values = values * block_scale(stream_key, dims, shards, -0.22, 0.18)
    return jnp.clip(values, -reach, reach).astype(held_as)


def setup_inputs(seed: int = 0) -> dict:
    keys = jax.random.split(jax.random.key(seed), 12)
    pressure0 = noise(keys[0], (LAYERS, NX, NY), 1.0, 6.0, ((1, 8), (2, 4)), jnp.float32)
    saturation0 = jnp.clip(0.1 + 0.79999997 * jax.random.uniform(keys[1], (LAYERS, NX, NY), jnp.float32) ** block_scale(keys[1], (LAYERS, NX, NY), ((1, 8), (2, 4)), -0.2, 0.2), 0.1, 0.9)
    trans_x = jnp.clip(jnp.exp(math.log(2.0) - 2.9957323 * jax.random.uniform(keys[2], (LAYERS, NX, NY), jnp.float32) ** block_scale(keys[2], (LAYERS, NX, NY), ((1, 8), (2, 4)), -0.2, 0.2)), 0.1, 2.0)
    trans_y = jnp.clip(jnp.exp(math.log(2.0) - 2.9957323 * jax.random.uniform(keys[3], (LAYERS, NX, NY), jnp.float32) ** block_scale(keys[3], (LAYERS, NX, NY), ((1, 8), (2, 4)), -0.2, 0.2)), 0.1, 2.0)
    trans_z = jnp.clip(jnp.exp(math.log(1.0) - 2.9957323 * jax.random.uniform(keys[4], (LAYERS - 1, NX, NY), jnp.float32) ** block_scale(keys[4], (LAYERS - 1, NX, NY), ((1, 8), (2, 4)), -0.2, 0.2)), 0.05, 1.0)
    pore_volume = jnp.clip(jnp.exp(math.log(2.0) - 1.3862944 * jax.random.uniform(keys[5], (LAYERS, NX, NY), jnp.float32) ** block_scale(keys[5], (LAYERS, NX, NY), ((1, 8), (2, 4)), -0.2, 0.2)), 0.5, 2.0)
    upwind = set_ends(jax.random.randint(keys[6], (LAYERS, NX, NY), 0, 2 ** (3 * STEPS)), jax.random.fold_in(keys[6], 1), 0, (2 ** (3 * STEPS)) - 1).astype(jnp.int32)
    well_cell = set_ends(jax.random.randint(keys[7], (TILES_X, TILES_Y, WELL_DEV), 0, LAYERS * CX * CY), jax.random.fold_in(keys[7], 1), 0, (LAYERS * CX * CY) - 1).astype(jnp.int32)
    well_rate = noise(keys[8], (TILES_X, TILES_Y, WELL_DEV), 2.0, 8.0, ((0, 8), (1, 4)), jnp.float32)
    plan = set_ends(jax.random.randint(keys[9], (STEPS, TILES_X, TILES_Y, WELL_DEV), 0, 3), jax.random.fold_in(keys[9], 1), 0, 2).astype(jnp.int32)
    observed = noise(keys[10], (STEPS, 2, TILES_X, TILES_Y, WELL_DEV), 1.0, 6.0, ((2, 8), (3, 4)), jnp.float32)
    return dict(pressure0=pressure0, saturation0=saturation0, trans_x=trans_x, trans_y=trans_y, trans_z=trans_z, pore_volume=pore_volume, upwind=upwind, well_cell=well_cell, well_rate=well_rate, plan=plan, observed=observed)


storage_coef = 1.0
time_step = 0.05

def mobility(saturation):
    wetted = saturation * saturation
    return wetted / (wetted + 0.5 * (1.0 - saturation) * (1.0 - saturation))

def vertical(center, faces):
    empty_layer = jnp.zeros_like(center[:1])
    upper_cells = jnp.concatenate([center[1:], empty_layer], axis=0)
    lower_cells = jnp.concatenate([empty_layer, center[:-1]], axis=0)
    face_up = jnp.concatenate([faces, empty_layer], axis=0)
    face_down = jnp.concatenate([empty_layer, faces], axis=0)
    return (face_up, face_down, upper_cells, lower_cells)

def jacobi(pressure, pressure_old, trans_x, trans_y, trans_z, pore_space, source, outside):
    center = pressure[:, 1:-1, 1:-1]
    east_face = trans_x[:, 1:-1, 1:-1]
    west_face = trans_x[:, :-2, 1:-1]
    north_face = trans_y[:, 1:-1, 1:-1]
    south_face = trans_y[:, 1:-1, :-2]
    face_up, face_down, upper_cells, lower_cells = vertical(center, trans_z[:, 1:-1, 1:-1])
    storage = storage_coef * pore_space[:, 1:-1, 1:-1]
    numerator = storage * pressure_old[:, 1:-1, 1:-1] + source[:, 1:-1, 1:-1] + east_face * pressure[:, 2:, 1:-1] + west_face * pressure[:, :-2, 1:-1] + north_face * pressure[:, 1:-1, 2:] + south_face * pressure[:, 1:-1, :-2] + face_up * upper_cells + face_down * lower_cells
    denominator = storage + east_face + west_face + north_face + south_face + face_up + face_down + outside[:, 1:-1, 1:-1]
    return numerator / denominator

def transport(pressure, saturation, trans_x, trans_y, trans_z, upwind_x, upwind_y, upwind_z, pore_space, outside):
    mobile = mobility(saturation)
    flux_x = (pressure[:, :-1, :] - pressure[:, 1:, :]) * (upwind_x[:, :-1, :] * mobile[:, :-1, :] + (trans_x[:, :-1, :] - upwind_x[:, :-1, :]) * mobile[:, 1:, :])
    flux_y = (pressure[:, :, :-1] - pressure[:, :, 1:]) * (upwind_y[:, :, :-1] * mobile[:, :, :-1] + (trans_y[:, :, :-1] - upwind_y[:, :, :-1]) * mobile[:, :, 1:])
    mid_pressure = pressure[:, 1:-1, 1:-1]
    mid_mobile = mobile[:, 1:-1, 1:-1]
    rise_upwind = upwind_z[:, 1:-1, 1:-1]
    rise_trans = trans_z[:, 1:-1, 1:-1]
    flux_z = (mid_pressure[:-1] - mid_pressure[1:]) * (rise_upwind * mid_mobile[:-1] + (rise_trans - rise_upwind) * mid_mobile[1:])
    empty_layer = jnp.zeros_like(mid_pressure[:1])
    net_outflow = flux_x[:, 1:, 1:-1] - flux_x[:, :-1, 1:-1] + flux_y[:, 1:-1, 1:] - flux_y[:, 1:-1, :-1] + jnp.concatenate([flux_z, empty_layer], axis=0) - jnp.concatenate([empty_layer, flux_z], axis=0)
    return saturation[:, 1:-1, 1:-1] - time_step * net_outflow / (pore_space[:, 1:-1, 1:-1] + outside[:, 1:-1, 1:-1])

def widen(array):
    return jnp.pad(array, ((0, 0), (1, 1), (1, 1)))

def advance(pressure, saturation, trans_x, trans_y, trans_z, upwind_x, upwind_y, upwind_z, pore_space, source, outside):
    padded = widen(pressure)
    first = jacobi(padded, padded, trans_x, trans_y, trans_z, pore_space, source, outside)
    second = jacobi(widen(first), padded, trans_x, trans_y, trans_z, pore_space, source, outside)
    moved = transport(widen(second), widen(saturation), trans_x, trans_y, trans_z, upwind_x, upwind_y, upwind_z, pore_space, outside)
    return (second, moved)

def reference(pressure0, saturation0, trans_x, trans_y, trans_z, pore_volume, upwind, well_cell, well_rate, plan, observed):
    grid_shape = pressure0.shape
    row_ids = lax.broadcasted_iota(jnp.int32, grid_shape, 1)
    col_ids = lax.broadcasted_iota(jnp.int32, grid_shape, 2)
    keep_x = row_ids < NX - 1
    keep_y = col_ids < NY - 1
    tile_rows = lax.broadcasted_iota(jnp.int32, well_cell.shape, 0)
    tile_cols = lax.broadcasted_iota(jnp.int32, well_cell.shape, 1)
    layer_of = well_cell // (CX * CY)
    row_of = tile_rows * CX + well_cell // CY % CX
    col_of = tile_cols * CY + well_cell % CY
    cells = (layer_of * (NX * NY) + row_of * NY + col_of).reshape(-1).astype(jnp.int32)
    outside = jnp.zeros((1, NX + 2, NY + 2), jnp.float32)
    pore_space = widen(pore_volume)

    def mismatch(trans_x, trans_y, trans_z):
        trans_xe = widen(jnp.where(keep_x, trans_x, 0.0))
        trans_ye = widen(jnp.where(keep_y, trans_y, 0.0))
        trans_zp = widen(trans_z)
        pressure, saturation = (pressure0, saturation0)
        total = jnp.zeros((), jnp.float32)
        for step_index in range(STEPS):
            rates = (well_rate * plan[step_index].astype(jnp.float32) * 0.5).reshape(-1)
            source = widen(jnp.zeros((LAYERS * NX * NY,), jnp.float32).at[cells].add(rates).reshape(grid_shape))
            bits = [jnp.bitwise_and(jnp.right_shift(upwind, 3 * step_index + direction), 1).astype(jnp.float32) for direction in range(3)]
            pressure, saturation = jax.checkpoint(advance)(pressure, saturation, trans_xe, trans_ye, trans_zp, trans_xe * widen(bits[0]), trans_ye * widen(bits[1]), trans_zp * widen(bits[2][:LAYERS - 1]), pore_space, source, outside)
            miss_p = pressure.reshape(-1)[cells] - observed[step_index, 0].reshape(-1)
            miss_s = saturation.reshape(-1)[cells] - observed[step_index, 1].reshape(-1)
            total = total + 0.5 * jnp.sum(miss_p * miss_p) + 0.5 * jnp.sum(miss_s * miss_s)
        return total
    gradients = jax.grad(mismatch, argnums=(0, 1, 2))(trans_x, trans_y, trans_z)
    return (gradients[0], gradients[1], gradients[2])
```

```python
import jax
import jax.numpy as jnp
from jax import lax
from jax.experimental import pallas as pl
from jax.experimental.pallas import tpu as pltpu
from jax.sharding import PartitionSpec as P

time_step = 0.05

GROUPS = {"p": (0, 4), "s": (4, 4), "tx": (8, 4), "ty": (12, 4), "tz": (16, 3), "pv": (19, 4), "up": (23, 4)}
ORDER = ("p", "s", "tx", "ty", "tz", "pv", "up")
COUNT = 27
SLOT = 10
SLOTS = 12
PIECES = COUNT * 4 + 4
PACKED = -(-PIECES // SLOTS)


def owned(ref, layer, rows):
    value = ref[layer, rows, :]
    return value.astype(jnp.float32)


def pack_rows(p, s, tx, ty, tz, pv, up, cell, rate, plan, observed, low, high):
    refs = dict(zip(ORDER, (p, s, tx, ty, tz, pv, up)))
    for name in ORDER:
        first, layers = GROUPS[name]
        for layer in range(layers):
            low[first + layer] = owned(refs[name], layer, slice(8, 16))
            high[first + layer] = owned(refs[name], layer, slice(0, 8))
    high[COUNT + 1] = jnp.zeros((8, 128), jnp.float32)
    for layer in range(4):
        low[COUNT, pl.ds(layer, 1), :] = p[layer, pl.ds(7, 1), :]
        low[COUNT, pl.ds(4 + layer, 1), :] = tx[layer, pl.ds(7, 1), :]
        high[COUNT, pl.ds(layer, 1), :] = p[layer, pl.ds(8, 1), :]
        high[COUNT, pl.ds(4 + layer, 1), :] = tx[layer, pl.ds(8, 1), :]
        high[COUNT + 1, pl.ds(layer, 1), :] = ty[layer, pl.ds(8, 1), :]
        if layer < 3:
            high[COUNT + 1, pl.ds(4 + layer, 1), :] = tz[layer, pl.ds(8, 1), :]
        high[COUNT + 2, pl.ds(layer, 1), :] = pv[layer, pl.ds(8, 1), :]
        high[COUNT + 2, pl.ds(4 + layer, 1), :] = p[layer, pl.ds(9, 1), :]
    for out, at in ((low, COUNT + 1), (high, COUNT + 3)):
        out[at] = jnp.zeros((8, 128), jnp.float32)
        out[at, 0:1, 0:64] = cell[0].astype(jnp.float32)
        out[at, 1:2, 0:64] = rate[0]
        for n in range(2):
            out[at, 2 + n : 3 + n, 0:64] = plan[n, 0].astype(jnp.float32)
            for k in range(2):
                row = 4 + 2 * n + k
                out[at, row : row + 1, 0:64] = observed[n, k, 0]


def lanes():
    return lax.broadcasted_iota(jnp.int32, (8, 128), 1)


def slot_masks(lane):
    from_next = [(lane >= SLOT * j) & (lane < SLOT * j + SLOT) for j in range(SLOTS)]
    from_prev = [lane >= 128 - SLOT] + from_next[: SLOTS - 1]
    return from_next, from_prev


def pack_cols(p, s, tx, ty, tz, pv, up, low, high, mine, to_prev, to_next):
    refs = dict(zip(ORDER, (p, s, tx, ty, tz, pv, up)))
    lane = lanes()
    first_cols, last_cols = slot_masks(lane)
    zero = jnp.zeros((8, 128), jnp.float32)
    blocks = []
    for name in ORDER:
        first, layers = GROUPS[name]
        for layer in range(layers):
            blocks.append(lambda g=first + layer: low[g])
            blocks.append(lambda r=refs[name], k=layer: owned(r, k, slice(0, 8)))
            blocks.append(lambda r=refs[name], k=layer: owned(r, k, slice(8, 16)))
            blocks.append(lambda g=first + layer: high[g])
    blocks.append(lambda: low[COUNT])
    for extra in range(3):
        blocks.append(lambda g=COUNT + extra: high[g])
    for at in range(PACKED):
        prev_part, next_part = zero, zero
        for j, block in enumerate(blocks[at * SLOTS : (at + 1) * SLOTS]):
            moved = block()
            if j:
                moved = pltpu.roll(moved, SLOT * j, 1)
            prev_part = jnp.where(first_cols[j], moved, prev_part)
            next_part = jnp.where(last_cols[j], moved, next_part)
        to_prev[at] = prev_part
        to_next[at] = next_part
    pair = jnp.where(lane < 64, mine[COUNT + 1], pltpu.roll(low[COUNT + 1], 64, 1))
    for out in (to_prev, to_next):
        out[PACKED] = pair
        out[PACKED + 1] = high[COUNT + 3]


def split3(value):
    hi = value.astype(jnp.bfloat16).astype(jnp.float32)
    rest = value - hi
    mid = rest.astype(jnp.bfloat16).astype(jnp.float32)
    return hi, mid, rest - mid


def scatter_wells(lists, keep, dense, half):
    info = jnp.concatenate(lists, axis=1)
    width = info.shape[1]
    cell = info[0:1].astype(jnp.int32)
    lane = lax.broadcasted_iota(jnp.int32, (1, width), 1)
    base, low, high = keep(lane)
    layer = lax.shift_right_logical(cell, 11)
    row = lax.shift_right_logical(cell, 7) & 15
    col = cell & 127
    place = row + base
    inside = (place >= 8) & (col >= low) & (col < high)
    target = jnp.where(inside, layer * 40 + place - 8, -1)
    rows = lax.broadcasted_iota(jnp.int32, (160, width), 0)
    hit = rows == target
    cols = lax.broadcasted_iota(jnp.int32, (128, width), 0)
    to_col = jnp.where(cols == col, 1.0, 0.0).astype(jnp.bfloat16)
    rate = info[1:2] * 0.5
    values = [
        rate * info[2:3],
        rate * info[3:4],
        info[4:5],
        info[5:6],
        info[6:7],
        info[7:8],
    ]
    dims = (((1,), (1,)), ((), ()))
    for number, value in enumerate(values):
        total = None
        for part in split3(value):
            left = jnp.where(hit, part, 0.0).astype(jnp.bfloat16)
            term = lax.dot_general(left, to_col, dims, preferred_element_type=jnp.float32)
            total = term if total is None else total + term
        for k in range(4):
            dense[number, k, half, 8:48, :] = total[k * 40 : k * 40 + 40]
    left = jnp.where(hit, 1.0, 0.0).astype(jnp.bfloat16)
    total = lax.dot_general(left, to_col, dims, preferred_element_type=jnp.float32)
    for k in range(4):
        dense[6, k, half, 8:48, :] = total[k * 40 : k * 40 + 40]


SRC0, SRC1, OP0, OS0, OP1, OS1, CNT = range(7)


def model(
    p, s, tx, ty, tz, pv, up, low, high, mine, from_prev, from_next,
    grad_x, grad_y, grad_z,
    fld, dense, upi, rcp, tym, q0, p1, q1, p2, f0, d0, s1, f1, d1, fup0, fup1, dp1, dp2,
    sig2, psi2, psi1, mup2, muq1, mup1, muq0, flux, rest,
):
    refs = dict(zip(ORDER, (p, s, tx, ty, tz, pv, up)))
    lane = lanes()
    at_end = lane == 127
    at_start = lane == 0
    first_cols, last_cols = slot_masks(lane)

    def unpack(piece):
        at, j = piece // SLOTS, piece % SLOTS
        both = jnp.where(first_cols[j], from_next[at], from_prev[at])
        return pltpu.roll(both, 128 - SLOT * j, 1) if j else both

    for name in ORDER:
        first, layers = GROUPS[name]
        for layer in range(layers):
            g = first + layer
            center = [
                low[g],
                owned(refs[name], layer, slice(0, 8)),
                owned(refs[name], layer, slice(8, 16)),
                high[g],
            ]
            halo = [unpack(g * 4 + k) for k in range(4)]
            for k in range(4):
                rows = slice(8 + 8 * k, 16 + 8 * k)
                if name == "up":
                    upi[layer, 0, rows, :] = center[k].astype(jnp.int32)
                    upi[layer, 1, rows, :] = halo[k].astype(jnp.int32)
                else:
                    fld[g, 0, rows, :] = center[k]
                    fld[g, 1, rows, :] = halo[k]
    PB, SB, XB, YB, ZB, VB = (GROUPS[name][0] for name in ORDER[:6])
    extras = [
        (low[COUNT], unpack(COUNT * 4), [(PB, 7), (XB, 7)]),
        (high[COUNT], unpack(COUNT * 4 + 1), [(PB, 40), (XB, 40)]),
        (high[COUNT + 1], unpack(COUNT * 4 + 2), [(YB, 40), (ZB, 40)]),
        (high[COUNT + 2], unpack(COUNT * 4 + 3), [(VB, 40), (PB, 41)]),
    ]
    for center, halo, places in extras:
        for block, (base, row) in enumerate(places):
            for layer in range(3 if base == ZB else 4):
                k = 4 * block + layer
                fld[base + layer, 0, row : row + 1, :] = center[k : k + 1]
                fld[base + layer, 1, row : row + 1, :] = halo[k : k + 1]

    def across(at):
        return [at[PACKED], at[PACKED + 1][:, 0:64]]

    def base_of(lane, own_first):
        return own_first

    scatter_wells(
        [mine[COUNT + 1][:, 0:64], low[COUNT + 1][:, 0:64], high[COUNT + 3][:, 0:64]],
        lambda w: (jnp.where(w < 64, 16, jnp.where(w < 128, 0, 32)), 0, 128),
        dense,
        0,
    )

    def beside(w):
        within = jnp.where(w >= 192, w - 192, w)
        base = jnp.where(within < 64, 16, jnp.where(within < 128, 0, 32))
        return base, jnp.where(w < 192, 128 - SLOT, 0), jnp.where(w < 192, 128, SLOT)

    scatter_wells(across(from_prev) + across(from_next), beside, dense, 1)

    def here(ref, k, t):
        rows = slice(8 * t, 8 * t + 8)
        return ref[k, 0, rows, :], ref[k, 1, rows, :]

    def down(ref, k, t):
        rows = slice(8 * t + 1, 8 * t + 9)
        return ref[k, 0, rows, :], ref[k, 1, rows, :]

    def above(ref, k, t):
        rows = slice(8 * t - 1, 8 * t + 7)
        return ref[k, 0, rows, :], ref[k, 1, rows, :]

    def put(ref, k, t, pair):
        rows = slice(8 * t, 8 * t + 8)
        ref[k, 0, rows, :] = pair[0]
        ref[k, 1, rows, :] = pair[1]

    def right(pair):
        a, b = pltpu.roll(pair[0], 127, 1), pltpu.roll(pair[1], 127, 1)
        return jnp.where(at_end, b, a), jnp.where(at_end, a, b)

    def left(pair):
        a, b = pltpu.roll(pair[0], 1, 1), pltpu.roll(pair[1], 1, 1)
        return jnp.where(at_start, b, a), jnp.where(at_start, a, b)

    def both(f, *pairs):
        return tuple(f(*(pair[h] for pair in pairs)) for h in range(2))

    def add(a, b):
        return both(lambda x, y: x + y, a, b)

    def sub(a, b):
        return both(lambda x, y: x - y, a, b)

    def mul(a, b):
        return both(lambda x, y: x * y, a, b)

    for t in range(1, 6):
        for k in range(4):
            volume = here(fld, VB + k, t)
            beyond = right(volume)
            put(fld, YB + k, t, both(lambda v, y: jnp.where(v == 0.0, 0.0, y), beyond, here(fld, YB + k, t)))
    for k in range(4):
        volume_below = fld[VB + k, 0, 32:33, :], fld[VB + k, 1, 32:33, :]
        for h in range(2):
            fld[XB + k, h, 31:32, :] = jnp.where(volume_below[h] == 0.0, 0.0, fld[XB + k, h, 31:32, :])
    for t in range(1, 6):
        for k in range(4):
            volume = both(lambda v: jnp.where(v == 0.0, 1.0, v), here(fld, VB + k, t))
            put(fld, VB + k, t, volume)
            west = left(here(fld, YB + k, t))
            put(tym, k, t, west)
            total = add(volume, add(here(fld, XB + k, t), above(fld, XB + k, t)))
            total = add(total, add(here(fld, YB + k, t), west))
            if k < 3:
                total = add(total, here(fld, ZB + k, t))
            if k > 0:
                total = add(total, here(fld, ZB + k - 1, t))
            put(rcp, k, t, both(lambda v: 1.0 / v, total))

    def neighbours(ref, base, k, t):
        value = here(ref, base + k, t)
        total = mul(here(fld, XB + k, t), down(ref, base + k, t))
        total = add(total, mul(above(fld, XB + k, t), above(ref, base + k, t)))
        total = add(total, mul(here(fld, YB + k, t), right(value)))
        total = add(total, mul(here(tym, k, t), left(value)))
        if k < 3:
            total = add(total, mul(here(fld, ZB + k, t), here(ref, base + k + 1, t)))
        if k > 0:
            total = add(total, mul(here(fld, ZB + k - 1, t), here(ref, base + k - 1, t)))
        return total

    def relax(out, ref, base, old, old_base, source, tiles):
        for t in tiles:
            for k in range(4):
                total = add(
                    mul(here(fld, VB + k, t), here(old, old_base + k, t)), here(dense.at[source], k, t)
                )
                total = add(total, neighbours(ref, base, k, t))
                put(out, k, t, mul(total, here(rcp, k, t)))

    def mobility(value):
        rest_of = 1.0 - value
        wetted = value * value
        inverse = 1.0 / (wetted + 0.5 * rest_of * rest_of)
        return wetted * inverse, value * rest_of * inverse * inverse

    def put_mobility(value, k, t, mobile, slope):
        pairs = [mobility(v) for v in value]
        put(mobile, k, t, (pairs[0][0], pairs[1][0]))
        put(slope, k, t, (pairs[0][1], pairs[1][1]))

    def bit(k, t, number):
        return both(lambda v: (v & (1 << number)) != 0, here(upi, k, t))

    def choose(mask, a, b):
        return both(lambda m, x, y: jnp.where(m, x, y), mask, a, b)

    def transport(pressure, sat, sat_base, mobile, n, fup, dp, finish):
        for t in range(1, 5):
            below = None
            for k in range(4):
                mob = here(mobile, k, t)
                pres = here(pressure, k, t)
                drop_x = sub(pres, down(pressure, k, t))
                drop_y = sub(pres, right(pres))
                up_x = choose(bit(k, t, 3 * n), mob, down(mobile, k, t))
                up_y = choose(bit(k, t, 3 * n + 1), mob, right(mob))
                put(fup, k, t, up_x)
                put(fup, 4 + k, t, up_y)
                put(dp, k, t, drop_x)
                put(dp, 4 + k, t, drop_y)
                flux_x = mul(mul(here(fld, XB + k, t), up_x), drop_x)
                flux_y = mul(mul(here(fld, YB + k, t), up_y), drop_y)
                put(flux, k, t, flux_x)
                net = add(sub(flux_x, above(flux, k, t)), sub(flux_y, left(flux_y)))
                if k < 3:
                    drop_z = sub(pres, here(pressure, k + 1, t))
                    up_z = choose(bit(k, t, 3 * n + 2), mob, here(mobile, k + 1, t))
                    put(fup, 8 + k, t, up_z)
                    put(dp, 8 + k, t, drop_z)
                    flux_z = mul(mul(here(fld, ZB + k, t), up_z), drop_z)
                    net = add(net, flux_z)
                if k > 0:
                    net = sub(net, below)
                below = flux_z
                moved = both(
                    lambda o, f, v: o - time_step * f / v,
                    here(sat, sat_base + k, t),
                    net,
                    here(fld, VB + k, t),
                )
                finish(moved, k, t)

    tiles = range(1, 5)
    relax(q0, fld, PB, fld, PB, SRC0, range(1, 6))
    relax(p1, q0, 0, fld, PB, SRC0, tiles)
    for t in tiles:
        for k in range(4):
            put_mobility(here(fld, SB + k, t), k, t, f0, d0)

    def finish_first(moved, k, t):
        put(s1, k, t, moved)
        put_mobility(moved, k, t, f1, d1)

    transport(p1, fld, SB, f0, 0, fup0, dp1, finish_first)
    relax(q1, p1, 0, p1, 0, SRC1, tiles)
    relax(p2, q1, 0, p1, 0, SRC1, tiles)

    def finish_second(moved, k, t):
        miss = sub(mul(here(dense.at[CNT], k, t), moved), here(dense.at[OS1], k, t))
        put(sig2, k, t, miss)
        put(psi2, k, t, both(lambda m, v: time_step * m / v, miss, here(fld, VB + k, t)))

    transport(p2, s1, 0, f1, 1, fup1, dp2, finish_second)

    for t in tiles:
        below_h = below_r = None
        for k in range(4):
            psi = here(psi2, k, t)
            phi_x = mul(sub(down(psi2, k, t), psi), here(fld, XB + k, t))
            phi_y = mul(sub(right(psi), psi), here(fld, YB + k, t))
            h_x = mul(phi_x, here(fup1, k, t))
            h_y = mul(phi_y, here(fup1, 4 + k, t))
            k_x = mul(phi_x, here(dp2, k, t))
            k_y = mul(phi_y, here(dp2, 4 + k, t))
            zero = (jnp.zeros((8, 128), jnp.float32),) * 2
            s_x = choose(bit(k, t, 3), k_x, zero)
            s_y = choose(bit(k, t, 4), k_y, zero)
            r_x = sub(k_x, s_x)
            r_y = sub(k_y, s_y)
            put(flux, k, t, h_x)
            put(rest, k, t, r_x)
            press = add(sub(h_x, above(flux, k, t)), sub(h_y, left(h_y)))
            satur = add(add(s_x, above(rest, k, t)), add(s_y, left(r_y)))
            if k < 3:
                phi_z = mul(sub(here(psi2, k + 1, t), psi), here(fld, ZB + k, t))
                h_z = mul(phi_z, here(fup1, 8 + k, t))
                k_z = mul(phi_z, here(dp2, 8 + k, t))
                s_z = choose(bit(k, t, 5), k_z, zero)
                press = add(press, h_z)
                satur = add(satur, s_z)
            if k > 0:
                press = sub(press, below_h)
                satur = add(satur, below_r)
            if k < 3:
                below_h, below_r = h_z, sub(k_z, s_z)
            count = here(dense.at[CNT], k, t)
            press = add(press, sub(mul(count, here(p2, k, t)), here(dense.at[OP1], k, t)))
            put(mup2, k, t, mul(press, here(rcp, k, t)))
            sigma = add(here(sig2, k, t), mul(satur, here(d1, k, t)))
            sigma = add(sigma, sub(mul(count, here(s1, k, t)), here(dense.at[OS0], k, t)))
            put(psi1, k, t, both(lambda m, v: time_step * m / v, sigma, here(fld, VB + k, t)))

    for t in tiles:
        for k in range(4):
            put(muq1, k, t, mul(neighbours(mup2, 0, k, t), here(rcp, k, t)))

    for t in tiles:
        below_h = None
        for k in range(4):
            psi = here(psi1, k, t)
            h_x = mul(mul(sub(down(psi1, k, t), psi), here(fld, XB + k, t)), here(fup0, k, t))
            h_y = mul(mul(sub(right(psi), psi), here(fld, YB + k, t)), here(fup0, 4 + k, t))
            put(flux, k, t, h_x)
            press = add(sub(h_x, above(flux, k, t)), sub(h_y, left(h_y)))
            if k < 3:
                h_z = mul(mul(sub(here(psi1, k + 1, t), psi), here(fld, ZB + k, t)), here(fup0, 8 + k, t))
                press = add(press, h_z)
            if k > 0:
                press = sub(press, below_h)
            below_h = h_z
            count = here(dense.at[CNT], k, t)
            press = add(press, sub(mul(count, here(p1, k, t)), here(dense.at[OP0], k, t)))
            carried = mul(here(fld, VB + k, t), add(here(mup2, k, t), here(muq1, k, t)))
            press = add(press, add(carried, neighbours(muq1, 0, k, t)))
            put(mup1, k, t, mul(press, here(rcp, k, t)))

    for t in range(2, 5):
        for k in range(4):
            put(muq0, k, t, mul(neighbours(mup1, 0, k, t), here(rcp, k, t)))

    stages = (
        (mup2, q1, 0, p2, 0),
        (muq1, p1, 0, q1, 0),
        (mup1, q0, 0, p1, 0),
        (muq0, fld, PB, q0, 0),
    )
    for t in range(2, 4):
        rows = slice(8 * t - 16, 8 * t - 8)
        for k in range(4):
            sum_x = sum_y = sum_z = None
            for mu, value, value_base, out, out_base in stages:
                mu_c, v_c, o_c = here(mu, k, t), here(value, value_base + k, t), here(out, out_base + k, t)
                mu_d, v_d, o_d = down(mu, k, t), down(value, value_base + k, t), down(out, out_base + k, t)
                term = mu_c[0] * (v_d[0] - o_c[0]) + mu_d[0] * (v_c[0] - o_d[0])
                sum_x = term if sum_x is None else sum_x + term
                mu_r, v_r, o_r = right(mu_c), right(v_c), right(o_c)
                term = mu_c[0] * (v_r[0] - o_c[0]) + mu_r[0] * (v_c[0] - o_r[0])
                sum_y = term if sum_y is None else sum_y + term
                if k < 3:
                    mu_u = here(mu, k + 1, t)
                    v_u = here(value, value_base + k + 1, t)
                    o_u = here(out, out_base + k + 1, t)
                    term = mu_c[0] * (v_u[0] - o_c[0]) + mu_u[0] * (v_c[0] - o_u[0])
                    sum_z = term if sum_z is None else sum_z + term
            for psi, fup, dp in ((psi2, fup1, dp2), (psi1, fup0, dp1)):
                mid = here(psi, k, t)
                phi = down(psi, k, t)[0] - mid[0]
                sum_x = sum_x + phi * here(fup, k, t)[0] * here(dp, k, t)[0]
                phi = right(mid)[0] - mid[0]
                sum_y = sum_y + phi * here(fup, 4 + k, t)[0] * here(dp, 4 + k, t)[0]
                if k < 3:
                    phi = here(psi, k + 1, t)[0] - mid[0]
                    sum_z = sum_z + phi * here(fup, 8 + k, t)[0] * here(dp, 8 + k, t)[0]
            grad_x[k, rows, :] = jnp.where(here(fld, XB + k, t)[0] == 0.0, 0.0, sum_x)
            grad_y[k, rows, :] = jnp.where(here(fld, YB + k, t)[0] == 0.0, 0.0, sum_y)
            if k < 3:
                grad_z[k, rows, :] = sum_z


def shifted(value, axis, by):
    count = lax.axis_size(axis)
    pairs = [(i, i + by) for i in range(count) if 0 <= i + by < count]
    return lax.ppermute(value, axis, pairs)


def on_device(p, s, tx, ty, tz, pv, up, cell, rate, plan, observed):
    f32 = jnp.float32

    def shape(*dims):
        return jax.ShapeDtypeStruct(dims, f32)

    limit = pltpu.CompilerParams(vmem_limit_bytes=48 * 1024 * 1024)
    fields = (p, s, tx, ty, tz, pv, up)
    to_down, to_up = pl.pallas_call(
        pack_rows,
        out_shape=(shape(COUNT + 2, 8, 128), shape(COUNT + 4, 8, 128)),
        compiler_params=limit,
        name="pack_rows",
    )(*fields, cell, rate, plan, observed)
    low = shifted(to_down, "gx", 1)
    high = shifted(to_up, "gx", -1)
    to_prev, to_next = pl.pallas_call(
        pack_cols,
        out_shape=(shape(PACKED + 2, 8, 128), shape(PACKED + 2, 8, 128)),
        compiler_params=limit,
        name="pack_cols",
    )(*fields, low, high, to_down)
    from_prev = shifted(to_next, "gy", 1)
    from_next = shifted(to_prev, "gy", -1)

    def cells(count, dtype=f32):
        return pltpu.VMEM((count, 2, 56, 128), dtype)

    scratch = [cells(23), pltpu.VMEM((7, 4, 2, 56, 128), f32), cells(4, jnp.int32)]
    scratch += [cells(4) for _ in range(11)]
    scratch += [cells(11) for _ in range(4)]
    scratch += [cells(4) for _ in range(9)]
    return pl.pallas_call(
        model,
        out_shape=(shape(*tx.shape), shape(*ty.shape), shape(*tz.shape)),
        scratch_shapes=scratch,
        compiler_params=limit,
        name="model",
    )(*fields, low, high, to_down, from_prev, from_next)


def solution(mesh):
    cells = P(None, "gx", "gy")
    in_specs = (cells,) * 7 + (
        P("gx", "gy", None),
        P("gx", "gy", None),
        P(None, "gx", "gy", None),
        P(None, None, "gx", "gy", None),
    )
    return jax.shard_map(
        on_device, mesh=mesh, in_specs=in_specs, out_specs=(cells,) * 3, check_vma=False
    )
```

```python
import jax
import jax.numpy as jnp
from jax import lax
from jax.experimental import pallas as pl
from jax.experimental.pallas import tpu as pltpu
from jax.sharding import PartitionSpec as P

time_step = 0.05

GROUPS = {"p": (0, 4), "s": (4, 4), "tx": (8, 4), "ty": (12, 4), "tz": (16, 3), "pv": (19, 4), "up": (23, 4)}
ORDER = ("p", "s", "tx", "ty", "tz", "pv", "up")
COUNT = 27
SLOT = 10
SLOTS = 12
PIECES = COUNT * 4 + 4
PACKED = -(-PIECES // SLOTS)


FIELDS = 11


def pack_rows(*refs):
    p, s, tx, ty, tz, pv, up, cell, rate, plan, observed = refs[:FIELDS]
    own, far, near, upi, cells, rates, plans, seen, sems = refs[FIELDS:]
    targets = [own.at[pl.ds(*GROUPS[name])] for name in ORDER[:6]] + [upi, cells, rates, plans, seen]
    copies = [
        pltpu.make_async_copy(source, target, sems.at[k])
        for k, (source, target) in enumerate(zip(refs[:FIELDS], targets))
    ]
    for copy in copies:
        copy.start()
    for copy in copies:
        copy.wait()
    first = GROUPS["up"][0]
    for layer in range(4):
        own[first + layer] = upi[layer].astype(jnp.float32)
    own[COUNT] = jnp.zeros((16, 128), jnp.float32)
    own[COUNT, 0:1, 0:64] = cells[0].astype(jnp.float32)
    own[COUNT, 1:2, 0:64] = rates[0]
    for n in range(2):
        own[COUNT, 2 + n : 3 + n, 0:64] = plans[n, 0].astype(jnp.float32)
        for k in range(2):
            row = 4 + 2 * n + k
            own[COUNT, row : row + 1, 0:64] = seen[n, k, 0]
    odd = lax.axis_index("gx") & 1
    for g in range(COUNT):
        far[g] = own[g, pl.ds(pl.multiple_of(8 * odd, 8), 8), :]
        near[g] = own[g, pl.ds(pl.multiple_of(8 - 8 * odd, 8), 8), :]
    base = {name: GROUPS[name][0] for name in ORDER}

    def rows_of(name, row):
        return [own[base[name] + layer, row : row + 1, :] for layer in range(GROUPS[name][1])]

    blank = jnp.zeros((1, 128), jnp.float32)
    for_next = [jnp.concatenate(rows_of("p", 7) + rows_of("tx", 7), axis=0)]
    for_next += [jnp.zeros((8, 128), jnp.float32)] * 2
    for_prev = [
        jnp.concatenate(rows_of("p", 8) + rows_of("tx", 8), axis=0),
        jnp.concatenate(rows_of("ty", 8) + rows_of("tz", 8) + [blank], axis=0),
        jnp.concatenate(rows_of("pv", 8) + rows_of("p", 9), axis=0),
    ]
    for k in range(3):
        far[COUNT + k] = jnp.where(odd == 1, for_next[k], for_prev[k])
        near[COUNT + k] = jnp.where(odd == 1, for_prev[k], for_next[k])
    far[COUNT + 3] = own[COUNT, 0:8, :]
    near[COUNT + 3] = own[COUNT, 0:8, :]


def lanes():
    return lax.broadcasted_iota(jnp.int32, (8, 128), 1)


def in_slot(lane, start):
    return ((lane - start) & 127) < SLOT


def sorted_ends(axis, far, near):
    odd = (lax.axis_index(axis) & 1) == 1

    def before(g):
        return jnp.where(odd, near[g], far[g])

    def after(g):
        return jnp.where(odd, far[g], near[g])

    return before, after


def pack_cols(own, row_far, row_near, far, near):
    low, high = sorted_ends("gx", row_far, row_near)
    odd = lax.axis_index("gy") & 1
    lane = lanes()
    far_cols = [in_slot(lane, SLOT * (j - odd)) for j in range(SLOTS)]
    near_cols = [in_slot(lane, SLOT * (j - 1 + odd)) for j in range(SLOTS)]
    zero = jnp.zeros((8, 128), jnp.float32)
    blocks = []
    for g in range(COUNT):
        blocks.append(lambda g=g: low(g))
        blocks.append(lambda g=g: own[g, 0:8, :])
        blocks.append(lambda g=g: own[g, 8:16, :])
        blocks.append(lambda g=g: high(g))
    blocks.append(lambda: low(COUNT))
    for extra in range(3):
        blocks.append(lambda g=COUNT + extra: high(g))
    for at in range(PACKED):
        far_part, near_part = zero, zero
        for j, block in enumerate(blocks[at * SLOTS : (at + 1) * SLOTS]):
            moved = block()
            if j:
                moved = pltpu.roll(moved, SLOT * j, 1)
            far_part = jnp.where(far_cols[j], moved, far_part)
            near_part = jnp.where(near_cols[j], moved, near_part)
        far[at] = far_part
        near[at] = near_part
    pair = jnp.where(lane < 64, own[COUNT, 0:8, :], pltpu.roll(low(COUNT + 3), 64, 1))
    for out in (far, near):
        out[PACKED] = pair
        out[PACKED + 1] = high(COUNT + 3)


def split3(value):
    hi = value.astype(jnp.bfloat16).astype(jnp.float32)
    rest = value - hi
    mid = rest.astype(jnp.bfloat16).astype(jnp.float32)
    return hi, mid, rest - mid


def scatter_wells(lists, keep, dense, half):
    info = jnp.concatenate(lists, axis=1)
    width = info.shape[1]
    cell = info[0:1].astype(jnp.int32)
    lane = lax.broadcasted_iota(jnp.int32, (1, width), 1)
    base, low, high = keep(lane)
    layer = lax.shift_right_logical(cell, 11)
    row = lax.shift_right_logical(cell, 7) & 15
    col = cell & 127
    place = row + base
    inside = (place >= 8) & (col >= low) & (col < high)
    target = jnp.where(inside, layer * 40 + place - 8, -1)
    rows = lax.broadcasted_iota(jnp.int32, (160, width), 0)
    hit = rows == target
    cols = lax.broadcasted_iota(jnp.int32, (128, width), 0)
    to_col = jnp.where(cols == col, 1.0, 0.0).astype(jnp.bfloat16)
    rate = info[1:2] * 0.5
    values = [
        rate * info[2:3],
        rate * info[3:4],
        info[4:5],
        info[5:6],
        info[6:7],
        info[7:8],
    ]
    dims = (((1,), (1,)), ((), ()))
    for number, value in enumerate(values):
        total = None
        for part in split3(value):
            left = jnp.where(hit, part, 0.0).astype(jnp.bfloat16)
            term = lax.dot_general(left, to_col, dims, preferred_element_type=jnp.float32)
            total = term if total is None else total + term
        for k in range(4):
            dense[number, k, half, 8:48, :] = total[k * 40 : k * 40 + 40]
    left = jnp.where(hit, 1.0, 0.0).astype(jnp.bfloat16)
    total = lax.dot_general(left, to_col, dims, preferred_element_type=jnp.float32)
    for k in range(4):
        dense[6, k, half, 8:48, :] = total[k * 40 : k * 40 + 40]


SRC0, SRC1, OP0, OS0, OP1, OS1, CNT = range(7)


def model(
    own, row_far, row_near, col_far, col_near,
    grad_x, grad_y, grad_z,
    fld, dense, upi, rcp, tym, q0, p1, q1, p2, f0, d0, s1, f1, d1, fup0, fup1, dp1, dp2,
    sig2, psi2, psi1, mup2, muq1, mup1, muq0, flux, rest,
):
    low, high = sorted_ends("gx", row_far, row_near)
    from_prev, from_next = sorted_ends("gy", col_far, col_near)
    lane = lanes()
    at_end = lane == 127
    at_start = lane == 0
    odd_col = lax.axis_index("gy") & 1
    far_cols = [in_slot(lane, SLOT * (j - 1 + odd_col)) for j in range(SLOTS)]

    def unpack(piece):
        at, j = piece // SLOTS, piece % SLOTS
        both = jnp.where(far_cols[j], col_far[at], col_near[at])
        return pltpu.roll(both, 128 - SLOT * j, 1) if j else both

    for name in ORDER:
        first, layers = GROUPS[name]
        for layer in range(layers):
            g = first + layer
            center = [
                low(g),
                own[g, 0:8, :],
                own[g, 8:16, :],
                high(g),
            ]
            halo = [unpack(g * 4 + k) for k in range(4)]
            for k in range(4):
                rows = slice(8 + 8 * k, 16 + 8 * k)
                if name == "up":
                    upi[layer, 0, rows, :] = center[k].astype(jnp.int32)
                    upi[layer, 1, rows, :] = halo[k].astype(jnp.int32)
                else:
                    fld[g, 0, rows, :] = center[k]
                    fld[g, 1, rows, :] = halo[k]
    PB, SB, XB, YB, ZB, VB = (GROUPS[name][0] for name in ORDER[:6])
    extras = [
        (low(COUNT), unpack(COUNT * 4), [(PB, 7), (XB, 7)]),
        (high(COUNT), unpack(COUNT * 4 + 1), [(PB, 40), (XB, 40)]),
        (high(COUNT + 1), unpack(COUNT * 4 + 2), [(YB, 40), (ZB, 40)]),
        (high(COUNT + 2), unpack(COUNT * 4 + 3), [(VB, 40), (PB, 41)]),
    ]
    for center, halo, places in extras:
        for block, (base, row) in enumerate(places):
            for layer in range(3 if base == ZB else 4):
                k = 4 * block + layer
                fld[base + layer, 0, row : row + 1, :] = center[k : k + 1]
                fld[base + layer, 1, row : row + 1, :] = halo[k : k + 1]

    def across(at):
        return [at(PACKED), at(PACKED + 1)[:, 0:64]]

    scatter_wells(
        [own[COUNT, 0:8, 0:64], low(COUNT + 3)[:, 0:64], high(COUNT + 3)[:, 0:64]],
        lambda w: (jnp.where(w < 64, 16, jnp.where(w < 128, 0, 32)), 0, 128),
        dense,
        0,
    )

    def beside(w):
        within = jnp.where(w >= 192, w - 192, w)
        base = jnp.where(within < 64, 16, jnp.where(within < 128, 0, 32))
        return base, jnp.where(w < 192, 128 - SLOT, 0), jnp.where(w < 192, 128, SLOT)

    scatter_wells(across(from_prev) + across(from_next), beside, dense, 1)

    def here(ref, k, t):
        rows = slice(8 * t, 8 * t + 8)
        return ref[k, 0, rows, :], ref[k, 1, rows, :]

    def down(ref, k, t):
        rows = slice(8 * t + 1, 8 * t + 9)
        return ref[k, 0, rows, :], ref[k, 1, rows, :]

    def above(ref, k, t):
        rows = slice(8 * t - 1, 8 * t + 7)
        return ref[k, 0, rows, :], ref[k, 1, rows, :]

    def put(ref, k, t, pair):
        rows = slice(8 * t, 8 * t + 8)
        ref[k, 0, rows, :] = pair[0]
        ref[k, 1, rows, :] = pair[1]

    def right(pair):
        a, b = pltpu.roll(pair[0], 127, 1), pltpu.roll(pair[1], 127, 1)
        return jnp.where(at_end, b, a), jnp.where(at_end, a, b)

    def left(pair):
        a, b = pltpu.roll(pair[0], 1, 1), pltpu.roll(pair[1], 1, 1)
        return jnp.where(at_start, b, a), jnp.where(at_start, a, b)

    def both(f, *pairs):
        return tuple(f(*(pair[h] for pair in pairs)) for h in range(2))

    def add(a, b):
        return both(lambda x, y: x + y, a, b)

    def sub(a, b):
        return both(lambda x, y: x - y, a, b)

    def mul(a, b):
        return both(lambda x, y: x * y, a, b)

    for t in range(1, 6):
        for k in range(4):
            volume = here(fld, VB + k, t)
            beyond = right(volume)
            put(fld, YB + k, t, both(lambda v, y: jnp.where(v == 0.0, 0.0, y), beyond, here(fld, YB + k, t)))
    for k in range(4):
        volume_below = fld[VB + k, 0, 32:33, :], fld[VB + k, 1, 32:33, :]
        for h in range(2):
            fld[XB + k, h, 31:32, :] = jnp.where(volume_below[h] == 0.0, 0.0, fld[XB + k, h, 31:32, :])
    for t in range(1, 6):
        for k in range(4):
            volume = both(lambda v: jnp.where(v == 0.0, 1.0, v), here(fld, VB + k, t))
            put(fld, VB + k, t, volume)
            west = left(here(fld, YB + k, t))
            put(tym, k, t, west)
            total = add(volume, add(here(fld, XB + k, t), above(fld, XB + k, t)))
            total = add(total, add(here(fld, YB + k, t), west))
            if k < 3:
                total = add(total, here(fld, ZB + k, t))
            if k > 0:
                total = add(total, here(fld, ZB + k - 1, t))
            put(rcp, k, t, both(lambda v: 1.0 / v, total))

    def neighbours(ref, base, k, t):
        value = here(ref, base + k, t)
        total = mul(here(fld, XB + k, t), down(ref, base + k, t))
        total = add(total, mul(above(fld, XB + k, t), above(ref, base + k, t)))
        total = add(total, mul(here(fld, YB + k, t), right(value)))
        total = add(total, mul(here(tym, k, t), left(value)))
        if k < 3:
            total = add(total, mul(here(fld, ZB + k, t), here(ref, base + k + 1, t)))
        if k > 0:
            total = add(total, mul(here(fld, ZB + k - 1, t), here(ref, base + k - 1, t)))
        return total

    def relax(out, ref, base, old, old_base, source, tiles):
        for t in tiles:
            for k in range(4):
                total = add(
                    mul(here(fld, VB + k, t), here(old, old_base + k, t)), here(dense.at[source], k, t)
                )
                total = add(total, neighbours(ref, base, k, t))
                put(out, k, t, mul(total, here(rcp, k, t)))

    def mobility(value):
        rest_of = 1.0 - value
        wetted = value * value
        inverse = 1.0 / (wetted + 0.5 * rest_of * rest_of)
        return wetted * inverse, value * rest_of * inverse * inverse

    def put_mobility(value, k, t, mobile, slope):
        pairs = [mobility(v) for v in value]
        put(mobile, k, t, (pairs[0][0], pairs[1][0]))
        put(slope, k, t, (pairs[0][1], pairs[1][1]))

    def bit(k, t, number):
        return both(lambda v: (v & (1 << number)) != 0, here(upi, k, t))

    def choose(mask, a, b):
        return both(lambda m, x, y: jnp.where(m, x, y), mask, a, b)

    def transport(pressure, sat, sat_base, mobile, n, fup, dp, finish):
        for t in range(1, 5):
            below = None
            for k in range(4):
                mob = here(mobile, k, t)
                pres = here(pressure, k, t)
                drop_x = sub(pres, down(pressure, k, t))
                drop_y = sub(pres, right(pres))
                up_x = choose(bit(k, t, 3 * n), mob, down(mobile, k, t))
                up_y = choose(bit(k, t, 3 * n + 1), mob, right(mob))
                put(fup, k, t, up_x)
                put(fup, 4 + k, t, up_y)
                put(dp, k, t, drop_x)
                put(dp, 4 + k, t, drop_y)
                flux_x = mul(mul(here(fld, XB + k, t), up_x), drop_x)
                flux_y = mul(mul(here(fld, YB + k, t), up_y), drop_y)
                put(flux, k, t, flux_x)
                net = add(sub(flux_x, above(flux, k, t)), sub(flux_y, left(flux_y)))
                if k < 3:
                    drop_z = sub(pres, here(pressure, k + 1, t))
                    up_z = choose(bit(k, t, 3 * n + 2), mob, here(mobile, k + 1, t))
                    put(fup, 8 + k, t, up_z)
                    put(dp, 8 + k, t, drop_z)
                    flux_z = mul(mul(here(fld, ZB + k, t), up_z), drop_z)
                    net = add(net, flux_z)
                if k > 0:
                    net = sub(net, below)
                below = flux_z
                moved = both(
                    lambda o, f, v: o - time_step * f / v,
                    here(sat, sat_base + k, t),
                    net,
                    here(fld, VB + k, t),
                )
                finish(moved, k, t)

    tiles = range(1, 5)
    relax(q0, fld, PB, fld, PB, SRC0, range(1, 6))
    relax(p1, q0, 0, fld, PB, SRC0, tiles)
    for t in tiles:
        for k in range(4):
            put_mobility(here(fld, SB + k, t), k, t, f0, d0)

    def finish_first(moved, k, t):
        put(s1, k, t, moved)
        put_mobility(moved, k, t, f1, d1)

    transport(p1, fld, SB, f0, 0, fup0, dp1, finish_first)
    relax(q1, p1, 0, p1, 0, SRC1, tiles)
    relax(p2, q1, 0, p1, 0, SRC1, tiles)

    def finish_second(moved, k, t):
        miss = sub(mul(here(dense.at[CNT], k, t), moved), here(dense.at[OS1], k, t))
        put(sig2, k, t, miss)
        put(psi2, k, t, both(lambda m, v: time_step * m / v, miss, here(fld, VB + k, t)))

    transport(p2, s1, 0, f1, 1, fup1, dp2, finish_second)

    for t in tiles:
        below_h = below_r = None
        for k in range(4):
            psi = here(psi2, k, t)
            phi_x = mul(sub(down(psi2, k, t), psi), here(fld, XB + k, t))
            phi_y = mul(sub(right(psi), psi), here(fld, YB + k, t))
            h_x = mul(phi_x, here(fup1, k, t))
            h_y = mul(phi_y, here(fup1, 4 + k, t))
            k_x = mul(phi_x, here(dp2, k, t))
            k_y = mul(phi_y, here(dp2, 4 + k, t))
            zero = (jnp.zeros((8, 128), jnp.float32),) * 2
            s_x = choose(bit(k, t, 3), k_x, zero)
            s_y = choose(bit(k, t, 4), k_y, zero)
            r_x = sub(k_x, s_x)
            r_y = sub(k_y, s_y)
            put(flux, k, t, h_x)
            put(rest, k, t, r_x)
            press = add(sub(h_x, above(flux, k, t)), sub(h_y, left(h_y)))
            satur = add(add(s_x, above(rest, k, t)), add(s_y, left(r_y)))
            if k < 3:
                phi_z = mul(sub(here(psi2, k + 1, t), psi), here(fld, ZB + k, t))
                h_z = mul(phi_z, here(fup1, 8 + k, t))
                k_z = mul(phi_z, here(dp2, 8 + k, t))
                s_z = choose(bit(k, t, 5), k_z, zero)
                press = add(press, h_z)
                satur = add(satur, s_z)
            if k > 0:
                press = sub(press, below_h)
                satur = add(satur, below_r)
            if k < 3:
                below_h, below_r = h_z, sub(k_z, s_z)
            count = here(dense.at[CNT], k, t)
            press = add(press, sub(mul(count, here(p2, k, t)), here(dense.at[OP1], k, t)))
            put(mup2, k, t, mul(press, here(rcp, k, t)))
            sigma = add(here(sig2, k, t), mul(satur, here(d1, k, t)))
            sigma = add(sigma, sub(mul(count, here(s1, k, t)), here(dense.at[OS0], k, t)))
            put(psi1, k, t, both(lambda m, v: time_step * m / v, sigma, here(fld, VB + k, t)))

    for t in tiles:
        for k in range(4):
            put(muq1, k, t, mul(neighbours(mup2, 0, k, t), here(rcp, k, t)))

    for t in tiles:
        below_h = None
        for k in range(4):
            psi = here(psi1, k, t)
            h_x = mul(mul(sub(down(psi1, k, t), psi), here(fld, XB + k, t)), here(fup0, k, t))
            h_y = mul(mul(sub(right(psi), psi), here(fld, YB + k, t)), here(fup0, 4 + k, t))
            put(flux, k, t, h_x)
            press = add(sub(h_x, above(flux, k, t)), sub(h_y, left(h_y)))
            if k < 3:
                h_z = mul(mul(sub(here(psi1, k + 1, t), psi), here(fld, ZB + k, t)), here(fup0, 8 + k, t))
                press = add(press, h_z)
            if k > 0:
                press = sub(press, below_h)
            below_h = h_z
            count = here(dense.at[CNT], k, t)
            press = add(press, sub(mul(count, here(p1, k, t)), here(dense.at[OP0], k, t)))
            carried = mul(here(fld, VB + k, t), add(here(mup2, k, t), here(muq1, k, t)))
            press = add(press, add(carried, neighbours(muq1, 0, k, t)))
            put(mup1, k, t, mul(press, here(rcp, k, t)))

    for t in range(2, 5):
        for k in range(4):
            put(muq0, k, t, mul(neighbours(mup1, 0, k, t), here(rcp, k, t)))

    stages = (
        (mup2, q1, 0, p2, 0),
        (muq1, p1, 0, q1, 0),
        (mup1, q0, 0, p1, 0),
        (muq0, fld, PB, q0, 0),
    )
    for t in range(2, 4):
        rows = slice(8 * t - 16, 8 * t - 8)
        for k in range(4):
            sum_x = sum_y = sum_z = None
            for mu, value, value_base, out, out_base in stages:
                mu_c, v_c, o_c = here(mu, k, t), here(value, value_base + k, t), here(out, out_base + k, t)
                mu_d, v_d, o_d = down(mu, k, t), down(value, value_base + k, t), down(out, out_base + k, t)
                term = mu_c[0] * (v_d[0] - o_c[0]) + mu_d[0] * (v_c[0] - o_d[0])
                sum_x = term if sum_x is None else sum_x + term
                mu_r, v_r, o_r = right(mu_c), right(v_c), right(o_c)
                term = mu_c[0] * (v_r[0] - o_c[0]) + mu_r[0] * (v_c[0] - o_r[0])
                sum_y = term if sum_y is None else sum_y + term
                if k < 3:
                    mu_u = here(mu, k + 1, t)
                    v_u = here(value, value_base + k + 1, t)
                    o_u = here(out, out_base + k + 1, t)
                    term = mu_c[0] * (v_u[0] - o_c[0]) + mu_u[0] * (v_c[0] - o_u[0])
                    sum_z = term if sum_z is None else sum_z + term
            for psi, fup, dp in ((psi2, fup1, dp2), (psi1, fup0, dp1)):
                mid = here(psi, k, t)
                phi = down(psi, k, t)[0] - mid[0]
                sum_x = sum_x + phi * here(fup, k, t)[0] * here(dp, k, t)[0]
                phi = right(mid)[0] - mid[0]
                sum_y = sum_y + phi * here(fup, 4 + k, t)[0] * here(dp, 4 + k, t)[0]
                if k < 3:
                    phi = here(psi, k + 1, t)[0] - mid[0]
                    sum_z = sum_z + phi * here(fup, 8 + k, t)[0] * here(dp, 8 + k, t)[0]
            grad_x[k, rows, :] = jnp.where(here(fld, XB + k, t)[0] == 0.0, 0.0, sum_x)
            grad_y[k, rows, :] = jnp.where(here(fld, YB + k, t)[0] == 0.0, 0.0, sum_y)
            if k < 3:
                grad_z[k, rows, :] = sum_z


def swapped(value, axis, first):
    count = lax.axis_size(axis)
    pairs = []
    for i in range(first, count - 1, 2):
        pairs += [(i, i + 1), (i + 1, i)]
    return lax.ppermute(value, axis, pairs)


def on_device(p, s, tx, ty, tz, pv, up, cell, rate, plan, observed):
    f32 = jnp.float32

    def shape(*dims):
        return jax.ShapeDtypeStruct(dims, f32)

    limit = pltpu.CompilerParams(vmem_limit_bytes=48 * 1024 * 1024)
    inputs = (p, s, tx, ty, tz, pv, up, cell, rate, plan, observed)
    inputs = [pltpu.with_memory_space_constraint(value, pltpu.HBM) for value in inputs]
    strip = shape(COUNT + 4, 8, 128)
    own, far, near = pl.pallas_call(
        pack_rows,
        out_shape=(shape(COUNT + 1, 16, 128), strip, strip),
        in_specs=[pl.BlockSpec(memory_space=pltpu.HBM)] * len(inputs),
        scratch_shapes=[pltpu.VMEM(value.shape, value.dtype) for value in inputs[6:]]
        + [pltpu.SemaphoreType.DMA((len(inputs),))],
        compiler_params=limit,
        name="pack_rows",
    )(*inputs)
    row_far = swapped(far, "gx", 1)
    row_near = swapped(near, "gx", 0)
    strip = shape(PACKED + 2, 8, 128)
    far, near = pl.pallas_call(
        pack_cols,
        out_shape=(strip, strip),
        compiler_params=limit,
        name="pack_cols",
    )(own, row_far, row_near)
    col_far = swapped(far, "gy", 1)
    col_near = swapped(near, "gy", 0)

    def cells(count, dtype=f32):
        return pltpu.VMEM((count, 2, 56, 128), dtype)

    scratch = [cells(23), pltpu.VMEM((7, 4, 2, 56, 128), f32), cells(4, jnp.int32)]
    scratch += [cells(4) for _ in range(11)]
    scratch += [cells(11) for _ in range(4)]
    scratch += [cells(4) for _ in range(9)]
    return pl.pallas_call(
        model,
        out_shape=(shape(*tx.shape), shape(*ty.shape), shape(*tz.shape)),
        scratch_shapes=scratch,
        compiler_params=limit,
        name="model",
    )(own, row_far, row_near, col_far, col_near)


def solution(mesh):
    cells = P(None, "gx", "gy")
    in_specs = (cells,) * 7 + (
        P("gx", "gy", None),
        P("gx", "gy", None),
        P(None, "gx", "gy", None),
        P(None, None, "gx", "gy", None),
    )
    return jax.shard_map(
        on_device, mesh=mesh, in_specs=in_specs, out_specs=(cells,) * 3, check_vma=False
    )
```

```python
import jax
import jax.numpy as jnp
from jax import lax
from jax.experimental import pallas as pl
from jax.experimental.pallas import tpu as pltpu
from jax.sharding import PartitionSpec as P

time_step = 0.05

GROUPS = {"p": (0, 4), "s": (4, 4), "tx": (8, 4), "ty": (12, 4), "tz": (16, 3), "pv": (19, 4), "up": (23, 4)}
ORDER = ("p", "s", "tx", "ty", "tz", "pv", "up")
COUNT = 27
SLOT = 10
SLOTS = 12
PACKED = 3


def lanes():
    return lax.broadcasted_iota(jnp.int32, (8, 128), 1)


def in_slot(lane, start):
    return ((lane - start) & 127) < SLOT


FIELDS = 11


def pack_tile(*refs):
    p, s, tx, ty, tz, pv, up, cell, rate, plan, observed = refs[:FIELDS]
    own, col_far, col_near, far, near, upi, cells, rates, plans, seen, sems = refs[FIELDS:]
    targets = [own.at[pl.ds(*GROUPS[name])] for name in ORDER[:6]] + [upi, cells, rates, plans, seen]
    copies = [
        pltpu.make_async_copy(source, target, sems.at[k])
        for k, (source, target) in enumerate(zip(refs[:FIELDS], targets))
    ]
    for copy in copies:
        copy.start()
    for copy in copies:
        copy.wait()
    first = GROUPS["up"][0]
    for layer in range(4):
        own[first + layer] = upi[layer].astype(jnp.float32)
    own[COUNT] = jnp.zeros((16, 128), jnp.float32)
    own[COUNT, 0:1, 0:64] = cells[0].astype(jnp.float32)
    own[COUNT, 1:2, 0:64] = rates[0]
    for n in range(2):
        own[COUNT, 2 + n : 3 + n, 0:64] = plans[n, 0].astype(jnp.float32)
        for k in range(2):
            row = 4 + 2 * n + k
            own[COUNT, row : row + 1, 0:64] = seen[n, k, 0]
    odd = lax.axis_index("gx") & 1
    for g in range(COUNT):
        far[g] = own[g, pl.ds(pl.multiple_of(8 * odd, 8), 8), :]
        near[g] = own[g, pl.ds(pl.multiple_of(8 - 8 * odd, 8), 8), :]
    base = {name: GROUPS[name][0] for name in ORDER}

    def rows_of(name, row):
        return [own[base[name] + layer, row : row + 1, :] for layer in range(GROUPS[name][1])]

    blank = jnp.zeros((1, 128), jnp.float32)
    for_next = [jnp.concatenate(rows_of("p", 7) + rows_of("tx", 7), axis=0)]
    for_next += [jnp.zeros((8, 128), jnp.float32)] * 2
    for_prev = [
        jnp.concatenate(rows_of("p", 8) + rows_of("tx", 8), axis=0),
        jnp.concatenate(rows_of("ty", 8) + rows_of("tz", 8) + [blank], axis=0),
        jnp.concatenate(rows_of("pv", 8) + rows_of("p", 9), axis=0),
    ]
    for k in range(3):
        far[COUNT + k] = jnp.where(odd == 1, for_next[k], for_prev[k])
        near[COUNT + k] = jnp.where(odd == 1, for_prev[k], for_next[k])
    far[COUNT + 3] = own[COUNT, 0:8, :]
    near[COUNT + 3] = own[COUNT, 0:8, :]
    odd_col = lax.axis_index("gy") & 1
    lane = lanes()
    far_cols = [in_slot(lane, SLOT * (j - odd_col)) for j in range(SLOTS)]
    near_cols = [in_slot(lane, SLOT * (j - 1 + odd_col)) for j in range(SLOTS)]
    for half, beyond in ((0, for_prev), (1, for_next[:1])):
        blocks = [own[g, 8 * half : 8 * half + 8, :] for g in range(COUNT)] + beyond
        for at in range(PACKED):
            far_part = near_part = jnp.zeros((8, 128), jnp.float32)
            for j, block in enumerate(blocks[at * SLOTS : (at + 1) * SLOTS]):
                moved = pltpu.roll(block, SLOT * j, 1) if j else block
                far_part = jnp.where(far_cols[j], moved, far_part)
                near_part = jnp.where(near_cols[j], moved, near_part)
            col_far[PACKED * half + at] = far_part
            col_near[PACKED * half + at] = near_part
    col_far[2 * PACKED] = own[COUNT, 0:8, :]
    col_near[2 * PACKED] = own[COUNT, 0:8, :]


def sorted_ends(axis, far, near):
    odd = (lax.axis_index(axis) & 1) == 1

    def before(g):
        return jnp.where(odd, near[g], far[g])

    def after(g):
        return jnp.where(odd, far[g], near[g])

    return before, after


def pack_corners(col_far, col_near, far, near):
    before, after = sorted_ends("gy", col_far, col_near)
    odd = lax.axis_index("gx") & 1
    for at in range(PACKED):
        for out, first in ((far, PACKED * odd), (near, PACKED - PACKED * odd)):
            out[at] = after(first + at)
            out[PACKED + at] = before(first + at)
    both = jnp.where(lanes() < 64, before(2 * PACKED), pltpu.roll(after(2 * PACKED), 64, 1))
    far[2 * PACKED] = both
    near[2 * PACKED] = both


def split3(value):
    hi = value.astype(jnp.bfloat16).astype(jnp.float32)
    rest = value - hi
    mid = rest.astype(jnp.bfloat16).astype(jnp.float32)
    return hi, mid, rest - mid


def scatter_wells(lists, keep, dense, half):
    info = jnp.concatenate(lists, axis=1)
    width = info.shape[1]
    cell = info[0:1].astype(jnp.int32)
    lane = lax.broadcasted_iota(jnp.int32, (1, width), 1)
    base, low, high = keep(lane)
    layer = lax.shift_right_logical(cell, 11)
    row = lax.shift_right_logical(cell, 7) & 15
    col = cell & 127
    place = row + base
    inside = (place >= 8) & (col >= low) & (col < high)
    target = jnp.where(inside, layer * 40 + place - 8, -1)
    rows = lax.broadcasted_iota(jnp.int32, (160, width), 0)
    hit = rows == target
    cols = lax.broadcasted_iota(jnp.int32, (128, width), 0)
    to_col = jnp.where(cols == col, 1.0, 0.0).astype(jnp.bfloat16)
    rate = info[1:2] * 0.5
    values = [
        rate * info[2:3],
        rate * info[3:4],
        info[4:5],
        info[5:6],
        info[6:7],
        info[7:8],
    ]
    dims = (((1,), (1,)), ((), ()))
    for number, value in enumerate(values):
        total = None
        for part in split3(value):
            left = jnp.where(hit, part, 0.0).astype(jnp.bfloat16)
            term = lax.dot_general(left, to_col, dims, preferred_element_type=jnp.float32)
            total = term if total is None else total + term
        for k in range(4):
            dense[number, k, half, 8:48, :] = total[k * 40 : k * 40 + 40]
    left = jnp.where(hit, 1.0, 0.0).astype(jnp.bfloat16)
    total = lax.dot_general(left, to_col, dims, preferred_element_type=jnp.float32)
    for k in range(4):
        dense[6, k, half, 8:48, :] = total[k * 40 : k * 40 + 40]


SRC0, SRC1, OP0, OS0, OP1, OS1, CNT = range(7)


def model(
    col_far, col_near, corner_far, corner_near, row_far, row_near, own,
    grad_x, grad_y, grad_z,
    fld, dense, upi, rcp, tym, q0, p1, q1, p2, f0, d0, s1, f1, d1, fup0, fup1, dp1, dp2,
    sig2, psi2, psi1, mup2, muq1, mup1, muq0, flux, rest,
):
    low, high = sorted_ends("gx", row_far, row_near)
    before, after = sorted_ends("gy", col_far, col_near)
    low_corner, high_corner = sorted_ends("gx", corner_far, corner_near)
    lane = lanes()
    at_end = lane == 127
    at_start = lane == 0
    odd_col = lax.axis_index("gy") & 1
    far_cols = [in_slot(lane, SLOT * (j - 1 + odd_col)) for j in range(SLOTS)]
    first_cols = [in_slot(lane, SLOT * j) for j in range(SLOTS)]

    def back(value, j):
        return pltpu.roll(value, 128 - SLOT * j, 1) if j else value

    def beside_own(g, half):
        at, j = PACKED * half + g // SLOTS, g % SLOTS
        return back(jnp.where(far_cols[j], col_far[at], col_near[at]), j)

    def beside_other(corner, g):
        at, j = g // SLOTS, g % SLOTS
        return back(jnp.where(first_cols[j], corner(at), corner(PACKED + at)), j)

    for name in ORDER:
        first, layers = GROUPS[name]
        for layer in range(layers):
            g = first + layer
            center = [
                low(g),
                own[g, 0:8, :],
                own[g, 8:16, :],
                high(g),
            ]
            halo = [
                beside_other(low_corner, g),
                beside_own(g, 0),
                beside_own(g, 1),
                beside_other(high_corner, g),
            ]
            for k in range(4):
                rows = slice(8 + 8 * k, 16 + 8 * k)
                if name == "up":
                    upi[layer, 0, rows, :] = center[k].astype(jnp.int32)
                    upi[layer, 1, rows, :] = halo[k].astype(jnp.int32)
                else:
                    fld[g, 0, rows, :] = center[k]
                    fld[g, 1, rows, :] = halo[k]
    PB, SB, XB, YB, ZB, VB = (GROUPS[name][0] for name in ORDER[:6])
    extras = [
        (low(COUNT), beside_other(low_corner, COUNT), [(PB, 7), (XB, 7)]),
        (high(COUNT), beside_other(high_corner, COUNT + 0), [(PB, 40), (XB, 40)]),
        (high(COUNT + 1), beside_other(high_corner, COUNT + 1), [(YB, 40), (ZB, 40)]),
        (high(COUNT + 2), beside_other(high_corner, COUNT + 2), [(VB, 40), (PB, 41)]),
    ]
    for center, halo, places in extras:
        for block, (base, row) in enumerate(places):
            for layer in range(3 if base == ZB else 4):
                k = 4 * block + layer
                fld[base + layer, 0, row : row + 1, :] = center[k : k + 1]
                fld[base + layer, 1, row : row + 1, :] = halo[k : k + 1]

    scatter_wells(
        [own[COUNT, 0:8, 0:64], low(COUNT + 3)[:, 0:64], high(COUNT + 3)[:, 0:64]],
        lambda w: (jnp.where(w < 64, 16, jnp.where(w < 128, 0, 32)), 0, 128),
        dense,
        0,
    )

    def beside(w):
        block = lax.shift_right_logical(w, 6)
        base = jnp.where(block < 2, 16, jnp.where(block < 4, 0, 32))
        ahead = (block & 1) == 1
        return base, jnp.where(ahead, 0, 128 - SLOT), jnp.where(ahead, SLOT, 128)

    wells = 2 * PACKED
    lists = [before(wells)[:, 0:64], after(wells)[:, 0:64], low_corner(wells), high_corner(wells)]
    scatter_wells(lists, beside, dense, 1)

    def here(ref, k, t):
        rows = slice(8 * t, 8 * t + 8)
        return ref[k, 0, rows, :], ref[k, 1, rows, :]

    def down(ref, k, t):
        rows = slice(8 * t + 1, 8 * t + 9)
        return ref[k, 0, rows, :], ref[k, 1, rows, :]

    def above(ref, k, t):
        rows = slice(8 * t - 1, 8 * t + 7)
        return ref[k, 0, rows, :], ref[k, 1, rows, :]

    def put(ref, k, t, pair):
        rows = slice(8 * t, 8 * t + 8)
        ref[k, 0, rows, :] = pair[0]
        ref[k, 1, rows, :] = pair[1]

    def right(pair):
        a, b = pltpu.roll(pair[0], 127, 1), pltpu.roll(pair[1], 127, 1)
        return jnp.where(at_end, b, a), jnp.where(at_end, a, b)

    def left(pair):
        a, b = pltpu.roll(pair[0], 1, 1), pltpu.roll(pair[1], 1, 1)
        return jnp.where(at_start, b, a), jnp.where(at_start, a, b)

    def both(f, *pairs):
        return tuple(f(*(pair[h] for pair in pairs)) for h in range(2))

    def add(a, b):
        return both(lambda x, y: x + y, a, b)

    def sub(a, b):
        return both(lambda x, y: x - y, a, b)

    def mul(a, b):
        return both(lambda x, y: x * y, a, b)

    for t in range(1, 6):
        for k in range(4):
            volume = here(fld, VB + k, t)
            beyond = right(volume)
            put(fld, YB + k, t, both(lambda v, y: jnp.where(v == 0.0, 0.0, y), beyond, here(fld, YB + k, t)))
    for k in range(4):
        volume_below = fld[VB + k, 0, 32:33, :], fld[VB + k, 1, 32:33, :]
        for h in range(2):
            fld[XB + k, h, 31:32, :] = jnp.where(volume_below[h] == 0.0, 0.0, fld[XB + k, h, 31:32, :])
    for t in range(1, 6):
        for k in range(4):
            volume = both(lambda v: jnp.where(v == 0.0, 1.0, v), here(fld, VB + k, t))
            put(fld, VB + k, t, volume)
            west = left(here(fld, YB + k, t))
            put(tym, k, t, west)
            total = add(volume, add(here(fld, XB + k, t), above(fld, XB + k, t)))
            total = add(total, add(here(fld, YB + k, t), west))
            if k < 3:
                total = add(total, here(fld, ZB + k, t))
            if k > 0:
                total = add(total, here(fld, ZB + k - 1, t))
            put(rcp, k, t, both(lambda v: 1.0 / v, total))

    def neighbours(ref, base, k, t):
        value = here(ref, base + k, t)
        total = mul(here(fld, XB + k, t), down(ref, base + k, t))
        total = add(total, mul(above(fld, XB + k, t), above(ref, base + k, t)))
        total = add(total, mul(here(fld, YB + k, t), right(value)))
        total = add(total, mul(here(tym, k, t), left(value)))
        if k < 3:
            total = add(total, mul(here(fld, ZB + k, t), here(ref, base + k + 1, t)))
        if k > 0:
            total = add(total, mul(here(fld, ZB + k - 1, t), here(ref, base + k - 1, t)))
        return total

    def relax(out, ref, base, old, old_base, source, tiles):
        for t in tiles:
            for k in range(4):
                total = add(
                    mul(here(fld, VB + k, t), here(old, old_base + k, t)), here(dense.at[source], k, t)
                )
                total = add(total, neighbours(ref, base, k, t))
                put(out, k, t, mul(total, here(rcp, k, t)))

    def mobility(value):
        rest_of = 1.0 - value
        wetted = value * value
        inverse = 1.0 / (wetted + 0.5 * rest_of * rest_of)
        return wetted * inverse, value * rest_of * inverse * inverse

    def put_mobility(value, k, t, mobile, slope):
        pairs = [mobility(v) for v in value]
        put(mobile, k, t, (pairs[0][0], pairs[1][0]))
        put(slope, k, t, (pairs[0][1], pairs[1][1]))

    def bit(k, t, number):
        return both(lambda v: (v & (1 << number)) != 0, here(upi, k, t))

    def choose(mask, a, b):
        return both(lambda m, x, y: jnp.where(m, x, y), mask, a, b)

    def transport(pressure, sat, sat_base, mobile, n, fup, dp, finish):
        for t in range(1, 5):
            below = None
            for k in range(4):
                mob = here(mobile, k, t)
                pres = here(pressure, k, t)
                drop_x = sub(pres, down(pressure, k, t))
                drop_y = sub(pres, right(pres))
                up_x = choose(bit(k, t, 3 * n), mob, down(mobile, k, t))
                up_y = choose(bit(k, t, 3 * n + 1), mob, right(mob))
                put(fup, k, t, up_x)
                put(fup, 4 + k, t, up_y)
                put(dp, k, t, drop_x)
                put(dp, 4 + k, t, drop_y)
                flux_x = mul(mul(here(fld, XB + k, t), up_x), drop_x)
                flux_y = mul(mul(here(fld, YB + k, t), up_y), drop_y)
                put(flux, k, t, flux_x)
                net = add(sub(flux_x, above(flux, k, t)), sub(flux_y, left(flux_y)))
                if k < 3:
                    drop_z = sub(pres, here(pressure, k + 1, t))
                    up_z = choose(bit(k, t, 3 * n + 2), mob, here(mobile, k + 1, t))
                    put(fup, 8 + k, t, up_z)
                    put(dp, 8 + k, t, drop_z)
                    flux_z = mul(mul(here(fld, ZB + k, t), up_z), drop_z)
                    net = add(net, flux_z)
                if k > 0:
                    net = sub(net, below)
                below = flux_z
                moved = both(
                    lambda o, f, v: o - time_step * f / v,
                    here(sat, sat_base + k, t),
                    net,
                    here(fld, VB + k, t),
                )
                finish(moved, k, t)

    tiles = range(1, 5)
    relax(q0, fld, PB, fld, PB, SRC0, range(1, 6))
    relax(p1, q0, 0, fld, PB, SRC0, tiles)
    for t in tiles:
        for k in range(4):
            put_mobility(here(fld, SB + k, t), k, t, f0, d0)

    def finish_first(moved, k, t):
        put(s1, k, t, moved)
        put_mobility(moved, k, t, f1, d1)

    transport(p1, fld, SB, f0, 0, fup0, dp1, finish_first)
    relax(q1, p1, 0, p1, 0, SRC1, tiles)
    relax(p2, q1, 0, p1, 0, SRC1, tiles)

    def finish_second(moved, k, t):
        miss = sub(mul(here(dense.at[CNT], k, t), moved), here(dense.at[OS1], k, t))
        put(sig2, k, t, miss)
        put(psi2, k, t, both(lambda m, v: time_step * m / v, miss, here(fld, VB + k, t)))

    transport(p2, s1, 0, f1, 1, fup1, dp2, finish_second)

    for t in tiles:
        below_h = below_r = None
        for k in range(4):
            psi = here(psi2, k, t)
            phi_x = mul(sub(down(psi2, k, t), psi), here(fld, XB + k, t))
            phi_y = mul(sub(right(psi), psi), here(fld, YB + k, t))
            h_x = mul(phi_x, here(fup1, k, t))
            h_y = mul(phi_y, here(fup1, 4 + k, t))
            k_x = mul(phi_x, here(dp2, k, t))
            k_y = mul(phi_y, here(dp2, 4 + k, t))
            zero = (jnp.zeros((8, 128), jnp.float32),) * 2
            s_x = choose(bit(k, t, 3), k_x, zero)
            s_y = choose(bit(k, t, 4), k_y, zero)
            r_x = sub(k_x, s_x)
            r_y = sub(k_y, s_y)
            put(flux, k, t, h_x)
            put(rest, k, t, r_x)
            press = add(sub(h_x, above(flux, k, t)), sub(h_y, left(h_y)))
            satur = add(add(s_x, above(rest, k, t)), add(s_y, left(r_y)))
            if k < 3:
                phi_z = mul(sub(here(psi2, k + 1, t), psi), here(fld, ZB + k, t))
                h_z = mul(phi_z, here(fup1, 8 + k, t))
                k_z = mul(phi_z, here(dp2, 8 + k, t))
                s_z = choose(bit(k, t, 5), k_z, zero)
                press = add(press, h_z)
                satur = add(satur, s_z)
            if k > 0:
                press = sub(press, below_h)
                satur = add(satur, below_r)
            if k < 3:
                below_h, below_r = h_z, sub(k_z, s_z)
            count = here(dense.at[CNT], k, t)
            press = add(press, sub(mul(count, here(p2, k, t)), here(dense.at[OP1], k, t)))
            put(mup2, k, t, mul(press, here(rcp, k, t)))
            sigma = add(here(sig2, k, t), mul(satur, here(d1, k, t)))
            sigma = add(sigma, sub(mul(count, here(s1, k, t)), here(dense.at[OS0], k, t)))
            put(psi1, k, t, both(lambda m, v: time_step * m / v, sigma, here(fld, VB + k, t)))

    for t in tiles:
        for k in range(4):
            put(muq1, k, t, mul(neighbours(mup2, 0, k, t), here(rcp, k, t)))

    for t in tiles:
        below_h = None
        for k in range(4):
            psi = here(psi1, k, t)
            h_x = mul(mul(sub(down(psi1, k, t), psi), here(fld, XB + k, t)), here(fup0, k, t))
            h_y = mul(mul(sub(right(psi), psi), here(fld, YB + k, t)), here(fup0, 4 + k, t))
            put(flux, k, t, h_x)
            press = add(sub(h_x, above(flux, k, t)), sub(h_y, left(h_y)))
            if k < 3:
                h_z = mul(mul(sub(here(psi1, k + 1, t), psi), here(fld, ZB + k, t)), here(fup0, 8 + k, t))
                press = add(press, h_z)
            if k > 0:
                press = sub(press, below_h)
            below_h = h_z
            count = here(dense.at[CNT], k, t)
            press = add(press, sub(mul(count, here(p1, k, t)), here(dense.at[OP0], k, t)))
            carried = mul(here(fld, VB + k, t), add(here(mup2, k, t), here(muq1, k, t)))
            press = add(press, add(carried, neighbours(muq1, 0, k, t)))
            put(mup1, k, t, mul(press, here(rcp, k, t)))

    for t in range(2, 5):
        for k in range(4):
            put(muq0, k, t, mul(neighbours(mup1, 0, k, t), here(rcp, k, t)))

    stages = (
        (mup2, q1, 0, p2, 0),
        (muq1, p1, 0, q1, 0),
        (mup1, q0, 0, p1, 0),
        (muq0, fld, PB, q0, 0),
    )
    for t in range(2, 4):
        rows = slice(8 * t - 16, 8 * t - 8)
        for k in range(4):
            sum_x = sum_y = sum_z = None
            for mu, value, value_base, out, out_base in stages:
                mu_c, v_c, o_c = here(mu, k, t), here(value, value_base + k, t), here(out, out_base + k, t)
                mu_d, v_d, o_d = down(mu, k, t), down(value, value_base + k, t), down(out, out_base + k, t)
                term = mu_c[0] * (v_d[0] - o_c[0]) + mu_d[0] * (v_c[0] - o_d[0])
                sum_x = term if sum_x is None else sum_x + term
                mu_r, v_r, o_r = right(mu_c), right(v_c), right(o_c)
                term = mu_c[0] * (v_r[0] - o_c[0]) + mu_r[0] * (v_c[0] - o_r[0])
                sum_y = term if sum_y is None else sum_y + term
                if k < 3:
                    mu_u = here(mu, k + 1, t)
                    v_u = here(value, value_base + k + 1, t)
                    o_u = here(out, out_base + k + 1, t)
                    term = mu_c[0] * (v_u[0] - o_c[0]) + mu_u[0] * (v_c[0] - o_u[0])
                    sum_z = term if sum_z is None else sum_z + term
            for psi, fup, dp in ((psi2, fup1, dp2), (psi1, fup0, dp1)):
                mid = here(psi, k, t)
                phi = down(psi, k, t)[0] - mid[0]
                sum_x = sum_x + phi * here(fup, k, t)[0] * here(dp, k, t)[0]
                phi = right(mid)[0] - mid[0]
                sum_y = sum_y + phi * here(fup, 4 + k, t)[0] * here(dp, 4 + k, t)[0]
                if k < 3:
                    phi = here(psi, k + 1, t)[0] - mid[0]
                    sum_z = sum_z + phi * here(fup, 8 + k, t)[0] * here(dp, 8 + k, t)[0]
            grad_x[k, rows, :] = jnp.where(here(fld, XB + k, t)[0] == 0.0, 0.0, sum_x)
            grad_y[k, rows, :] = jnp.where(here(fld, YB + k, t)[0] == 0.0, 0.0, sum_y)
            if k < 3:
                grad_z[k, rows, :] = sum_z


def swapped(value, axis, first):
    count = lax.axis_size(axis)
    pairs = []
    for i in range(first, count - 1, 2):
        pairs += [(i, i + 1), (i + 1, i)]
    return lax.ppermute(value, axis, pairs)


def on_device(p, s, tx, ty, tz, pv, up, cell, rate, plan, observed):
    f32 = jnp.float32

    def shape(*dims):
        return jax.ShapeDtypeStruct(dims, f32)

    limit = pltpu.CompilerParams(vmem_limit_bytes=48 * 1024 * 1024)
    inputs = (p, s, tx, ty, tz, pv, up, cell, rate, plan, observed)
    inputs = [pltpu.with_memory_space_constraint(value, pltpu.HBM) for value in inputs]
    strip = shape(COUNT + 4, 8, 128)
    packed = shape(2 * PACKED + 1, 8, 128)
    own, col_far, col_near, row_far, row_near = pl.pallas_call(
        pack_tile,
        out_shape=(shape(COUNT + 1, 16, 128), packed, packed, strip, strip),
        in_specs=[pl.BlockSpec(memory_space=pltpu.HBM)] * len(inputs),
        scratch_shapes=[pltpu.VMEM(value.shape, value.dtype) for value in inputs[6:]]
        + [pltpu.SemaphoreType.DMA((len(inputs),))],
        compiler_params=limit,
        name="pack_tile",
    )(*inputs)
    col_far = swapped(col_far, "gy", 1)
    col_near = swapped(col_near, "gy", 0)
    row_far = swapped(row_far, "gx", 1)
    row_near = swapped(row_near, "gx", 0)
    far, near = pl.pallas_call(
        pack_corners,
        out_shape=(packed, packed),
        compiler_params=limit,
        cost_estimate=pl.CostEstimate(flops=10**11, bytes_accessed=1 << 28, transcendentals=0),
        name="pack_corners",
    )(col_far, col_near)
    corner_far = swapped(far, "gx", 1)
    corner_near = swapped(near, "gx", 0)

    def cells(count, dtype=f32):
        return pltpu.VMEM((count, 2, 56, 128), dtype)

    scratch = [cells(23), pltpu.VMEM((7, 4, 2, 56, 128), f32), cells(4, jnp.int32)]
    scratch += [cells(4) for _ in range(11)]
    scratch += [cells(11) for _ in range(4)]
    scratch += [cells(4) for _ in range(9)]
    return pl.pallas_call(
        model,
        out_shape=(shape(*tx.shape), shape(*ty.shape), shape(*tz.shape)),
        scratch_shapes=scratch,
        compiler_params=limit,
        name="model",
    )(col_far, col_near, corner_far, corner_near, row_far, row_near, own)


def solution(mesh):
    cells = P(None, "gx", "gy")
    in_specs = (cells,) * 7 + (
        P("gx", "gy", None),
        P("gx", "gy", None),
        P(None, "gx", "gy", None),
        P(None, None, "gx", "gy", None),
    )
    return jax.shard_map(
        on_device, mesh=mesh, in_specs=in_specs, out_specs=(cells,) * 3, check_vma=False
    )
```

```python
import jax
import jax.numpy as jnp
from jax import lax
from jax.experimental import pallas as pl
from jax.experimental.pallas import tpu as pltpu
from jax.sharding import PartitionSpec as P

time_step = 0.05

GROUPS = {"p": (0, 4), "s": (4, 4), "tx": (8, 4), "ty": (12, 4), "tz": (16, 3), "pv": (19, 4), "up": (23, 4)}
ORDER = ("p", "s", "tx", "ty", "tz", "pv", "up")
COUNT = 27
SLOT = 10
SLOTS = 12
PIECES = COUNT * 4 + 4
PACKED = -(-PIECES // SLOTS)
ROWS = 56


FIELDS = 11


def pack_rows(*refs):
    p, s, tx, ty, tz, pv, up, cell, rate, plan, observed = refs[:FIELDS]
    own, far, near, upi, cells, rates, plans, seen, sems = refs[FIELDS:]
    targets = [own.at[pl.ds(*GROUPS[name])] for name in ORDER[:6]] + [upi, cells, rates, plans, seen]
    copies = [
        pltpu.make_async_copy(source, target, sems.at[k])
        for k, (source, target) in enumerate(zip(refs[:FIELDS], targets))
    ]
    for copy in copies:
        copy.start()
    for copy in copies:
        copy.wait()
    first = GROUPS["up"][0]
    for layer in range(4):
        own[first + layer] = upi[layer].astype(jnp.float32)
    own[COUNT] = jnp.zeros((16, 128), jnp.float32)
    own[COUNT, 0:1, 0:64] = cells[0].astype(jnp.float32)
    own[COUNT, 1:2, 0:64] = rates[0]
    for n in range(2):
        own[COUNT, 2 + n : 3 + n, 0:64] = plans[n, 0].astype(jnp.float32)
        for k in range(2):
            row = 4 + 2 * n + k
            own[COUNT, row : row + 1, 0:64] = seen[n, k, 0]
    odd = lax.axis_index("gx") & 1
    for g in range(COUNT):
        far[g] = own[g, pl.ds(pl.multiple_of(8 * odd, 8), 8), :]
        near[g] = own[g, pl.ds(pl.multiple_of(8 - 8 * odd, 8), 8), :]
    base = {name: GROUPS[name][0] for name in ORDER}

    def rows_of(name, row):
        return [own[base[name] + layer, row : row + 1, :] for layer in range(GROUPS[name][1])]

    blank = jnp.zeros((1, 128), jnp.float32)
    for_next = [jnp.concatenate(rows_of("p", 7) + rows_of("tx", 7), axis=0)]
    for_next += [jnp.zeros((8, 128), jnp.float32)] * 2
    for_prev = [
        jnp.concatenate(rows_of("p", 8) + rows_of("tx", 8), axis=0),
        jnp.concatenate(rows_of("ty", 8) + rows_of("tz", 8) + [blank], axis=0),
        jnp.concatenate(rows_of("pv", 8) + rows_of("p", 9), axis=0),
    ]
    for k in range(3):
        far[COUNT + k] = jnp.where(odd == 1, for_next[k], for_prev[k])
        near[COUNT + k] = jnp.where(odd == 1, for_prev[k], for_next[k])
    far[COUNT + 3] = own[COUNT, 0:8, :]
    near[COUNT + 3] = own[COUNT, 0:8, :]


def lanes():
    return lax.broadcasted_iota(jnp.int32, (8, 128), 1)


def in_slot(lane, start):
    return ((lane - start) & 127) < SLOT


def sorted_ends(axis, far, near):
    odd = (lax.axis_index(axis) & 1) == 1

    def before(g):
        return jnp.where(odd, near[g], far[g])

    def after(g):
        return jnp.where(odd, far[g], near[g])

    return before, after


def pack_cols(own, row_far, row_near, far, near):
    low, high = sorted_ends("gx", row_far, row_near)
    odd = lax.axis_index("gy") & 1
    lane = lanes()
    blocks = []
    for g in range(COUNT):
        blocks.append(lambda g=g: low(g))
        blocks.append(lambda g=g: own[g, 0:8, :])
        blocks.append(lambda g=g: own[g, 8:16, :])
        blocks.append(lambda g=g: high(g))
    blocks.append(lambda: low(COUNT))
    for extra in range(3):
        blocks.append(lambda g=COUNT + extra: high(g))
    for out, ends in ((far, odd), (near, 1 - odd)):
        masks = [in_slot(lane, SLOT * (j + ends)) for j in range(SLOTS)]
        for at in range(PACKED):
            part = jnp.zeros((8, 128), jnp.float32)
            for j, block in enumerate(blocks[at * SLOTS : (at + 1) * SLOTS]):
                part = jnp.where(masks[j], pltpu.roll(block(), SLOT * j + 2 * SLOT * ends, 1), part)
            out[at] = part
    pair = jnp.where(lane < 64, own[COUNT, 0:8, :], pltpu.roll(low(COUNT + 3), 64, 1))
    for out in (far, near):
        out[PACKED] = pair
        out[PACKED + 1] = high(COUNT + 3)


def split3(value):
    hi = value.astype(jnp.bfloat16).astype(jnp.float32)
    rest = value - hi
    mid = rest.astype(jnp.bfloat16).astype(jnp.float32)
    return hi, mid, rest - mid


SRC0, SRC1, OP0, OS0, OP1, OS1, CNT = range(7)


def well_fields(info):
    rate = info[1:2] * 0.5
    values = [rate * info[2:3], rate * info[3:4]] + [info[k : k + 1] for k in range(4, 8)]
    cell = info[0:1].astype(jnp.int32)
    layer = lax.shift_right_logical(cell, 11)
    row = lax.shift_right_logical(cell, 7) & 15
    return values, layer, row, cell & 127


def hits(layer, place, inside):
    target = jnp.where(inside & (place >= 8), layer * 40 + place - 8, -1)
    rows = lax.broadcasted_iota(jnp.int32, (160, target.shape[1]), 0)
    return rows == target


def dot(left, right):
    return lax.dot_general(left, right, (((1,), (1,)), ((), ())), preferred_element_type=jnp.float32)


def scatter_center(lists, dense):
    info = jnp.concatenate(lists, axis=1)
    values, layer, row, col = well_fields(info)
    lane = lax.broadcasted_iota(jnp.int32, (1, info.shape[1]), 1)
    hit = hits(layer, row + jnp.where(lane < 64, 16, jnp.where(lane < 128, 0, 32)), lane >= 0)
    cols = lax.broadcasted_iota(jnp.int32, (128, info.shape[1]), 0)
    to_col = jnp.where(cols == col, 1.0, 0.0).astype(jnp.bfloat16)
    for number, value in enumerate(values + [None]):
        parts = (1.0,) if value is None else split3(value)
        total = None
        for part in parts:
            term = dot(jnp.where(hit, part, 0.0).astype(jnp.bfloat16), to_col)
            total = term if total is None else total + term
        for k in range(4):
            dense[number, k, 8:48, :] = total[k * 40 : k * 40 + 40]


def scatter_beside(lists, dense, lane):
    info = jnp.concatenate(lists, axis=1)
    width = info.shape[1]
    values, layer, row, col = well_fields(info)
    block = lax.shift_right_logical(lax.broadcasted_iota(jnp.int32, (1, width), 1), 6)
    base = jnp.where(block < 2, 16, jnp.where(block < 4, 0, 32))
    ahead = (block & 1) == 1
    spot = jnp.where(ahead, col, col - 128 + 2 * SLOT)
    inside = (spot >= jnp.where(ahead, 0, SLOT)) & (spot < jnp.where(ahead, SLOT, 2 * SLOT))
    left = jnp.where(hits(layer, row + base, inside), 1.0, 0.0).astype(jnp.bfloat16)
    spots = lax.broadcasted_iota(jnp.int32, (24, width), 0)
    hit = spots == spot
    parts = [split3(value) for value in values]
    for first, last in ((0, 5), (5, 7)):
        total = None
        for piece in range(3):
            rights = []
            for number in range(first, last):
                part = jnp.float32(1.0 if piece == 0 else 0.0) if number == CNT else parts[number][piece]
                rights.append(jnp.where(hit, part, 0.0))
            rights += [jnp.zeros((128 - 24 * (last - first), width), jnp.float32)]
            term = dot(left, jnp.concatenate(rights, axis=0).astype(jnp.bfloat16))
            total = term if total is None else total + term
        for number in range(first, last):
            shift = 24 * (number - first)
            for k in range(4):
                for t in range(5):
                    rows = slice(8 + 8 * t, 16 + 8 * t)
                    value = total[k * 40 + 8 * t : k * 40 + 8 * t + 8]
                    value = pltpu.roll(value, 128 - shift, 1) if shift else value
                    dense[number, k, rows, :] = jnp.where(lane < 2 * SLOT, value, dense[number, k, rows, :])


SCRATCH = (4,) * 11 + (11,) * 4 + (4,) * 9


def simulate(fld, dense, upi, scratch, emit_x, emit_y, emit_z):
    (rcp, tym, q0, p1, q1, p2, f0, d0, s1, f1, d1, fup0, fup1, dp1, dp2,
     sig2, psi2, psi1, mup2, muq1, mup1, muq0, flux, rest) = scratch
    PB, SB, XB, YB, ZB, VB = (GROUPS[name][0] for name in ORDER[:6])

    def here(ref, k, t):
        return ref[k, 8 * t : 8 * t + 8, :]

    def down(ref, k, t):
        return ref[k, 8 * t + 1 : 8 * t + 9, :]

    def above(ref, k, t):
        return ref[k, 8 * t - 1 : 8 * t + 7, :]

    def put(ref, k, t, value):
        ref[k, 8 * t : 8 * t + 8, :] = value

    def right(value):
        return pltpu.roll(value, 127, 1)

    def left(value):
        return pltpu.roll(value, 1, 1)

    for k in range(4):
        for t in range(1, 6):
            beyond = right(here(fld, VB + k, t))
            put(fld, YB + k, t, jnp.where(beyond == 0.0, 0.0, here(fld, YB + k, t)))
        last = slice(31, 32)
        fld[XB + k, last, :] = jnp.where(fld[VB + k, 32:33, :] == 0.0, 0.0, fld[XB + k, last, :])
    for t in range(1, 6):
        for k in range(4):
            volume = here(fld, VB + k, t)
            volume = jnp.where(volume == 0.0, 1.0, volume)
            put(fld, VB + k, t, volume)
            west = left(here(fld, YB + k, t))
            put(tym, k, t, west)
            total = volume + (here(fld, XB + k, t) + above(fld, XB + k, t)) + (here(fld, YB + k, t) + west)
            if k < 3:
                total = total + here(fld, ZB + k, t)
            if k > 0:
                total = total + here(fld, ZB + k - 1, t)
            put(rcp, k, t, 1.0 / total)

    def neighbours(ref, base, k, t):
        value = here(ref, base + k, t)
        total = here(fld, XB + k, t) * down(ref, base + k, t) + above(fld, XB + k, t) * above(ref, base + k, t)
        total = total + (here(fld, YB + k, t) * right(value) + here(tym, k, t) * left(value))
        if k < 3:
            total = total + here(fld, ZB + k, t) * here(ref, base + k + 1, t)
        if k > 0:
            total = total + here(fld, ZB + k - 1, t) * here(ref, base + k - 1, t)
        return total

    def relax(out, ref, base, old, old_base, source, tiles):
        for t in tiles:
            for k in range(4):
                total = here(fld, VB + k, t) * here(old, old_base + k, t) + here(dense.at[source], k, t)
                put(out, k, t, (total + neighbours(ref, base, k, t)) * here(rcp, k, t))

    def put_mobility(value, k, t, mobile, slope):
        rest_of = 1.0 - value
        wetted = value * value
        inverse = 1.0 / (wetted + 0.5 * rest_of * rest_of)
        put(mobile, k, t, wetted * inverse)
        put(slope, k, t, value * rest_of * (inverse * inverse))

    def bit(k, t, number):
        return (here(upi, k, t) & (1 << number)) != 0

    def transport(pressure, sat, sat_base, mobile, n, fup, dp, finish):
        for t in range(1, 5):
            below = None
            for k in range(4):
                mob = here(mobile, k, t)
                pres = here(pressure, k, t)
                drop_x = pres - down(pressure, k, t)
                drop_y = pres - right(pres)
                up_x = jnp.where(bit(k, t, 3 * n), mob, down(mobile, k, t))
                up_y = jnp.where(bit(k, t, 3 * n + 1), mob, right(mob))
                put(fup, k, t, up_x)
                put(fup, 4 + k, t, up_y)
                put(dp, k, t, drop_x)
                put(dp, 4 + k, t, drop_y)
                flux_x = here(fld, XB + k, t) * up_x * drop_x
                flux_y = here(fld, YB + k, t) * up_y * drop_y
                put(flux, k, t, flux_x)
                net = (flux_x - above(flux, k, t)) + (flux_y - left(flux_y))
                if k > 0:
                    net = net - below
                if k < 3:
                    drop_z = pres - here(pressure, k + 1, t)
                    up_z = jnp.where(bit(k, t, 3 * n + 2), mob, here(mobile, k + 1, t))
                    put(fup, 8 + k, t, up_z)
                    put(dp, 8 + k, t, drop_z)
                    below = here(fld, ZB + k, t) * up_z * drop_z
                    net = net + below
                finish(here(sat, sat_base + k, t) - time_step * net / here(fld, VB + k, t), k, t)

    tiles = range(1, 5)
    relax(q0, fld, PB, fld, PB, SRC0, range(1, 6))
    relax(p1, q0, 0, fld, PB, SRC0, tiles)
    for t in tiles:
        for k in range(4):
            put_mobility(here(fld, SB + k, t), k, t, f0, d0)

    def finish_first(moved, k, t):
        put(s1, k, t, moved)
        put_mobility(moved, k, t, f1, d1)

    transport(p1, fld, SB, f0, 0, fup0, dp1, finish_first)
    relax(q1, p1, 0, p1, 0, SRC1, tiles)
    relax(p2, q1, 0, p1, 0, SRC1, tiles)

    def finish_second(moved, k, t):
        miss = here(dense.at[CNT], k, t) * moved - here(dense.at[OS1], k, t)
        put(sig2, k, t, miss)
        put(psi2, k, t, time_step * miss / here(fld, VB + k, t))

    transport(p2, s1, 0, f1, 1, fup1, dp2, finish_second)

    for t in tiles:
        below_h = below_r = None
        for k in range(4):
            psi = here(psi2, k, t)
            phi_x = (down(psi2, k, t) - psi) * here(fld, XB + k, t)
            phi_y = (right(psi) - psi) * here(fld, YB + k, t)
            h_x = phi_x * here(fup1, k, t)
            h_y = phi_y * here(fup1, 4 + k, t)
            k_x = phi_x * here(dp2, k, t)
            k_y = phi_y * here(dp2, 4 + k, t)
            s_x = jnp.where(bit(k, t, 3), k_x, 0.0)
            s_y = jnp.where(bit(k, t, 4), k_y, 0.0)
            put(flux, k, t, h_x)
            put(rest, k, t, k_x - s_x)
            press = (h_x - above(flux, k, t)) + (h_y - left(h_y))
            satur = (s_x + above(rest, k, t)) + (s_y + left(k_y - s_y))
            if k > 0:
                press = press - below_h
                satur = satur + below_r
            if k < 3:
                phi_z = (here(psi2, k + 1, t) - psi) * here(fld, ZB + k, t)
                below_h = phi_z * here(fup1, 8 + k, t)
                k_z = phi_z * here(dp2, 8 + k, t)
                s_z = jnp.where(bit(k, t, 5), k_z, 0.0)
                below_r = k_z - s_z
                press = press + below_h
                satur = satur + s_z
            count = here(dense.at[CNT], k, t)
            press = press + (count * here(p2, k, t) - here(dense.at[OP1], k, t))
            put(mup2, k, t, press * here(rcp, k, t))
            sigma = here(sig2, k, t) + satur * here(d1, k, t)
            sigma = sigma + (count * here(s1, k, t) - here(dense.at[OS0], k, t))
            put(psi1, k, t, time_step * sigma / here(fld, VB + k, t))

    for t in tiles:
        for k in range(4):
            put(muq1, k, t, neighbours(mup2, 0, k, t) * here(rcp, k, t))

    for t in tiles:
        below_h = None
        for k in range(4):
            psi = here(psi1, k, t)
            h_x = (down(psi1, k, t) - psi) * here(fld, XB + k, t) * here(fup0, k, t)
            h_y = (right(psi) - psi) * here(fld, YB + k, t) * here(fup0, 4 + k, t)
            put(flux, k, t, h_x)
            press = (h_x - above(flux, k, t)) + (h_y - left(h_y))
            if k > 0:
                press = press - below_h
            if k < 3:
                below_h = (here(psi1, k + 1, t) - psi) * here(fld, ZB + k, t) * here(fup0, 8 + k, t)
                press = press + below_h
            count = here(dense.at[CNT], k, t)
            press = press + (count * here(p1, k, t) - here(dense.at[OP0], k, t))
            press = press + here(fld, VB + k, t) * (here(mup2, k, t) + here(muq1, k, t))
            press = press + neighbours(muq1, 0, k, t)
            put(mup1, k, t, press * here(rcp, k, t))

    for t in range(2, 5):
        for k in range(4):
            put(muq0, k, t, neighbours(mup1, 0, k, t) * here(rcp, k, t))

    stages = (
        (mup2, q1, 0, p2, 0),
        (muq1, p1, 0, q1, 0),
        (mup1, q0, 0, p1, 0),
        (muq0, fld, PB, q0, 0),
    )
    for t in range(2, 4):
        for k in range(4):
            sum_x = sum_y = sum_z = 0.0
            for psi, fup, dp in ((psi2, fup1, dp2), (psi1, fup0, dp1)):
                mid = here(psi, k, t)
                sum_x = sum_x + (down(psi, k, t) - mid) * here(fup, k, t) * here(dp, k, t)
                sum_y = sum_y + (right(mid) - mid) * here(fup, 4 + k, t) * here(dp, 4 + k, t)
                if k < 3:
                    sum_z = sum_z + (here(psi, k + 1, t) - mid) * here(fup, 8 + k, t) * here(dp, 8 + k, t)
            for mu, value, base, out, out_base in stages:
                mu_c, v_c, o_c = here(mu, k, t), here(value, base + k, t), here(out, out_base + k, t)
                mu_d, v_d, o_d = down(mu, k, t), down(value, base + k, t), down(out, out_base + k, t)
                sum_x = sum_x + (mu_c * (v_d - o_c) + mu_d * (v_c - o_d))
                sum_y = sum_y + (mu_c * (right(v_c) - o_c) + right(mu_c) * (v_c - right(o_c)))
                if k < 3:
                    mu_u = here(mu, k + 1, t)
                    v_u = here(value, base + k + 1, t)
                    o_u = here(out, out_base + k + 1, t)
                    sum_z = sum_z + (mu_c * (v_u - o_c) + mu_u * (v_c - o_u))
            emit_x(k, t, jnp.where(here(fld, XB + k, t) == 0.0, 0.0, sum_x))
            emit_y(k, t, jnp.where(here(fld, YB + k, t) == 0.0, 0.0, sum_y))
            if k < 3:
                emit_z(k, t, sum_z)


PLACES = (
    (("p", 7), ("tx", 7)),
    (("p", 40), ("tx", 40)),
    (("ty", 40), ("tz", 40)),
    (("pv", 40), ("p", 41)),
)


def put_beyond(fld, values):
    for value, places in zip(values, PLACES):
        for block, (name, row) in enumerate(places):
            first, layers = GROUPS[name]
            for layer in range(layers):
                k = 4 * block + layer
                fld[first + layer, row : row + 1, :] = value[k : k + 1]


def model_center(own, row_far, row_near, grads, edge, edge_dense, fld, dense, upi, *scratch):
    low, high = sorted_ends("gx", row_far, row_near)
    lane = lanes()

    def edge_of(value):
        return jnp.where(lane < 99, pltpu.roll(value, 2 * SLOT, 1), value)

    for g in range(COUNT):
        blocks = [low(g), own[g, 0:8, :], own[g, 8:16, :], high(g)]
        for k, block in enumerate(blocks):
            rows = slice(8 + 8 * k, 16 + 8 * k)
            fld[g, rows, :] = block
            edge[g, rows, :] = edge_of(block)
            if g >= GROUPS["up"][0]:
                upi[g - GROUPS["up"][0], rows, :] = block.astype(jnp.int32)
    extras = [low(COUNT)] + [high(COUNT + k) for k in range(3)]
    put_beyond(fld, extras)
    put_beyond(edge, [edge_of(value) for value in extras])
    scatter_center(
        [own[COUNT, 0:8, 0:64], low(COUNT + 3)[:, 0:64], high(COUNT + 3)[:, 0:64]], dense
    )
    for number in range(7):
        for k in range(4):
            for t in range(1, 6):
                rows = slice(8 * t, 8 * t + 8)
                edge_dense[number, k, rows, :] = edge_of(dense[number, k, rows, :])

    def emit(first):
        def write(k, t, value):
            grads[first + k, 8 * t - 16 : 8 * t - 8, :] = value

        return write

    simulate(fld, dense, upi, scratch, emit(0), emit(4), emit(8))


def model_edge(
    col_far, col_near, edge, edge_dense, center, grad_x, grad_y, grad_z, fld, dense, upi, *scratch
):
    before, after = sorted_ends("gy", col_far, col_near)
    odd = lax.axis_index("gy") & 1
    lane = lanes()
    far_cols = [in_slot(lane, SLOT * (j + 1 - odd)) for j in range(SLOTS)]
    beside = lane < 2 * SLOT

    def unpack(piece):
        at, j = piece // SLOTS, piece % SLOTS
        both = jnp.where(far_cols[j], col_far[at], col_near[at])
        return pltpu.roll(both, 128 - SLOT * j, 1) if j else both

    for g in range(COUNT):
        for k in range(4):
            rows = slice(8 + 8 * k, 16 + 8 * k)
            block = jnp.where(beside, unpack(g * 4 + k), edge[g, rows, :])
            if g >= GROUPS["up"][0]:
                upi[g - GROUPS["up"][0], rows, :] = block.astype(jnp.int32)
            else:
                fld[g, rows, :] = block
    for extra, places in enumerate(PLACES):
        value = unpack(COUNT * 4 + extra)
        for block, (name, row) in enumerate(places):
            first, layers = GROUPS[name]
            for layer in range(layers):
                k = 4 * block + layer
                at = (first + layer, slice(row, row + 1), slice(None))
                fld[at] = jnp.where(beside[0:1], value[k : k + 1], edge[at])
    for number in range(7):
        for k in range(4):
            dense[number, k, 8:48, :] = edge_dense[number, k, 8:48, :]
    first, second = PACKED, PACKED + 1
    own_lists = [before(first)[:, 0:64], after(first)[:, 0:64]]
    low_lists = [before(first)[:, 64:128], after(first)[:, 64:128]]
    high_lists = [before(second)[:, 0:64], after(second)[:, 0:64]]
    scatter_beside(own_lists + low_lists + high_lists, dense, lane)

    def emit(out, group):
        def write(k, t, value):
            rows = slice(8 * t - 16, 8 * t - 8)
            value = jnp.where(lane < 64, pltpu.roll(value, 128 - 2 * SLOT, 1), value)
            inner = (lane >= SLOT - 1) & (lane < 128 - SLOT)
            out[k, rows, :] = jnp.where(inner, center[group + k, rows, :], value)

        return write

    simulate(fld, dense, upi, scratch, emit(grad_x, 0), emit(grad_y, 4), emit(grad_z, 8))


def swapped(value, axis, first):
    count = lax.axis_size(axis)
    pairs = []
    for i in range(first, count - 1, 2):
        pairs += [(i, i + 1), (i + 1, i)]
    return lax.ppermute(value, axis, pairs)


def on_device(p, s, tx, ty, tz, pv, up, cell, rate, plan, observed):
    f32 = jnp.float32

    def shape(*dims):
        return jax.ShapeDtypeStruct(dims, f32)

    limit = pltpu.CompilerParams(vmem_limit_bytes=24 * 1024 * 1024)
    inputs = (p, s, tx, ty, tz, pv, up, cell, rate, plan, observed)
    inputs = [pltpu.with_memory_space_constraint(value, pltpu.HBM) for value in inputs]
    strip = shape(COUNT + 4, 8, 128)
    own, far, near = pl.pallas_call(
        pack_rows,
        out_shape=(shape(COUNT + 1, 16, 128), strip, strip),
        in_specs=[pl.BlockSpec(memory_space=pltpu.HBM)] * len(inputs),
        scratch_shapes=[pltpu.VMEM(value.shape, value.dtype) for value in inputs[6:]]
        + [pltpu.SemaphoreType.DMA((len(inputs),))],
        compiler_params=limit,
        name="pack_rows",
    )(*inputs)
    row_far = swapped(far, "gx", 1)
    row_near = swapped(near, "gx", 0)
    strip = shape(PACKED + 2, 8, 128)
    far, near = pl.pallas_call(
        pack_cols,
        out_shape=(strip, strip),
        compiler_params=limit,
        name="pack_cols",
    )(own, row_far, row_near)
    col_far = swapped(far, "gy", 1)
    col_near = swapped(near, "gy", 0)

    scratch = [pltpu.VMEM((23, ROWS, 128), f32), pltpu.VMEM((7, 4, ROWS, 128), f32)]
    scratch += [pltpu.VMEM((4, ROWS, 128), jnp.int32)]
    scratch += [pltpu.VMEM((count, ROWS, 128), f32) for count in SCRATCH]
    center, edge, edge_dense = pl.pallas_call(
        model_center,
        out_shape=(shape(11, 16, 128), shape(COUNT, ROWS, 128), shape(7, 4, ROWS, 128)),
        scratch_shapes=[pltpu.VMEM((COUNT, ROWS, 128), f32)] + scratch[1:],
        compiler_params=limit,
        cost_estimate=pl.CostEstimate(flops=10**11, bytes_accessed=1 << 28, transcendentals=0),
        name="model_center",
    )(own, row_far, row_near)
    return pl.pallas_call(
        model_edge,
        out_shape=(shape(*tx.shape), shape(*ty.shape), shape(*tz.shape)),
        scratch_shapes=scratch,
        compiler_params=limit,
        name="model_edge",
    )(col_far, col_near, edge, edge_dense, center)


def solution(mesh):
    cells = P(None, "gx", "gy")
    in_specs = (cells,) * 7 + (
        P("gx", "gy", None),
        P("gx", "gy", None),
        P(None, "gx", "gy", None),
        P(None, None, "gx", "gy", None),
    )
    return jax.shard_map(
        on_device, mesh=mesh, in_specs=in_specs, out_specs=(cells,) * 3, check_vma=False
    )
```

```python
import jax
import jax.numpy as jnp
from jax import lax
from jax.experimental import pallas as pl
from jax.experimental.pallas import tpu as pltpu
from jax.sharding import PartitionSpec as P

time_step = 0.05

GROUPS = {"p": (0, 4), "s": (4, 4), "tx": (8, 4), "ty": (12, 4), "tz": (16, 3), "pv": (19, 4), "up": (23, 4)}
ORDER = ("p", "s", "tx", "ty", "tz", "pv", "up")
COUNT = 27
SLOT = 10
SLOTS = 6
PAIRS = 14
PACKED = 5
ROWS = 56
HALO = 19


FIELDS = 11


def pack_rows(*refs):
    p, s, tx, ty, tz, pv, up, cell, rate, plan, observed = refs[:FIELDS]
    own, far, near, upi, cells, rates, plans, seen, sems = refs[FIELDS:]
    targets = [own.at[pl.ds(*GROUPS[name])] for name in ORDER[:6]] + [upi, cells, rates, plans, seen]
    copies = [
        pltpu.make_async_copy(source, target, sems.at[k])
        for k, (source, target) in enumerate(zip(refs[:FIELDS], targets))
    ]
    for copy in copies:
        copy.start()
    for copy in copies:
        copy.wait()
    first = GROUPS["up"][0]
    for layer in range(4):
        own[first + layer] = upi[layer].astype(jnp.float32)
    own[COUNT] = jnp.zeros((16, 128), jnp.float32)
    own[COUNT, 0:1, 0:64] = cells[0].astype(jnp.float32)
    own[COUNT, 1:2, 0:64] = rates[0]
    for n in range(2):
        own[COUNT, 2 + n : 3 + n, 0:64] = plans[n, 0].astype(jnp.float32)
        for k in range(2):
            row = 4 + 2 * n + k
            own[COUNT, row : row + 1, 0:64] = seen[n, k, 0]
    odd = lax.axis_index("gx") & 1
    for g in range(COUNT):
        far[g] = own[g, pl.ds(pl.multiple_of(8 * odd, 8), 8), :]
        near[g] = own[g, pl.ds(pl.multiple_of(8 - 8 * odd, 8), 8), :]
    base = {name: GROUPS[name][0] for name in ORDER}

    blank = jnp.zeros((1, 128), jnp.float32)

    def gathered(*places):
        rows = []
        for layer in (0, 2, 1, 3):
            for name, row in places:
                there = layer < GROUPS[name][1]
                rows.append(own[base[name] + layer, row : row + 1, :] if there else blank)
        return jnp.concatenate([rows[k] for k in (0, 2, 1, 3, 4, 6, 5, 7)], axis=0)

    for_next = [gathered(("p", 7), ("tx", 7))]
    for_next += [jnp.zeros((8, 128), jnp.float32)] * 2
    for_prev = [
        gathered(("p", 8), ("tx", 8)),
        gathered(("ty", 8), ("tz", 8)),
        gathered(("pv", 8), ("p", 9)),
    ]
    for k in range(3):
        far[COUNT + k] = jnp.where(odd == 1, for_next[k], for_prev[k])
        near[COUNT + k] = jnp.where(odd == 1, for_prev[k], for_next[k])
    far[COUNT + 3] = own[COUNT, 0:8, :]
    near[COUNT + 3] = own[COUNT, 0:8, :]


def lanes():
    return lax.broadcasted_iota(jnp.int32, (8, 128), 1)


def in_slot(lane, start):
    return ((lane - start) & 63) < SLOT


def sorted_ends(axis, far, near):
    odd = (lax.axis_index(axis) & 1) == 1

    def before(g):
        return jnp.where(odd, near[g], far[g])

    def after(g):
        return jnp.where(odd, far[g], near[g])

    return before, after


def layer_pairs(block):
    pairs = []
    for name in ORDER:
        first, layers = GROUPS[name]
        for layer in (0, 2):
            second = block(first + layer + 1) if layer + 1 < layers else jnp.zeros((8, 128), jnp.float32)
            pairs.append((block(first + layer), second))
    return pairs


def pack_pairs(pairs, far, near, at):
    odd = lax.axis_index("gy") & 1
    lane = lanes()
    moved = [pltpu.roll(second, 64, 1) for _, second in pairs]
    for out, ends in ((far, odd), (near, 1 - odd)):
        masks = [in_slot(lane, SLOT * (j + ends)) for j in range(SLOTS)]
        straight = ((lane >> 6) ^ ends) == 0
        for k in range(0, len(pairs), SLOTS):
            part = jnp.zeros((8, 128), jnp.float32)
            for j in range(min(SLOTS, len(pairs) - k)):
                pair = jnp.where(straight, pairs[k + j][0], moved[k + j])
                part = jnp.where(masks[j], pltpu.roll(pair, SLOT * j + 2 * SLOT * ends, 1), part)
            out[at + k // SLOTS] = part


def pack_own(own, far, near):
    pairs = []
    for rows in (slice(0, 8), slice(8, 16)):
        pairs += layer_pairs(lambda g: own[g, rows, :])
    pack_pairs(pairs, far, near, 0)


def pack_cols(own, own_far, own_near, row_far, row_near, far, near):
    low, high = sorted_ends("gx", row_far, row_near)
    for out, part in ((far, own_far), (near, own_near)):
        for at in range(PACKED):
            out[at] = part[at]
    pairs = layer_pairs(low) + layer_pairs(high)
    for one, two in ((low(COUNT), high(COUNT)), (high(COUNT + 1), high(COUNT + 2))):
        pairs.append(tuple(jnp.concatenate([one[k : k + 4], two[k : k + 4]], axis=0) for k in (0, 4)))
    pack_pairs(pairs, far, near, PACKED)
    both = jnp.where(lanes() < 64, own[COUNT, 0:8, :], pltpu.roll(low(COUNT + 3), 64, 1))
    for out in (far, near):
        out[2 * PACKED] = both
        out[2 * PACKED + 1] = high(COUNT + 3)


def split3(value):
    hi = value.astype(jnp.bfloat16).astype(jnp.float32)
    rest = value - hi
    mid = rest.astype(jnp.bfloat16).astype(jnp.float32)
    return hi, mid, rest - mid


SRC0, SRC1, OP0, OS0, OP1, OS1, CNT = range(7)


def well_fields(info):
    rate = info[1:2] * 0.5
    values = [rate * info[2:3], rate * info[3:4]] + [info[k : k + 1] for k in range(4, 8)]
    cell = info[0:1].astype(jnp.int32)
    layer = lax.shift_right_logical(cell, 11)
    row = lax.shift_right_logical(cell, 7) & 15
    return values, layer, row, cell & 127


def hits(layer, place, inside):
    target = jnp.where(inside & (place >= 8), layer * 40 + place - 8, -1)
    rows = lax.broadcasted_iota(jnp.int32, (160, target.shape[1]), 0)
    return rows == target


def dot(left, right):
    return lax.dot_general(left, right, (((1,), (1,)), ((), ())), preferred_element_type=jnp.float32)


def scatter_center(lists, dense):
    info = jnp.concatenate(lists, axis=1)
    values, layer, row, col = well_fields(info)
    lane = lax.broadcasted_iota(jnp.int32, (1, info.shape[1]), 1)
    hit = hits(layer, row + jnp.where(lane < 64, 16, jnp.where(lane < 128, 0, 32)), lane >= 0)
    cols = lax.broadcasted_iota(jnp.int32, (128, info.shape[1]), 0)
    to_col = jnp.where(cols == col, 1.0, 0.0).astype(jnp.bfloat16)
    for number, value in enumerate(values + [None]):
        parts = (1.0,) if value is None else split3(value)
        total = None
        for part in parts:
            term = dot(jnp.where(hit, part, 0.0).astype(jnp.bfloat16), to_col)
            total = term if total is None else total + term
        for k in range(4):
            dense[number, k, 8:48, :] = total[k * 40 : k * 40 + 40]


def scatter_beside(lists, edge_dense, dense, beside, lower):
    info = jnp.concatenate(lists, axis=1)
    width = info.shape[1]
    values, layer, row, col = well_fields(info)
    block = lax.shift_right_logical(lax.broadcasted_iota(jnp.int32, (1, width), 1), 6)
    base = jnp.where(block < 2, 16, jnp.where(block < 4, 0, 32))
    ahead = (block & 1) == 1
    spot = jnp.where(ahead, col, col - 128 + 2 * SLOT)
    inside = (spot >= jnp.where(ahead, 0, SLOT)) & (spot < jnp.where(ahead, SLOT, 2 * SLOT))
    left = jnp.where(hits(layer, row + base, inside), 1.0, 0.0).astype(jnp.bfloat16)
    spots = lax.broadcasted_iota(jnp.int32, (24, width), 0)
    hit = spots == spot
    parts = [split3(value) for value in values]
    for first, last in ((0, 5), (5, 7)):
        total = None
        for piece in range(3):
            rights = []
            for number in range(first, last):
                part = jnp.float32(1.0 if piece == 0 else 0.0) if number == CNT else parts[number][piece]
                rights.append(jnp.where(hit, part, 0.0))
            rights += [jnp.zeros((128 - 24 * (last - first), width), jnp.float32)]
            term = dot(left, jnp.concatenate(rights, axis=0).astype(jnp.bfloat16))
            total = term if total is None else total + term
        for number in range(first, last):
            shift = HALO - 24 * (number - first)
            for pair in range(2):
                for t in range(5):
                    rows = slice(8 + 8 * t, 16 + 8 * t)
                    at = 80 * pair + 8 * t
                    one = pltpu.roll(total[at : at + 8], shift % 128, 1)
                    two = pltpu.roll(total[at + 40 : at + 48], (shift + 64) % 128, 1)
                    value = jnp.where(lower, one, two)
                    dense[number, pair, rows, :] = jnp.where(beside, value, edge_dense[number, pair, rows, :])


def scratch_of(slabs, groups):
    counts = (slabs,) * 12 + (3 * slabs,) * 4 + (slabs,) * 9
    f32 = jnp.float32
    shapes = [pltpu.VMEM((groups, ROWS, 128), f32), pltpu.VMEM((7, slabs, ROWS, 128), f32)]
    shapes += [pltpu.VMEM((slabs, ROWS, 128), jnp.int32)]
    return shapes + [pltpu.VMEM((count, ROWS, 128), f32) for count in counts]


class Single:
    slabs = 4
    first = {name: GROUPS[name][0] for name in ORDER}

    def above(self, values):
        return values[1:] + [None]

    def below(self, values):
        return [None] + values[:-1]


class Paired:
    slabs = 2
    first = {name: 2 * k for k, name in enumerate(ORDER)}

    def __init__(self, lower):
        self.lower = lower

    def turned(self, values):
        turned = [pltpu.roll(value, 64, 1) for value in values]
        return turned, jnp.where(self.lower, turned[0], turned[1])

    def above(self, values):
        turned, middle = self.turned(values)
        return [middle, turned[1]]

    def below(self, values):
        turned, middle = self.turned(values)
        return [jnp.where(self.lower, 0.0, turned[0]), middle]

    def around(self, values):
        turned, middle = self.turned(values)
        return [middle, turned[1]], [turned[0], middle]


def simulate(form, fld, dense, upi, scratch, emit_x, emit_y, emit_z):
    (rcp, tym, tzd, q0, p1, q1, p2, f0, d0, s1, f1, d1, fup0, fup1, dp1, dp2,
     sig2, psi2, psi1, mup2, muq1, mup1, muq0, flux, rest) = scratch
    slabs = range(form.slabs)
    n = form.slabs
    paired = n == 2
    PB, SB, XB, YB, ZB, VB = (form.first[name] for name in ORDER[:6])
    Z_UP = [paired or k < n - 1 for k in slabs]
    Z_DOWN = [paired or k > 0 for k in slabs]

    def here(ref, k, t):
        return ref[k, 8 * t : 8 * t + 8, :]

    def down(ref, k, t):
        return ref[k, 8 * t + 1 : 8 * t + 9, :]

    def above(ref, k, t):
        return ref[k, 8 * t - 1 : 8 * t + 7, :]

    def put(ref, k, t, value):
        ref[k, 8 * t : 8 * t + 8, :] = value

    def all_of(ref, base, t):
        return [here(ref, base + k, t) for k in slabs]

    def right(value):
        return pltpu.roll(value, 127, 1)

    def left(value):
        return pltpu.roll(value, 1, 1)

    def around(values):
        if paired:
            return form.around(values)
        return form.above(values), form.below(values)

    def z_below(k, t):
        return here(tzd, k, t) if paired else here(fld, ZB + k - 1, t)

    for k in slabs:
        for t in range(1, 6):
            beyond = right(here(fld, VB + k, t))
            put(fld, YB + k, t, jnp.where(beyond == 0.0, 0.0, here(fld, YB + k, t)))
        last = slice(31, 32)
        fld[XB + k, last, :] = jnp.where(fld[VB + k, 32:33, :] == 0.0, 0.0, fld[XB + k, last, :])
    for t in range(1, 6):
        if paired:
            for k, value in enumerate(form.below(all_of(fld, ZB, t))):
                put(tzd, k, t, value)
        for k in slabs:
            volume = here(fld, VB + k, t)
            volume = jnp.where(volume == 0.0, 1.0, volume)
            put(fld, VB + k, t, volume)
            west = left(here(fld, YB + k, t))
            put(tym, k, t, west)
            total = volume + (here(fld, XB + k, t) + above(fld, XB + k, t)) + (here(fld, YB + k, t) + west)
            if Z_UP[k]:
                total = total + here(fld, ZB + k, t)
            if Z_DOWN[k]:
                total = total + z_below(k, t)
            put(rcp, k, t, 1.0 / total)

    def neighbours(ref, base, t):
        values = all_of(ref, base, t)
        ups, downs = around(values)
        totals = []
        for k in slabs:
            total = here(fld, XB + k, t) * down(ref, base + k, t) + above(fld, XB + k, t) * above(ref, base + k, t)
            total = total + (here(fld, YB + k, t) * right(values[k]) + here(tym, k, t) * left(values[k]))
            if Z_UP[k]:
                total = total + here(fld, ZB + k, t) * ups[k]
            if Z_DOWN[k]:
                total = total + z_below(k, t) * downs[k]
            totals.append(total)
        return totals

    def relax(out, ref, base, old, old_base, source, tiles):
        for t in tiles:
            totals = neighbours(ref, base, t)
            for k in slabs:
                total = here(fld, VB + k, t) * here(old, old_base + k, t) + here(dense.at[source], k, t)
                put(out, k, t, (total + totals[k]) * here(rcp, k, t))

    def put_mobility(value, k, t, mobile, slope):
        rest_of = 1.0 - value
        wetted = value * value
        inverse = 1.0 / (wetted + 0.5 * rest_of * rest_of)
        put(mobile, k, t, wetted * inverse)
        put(slope, k, t, value * rest_of * (inverse * inverse))

    def bit(k, t, number):
        return (here(upi, k, t) & (1 << number)) != 0

    def net_of(parts_x, parts_y, parts_z, ref, t, sign):
        below = form.below(parts_z)
        nets = []
        for k in slabs:
            put(ref, k, t, parts_x[k])
            before_x, before_y = above(ref, k, t), left(parts_y[k])
            if sign < 0:
                net = (parts_x[k] - before_x) + (parts_y[k] - before_y)
            else:
                net = before_x + before_y
            if Z_UP[k] and sign < 0:
                net = net + parts_z[k]
            if Z_DOWN[k]:
                net = net - below[k] if sign < 0 else net + below[k]
            nets.append(net)
        return nets

    def transport(pressure, sat, sat_base, mobile, number, fup, dp, finish):
        for t in range(1, 5):
            mobs, press = all_of(mobile, 0, t), all_of(pressure, 0, t)
            mobs_up, press_up = form.above(mobs), form.above(press)
            flux_x, flux_y, flux_z = [], [], []
            for k in slabs:
                drop_x = press[k] - down(pressure, k, t)
                drop_y = press[k] - right(press[k])
                up_x = jnp.where(bit(k, t, 3 * number), mobs[k], down(mobile, k, t))
                up_y = jnp.where(bit(k, t, 3 * number + 1), mobs[k], right(mobs[k]))
                put(fup, k, t, up_x)
                put(fup, n + k, t, up_y)
                put(dp, k, t, drop_x)
                put(dp, n + k, t, drop_y)
                flux_x.append(here(fld, XB + k, t) * up_x * drop_x)
                flux_y.append(here(fld, YB + k, t) * up_y * drop_y)
                if Z_UP[k]:
                    drop_z = press[k] - press_up[k]
                    up_z = jnp.where(bit(k, t, 3 * number + 2), mobs[k], mobs_up[k])
                    put(fup, 2 * n + k, t, up_z)
                    put(dp, 2 * n + k, t, drop_z)
                    flux_z.append(here(fld, ZB + k, t) * up_z * drop_z)
                else:
                    flux_z.append(None)
            nets = net_of(flux_x, flux_y, flux_z, flux, t, -1)
            for k in slabs:
                finish(here(sat, sat_base + k, t) - time_step * nets[k] / here(fld, VB + k, t), k, t)

    tiles = range(1, 5)
    relax(q0, fld, PB, fld, PB, SRC0, range(1, 6))
    relax(p1, q0, 0, fld, PB, SRC0, tiles)
    for t in tiles:
        for k in slabs:
            put_mobility(here(fld, SB + k, t), k, t, f0, d0)

    def finish_first(moved, k, t):
        put(s1, k, t, moved)
        put_mobility(moved, k, t, f1, d1)

    transport(p1, fld, SB, f0, 0, fup0, dp1, finish_first)
    relax(q1, p1, 0, p1, 0, SRC1, tiles)
    relax(p2, q1, 0, p1, 0, SRC1, tiles)

    def finish_second(moved, k, t):
        miss = here(dense.at[CNT], k, t) * moved - here(dense.at[OS1], k, t)
        put(sig2, k, t, miss)
        put(psi2, k, t, time_step * miss / here(fld, VB + k, t))

    transport(p2, s1, 0, f1, 1, fup1, dp2, finish_second)

    for t in tiles:
        psis = all_of(psi2, 0, t)
        psis_up = form.above(psis)
        hs, rests, sums = ([], [], []), ([], [], []), []
        for k in slabs:
            ahead = [down(psi2, k, t), right(psis[k]), psis_up[k]]
            total = None
            for d, base in enumerate((XB, YB, ZB)):
                if d == 2 and not Z_UP[k]:
                    hs[d].append(None)
                    rests[d].append(None)
                    continue
                phi = (ahead[d] - psis[k]) * here(fld, base + k, t)
                hs[d].append(phi * here(fup1, d * n + k, t))
                part = phi * here(dp2, d * n + k, t)
                mine = jnp.where(bit(k, t, 3 + d), part, 0.0)
                rests[d].append(part - mine)
                total = mine if total is None else total + mine
            sums.append(total)
        press = net_of(*hs, flux, t, -1)
        satur = net_of(*rests, rest, t, 1)
        for k in slabs:
            count = here(dense.at[CNT], k, t)
            total = press[k] + (count * here(p2, k, t) - here(dense.at[OP1], k, t))
            put(mup2, k, t, total * here(rcp, k, t))
            sigma = here(sig2, k, t) + (sums[k] + satur[k]) * here(d1, k, t)
            sigma = sigma + (count * here(s1, k, t) - here(dense.at[OS0], k, t))
            put(psi1, k, t, time_step * sigma / here(fld, VB + k, t))

    for t in tiles:
        totals = neighbours(mup2, 0, t)
        for k in slabs:
            put(muq1, k, t, totals[k] * here(rcp, k, t))

    for t in tiles:
        psis = all_of(psi1, 0, t)
        psis_up = form.above(psis)
        hs = ([], [], [])
        for k in slabs:
            ahead = [down(psi1, k, t), right(psis[k]), psis_up[k]]
            for d, base in enumerate((XB, YB, ZB)):
                there = d < 2 or Z_UP[k]
                hs[d].append(
                    (ahead[d] - psis[k]) * here(fld, base + k, t) * here(fup0, d * n + k, t) if there else None
                )
        press = net_of(*hs, flux, t, -1)
        totals = neighbours(muq1, 0, t)
        for k in slabs:
            count = here(dense.at[CNT], k, t)
            total = press[k] + (count * here(p1, k, t) - here(dense.at[OP0], k, t))
            total = total + here(fld, VB + k, t) * (here(mup2, k, t) + here(muq1, k, t))
            put(mup1, k, t, (total + totals[k]) * here(rcp, k, t))

    for t in range(2, 5):
        totals = neighbours(mup1, 0, t)
        for k in slabs:
            put(muq0, k, t, totals[k] * here(rcp, k, t))

    stages = (
        (mup2, q1, 0, p2, 0),
        (muq1, p1, 0, q1, 0),
        (mup1, q0, 0, p1, 0),
        (muq0, fld, PB, q0, 0),
    )
    for t in range(2, 4):
        sums = [[0.0, 0.0, 0.0] for k in slabs]
        for psi, fup, dp in ((psi2, fup1, dp2), (psi1, fup0, dp1)):
            psis = all_of(psi, 0, t)
            psis_up = form.above(psis)
            for k in slabs:
                ahead = [down(psi, k, t), right(psis[k]), psis_up[k]]
                for d in range(3 if Z_UP[k] else 2):
                    part = (ahead[d] - psis[k]) * here(fup, d * n + k, t) * here(dp, d * n + k, t)
                    sums[k][d] = sums[k][d] + part
        for mu, value, base, out, out_base in stages:
            mu_c, v_c, o_c = all_of(mu, 0, t), all_of(value, base, t), all_of(out, out_base, t)
            mu_u, v_u, o_u = form.above(mu_c), form.above(v_c), form.above(o_c)
            for k in slabs:
                ahead = [
                    (down(mu, k, t), down(value, base + k, t), down(out, out_base + k, t)),
                    (right(mu_c[k]), right(v_c[k]), right(o_c[k])),
                    (mu_u[k], v_u[k], o_u[k]),
                ]
                for d in range(3 if Z_UP[k] else 2):
                    mu_n, v_n, o_n = ahead[d]
                    sums[k][d] = sums[k][d] + (mu_c[k] * (v_n - o_c[k]) + mu_n * (v_c[k] - o_n))
        for k in slabs:
            emit_x(k, t, jnp.where(here(fld, XB + k, t) == 0.0, 0.0, sums[k][0]))
            emit_y(k, t, jnp.where(here(fld, YB + k, t) == 0.0, 0.0, sums[k][1]))
            if Z_UP[k]:
                emit_z(k, t, sums[k][2])


PLACES = (
    (("p", 7), ("tx", 7)),
    (("p", 40), ("tx", 40)),
    (("ty", 40), ("tz", 40)),
    (("pv", 40), ("p", 41)),
)


def model_center(own, row_far, row_near, grads, edge, edge_dense, fld, dense, upi, *scratch):
    low, high = sorted_ends("gx", row_far, row_near)
    lane = lanes()

    def edge_of(one, two):
        count = one.shape[0]
        turned = pltpu.roll(two, 64, 1)
        lower = lane[:count] < 64
        firsts = pltpu.roll(jnp.where(lower, one, turned), HALO + 2 * SLOT, 1)
        lasts = pltpu.roll(jnp.where(lower, turned, one), HALO, 1)
        return jnp.where((lane[:count] & 63) < HALO, lasts, firsts)

    for g in range(COUNT):
        for k, block in enumerate((low(g), own[g, 0:8, :], own[g, 8:16, :], high(g))):
            rows = slice(8 + 8 * k, 16 + 8 * k)
            fld[g, rows, :] = block
            if g >= GROUPS["up"][0]:
                upi[g - GROUPS["up"][0], rows, :] = block.astype(jnp.int32)
    for value, places in zip([low(COUNT)] + [high(COUNT + k) for k in range(3)], PLACES):
        for block, (name, row) in enumerate(places):
            first, layers = GROUPS[name]
            for layer in range(layers):
                k = 4 * (layer & 1) + 2 * block + layer // 2
                fld[first + layer, row : row + 1, :] = value[k : k + 1]

    def pair_up(name, rows):
        first, layers = GROUPS[name]
        for pair in range(2):
            one = fld[first + 2 * pair, rows, :]
            there = 2 * pair + 1 < layers
            two = fld[first + 2 * pair + 1, rows, :] if there else jnp.zeros_like(one)
            edge[Paired.first[name] + pair, rows, :] = edge_of(one, two)

    for name in ORDER:
        for t in range(1, 5):
            pair_up(name, slice(8 * t, 8 * t + 8))
    for places in PLACES:
        for name, row in places:
            pair_up(name, slice(row, row + 1))
    scatter_center(
        [own[COUNT, 0:8, 0:64], low(COUNT + 3)[:, 0:64], high(COUNT + 3)[:, 0:64]], dense
    )
    for number in range(7):
        for pair in range(2):
            for t in range(1, 6):
                rows = slice(8 * t, 8 * t + 8)
                one, two = dense[number, 2 * pair, rows, :], dense[number, 2 * pair + 1, rows, :]
                edge_dense[number, pair, rows, :] = edge_of(one, two)

    def emit(first):
        def write(k, t, value):
            grads[first + k, 8 * t - 16 : 8 * t - 8, :] = value

        return write

    simulate(Single(), fld, dense, upi, scratch, emit(0), emit(4), emit(8))


def model_edge(
    col_far, col_near, edge, edge_dense, center, grad_x, grad_y, grad_z, fld, dense, upi, *scratch
):
    before, after = sorted_ends("gy", col_far, col_near)
    odd = lax.axis_index("gy") & 1
    lane = lanes()
    lower = lane < 64
    far_cols = [in_slot(lane, SLOT * (j + 1 - odd)) for j in range(SLOTS)]
    beside = ((lane - HALO) & 63) < 2 * SLOT

    def unpack(at, piece):
        at, j = at + piece // SLOTS, piece % SLOTS
        both = jnp.where(far_cols[j], col_far[at], col_near[at])
        return pltpu.roll(both, (HALO - SLOT * j) % 128, 1)

    for name in ORDER:
        for pair in range(2):
            g = Paired.first[name] + pair
            places = ((PACKED, g), (0, g), (0, PAIRS + g), (PACKED, PAIRS + g))
            for k, place in enumerate(places):
                rows = slice(8 + 8 * k, 16 + 8 * k)
                block = jnp.where(beside, unpack(*place), edge[g, rows, :])
                if name == "up":
                    upi[pair, rows, :] = block.astype(jnp.int32)
                else:
                    fld[g, rows, :] = block
    for half in range(2):
        value = unpack(PACKED, 2 * PAIRS + half)
        for number, places in enumerate(PLACES[2 * half : 2 * half + 2]):
            for block, (name, row) in enumerate(places):
                for pair in range(2):
                    k = 4 * number + 2 * block + pair
                    at = (Paired.first[name] + pair, slice(row, row + 1), slice(None))
                    fld[at] = jnp.where(beside[0:1], value[k : k + 1], edge[at])
    first, second = 2 * PACKED, 2 * PACKED + 1
    own_lists = [before(first)[:, 0:64], after(first)[:, 0:64]]
    low_lists = [before(first)[:, 64:128], after(first)[:, 64:128]]
    high_lists = [before(second)[:, 0:64], after(second)[:, 0:64]]
    scatter_beside(own_lists + low_lists + high_lists, edge_dense, dense, beside, lower)

    def emit(out, group):
        def write(k, t, value):
            rows = slice(8 * t - 16, 8 * t - 8)
            for half in range(2):
                layer = 2 * k + half
                if layer < out.shape[0]:
                    firsts = pltpu.roll(value, 128 - (HALO + 2 * SLOT) - 64 * half, 1)
                    lasts = pltpu.roll(value, 128 - HALO - 64 * half, 1)
                    inner = jnp.where(lane < SLOT - 1, firsts, center[group + layer, rows, :])
                    out[layer, rows, :] = jnp.where(lane >= 128 - SLOT, lasts, inner)

        return write

    simulate(Paired(lower), fld, dense, upi, scratch, emit(grad_x, 0), emit(grad_y, 4), emit(grad_z, 8))


def swapped(value, axis, first):
    count = lax.axis_size(axis)
    pairs = []
    for i in range(first, count - 1, 2):
        pairs += [(i, i + 1), (i + 1, i)]
    return lax.ppermute(value, axis, pairs)


def on_device(p, s, tx, ty, tz, pv, up, cell, rate, plan, observed):
    f32 = jnp.float32

    def shape(*dims):
        return jax.ShapeDtypeStruct(dims, f32)

    limit = pltpu.CompilerParams(vmem_limit_bytes=24 * 1024 * 1024)
    inputs = (p, s, tx, ty, tz, pv, up, cell, rate, plan, observed)
    inputs = [pltpu.with_memory_space_constraint(value, pltpu.HBM) for value in inputs]
    strip = shape(COUNT + 4, 8, 128)
    own, far, near = pl.pallas_call(
        pack_rows,
        out_shape=(shape(COUNT + 1, 16, 128), strip, strip),
        in_specs=[pl.BlockSpec(memory_space=pltpu.HBM)] * len(inputs),
        scratch_shapes=[pltpu.VMEM(value.shape, value.dtype) for value in inputs[6:]]
        + [pltpu.SemaphoreType.DMA((len(inputs),))],
        compiler_params=limit,
        name="pack_rows",
    )(*inputs)
    row_far = swapped(far, "gx", 1)
    row_near = swapped(near, "gx", 0)
    hide = pl.CostEstimate(flops=10**11, bytes_accessed=1 << 28, transcendentals=0)
    strip = shape(PACKED, 8, 128)
    own_far, own_near = pl.pallas_call(
        pack_own,
        out_shape=(strip, strip),
        compiler_params=limit,
        cost_estimate=hide,
        name="pack_own",
    )(own)
    strip = shape(2 * PACKED + 2, 8, 128)
    far, near = pl.pallas_call(
        pack_cols,
        out_shape=(strip, strip),
        compiler_params=limit,
        name="pack_cols",
    )(own, own_far, own_near, row_far, row_near)
    col_far = swapped(far, "gy", 1)
    col_near = swapped(near, "gy", 0)
    center, edge, edge_dense = pl.pallas_call(
        model_center,
        out_shape=(shape(11, 16, 128), shape(PAIRS, ROWS, 128), shape(7, 2, ROWS, 128)),
        scratch_shapes=scratch_of(4, COUNT),
        compiler_params=limit,
        cost_estimate=hide,
        name="model_center",
    )(own, row_far, row_near)
    return pl.pallas_call(
        model_edge,
        out_shape=(shape(*tx.shape), shape(*ty.shape), shape(*tz.shape)),
        scratch_shapes=scratch_of(2, PAIRS),
        compiler_params=limit,
        name="model_edge",
    )(col_far, col_near, edge, edge_dense, center)


def solution(mesh):
    cells = P(None, "gx", "gy")
    in_specs = (cells,) * 7 + (
        P("gx", "gy", None),
        P("gx", "gy", None),
        P(None, "gx", "gy", None),
        P(None, None, "gx", "gy", None),
    )
    return jax.shard_map(
        on_device, mesh=mesh, in_specs=in_specs, out_specs=(cells,) * 3, check_vma=False
    )
```

```python
import jax
import jax.numpy as jnp
from jax import lax
from jax.experimental import pallas as pl
from jax.experimental.pallas import tpu as pltpu
from jax.sharding import PartitionSpec as P

time_step = 0.05

GROUPS = {"p": (0, 4), "s": (4, 4), "tx": (8, 4), "ty": (12, 4), "tz": (16, 3), "pv": (19, 4), "up": (23, 4)}
ORDER = ("p", "s", "tx", "ty", "tz", "pv", "up")
COUNT = 27
SLOT = 10
SLOTS = 6
PAIRS = 14
PACKED = 5
ROWS = 56
HALO = 19


FIELDS = 11


def pack_rows(*refs):
    p, s, tx, ty, tz, pv, up, cell, rate, plan, observed = refs[:FIELDS]
    own, far, near, upi, cells, rates, plans, seen, sems = refs[FIELDS:]
    targets = [own.at[pl.ds(*GROUPS[name])] for name in ORDER[:6]] + [upi, cells, rates, plans, seen]
    copies = [
        pltpu.make_async_copy(source, target, sems.at[k])
        for k, (source, target) in enumerate(zip(refs[:FIELDS], targets))
    ]
    for copy in copies:
        copy.start()
    for copy in copies:
        copy.wait()
    first = GROUPS["up"][0]
    for layer in range(4):
        own[first + layer] = upi[layer].astype(jnp.float32)
    own[COUNT] = jnp.zeros((16, 128), jnp.float32)
    own[COUNT, 0:1, 0:64] = cells[0].astype(jnp.float32)
    own[COUNT, 1:2, 0:64] = rates[0]
    for n in range(2):
        own[COUNT, 2 + n : 3 + n, 0:64] = plans[n, 0].astype(jnp.float32)
        for k in range(2):
            row = 4 + 2 * n + k
            own[COUNT, row : row + 1, 0:64] = seen[n, k, 0]
    odd = lax.axis_index("gx") & 1
    for g in range(COUNT):
        far[g] = own[g, pl.ds(pl.multiple_of(8 * odd, 8), 8), :]
        near[g] = own[g, pl.ds(pl.multiple_of(8 - 8 * odd, 8), 8), :]
    base = {name: GROUPS[name][0] for name in ORDER}

    blank = jnp.zeros((1, 128), jnp.float32)

    def gathered(*places):
        rows = []
        for layer in (0, 2, 1, 3):
            for name, row in places:
                there = layer < GROUPS[name][1]
                rows.append(own[base[name] + layer, row : row + 1, :] if there else blank)
        return jnp.concatenate([rows[k] for k in (0, 2, 1, 3, 4, 6, 5, 7)], axis=0)

    for_next = [gathered(("p", 7), ("tx", 7))]
    for_next += [jnp.zeros((8, 128), jnp.float32)] * 2
    for_prev = [
        gathered(("p", 8), ("tx", 8)),
        gathered(("ty", 8), ("tz", 8)),
        gathered(("pv", 8), ("p", 9)),
    ]
    for k in range(3):
        far[COUNT + k] = jnp.where(odd == 1, for_next[k], for_prev[k])
        near[COUNT + k] = jnp.where(odd == 1, for_prev[k], for_next[k])
    far[COUNT + 3] = own[COUNT, 0:8, :]
    near[COUNT + 3] = own[COUNT, 0:8, :]


def lanes():
    return lax.broadcasted_iota(jnp.int32, (8, 128), 1)


def in_slot(lane, start):
    return ((lane - start) & 63) < SLOT


def sorted_ends(axis, far, near):
    odd = (lax.axis_index(axis) & 1) == 1

    def before(g):
        return jnp.where(odd, near[g], far[g])

    def after(g):
        return jnp.where(odd, far[g], near[g])

    return before, after


def layer_pairs(block):
    pairs = []
    for name in ORDER:
        first, layers = GROUPS[name]
        for layer in (0, 2):
            second = block(first + layer + 1) if layer + 1 < layers else jnp.zeros((8, 128), jnp.float32)
            pairs.append((block(first + layer), second))
    return pairs


def pack_pairs(pairs, far, near, at):
    odd = lax.axis_index("gy") & 1
    lane = lanes()
    moved = [pltpu.roll(second, 64, 1) for _, second in pairs]
    for out, ends in ((far, odd), (near, 1 - odd)):
        masks = [in_slot(lane, SLOT * (j + ends)) for j in range(SLOTS)]
        straight = ((lane >> 6) ^ ends) == 0
        for k in range(0, len(pairs), SLOTS):
            part = jnp.zeros((8, 128), jnp.float32)
            for j in range(min(SLOTS, len(pairs) - k)):
                pair = jnp.where(straight, pairs[k + j][0], moved[k + j])
                part = jnp.where(masks[j], pltpu.roll(pair, SLOT * j + 2 * SLOT * ends, 1), part)
            out[at + k // SLOTS] = part


def extra_pair(one, two):
    row = lax.broadcasted_iota(jnp.int32, (8, 128), 0)
    return jnp.where(row < 4, one, pltpu.roll(two, 4, 0)), jnp.where(row < 4, pltpu.roll(one, 4, 0), two)


def pack_own(own, far, near):
    pairs = []
    for rows in (slice(0, 8), slice(8, 16)):
        pairs += layer_pairs(lambda g: own[g, rows, :])
    pack_pairs(pairs, far, near, 0)


def pack_cols(own, own_far, own_near, row_far, row_near, far, near):
    low, high = sorted_ends("gx", row_far, row_near)
    for out, part in ((far, own_far), (near, own_near)):
        for at in range(PACKED):
            out[at] = part[at]
    pairs = layer_pairs(low) + layer_pairs(high)
    pairs.append(extra_pair(low(COUNT), high(COUNT)))
    pairs.append(extra_pair(high(COUNT + 1), high(COUNT + 2)))
    pack_pairs(pairs, far, near, PACKED)
    both = jnp.where(lanes() < 64, own[COUNT, 0:8, :], pltpu.roll(low(COUNT + 3), 64, 1))
    for out in (far, near):
        out[2 * PACKED] = both
        out[2 * PACKED + 1] = high(COUNT + 3)


def split3(value):
    hi = value.astype(jnp.bfloat16).astype(jnp.float32)
    rest = value - hi
    mid = rest.astype(jnp.bfloat16).astype(jnp.float32)
    return hi, mid, rest - mid


SRC0, SRC1, OP0, OS0, OP1, OS1, CNT = range(7)


def well_fields(info):
    rate = info[1:2] * 0.5
    values = [rate * info[2:3], rate * info[3:4]] + [info[k : k + 1] for k in range(4, 8)]
    cell = info[0:1].astype(jnp.int32)
    layer = lax.shift_right_logical(cell, 11)
    row = lax.shift_right_logical(cell, 7) & 15
    return values, layer, row, cell & 127


def hits(layer, place, inside):
    target = jnp.where(inside & (place >= 8), layer * 40 + place - 8, -1)
    rows = lax.broadcasted_iota(jnp.int32, (160, target.shape[1]), 0)
    return rows == target


def dot(left, right):
    return lax.dot_general(left, right, (((1,), (1,)), ((), ())), preferred_element_type=jnp.float32)


def scatter_center(lists, dense):
    info = jnp.concatenate(lists, axis=1)
    values, layer, row, col = well_fields(info)
    lane = lax.broadcasted_iota(jnp.int32, (1, info.shape[1]), 1)
    hit = hits(layer, row + jnp.where(lane < 64, 16, jnp.where(lane < 128, 0, 32)), lane >= 0)
    cols = lax.broadcasted_iota(jnp.int32, (128, info.shape[1]), 0)
    to_col = jnp.where(cols == col, 1.0, 0.0).astype(jnp.bfloat16)
    for number, value in enumerate(values + [None]):
        parts = (1.0,) if value is None else split3(value)
        total = None
        for part in parts:
            term = dot(jnp.where(hit, part, 0.0).astype(jnp.bfloat16), to_col)
            total = term if total is None else total + term
        for k in range(4):
            dense[number, k, 8:48, :] = total[k * 40 : k * 40 + 40]


def scatter_beside(lists, edge_dense, dense, beside, lower):
    info = jnp.concatenate(lists, axis=1)
    width = info.shape[1]
    values, layer, row, col = well_fields(info)
    block = lax.shift_right_logical(lax.broadcasted_iota(jnp.int32, (1, width), 1), 6)
    base = jnp.where(block < 2, 16, jnp.where(block < 4, 0, 32))
    ahead = (block & 1) == 1
    spot = jnp.where(ahead, col, col - 128 + 2 * SLOT)
    inside = (spot >= jnp.where(ahead, 0, SLOT)) & (spot < jnp.where(ahead, SLOT, 2 * SLOT))
    left = jnp.where(hits(layer, row + base, inside), 1.0, 0.0).astype(jnp.bfloat16)
    spots = lax.broadcasted_iota(jnp.int32, (24, width), 0)
    hit = spots == spot
    parts = [split3(value) for value in values] + [(1.0, 0.0, 0.0)]
    rights = []
    for piece in range(3):
        right = [jnp.where(hit, part[piece], 0.0) for part in parts]
        right.insert(5, jnp.zeros((8, width), jnp.float32))
        right.append(jnp.zeros((80, width), jnp.float32))
        rights.append(jnp.concatenate(right, axis=0).astype(jnp.bfloat16))
    total = dot(jnp.concatenate([left] * 3, axis=1), jnp.concatenate(rights, axis=1))
    for number in range(7):
        column = 0 if number < 5 else 128
        shift = HALO - 24 * (number if number < 5 else number - 5)
        for pair in range(2):
            for t in range(5):
                rows = slice(8 + 8 * t, 16 + 8 * t)
                at = 80 * pair + 8 * t
                one = pltpu.roll(total[at : at + 8, column : column + 128], shift % 128, 1)
                two = pltpu.roll(total[at + 40 : at + 48, column : column + 128], (shift + 64) % 128, 1)
                value = jnp.where(lower, one, two)
                dense[number, pair, rows, :] = jnp.where(beside, value, edge_dense[number, pair, rows, :])


def scratch_of(slabs, groups):
    counts = (slabs,) * 12 + (3 * slabs,) * 4 + (slabs,) * 9
    f32 = jnp.float32
    shapes = [pltpu.VMEM((groups, ROWS, 128), f32), pltpu.VMEM((7, slabs, ROWS, 128), f32)]
    shapes += [pltpu.VMEM((slabs, ROWS, 128), jnp.int32)]
    return shapes + [pltpu.VMEM((count, ROWS, 128), f32) for count in counts]


class Single:
    slabs = 4
    first = {name: GROUPS[name][0] for name in ORDER}

    def above(self, values):
        return values[1:] + [None]

    def below(self, values):
        return [None] + values[:-1]


class Paired:
    slabs = 2
    first = {name: 2 * k for k, name in enumerate(ORDER)}

    def __init__(self, lower):
        self.lower = lower

    def turned(self, values):
        turned = [pltpu.roll(value, 64, 1) for value in values]
        return turned, jnp.where(self.lower, turned[0], turned[1])

    def above(self, values):
        turned, middle = self.turned(values)
        return [middle, turned[1]]

    def below(self, values):
        turned, middle = self.turned(values)
        return [jnp.where(self.lower, 0.0, turned[0]), middle]

    def around(self, values):
        turned, middle = self.turned(values)
        return [middle, turned[1]], [turned[0], middle]


def simulate(form, fld, dense, upi, scratch, emit_x, emit_y, emit_z):
    (rcp, tym, tzd, q0, p1, q1, p2, f0, d0, s1, f1, d1, fup0, fup1, dp1, dp2,
     sig2, psi2, psi1, mup2, muq1, mup1, muq0, flux, rest) = scratch
    slabs = range(form.slabs)
    n = form.slabs
    paired = n == 2
    PB, SB, XB, YB, ZB, VB = (form.first[name] for name in ORDER[:6])
    Z_UP = [paired or k < n - 1 for k in slabs]
    Z_DOWN = [paired or k > 0 for k in slabs]

    def here(ref, k, t):
        return ref[k, 8 * t : 8 * t + 8, :]

    def down(ref, k, t):
        return ref[k, 8 * t + 1 : 8 * t + 9, :]

    def above(ref, k, t):
        return ref[k, 8 * t - 1 : 8 * t + 7, :]

    def put(ref, k, t, value):
        ref[k, 8 * t : 8 * t + 8, :] = value

    def all_of(ref, base, t):
        return [here(ref, base + k, t) for k in slabs]

    def right(value):
        return pltpu.roll(value, 127, 1)

    def left(value):
        return pltpu.roll(value, 1, 1)

    def around(values):
        if paired:
            return form.around(values)
        return form.above(values), form.below(values)

    def z_below(k, t):
        return here(tzd, k, t) if paired else here(fld, ZB + k - 1, t)

    for k in slabs:
        for t in range(1, 6):
            beyond = right(here(fld, VB + k, t))
            put(fld, YB + k, t, jnp.where(beyond == 0.0, 0.0, here(fld, YB + k, t)))
        last = slice(31, 32)
        fld[XB + k, last, :] = jnp.where(fld[VB + k, 32:33, :] == 0.0, 0.0, fld[XB + k, last, :])
    for t in range(1, 6):
        if paired:
            for k, value in enumerate(form.below(all_of(fld, ZB, t))):
                put(tzd, k, t, value)
        for k in slabs:
            volume = here(fld, VB + k, t)
            volume = jnp.where(volume == 0.0, 1.0, volume)
            put(fld, VB + k, t, volume)
            west = left(here(fld, YB + k, t))
            put(tym, k, t, west)
            total = volume + (here(fld, XB + k, t) + above(fld, XB + k, t)) + (here(fld, YB + k, t) + west)
            if Z_UP[k]:
                total = total + here(fld, ZB + k, t)
            if Z_DOWN[k]:
                total = total + z_below(k, t)
            put(rcp, k, t, 1.0 / total)

    def neighbours(ref, base, t):
        values = all_of(ref, base, t)
        ups, downs = around(values)
        totals = []
        for k in slabs:
            total = here(fld, XB + k, t) * down(ref, base + k, t) + above(fld, XB + k, t) * above(ref, base + k, t)
            total = total + (here(fld, YB + k, t) * right(values[k]) + here(tym, k, t) * left(values[k]))
            if Z_UP[k]:
                total = total + here(fld, ZB + k, t) * ups[k]
            if Z_DOWN[k]:
                total = total + z_below(k, t) * downs[k]
            totals.append(total)
        return totals

    def relax(out, ref, base, old, old_base, source, tiles):
        for t in tiles:
            totals = neighbours(ref, base, t)
            for k in slabs:
                total = here(fld, VB + k, t) * here(old, old_base + k, t) + here(dense.at[source], k, t)
                put(out, k, t, (total + totals[k]) * here(rcp, k, t))

    def put_mobility(value, k, t, mobile, slope):
        rest_of = 1.0 - value
        wetted = value * value
        inverse = 1.0 / (wetted + 0.5 * rest_of * rest_of)
        put(mobile, k, t, wetted * inverse)
        put(slope, k, t, value * rest_of * (inverse * inverse))

    def bit(k, t, number):
        return (here(upi, k, t) & (1 << number)) != 0

    def net_of(parts_x, parts_y, parts_z, ref, t, sign):
        below = form.below(parts_z)
        nets = []
        for k in slabs:
            put(ref, k, t, parts_x[k])
            before_x, before_y = above(ref, k, t), left(parts_y[k])
            if sign < 0:
                net = (parts_x[k] - before_x) + (parts_y[k] - before_y)
            else:
                net = before_x + before_y
            if Z_UP[k] and sign < 0:
                net = net + parts_z[k]
            if Z_DOWN[k]:
                net = net - below[k] if sign < 0 else net + below[k]
            nets.append(net)
        return nets

    def transport(pressure, sat, sat_base, mobile, number, fup, dp, finish):
        for t in range(1, 5):
            mobs, press = all_of(mobile, 0, t), all_of(pressure, 0, t)
            mobs_up, press_up = form.above(mobs), form.above(press)
            flux_x, flux_y, flux_z = [], [], []
            for k in slabs:
                drop_x = press[k] - down(pressure, k, t)
                drop_y = press[k] - right(press[k])
                up_x = jnp.where(bit(k, t, 3 * number), mobs[k], down(mobile, k, t))
                up_y = jnp.where(bit(k, t, 3 * number + 1), mobs[k], right(mobs[k]))
                put(fup, k, t, up_x)
                put(fup, n + k, t, up_y)
                put(dp, k, t, drop_x)
                put(dp, n + k, t, drop_y)
                flux_x.append(here(fld, XB + k, t) * up_x * drop_x)
                flux_y.append(here(fld, YB + k, t) * up_y * drop_y)
                if Z_UP[k]:
                    drop_z = press[k] - press_up[k]
                    up_z = jnp.where(bit(k, t, 3 * number + 2), mobs[k], mobs_up[k])
                    put(fup, 2 * n + k, t, up_z)
                    put(dp, 2 * n + k, t, drop_z)
                    flux_z.append(here(fld, ZB + k, t) * up_z * drop_z)
                else:
                    flux_z.append(None)
            nets = net_of(flux_x, flux_y, flux_z, flux, t, -1)
            for k in slabs:
                finish(here(sat, sat_base + k, t) - time_step * nets[k] / here(fld, VB + k, t), k, t)

    tiles = range(1, 5)
    relax(q0, fld, PB, fld, PB, SRC0, range(1, 6))
    relax(p1, q0, 0, fld, PB, SRC0, tiles)
    for t in tiles:
        for k in slabs:
            put_mobility(here(fld, SB + k, t), k, t, f0, d0)

    def finish_first(moved, k, t):
        put(s1, k, t, moved)
        put_mobility(moved, k, t, f1, d1)

    transport(p1, fld, SB, f0, 0, fup0, dp1, finish_first)
    relax(q1, p1, 0, p1, 0, SRC1, tiles)
    relax(p2, q1, 0, p1, 0, SRC1, tiles)

    def finish_second(moved, k, t):
        miss = here(dense.at[CNT], k, t) * moved - here(dense.at[OS1], k, t)
        put(sig2, k, t, miss)
        put(psi2, k, t, time_step * miss / here(fld, VB + k, t))

    transport(p2, s1, 0, f1, 1, fup1, dp2, finish_second)

    for t in tiles:
        psis = all_of(psi2, 0, t)
        psis_up = form.above(psis)
        hs, rests, sums = ([], [], []), ([], [], []), []
        for k in slabs:
            ahead = [down(psi2, k, t), right(psis[k]), psis_up[k]]
            total = None
            for d, base in enumerate((XB, YB, ZB)):
                if d == 2 and not Z_UP[k]:
                    hs[d].append(None)
                    rests[d].append(None)
                    continue
                phi = (ahead[d] - psis[k]) * here(fld, base + k, t)
                hs[d].append(phi * here(fup1, d * n + k, t))
                part = phi * here(dp2, d * n + k, t)
                mine = jnp.where(bit(k, t, 3 + d), part, 0.0)
                rests[d].append(part - mine)
                total = mine if total is None else total + mine
            sums.append(total)
        press = net_of(*hs, flux, t, -1)
        satur = net_of(*rests, rest, t, 1)
        for k in slabs:
            count = here(dense.at[CNT], k, t)
            total = press[k] + (count * here(p2, k, t) - here(dense.at[OP1], k, t))
            put(mup2, k, t, total * here(rcp, k, t))
            sigma = here(sig2, k, t) + (sums[k] + satur[k]) * here(d1, k, t)
            sigma = sigma + (count * here(s1, k, t) - here(dense.at[OS0], k, t))
            put(psi1, k, t, time_step * sigma / here(fld, VB + k, t))

    for t in tiles:
        totals = neighbours(mup2, 0, t)
        for k in slabs:
            put(muq1, k, t, totals[k] * here(rcp, k, t))

    for t in tiles:
        psis = all_of(psi1, 0, t)
        psis_up = form.above(psis)
        hs = ([], [], [])
        for k in slabs:
            ahead = [down(psi1, k, t), right(psis[k]), psis_up[k]]
            for d, base in enumerate((XB, YB, ZB)):
                there = d < 2 or Z_UP[k]
                hs[d].append(
                    (ahead[d] - psis[k]) * here(fld, base + k, t) * here(fup0, d * n + k, t) if there else None
                )
        press = net_of(*hs, flux, t, -1)
        totals = neighbours(muq1, 0, t)
        for k in slabs:
            count = here(dense.at[CNT], k, t)
            total = press[k] + (count * here(p1, k, t) - here(dense.at[OP0], k, t))
            total = total + here(fld, VB + k, t) * (here(mup2, k, t) + here(muq1, k, t))
            put(mup1, k, t, (total + totals[k]) * here(rcp, k, t))

    for t in range(2, 5):
        totals = neighbours(mup1, 0, t)
        for k in slabs:
            put(muq0, k, t, totals[k] * here(rcp, k, t))

    stages = (
        (mup2, q1, 0, p2, 0),
        (muq1, p1, 0, q1, 0),
        (mup1, q0, 0, p1, 0),
        (muq0, fld, PB, q0, 0),
    )
    for t in range(2, 4):
        sums = [[0.0, 0.0, 0.0] for k in slabs]
        for psi, fup, dp in ((psi2, fup1, dp2), (psi1, fup0, dp1)):
            psis = all_of(psi, 0, t)
            psis_up = form.above(psis)
            for k in slabs:
                ahead = [down(psi, k, t), right(psis[k]), psis_up[k]]
                for d in range(3 if Z_UP[k] else 2):
                    part = (ahead[d] - psis[k]) * here(fup, d * n + k, t) * here(dp, d * n + k, t)
                    sums[k][d] = sums[k][d] + part
        for mu, value, base, out, out_base in stages:
            mu_c, v_c, o_c = all_of(mu, 0, t), all_of(value, base, t), all_of(out, out_base, t)
            mu_u, v_u, o_u = form.above(mu_c), form.above(v_c), form.above(o_c)
            for k in slabs:
                ahead = [
                    (down(mu, k, t), down(value, base + k, t), down(out, out_base + k, t)),
                    (right(mu_c[k]), right(v_c[k]), right(o_c[k])),
                    (mu_u[k], v_u[k], o_u[k]),
                ]
                for d in range(3 if Z_UP[k] else 2):
                    mu_n, v_n, o_n = ahead[d]
                    sums[k][d] = sums[k][d] + (mu_c[k] * (v_n - o_c[k]) + mu_n * (v_c[k] - o_n))
        for k in slabs:
            emit_x(k, t, jnp.where(here(fld, XB + k, t) == 0.0, 0.0, sums[k][0]))
            emit_y(k, t, jnp.where(here(fld, YB + k, t) == 0.0, 0.0, sums[k][1]))
            if Z_UP[k]:
                emit_z(k, t, sums[k][2])


PLACES = (
    (("p", 7), ("tx", 7)),
    (("p", 40), ("tx", 40)),
    (("ty", 40), ("tz", 40)),
    (("pv", 40), ("p", 41)),
)


def model_center(own, row_far, row_near, grads, edge, edge_dense, fld, dense, upi, *scratch):
    low, high = sorted_ends("gx", row_far, row_near)
    lane = lanes()

    def edge_of(one, two):
        turned = pltpu.roll(two, 64, 1)
        lower = lane < 64
        firsts = pltpu.roll(jnp.where(lower, one, turned), HALO + 2 * SLOT, 1)
        lasts = pltpu.roll(jnp.where(lower, turned, one), HALO, 1)
        return jnp.where((lane & 63) < HALO, lasts, firsts)

    for g in range(COUNT):
        for k, block in enumerate((low(g), own[g, 0:8, :], own[g, 8:16, :], high(g))):
            rows = slice(8 + 8 * k, 16 + 8 * k)
            fld[g, rows, :] = block
            if g >= GROUPS["up"][0]:
                upi[g - GROUPS["up"][0], rows, :] = block.astype(jnp.int32)
    extras = [low(COUNT)] + [high(COUNT + k) for k in range(3)]
    for value, places in zip(extras, PLACES):
        for block, (name, row) in enumerate(places):
            first, layers = GROUPS[name]
            for layer in range(layers):
                k = 4 * (layer & 1) + 2 * block + layer // 2
                fld[first + layer, row : row + 1, :] = value[k : k + 1]
    for half in range(2):
        value = edge_of(*extra_pair(*extras[2 * half : 2 * half + 2]))
        for number, places in enumerate(PLACES[2 * half : 2 * half + 2]):
            for block, (name, row) in enumerate(places):
                for pair in range(2):
                    k = 4 * number + 2 * block + pair
                    edge[Paired.first[name] + pair, row : row + 1, :] = value[k : k + 1]

    def pair_up(name, rows):
        first, layers = GROUPS[name]
        for pair in range(2):
            one = fld[first + 2 * pair, rows, :]
            there = 2 * pair + 1 < layers
            two = fld[first + 2 * pair + 1, rows, :] if there else jnp.zeros_like(one)
            edge[Paired.first[name] + pair, rows, :] = edge_of(one, two)

    for name in ORDER:
        for t in range(1, 5):
            pair_up(name, slice(8 * t, 8 * t + 8))
    scatter_center(
        [own[COUNT, 0:8, 0:64], low(COUNT + 3)[:, 0:64], high(COUNT + 3)[:, 0:64]], dense
    )
    for number in range(7):
        for pair in range(2):
            for t in range(1, 6):
                rows = slice(8 * t, 8 * t + 8)
                one, two = dense[number, 2 * pair, rows, :], dense[number, 2 * pair + 1, rows, :]
                edge_dense[number, pair, rows, :] = edge_of(one, two)

    def emit(first):
        def write(k, t, value):
            grads[first + k, 8 * t - 16 : 8 * t - 8, :] = value

        return write

    simulate(Single(), fld, dense, upi, scratch, emit(0), emit(4), emit(8))


def model_edge(
    col_far, col_near, edge, edge_dense, center, grad_x, grad_y, grad_z, fld, dense, upi, *scratch
):
    before, after = sorted_ends("gy", col_far, col_near)
    odd = lax.axis_index("gy") & 1
    lane = lanes()
    lower = lane < 64
    far_cols = [in_slot(lane, SLOT * (j + 1 - odd)) for j in range(SLOTS)]
    beside = ((lane - HALO) & 63) < 2 * SLOT

    def unpack(at, piece):
        at, j = at + piece // SLOTS, piece % SLOTS
        both = jnp.where(far_cols[j], col_far[at], col_near[at])
        return pltpu.roll(both, (HALO - SLOT * j) % 128, 1)

    for name in ORDER:
        for pair in range(2):
            g = Paired.first[name] + pair
            places = ((PACKED, g), (0, g), (0, PAIRS + g), (PACKED, PAIRS + g))
            for k, place in enumerate(places):
                rows = slice(8 + 8 * k, 16 + 8 * k)
                block = jnp.where(beside, unpack(*place), edge[g, rows, :])
                if name == "up":
                    upi[pair, rows, :] = block.astype(jnp.int32)
                else:
                    fld[g, rows, :] = block
    for half in range(2):
        value = unpack(PACKED, 2 * PAIRS + half)
        for number, places in enumerate(PLACES[2 * half : 2 * half + 2]):
            for block, (name, row) in enumerate(places):
                for pair in range(2):
                    k = 4 * number + 2 * block + pair
                    at = (Paired.first[name] + pair, slice(row, row + 1), slice(None))
                    fld[at] = jnp.where(beside[0:1], value[k : k + 1], edge[at])
    first, second = 2 * PACKED, 2 * PACKED + 1
    own_lists = [before(first)[:, 0:64], after(first)[:, 0:64]]
    low_lists = [before(first)[:, 64:128], after(first)[:, 64:128]]
    high_lists = [before(second)[:, 0:64], after(second)[:, 0:64]]
    scatter_beside(own_lists + low_lists + high_lists, edge_dense, dense, beside, lower)

    def emit(out, group):
        def write(k, t, value):
            rows = slice(8 * t - 16, 8 * t - 8)
            for half in range(2):
                layer = 2 * k + half
                if layer < out.shape[0]:
                    firsts = pltpu.roll(value, 128 - (HALO + 2 * SLOT) - 64 * half, 1)
                    lasts = pltpu.roll(value, 128 - HALO - 64 * half, 1)
                    inner = jnp.where(lane < SLOT - 1, firsts, center[group + layer, rows, :])
                    out[layer, rows, :] = jnp.where(lane >= 128 - SLOT, lasts, inner)

        return write

    simulate(Paired(lower), fld, dense, upi, scratch, emit(grad_x, 0), emit(grad_y, 4), emit(grad_z, 8))


def swapped(value, axis, first):
    count = lax.axis_size(axis)
    pairs = []
    for i in range(first, count - 1, 2):
        pairs += [(i, i + 1), (i + 1, i)]
    return lax.ppermute(value, axis, pairs)


def on_device(p, s, tx, ty, tz, pv, up, cell, rate, plan, observed):
    f32 = jnp.float32

    def shape(*dims):
        return jax.ShapeDtypeStruct(dims, f32)

    limit = pltpu.CompilerParams(vmem_limit_bytes=24 * 1024 * 1024)
    inputs = (p, s, tx, ty, tz, pv, up, cell, rate, plan, observed)
    inputs = [pltpu.with_memory_space_constraint(value, pltpu.HBM) for value in inputs]
    strip = shape(COUNT + 4, 8, 128)
    own, far, near = pl.pallas_call(
        pack_rows,
        out_shape=(shape(COUNT + 1, 16, 128), strip, strip),
        in_specs=[pl.BlockSpec(memory_space=pltpu.HBM)] * len(inputs),
        scratch_shapes=[pltpu.VMEM(value.shape, value.dtype) for value in inputs[6:]]
        + [pltpu.SemaphoreType.DMA((len(inputs),))],
        compiler_params=limit,
        name="pack_rows",
    )(*inputs)
    row_far = swapped(far, "gx", 1)
    row_near = swapped(near, "gx", 0)
    hide = pl.CostEstimate(flops=10**11, bytes_accessed=1 << 28, transcendentals=0)
    strip = shape(PACKED, 8, 128)
    own_far, own_near = pl.pallas_call(
        pack_own,
        out_shape=(strip, strip),
        compiler_params=limit,
        cost_estimate=hide,
        name="pack_own",
    )(own)
    strip = shape(2 * PACKED + 2, 8, 128)
    far, near = pl.pallas_call(
        pack_cols,
        out_shape=(strip, strip),
        compiler_params=limit,
        name="pack_cols",
    )(own, own_far, own_near, row_far, row_near)
    col_far = swapped(far, "gy", 1)
    col_near = swapped(near, "gy", 0)
    center, edge, edge_dense = pl.pallas_call(
        model_center,
        out_shape=(shape(11, 16, 128), shape(PAIRS, ROWS, 128), shape(7, 2, ROWS, 128)),
        scratch_shapes=scratch_of(4, COUNT),
        compiler_params=limit,
        cost_estimate=hide,
        name="model_center",
    )(own, row_far, row_near)
    return pl.pallas_call(
        model_edge,
        out_shape=(shape(*tx.shape), shape(*ty.shape), shape(*tz.shape)),
        scratch_shapes=scratch_of(2, PAIRS),
        compiler_params=limit,
        name="model_edge",
    )(col_far, col_near, edge, edge_dense, center)


def solution(mesh):
    cells = P(None, "gx", "gy")
    in_specs = (cells,) * 7 + (
        P("gx", "gy", None),
        P("gx", "gy", None),
        P(None, "gx", "gy", None),
        P(None, None, "gx", "gy", None),
    )
    return jax.shard_map(
        on_device, mesh=mesh, in_specs=in_specs, out_specs=(cells,) * 3, check_vma=False
    )
```

```python
import jax
import jax.numpy as jnp
from jax import lax
from jax.experimental import pallas as pl
from jax.experimental.pallas import tpu as pltpu
from jax.sharding import PartitionSpec as P

time_step = 0.05

GROUPS = {"p": (0, 4), "s": (4, 4), "tx": (8, 4), "ty": (12, 4), "tz": (16, 3), "pv": (19, 4), "up": (23, 4)}
ORDER = ("p", "s", "tx", "ty", "tz", "pv", "up")
COUNT = 27
SLOT = 10
SLOTS = 6
PAIRS = 14
PACKED = 5
ROWS = 56
HALO = 19


FIELDS = 11


def pack_rows(*refs):
    p, s, tx, ty, tz, pv, up, cell, rate, plan, observed = refs[:FIELDS]
    own, far, near, upi, cells, rates, plans, seen, sems = refs[FIELDS:]
    targets = [own.at[pl.ds(*GROUPS[name])] for name in ORDER[:6]] + [upi, cells, rates, plans, seen]
    copies = [
        pltpu.make_async_copy(source, target, sems.at[k])
        for k, (source, target) in enumerate(zip(refs[:FIELDS], targets))
    ]
    for copy in copies:
        copy.start()
    for copy in copies:
        copy.wait()
    first = GROUPS["up"][0]
    for layer in range(4):
        own[first + layer] = upi[layer].astype(jnp.float32)
    own[COUNT] = jnp.zeros((16, 128), jnp.float32)
    own[COUNT, 0:1, 0:64] = cells[0].astype(jnp.float32)
    own[COUNT, 1:2, 0:64] = rates[0]
    for n in range(2):
        own[COUNT, 2 + n : 3 + n, 0:64] = plans[n, 0].astype(jnp.float32)
        for k in range(2):
            row = 4 + 2 * n + k
            own[COUNT, row : row + 1, 0:64] = seen[n, k, 0]
    odd = lax.axis_index("gx") & 1
    for g in range(COUNT):
        far[g] = own[g, pl.ds(pl.multiple_of(8 * odd, 8), 8), :]
        near[g] = own[g, pl.ds(pl.multiple_of(8 - 8 * odd, 8), 8), :]
    base = {name: GROUPS[name][0] for name in ORDER}

    blank = jnp.zeros((1, 128), jnp.float32)

    def gathered(*places):
        rows = []
        for layer in (0, 2, 1, 3):
            for name, row in places:
                there = layer < GROUPS[name][1]
                rows.append(own[base[name] + layer, row : row + 1, :] if there else blank)
        return jnp.concatenate([rows[k] for k in (0, 2, 1, 3, 4, 6, 5, 7)], axis=0)

    for_next = [gathered(("p", 7), ("tx", 7))]
    for_next += [jnp.zeros((8, 128), jnp.float32)] * 2
    for_prev = [
        gathered(("p", 8), ("tx", 8)),
        gathered(("ty", 8), ("tz", 8)),
        gathered(("pv", 8), ("p", 9)),
    ]
    for k in range(3):
        far[COUNT + k] = jnp.where(odd == 1, for_next[k], for_prev[k])
        near[COUNT + k] = jnp.where(odd == 1, for_prev[k], for_next[k])
    far[COUNT + 3] = own[COUNT, 0:8, :]
    near[COUNT + 3] = own[COUNT, 0:8, :]


def lanes():
    return lax.broadcasted_iota(jnp.int32, (8, 128), 1)


def in_slot(lane, start):
    return ((lane - start) & 63) < SLOT


def sorted_ends(axis, far, near):
    odd = (lax.axis_index(axis) & 1) == 1

    def before(g):
        return jnp.where(odd, near[g], far[g])

    def after(g):
        return jnp.where(odd, far[g], near[g])

    return before, after


def layer_pairs(block):
    pairs = []
    for name in ORDER:
        first, layers = GROUPS[name]
        for layer in (0, 2):
            second = block(first + layer + 1) if layer + 1 < layers else jnp.zeros((8, 128), jnp.float32)
            pairs.append((block(first + layer), second))
    return pairs


def pack_pairs(pairs, far, near, at):
    odd = lax.axis_index("gy") & 1
    lane = lanes()
    moved = [pltpu.roll(second, 64, 1) for _, second in pairs]
    for out, ends in ((far, odd), (near, 1 - odd)):
        masks = [in_slot(lane, SLOT * (j + ends)) for j in range(SLOTS)]
        straight = ((lane >> 6) ^ ends) == 0
        for k in range(0, len(pairs), SLOTS):
            part = jnp.zeros((8, 128), jnp.float32)
            for j in range(min(SLOTS, len(pairs) - k)):
                pair = jnp.where(straight, pairs[k + j][0], moved[k + j])
                part = jnp.where(masks[j], pltpu.roll(pair, SLOT * j + 2 * SLOT * ends, 1), part)
            out[at + k // SLOTS] = part


def extra_pair(one, two):
    row = lax.broadcasted_iota(jnp.int32, (8, 128), 0)
    return jnp.where(row < 4, one, pltpu.roll(two, 4, 0)), jnp.where(row < 4, pltpu.roll(one, 4, 0), two)


def pack_own(own, far, near):
    pairs = []
    for rows in (slice(0, 8), slice(8, 16)):
        pairs += layer_pairs(lambda g: own[g, rows, :])
    pack_pairs(pairs, far, near, 0)


def pack_cols(own, own_far, own_near, row_far, row_near, far, near):
    low, high = sorted_ends("gx", row_far, row_near)
    for out, part in ((far, own_far), (near, own_near)):
        for at in range(PACKED):
            out[at] = part[at]
    pairs = layer_pairs(low) + layer_pairs(high)
    pairs.append(extra_pair(low(COUNT), high(COUNT)))
    pairs.append(extra_pair(high(COUNT + 1), high(COUNT + 2)))
    pack_pairs(pairs, far, near, PACKED)
    both = jnp.where(lanes() < 64, own[COUNT, 0:8, :], pltpu.roll(low(COUNT + 3), 64, 1))
    for out in (far, near):
        out[2 * PACKED] = both
        out[2 * PACKED + 1] = high(COUNT + 3)


def split3(value):
    hi = value.astype(jnp.bfloat16).astype(jnp.float32)
    rest = value - hi
    mid = rest.astype(jnp.bfloat16).astype(jnp.float32)
    return hi, mid, rest - mid


SRC0, SRC1, OP0, OS0, OP1, OS1, CNT = range(7)


def well_fields(info):
    rate = info[1:2] * 0.5
    values = [rate * info[2:3], rate * info[3:4]] + [info[k : k + 1] for k in range(4, 8)]
    cell = info[0:1].astype(jnp.int32)
    layer = lax.shift_right_logical(cell, 11)
    row = lax.shift_right_logical(cell, 7) & 15
    return values, layer, row, cell & 127


def hits(layer, place, inside):
    target = jnp.where(inside & (place >= 8), layer * 40 + place - 8, -1)
    rows = lax.broadcasted_iota(jnp.int32, (160, target.shape[1]), 0)
    return rows == target


def dot(left, right):
    return lax.dot_general(left, right, (((1,), (1,)), ((), ())), preferred_element_type=jnp.float32)


def scatter_center(lists, dense):
    info = jnp.concatenate(lists, axis=1)
    values, layer, row, col = well_fields(info)
    lane = lax.broadcasted_iota(jnp.int32, (1, info.shape[1]), 1)
    hit = hits(layer, row + jnp.where(lane < 64, 16, jnp.where(lane < 128, 0, 32)), lane >= 0)
    cols = lax.broadcasted_iota(jnp.int32, (128, info.shape[1]), 0)
    to_col = jnp.where(cols == col, 1.0, 0.0).astype(jnp.bfloat16)
    for number, value in enumerate(values + [None]):
        parts = (1.0,) if value is None else split3(value)
        total = None
        for part in parts:
            term = dot(jnp.where(hit, part, 0.0).astype(jnp.bfloat16), to_col)
            total = term if total is None else total + term
        for k in range(4):
            dense[number, k, 8:48, :] = total[k * 40 : k * 40 + 40]


def scatter_beside(lists, edge_dense, dense, beside, lower):
    info = jnp.concatenate(lists, axis=1)
    width = info.shape[1]
    values, layer, row, col = well_fields(info)
    block = lax.shift_right_logical(lax.broadcasted_iota(jnp.int32, (1, width), 1), 6)
    base = jnp.where(block < 2, 16, jnp.where(block < 4, 0, 32))
    ahead = (block & 1) == 1
    spot = jnp.where(ahead, col, col - 128 + 2 * SLOT)
    inside = (spot >= jnp.where(ahead, 0, SLOT)) & (spot < jnp.where(ahead, SLOT, 2 * SLOT))
    left = jnp.where(hits(layer, row + base, inside), 1.0, 0.0).astype(jnp.bfloat16)
    spots = lax.broadcasted_iota(jnp.int32, (24, width), 0)
    hit = spots == spot
    parts = [split3(value) for value in values] + [(1.0, 0.0, 0.0)]
    rights = []
    for piece in range(3):
        right = [jnp.where(hit, part[piece], 0.0) for part in parts]
        right.insert(5, jnp.zeros((8, width), jnp.float32))
        right.append(jnp.zeros((80, width), jnp.float32))
        rights.append(jnp.concatenate(right, axis=0).astype(jnp.bfloat16))
    total = dot(jnp.concatenate([left] * 3, axis=1), jnp.concatenate(rights, axis=1))
    for number in range(7):
        column = 0 if number < 5 else 128
        shift = HALO - 24 * (number if number < 5 else number - 5)
        for pair in range(2):
            for t in range(5):
                rows = slice(8 + 8 * t, 16 + 8 * t)
                at = 80 * pair + 8 * t
                one = pltpu.roll(total[at : at + 8, column : column + 128], shift % 128, 1)
                two = pltpu.roll(total[at + 40 : at + 48, column : column + 128], (shift + 64) % 128, 1)
                value = jnp.where(lower, one, two)
                dense[number, pair, rows, :] = jnp.where(beside, value, edge_dense[number, pair, rows, :])


def scratch_of(slabs, groups):
    counts = (slabs,) * 12 + (3 * slabs,) * 4 + (slabs,) * 9
    f32 = jnp.float32
    shapes = [pltpu.VMEM((groups, ROWS, 128), f32), pltpu.VMEM((7, slabs, ROWS, 128), f32)]
    shapes += [pltpu.VMEM((slabs, ROWS, 128), jnp.int32)]
    return shapes + [pltpu.VMEM((count, ROWS, 128), f32) for count in counts]


class Single:
    slabs = 4
    paired = False
    first = {name: GROUPS[name][0] for name in ORDER}

    def carry(self, kept, k, value):
        return kept, value


class Paired:
    slabs = 2
    paired = True
    first = {name: 2 * k for k, name in enumerate(ORDER)}

    def __init__(self, lower):
        self.lower = lower

    def carry(self, kept, k, value):
        turned = pltpu.roll(value, 64, 1)
        return jnp.where(self.lower, kept if k else 0.0, turned), turned


def simulate(form, fld, dense, upi, scratch, emit_x, emit_y, emit_z):
    (rcp, tym, tzd, q0, p1, q1, p2, f0, d0, s1, f1, d1, fup0, fup1, dp1, dp2,
     sig2, psi2, psi1, mup2, muq1, mup1, muq0, flux, rest) = scratch
    n = form.slabs
    last_up = n if form.paired else n - 1
    first_down = 0 if form.paired else 1
    PB, SB, XB, YB, ZB, VB = (form.first[name] for name in ORDER[:6])

    def here(ref, k, t):
        return ref[k, 8 * t : 8 * t + 8, :]

    def down(ref, k, t):
        return ref[k, 8 * t + 1 : 8 * t + 9, :]

    def above(ref, k, t):
        return ref[k, 8 * t - 1 : 8 * t + 7, :]

    def put(ref, k, t, value):
        ref[k, 8 * t : 8 * t + 8, :] = value

    def right(value):
        return pltpu.roll(value, 127, 1)

    def left(value):
        return pltpu.roll(value, 1, 1)

    def up(ref, base, k, t):
        if not form.paired:
            return here(ref, base + k + 1, t)
        turned = pltpu.roll(here(ref, base + 1, t), 64, 1)
        return turned if k else jnp.where(form.lower, pltpu.roll(here(ref, base, t), 64, 1), turned)

    def under(ref, base, k, t):
        if not form.paired:
            return here(ref, base + k - 1, t)
        turned = pltpu.roll(here(ref, base, t), 64, 1)
        return jnp.where(form.lower, turned, pltpu.roll(here(ref, base + 1, t), 64, 1)) if k else turned

    def z_under(k, t):
        return here(tzd, k, t) if form.paired else here(fld, ZB + k - 1, t)

    for k in range(n):
        for t in range(1, 6):
            beyond = right(here(fld, VB + k, t))
            put(fld, YB + k, t, jnp.where(beyond == 0.0, 0.0, here(fld, YB + k, t)))
        last = slice(31, 32)
        fld[XB + k, last, :] = jnp.where(fld[VB + k, 32:33, :] == 0.0, 0.0, fld[XB + k, last, :])
    for t in range(1, 6):
        for k in range(n):
            volume = here(fld, VB + k, t)
            volume = jnp.where(volume == 0.0, 1.0, volume)
            put(fld, VB + k, t, volume)
            if form.paired:
                below = under(fld, ZB, k, t)
                put(tzd, k, t, below if k else jnp.where(form.lower, 0.0, below))
            west = left(here(fld, YB + k, t))
            put(tym, k, t, west)
            total = volume + (here(fld, XB + k, t) + above(fld, XB + k, t)) + (here(fld, YB + k, t) + west)
            if k < last_up:
                total = total + here(fld, ZB + k, t)
            if k >= first_down:
                total = total + z_under(k, t)
            put(rcp, k, t, 1.0 / total)

    def neighbours(ref, base, k, t):
        value = here(ref, base + k, t)
        total = here(fld, XB + k, t) * down(ref, base + k, t) + above(fld, XB + k, t) * above(ref, base + k, t)
        total = total + (here(fld, YB + k, t) * right(value) + here(tym, k, t) * left(value))
        if k < last_up:
            total = total + here(fld, ZB + k, t) * up(ref, base, k, t)
        if k >= first_down:
            total = total + z_under(k, t) * under(ref, base, k, t)
        return total

    def relax(out, ref, base, old, old_base, source, tiles):
        for t in tiles:
            for k in range(n):
                total = here(fld, VB + k, t) * here(old, old_base + k, t) + here(dense.at[source], k, t)
                put(out, k, t, (total + neighbours(ref, base, k, t)) * here(rcp, k, t))

    def put_mobility(value, k, t, mobile, slope):
        rest_of = 1.0 - value
        wetted = value * value
        inverse = 1.0 / (wetted + 0.5 * rest_of * rest_of)
        put(mobile, k, t, wetted * inverse)
        put(slope, k, t, value * rest_of * (inverse * inverse))

    def bit(k, t, number):
        return (here(upi, k, t) & (1 << number)) != 0

    def transport(pressure, sat, sat_base, mobile, number, fup, dp, finish):
        for t in range(1, 5):
            kept = None
            for k in range(n):
                mob = here(mobile, k, t)
                pres = here(pressure, k, t)
                drop_x = pres - down(pressure, k, t)
                drop_y = pres - right(pres)
                up_x = jnp.where(bit(k, t, 3 * number), mob, down(mobile, k, t))
                up_y = jnp.where(bit(k, t, 3 * number + 1), mob, right(mob))
                put(fup, k, t, up_x)
                put(fup, n + k, t, up_y)
                put(dp, k, t, drop_x)
                put(dp, n + k, t, drop_y)
                flux_x = here(fld, XB + k, t) * up_x * drop_x
                flux_y = here(fld, YB + k, t) * up_y * drop_y
                put(flux, k, t, flux_x)
                net = (flux_x - above(flux, k, t)) + (flux_y - left(flux_y))
                flux_z = None
                if k < last_up:
                    drop_z = pres - up(pressure, 0, k, t)
                    up_z = jnp.where(bit(k, t, 3 * number + 2), mob, up(mobile, 0, k, t))
                    put(fup, 2 * n + k, t, up_z)
                    put(dp, 2 * n + k, t, drop_z)
                    flux_z = here(fld, ZB + k, t) * up_z * drop_z
                    net = net + flux_z
                below, kept = form.carry(kept, k, flux_z)
                if k >= first_down:
                    net = net - below
                finish(here(sat, sat_base + k, t) - time_step * net / here(fld, VB + k, t), k, t)

    tiles = range(1, 5)
    relax(q0, fld, PB, fld, PB, SRC0, range(1, 6))
    relax(p1, q0, 0, fld, PB, SRC0, tiles)
    for t in tiles:
        for k in range(n):
            put_mobility(here(fld, SB + k, t), k, t, f0, d0)

    def finish_first(moved, k, t):
        put(s1, k, t, moved)
        put_mobility(moved, k, t, f1, d1)

    transport(p1, fld, SB, f0, 0, fup0, dp1, finish_first)
    relax(q1, p1, 0, p1, 0, SRC1, tiles)
    relax(p2, q1, 0, p1, 0, SRC1, tiles)

    def finish_second(moved, k, t):
        miss = here(dense.at[CNT], k, t) * moved - here(dense.at[OS1], k, t)
        put(sig2, k, t, miss)
        put(psi2, k, t, time_step * miss / here(fld, VB + k, t))

    transport(p2, s1, 0, f1, 1, fup1, dp2, finish_second)

    for t in tiles:
        kept_h = kept_r = None
        for k in range(n):
            psi = here(psi2, k, t)
            phi_x = (down(psi2, k, t) - psi) * here(fld, XB + k, t)
            phi_y = (right(psi) - psi) * here(fld, YB + k, t)
            h_x = phi_x * here(fup1, k, t)
            h_y = phi_y * here(fup1, n + k, t)
            k_x = phi_x * here(dp2, k, t)
            k_y = phi_y * here(dp2, n + k, t)
            s_x = jnp.where(bit(k, t, 3), k_x, 0.0)
            s_y = jnp.where(bit(k, t, 4), k_y, 0.0)
            put(flux, k, t, h_x)
            put(rest, k, t, k_x - s_x)
            press = (h_x - above(flux, k, t)) + (h_y - left(h_y))
            satur = (s_x + above(rest, k, t)) + (s_y + left(k_y - s_y))
            h_z = r_z = None
            if k < last_up:
                phi_z = (up(psi2, 0, k, t) - psi) * here(fld, ZB + k, t)
                h_z = phi_z * here(fup1, 2 * n + k, t)
                k_z = phi_z * here(dp2, 2 * n + k, t)
                s_z = jnp.where(bit(k, t, 5), k_z, 0.0)
                r_z = k_z - s_z
                press = press + h_z
                satur = satur + s_z
            below_h, kept_h = form.carry(kept_h, k, h_z)
            below_r, kept_r = form.carry(kept_r, k, r_z)
            if k >= first_down:
                press = press - below_h
                satur = satur + below_r
            count = here(dense.at[CNT], k, t)
            press = press + (count * here(p2, k, t) - here(dense.at[OP1], k, t))
            put(mup2, k, t, press * here(rcp, k, t))
            sigma = here(sig2, k, t) + satur * here(d1, k, t)
            sigma = sigma + (count * here(s1, k, t) - here(dense.at[OS0], k, t))
            put(psi1, k, t, time_step * sigma / here(fld, VB + k, t))

    for t in tiles:
        for k in range(n):
            put(muq1, k, t, neighbours(mup2, 0, k, t) * here(rcp, k, t))

    for t in tiles:
        kept_h = None
        for k in range(n):
            psi = here(psi1, k, t)
            h_x = (down(psi1, k, t) - psi) * here(fld, XB + k, t) * here(fup0, k, t)
            h_y = (right(psi) - psi) * here(fld, YB + k, t) * here(fup0, n + k, t)
            put(flux, k, t, h_x)
            press = (h_x - above(flux, k, t)) + (h_y - left(h_y))
            h_z = None
            if k < last_up:
                h_z = (up(psi1, 0, k, t) - psi) * here(fld, ZB + k, t) * here(fup0, 2 * n + k, t)
                press = press + h_z
            below_h, kept_h = form.carry(kept_h, k, h_z)
            if k >= first_down:
                press = press - below_h
            count = here(dense.at[CNT], k, t)
            press = press + (count * here(p1, k, t) - here(dense.at[OP0], k, t))
            press = press + here(fld, VB + k, t) * (here(mup2, k, t) + here(muq1, k, t))
            press = press + neighbours(muq1, 0, k, t)
            put(mup1, k, t, press * here(rcp, k, t))

    for t in range(2, 5):
        for k in range(n):
            put(muq0, k, t, neighbours(mup1, 0, k, t) * here(rcp, k, t))

    stages = (
        (mup2, q1, 0, p2, 0),
        (muq1, p1, 0, q1, 0),
        (mup1, q0, 0, p1, 0),
        (muq0, fld, PB, q0, 0),
    )
    for t in range(2, 4):
        for k in range(n):
            sum_x = sum_y = sum_z = 0.0
            for psi, fup, dp in ((psi2, fup1, dp2), (psi1, fup0, dp1)):
                mid = here(psi, k, t)
                sum_x = sum_x + (down(psi, k, t) - mid) * here(fup, k, t) * here(dp, k, t)
                sum_y = sum_y + (right(mid) - mid) * here(fup, n + k, t) * here(dp, n + k, t)
                if k < last_up:
                    sum_z = sum_z + (up(psi, 0, k, t) - mid) * here(fup, 2 * n + k, t) * here(dp, 2 * n + k, t)
            for mu, value, base, out, out_base in stages:
                mu_c, v_c, o_c = here(mu, k, t), here(value, base + k, t), here(out, out_base + k, t)
                mu_d, v_d, o_d = down(mu, k, t), down(value, base + k, t), down(out, out_base + k, t)
                sum_x = sum_x + (mu_c * (v_d - o_c) + mu_d * (v_c - o_d))
                sum_y = sum_y + (mu_c * (right(v_c) - o_c) + right(mu_c) * (v_c - right(o_c)))
                if k < last_up:
                    mu_u = up(mu, 0, k, t)
                    v_u = up(value, base, k, t)
                    o_u = up(out, out_base, k, t)
                    sum_z = sum_z + (mu_c * (v_u - o_c) + mu_u * (v_c - o_u))
            emit_x(k, t, jnp.where(here(fld, XB + k, t) == 0.0, 0.0, sum_x))
            emit_y(k, t, jnp.where(here(fld, YB + k, t) == 0.0, 0.0, sum_y))
            if k < last_up:
                emit_z(k, t, sum_z)


PLACES = (
    (("p", 7), ("tx", 7)),
    (("p", 40), ("tx", 40)),
    (("ty", 40), ("tz", 40)),
    (("pv", 40), ("p", 41)),
)


def model_center(own, row_far, row_near, grads, edge, edge_dense, fld, dense, upi, *scratch):
    low, high = sorted_ends("gx", row_far, row_near)
    lane = lanes()

    def edge_of(one, two):
        turned = pltpu.roll(two, 64, 1)
        lower = lane < 64
        firsts = pltpu.roll(jnp.where(lower, one, turned), HALO + 2 * SLOT, 1)
        lasts = pltpu.roll(jnp.where(lower, turned, one), HALO, 1)
        return jnp.where((lane & 63) < HALO, lasts, firsts)

    for g in range(COUNT):
        for k, block in enumerate((low(g), own[g, 0:8, :], own[g, 8:16, :], high(g))):
            rows = slice(8 + 8 * k, 16 + 8 * k)
            fld[g, rows, :] = block
            if g >= GROUPS["up"][0]:
                upi[g - GROUPS["up"][0], rows, :] = block.astype(jnp.int32)
    extras = [low(COUNT)] + [high(COUNT + k) for k in range(3)]
    for value, places in zip(extras, PLACES):
        for block, (name, row) in enumerate(places):
            first, layers = GROUPS[name]
            for layer in range(layers):
                k = 4 * (layer & 1) + 2 * block + layer // 2
                fld[first + layer, row : row + 1, :] = value[k : k + 1]
    for half in range(2):
        value = edge_of(*extra_pair(*extras[2 * half : 2 * half + 2]))
        for number, places in enumerate(PLACES[2 * half : 2 * half + 2]):
            for block, (name, row) in enumerate(places):
                for pair in range(2):
                    k = 4 * number + 2 * block + pair
                    edge[Paired.first[name] + pair, row : row + 1, :] = value[k : k + 1]

    def pair_up(name, rows):
        first, layers = GROUPS[name]
        for pair in range(2):
            one = fld[first + 2 * pair, rows, :]
            there = 2 * pair + 1 < layers
            two = fld[first + 2 * pair + 1, rows, :] if there else jnp.zeros_like(one)
            edge[Paired.first[name] + pair, rows, :] = edge_of(one, two)

    for name in ORDER:
        for t in range(1, 5):
            pair_up(name, slice(8 * t, 8 * t + 8))
    scatter_center(
        [own[COUNT, 0:8, 0:64], low(COUNT + 3)[:, 0:64], high(COUNT + 3)[:, 0:64]], dense
    )
    for number in range(7):
        for pair in range(2):
            for t in range(1, 6):
                rows = slice(8 * t, 8 * t + 8)
                one, two = dense[number, 2 * pair, rows, :], dense[number, 2 * pair + 1, rows, :]
                edge_dense[number, pair, rows, :] = edge_of(one, two)

    def emit(first):
        def write(k, t, value):
            grads[first + k, 8 * t - 16 : 8 * t - 8, :] = value

        return write

    simulate(Single(), fld, dense, upi, scratch, emit(0), emit(4), emit(8))


def model_edge(
    col_far, col_near, edge, edge_dense, center, grad_x, grad_y, grad_z, fld, dense, upi, *scratch
):
    before, after = sorted_ends("gy", col_far, col_near)
    odd = lax.axis_index("gy") & 1
    lane = lanes()
    lower = lane < 64
    far_cols = [in_slot(lane, SLOT * (j + 1 - odd)) for j in range(SLOTS)]
    beside = ((lane - HALO) & 63) < 2 * SLOT

    def unpack(at, piece):
        at, j = at + piece // SLOTS, piece % SLOTS
        both = jnp.where(far_cols[j], col_far[at], col_near[at])
        return pltpu.roll(both, (HALO - SLOT * j) % 128, 1)

    for name in ORDER:
        for pair in range(2):
            g = Paired.first[name] + pair
            places = ((PACKED, g), (0, g), (0, PAIRS + g), (PACKED, PAIRS + g))
            for k, place in enumerate(places):
                rows = slice(8 + 8 * k, 16 + 8 * k)
                block = jnp.where(beside, unpack(*place), edge[g, rows, :])
                if name == "up":
                    upi[pair, rows, :] = block.astype(jnp.int32)
                else:
                    fld[g, rows, :] = block
    for half in range(2):
        value = unpack(PACKED, 2 * PAIRS + half)
        for number, places in enumerate(PLACES[2 * half : 2 * half + 2]):
            for block, (name, row) in enumerate(places):
                for pair in range(2):
                    k = 4 * number + 2 * block + pair
                    at = (Paired.first[name] + pair, slice(row, row + 1), slice(None))
                    fld[at] = jnp.where(beside[0:1], value[k : k + 1], edge[at])
    first, second = 2 * PACKED, 2 * PACKED + 1
    own_lists = [before(first)[:, 0:64], after(first)[:, 0:64]]
    low_lists = [before(first)[:, 64:128], after(first)[:, 64:128]]
    high_lists = [before(second)[:, 0:64], after(second)[:, 0:64]]
    scatter_beside(own_lists + low_lists + high_lists, edge_dense, dense, beside, lower)

    def emit(out, group):
        def write(k, t, value):
            rows = slice(8 * t - 16, 8 * t - 8)
            for half in range(2):
                layer = 2 * k + half
                if layer < out.shape[0]:
                    firsts = pltpu.roll(value, 128 - (HALO + 2 * SLOT) - 64 * half, 1)
                    lasts = pltpu.roll(value, 128 - HALO - 64 * half, 1)
                    inner = jnp.where(lane < SLOT - 1, firsts, center[group + layer, rows, :])
                    out[layer, rows, :] = jnp.where(lane >= 128 - SLOT, lasts, inner)

        return write

    simulate(Paired(lower), fld, dense, upi, scratch, emit(grad_x, 0), emit(grad_y, 4), emit(grad_z, 8))


def swapped(value, axis, first):
    count = lax.axis_size(axis)
    pairs = []
    for i in range(first, count - 1, 2):
        pairs += [(i, i + 1), (i + 1, i)]
    return lax.ppermute(value, axis, pairs)


def on_device(p, s, tx, ty, tz, pv, up, cell, rate, plan, observed):
    f32 = jnp.float32

    def shape(*dims):
        return jax.ShapeDtypeStruct(dims, f32)

    limit = pltpu.CompilerParams(vmem_limit_bytes=24 * 1024 * 1024)
    inputs = (p, s, tx, ty, tz, pv, up, cell, rate, plan, observed)
    inputs = [pltpu.with_memory_space_constraint(value, pltpu.HBM) for value in inputs]
    strip = shape(COUNT + 4, 8, 128)
    own, far, near = pl.pallas_call(
        pack_rows,
        out_shape=(shape(COUNT + 1, 16, 128), strip, strip),
        in_specs=[pl.BlockSpec(memory_space=pltpu.HBM)] * len(inputs),
        scratch_shapes=[pltpu.VMEM(value.shape, value.dtype) for value in inputs[6:]]
        + [pltpu.SemaphoreType.DMA((len(inputs),))],
        compiler_params=limit,
        name="pack_rows",
    )(*inputs)
    row_far = swapped(far, "gx", 1)
    row_near = swapped(near, "gx", 0)
    hide = pl.CostEstimate(flops=10**11, bytes_accessed=1 << 28, transcendentals=0)
    strip = shape(PACKED, 8, 128)
    own_far, own_near = pl.pallas_call(
        pack_own,
        out_shape=(strip, strip),
        compiler_params=limit,
        cost_estimate=hide,
        name="pack_own",
    )(own)
    strip = shape(2 * PACKED + 2, 8, 128)
    far, near = pl.pallas_call(
        pack_cols,
        out_shape=(strip, strip),
        compiler_params=limit,
        name="pack_cols",
    )(own, own_far, own_near, row_far, row_near)
    col_far = swapped(far, "gy", 1)
    col_near = swapped(near, "gy", 0)
    center, edge, edge_dense = pl.pallas_call(
        model_center,
        out_shape=(shape(11, 16, 128), shape(PAIRS, ROWS, 128), shape(7, 2, ROWS, 128)),
        scratch_shapes=scratch_of(4, COUNT),
        compiler_params=limit,
        cost_estimate=hide,
        name="model_center",
    )(own, row_far, row_near)
    return pl.pallas_call(
        model_edge,
        out_shape=(shape(*tx.shape), shape(*ty.shape), shape(*tz.shape)),
        scratch_shapes=scratch_of(2, PAIRS),
        compiler_params=limit,
        name="model_edge",
    )(col_far, col_near, edge, edge_dense, center)


def solution(mesh):
    cells = P(None, "gx", "gy")
    in_specs = (cells,) * 7 + (
        P("gx", "gy", None),
        P("gx", "gy", None),
        P(None, "gx", "gy", None),
        P(None, None, "gx", "gy", None),
    )
    return jax.shard_map(
        on_device, mesh=mesh, in_specs=in_specs, out_specs=(cells,) * 3, check_vma=False
    )
```

```python
import jax
import jax.numpy as jnp
from jax import lax
from jax.experimental import pallas as pl
from jax.experimental.pallas import tpu as pltpu
from jax.sharding import PartitionSpec as P

time_step = 0.05

GROUPS = {"p": (0, 4), "s": (4, 4), "tx": (8, 4), "ty": (12, 4), "tz": (16, 3), "pv": (19, 4), "up": (23, 4)}
ORDER = ("p", "s", "tx", "ty", "tz", "pv", "up")
COUNT = 27
SLOT = 10
SLOTS = 6
PAIRS = 14
PACKED = 5
ROWS = 56
HALO = 19


FIELDS = 11


def pack_rows(*refs):
    p, s, tx, ty, tz, pv, up, cell, rate, plan, observed = refs[:FIELDS]
    own, far, near, upi, cells, rates, plans, seen, sems = refs[FIELDS:]
    targets = [own.at[pl.ds(*GROUPS[name])] for name in ORDER[:6]] + [upi, cells, rates, plans, seen]
    copies = [
        pltpu.make_async_copy(source, target, sems.at[k])
        for k, (source, target) in enumerate(zip(refs[:FIELDS], targets))
    ]
    for copy in copies:
        copy.start()
    for copy in copies:
        copy.wait()
    first = GROUPS["up"][0]
    for layer in range(4):
        own[first + layer] = upi[layer].astype(jnp.float32)
    own[COUNT] = jnp.zeros((16, 128), jnp.float32)
    own[COUNT, 0:1, 0:64] = cells[0].astype(jnp.float32)
    own[COUNT, 1:2, 0:64] = rates[0]
    for n in range(2):
        own[COUNT, 2 + n : 3 + n, 0:64] = plans[n, 0].astype(jnp.float32)
        for k in range(2):
            row = 4 + 2 * n + k
            own[COUNT, row : row + 1, 0:64] = seen[n, k, 0]
    odd = lax.axis_index("gx") & 1
    for g in range(COUNT):
        far[g] = own[g, pl.ds(pl.multiple_of(8 * odd, 8), 8), :]
        near[g] = own[g, pl.ds(pl.multiple_of(8 - 8 * odd, 8), 8), :]
    base = {name: GROUPS[name][0] for name in ORDER}

    blank = jnp.zeros((1, 128), jnp.float32)

    def gathered(*places):
        rows = []
        for layer in (0, 2, 1, 3):
            for name, row in places:
                there = layer < GROUPS[name][1]
                rows.append(own[base[name] + layer, row : row + 1, :] if there else blank)
        return jnp.concatenate([rows[k] for k in (0, 2, 1, 3, 4, 6, 5, 7)], axis=0)

    for_next = [gathered(("p", 7), ("tx", 7))]
    for_next += [jnp.zeros((8, 128), jnp.float32)] * 2
    for_prev = [
        gathered(("p", 8), ("tx", 8)),
        gathered(("ty", 8), ("tz", 8)),
        gathered(("pv", 8), ("p", 9)),
    ]
    for k in range(3):
        far[COUNT + k] = jnp.where(odd == 1, for_next[k], for_prev[k])
        near[COUNT + k] = jnp.where(odd == 1, for_prev[k], for_next[k])
    far[COUNT + 3] = own[COUNT, 0:8, :]
    near[COUNT + 3] = own[COUNT, 0:8, :]


def lanes():
    return lax.broadcasted_iota(jnp.int32, (8, 128), 1)


def in_slot(lane, start):
    return ((lane - start) & 63) < SLOT


def sorted_ends(axis, far, near):
    odd = (lax.axis_index(axis) & 1) == 1

    def before(g):
        return jnp.where(odd, near[g], far[g])

    def after(g):
        return jnp.where(odd, far[g], near[g])

    return before, after


def layer_pairs(block):
    pairs = []
    for name in ORDER:
        first, layers = GROUPS[name]
        for layer in (0, 2):
            second = block(first + layer + 1) if layer + 1 < layers else jnp.zeros((8, 128), jnp.float32)
            pairs.append((block(first + layer), second))
    return pairs


def pack_pairs(pairs, far, near, at):
    odd = lax.axis_index("gy") & 1
    lane = lanes()
    moved = [pltpu.roll(second, 64, 1) for _, second in pairs]
    for out, ends in ((far, odd), (near, 1 - odd)):
        masks = [in_slot(lane, SLOT * (j + ends)) for j in range(SLOTS)]
        straight = ((lane >> 6) ^ ends) == 0
        for k in range(0, len(pairs), SLOTS):
            part = jnp.zeros((8, 128), jnp.float32)
            for j in range(min(SLOTS, len(pairs) - k)):
                pair = jnp.where(straight, pairs[k + j][0], moved[k + j])
                part = jnp.where(masks[j], pltpu.roll(pair, SLOT * j + 2 * SLOT * ends, 1), part)
            out[at + k // SLOTS] = part


def extra_pair(one, two):
    row = lax.broadcasted_iota(jnp.int32, (8, 128), 0)
    return jnp.where(row < 4, one, pltpu.roll(two, 4, 0)), jnp.where(row < 4, pltpu.roll(one, 4, 0), two)


def pack_own(own, far, near):
    pairs = []
    for rows in (slice(0, 8), slice(8, 16)):
        pairs += layer_pairs(lambda g: own[g, rows, :])
    pack_pairs(pairs, far, near, 0)


def pack_cols(own, own_far, own_near, row_far, row_near, far, near):
    low, high = sorted_ends("gx", row_far, row_near)
    for out, part in ((far, own_far), (near, own_near)):
        for at in range(PACKED):
            out[at] = part[at]
    pairs = layer_pairs(low) + layer_pairs(high)
    pairs.append(extra_pair(low(COUNT), high(COUNT)))
    pairs.append(extra_pair(high(COUNT + 1), high(COUNT + 2)))
    pack_pairs(pairs, far, near, PACKED)
    both = jnp.where(lanes() < 64, own[COUNT, 0:8, :], pltpu.roll(low(COUNT + 3), 64, 1))
    for out in (far, near):
        out[2 * PACKED] = both
        out[2 * PACKED + 1] = high(COUNT + 3)


def split3(value):
    hi = value.astype(jnp.bfloat16).astype(jnp.float32)
    rest = value - hi
    mid = rest.astype(jnp.bfloat16).astype(jnp.float32)
    return hi, mid, rest - mid


SRC0, SRC1, OP0, OS0, OP1, OS1, CNT = range(7)


def spread_wells(info, base, to_spot, rows_of, count, write):
    width = info.shape[1]
    cell = info[0:1].astype(jnp.int32)
    layer = lax.shift_right_logical(cell, 11)
    place = (lax.shift_right_logical(cell, 7) & 15) + base
    target = jnp.where(place >= 8, rows_of(layer) * 40 + place - 8, -1)
    spot = to_spot(layer, cell & 127)
    hit = lax.broadcasted_iota(jnp.int32, (count, width), 0) == target
    hit = jnp.where(hit, 1.0, 0.0).astype(jnp.bfloat16)
    lane = lax.broadcasted_iota(jnp.int32, (128, width), 0)
    to_lane = jnp.where(lane == spot, 1.0, 0.0).astype(jnp.bfloat16)
    rate = info[1:2] * 0.5
    values = [rate * info[2:3], rate * info[3:4]] + [info[k : k + 1] for k in range(4, 8)]
    for number, value in enumerate(values):
        total = None
        for part in split3(value):
            part = jnp.broadcast_to(part, (16, width)).astype(jnp.bfloat16)
            left = hit * jnp.concatenate([part] * (count // 16), axis=0)
            term = dot(left, to_lane)
            total = term if total is None else total + term
        write(number, total)
    write(CNT, dot(hit, to_lane))


def dot(left, right):
    return lax.dot_general(left, right, (((1,), (1,)), ((), ())), preferred_element_type=jnp.float32)


def list_block(info):
    return lax.shift_right_logical(lax.broadcasted_iota(jnp.int32, (1, info.shape[1]), 1), 6)


def scratch_of(slabs, groups):
    counts = (slabs,) * 12 + (3 * slabs,) * 4 + (slabs,) * 9
    f32 = jnp.float32
    shapes = [pltpu.VMEM((groups, ROWS, 128), f32), pltpu.VMEM((7, slabs, ROWS, 128), f32)]
    shapes += [pltpu.VMEM((slabs, ROWS, 128), jnp.int32)]
    return shapes + [pltpu.VMEM((count, ROWS, 128), f32) for count in counts]


class Single:
    slabs = 4
    paired = False
    first = {name: GROUPS[name][0] for name in ORDER}

    def carry(self, kept, k, value):
        return kept, value


class Paired:
    slabs = 2
    paired = True
    first = {name: 2 * k for k, name in enumerate(ORDER)}

    def __init__(self, lower):
        self.lower = lower

    def carry(self, kept, k, value):
        turned = pltpu.roll(value, 64, 1)
        return jnp.where(self.lower, kept if k else 0.0, turned), turned


def simulate(form, fld, dense, upi, scratch, emit_x, emit_y, emit_z):
    (rcp, tym, tzd, q0, p1, q1, p2, f0, d0, s1, f1, d1, fup0, fup1, dp1, dp2,
     sig2, psi2, psi1, mup2, muq1, mup1, muq0, flux, rest) = scratch
    n = form.slabs
    last_up = n if form.paired else n - 1
    first_down = 0 if form.paired else 1
    PB, SB, XB, YB, ZB, VB = (form.first[name] for name in ORDER[:6])

    def here(ref, k, t):
        return ref[k, 8 * t : 8 * t + 8, :]

    def down(ref, k, t):
        return ref[k, 8 * t + 1 : 8 * t + 9, :]

    def above(ref, k, t):
        return ref[k, 8 * t - 1 : 8 * t + 7, :]

    def put(ref, k, t, value):
        ref[k, 8 * t : 8 * t + 8, :] = value

    def right(value):
        return pltpu.roll(value, 127, 1)

    def left(value):
        return pltpu.roll(value, 1, 1)

    def up(ref, base, k, t):
        if not form.paired:
            return here(ref, base + k + 1, t)
        turned = pltpu.roll(here(ref, base + 1, t), 64, 1)
        return turned if k else jnp.where(form.lower, pltpu.roll(here(ref, base, t), 64, 1), turned)

    def under(ref, base, k, t):
        if not form.paired:
            return here(ref, base + k - 1, t)
        turned = pltpu.roll(here(ref, base, t), 64, 1)
        return jnp.where(form.lower, turned, pltpu.roll(here(ref, base + 1, t), 64, 1)) if k else turned

    def z_under(k, t):
        return here(tzd, k, t) if form.paired else here(fld, ZB + k - 1, t)

    for k in range(n):
        for t in range(1, 6):
            beyond = right(here(fld, VB + k, t))
            put(fld, YB + k, t, jnp.where(beyond == 0.0, 0.0, here(fld, YB + k, t)))
        last = slice(31, 32)
        fld[XB + k, last, :] = jnp.where(fld[VB + k, 32:33, :] == 0.0, 0.0, fld[XB + k, last, :])
    for t in range(1, 6):
        for k in range(n):
            volume = here(fld, VB + k, t)
            volume = jnp.where(volume == 0.0, 1.0, volume)
            put(fld, VB + k, t, volume)
            if form.paired:
                below = under(fld, ZB, k, t)
                put(tzd, k, t, below if k else jnp.where(form.lower, 0.0, below))
            west = left(here(fld, YB + k, t))
            put(tym, k, t, west)
            total = volume + (here(fld, XB + k, t) + above(fld, XB + k, t)) + (here(fld, YB + k, t) + west)
            if k < last_up:
                total = total + here(fld, ZB + k, t)
            if k >= first_down:
                total = total + z_under(k, t)
            put(rcp, k, t, 1.0 / total)

    def neighbours(ref, base, k, t):
        value = here(ref, base + k, t)
        total = here(fld, XB + k, t) * down(ref, base + k, t) + above(fld, XB + k, t) * above(ref, base + k, t)
        total = total + (here(fld, YB + k, t) * right(value) + here(tym, k, t) * left(value))
        if k < last_up:
            total = total + here(fld, ZB + k, t) * up(ref, base, k, t)
        if k >= first_down:
            total = total + z_under(k, t) * under(ref, base, k, t)
        return total

    def relax(out, ref, base, old, old_base, source, tiles):
        for t in tiles:
            for k in range(n):
                total = here(fld, VB + k, t) * here(old, old_base + k, t) + here(dense.at[source], k, t)
                put(out, k, t, (total + neighbours(ref, base, k, t)) * here(rcp, k, t))

    def put_mobility(value, k, t, mobile, slope):
        rest_of = 1.0 - value
        wetted = value * value
        inverse = 1.0 / (wetted + 0.5 * rest_of * rest_of)
        put(mobile, k, t, wetted * inverse)
        put(slope, k, t, value * rest_of * (inverse * inverse))

    def bit(k, t, number):
        return (here(upi, k, t) & (1 << number)) != 0

    def transport(pressure, sat, sat_base, mobile, number, fup, dp, finish):
        for t in range(1, 5):
            kept = None
            for k in range(n):
                mob = here(mobile, k, t)
                pres = here(pressure, k, t)
                drop_x = pres - down(pressure, k, t)
                drop_y = pres - right(pres)
                up_x = jnp.where(bit(k, t, 3 * number), mob, down(mobile, k, t))
                up_y = jnp.where(bit(k, t, 3 * number + 1), mob, right(mob))
                put(fup, k, t, up_x)
                put(fup, n + k, t, up_y)
                put(dp, k, t, drop_x)
                put(dp, n + k, t, drop_y)
                flux_x = here(fld, XB + k, t) * up_x * drop_x
                flux_y = here(fld, YB + k, t) * up_y * drop_y
                put(flux, k, t, flux_x)
                net = (flux_x - above(flux, k, t)) + (flux_y - left(flux_y))
                flux_z = None
                if k < last_up:
                    drop_z = pres - up(pressure, 0, k, t)
                    up_z = jnp.where(bit(k, t, 3 * number + 2), mob, up(mobile, 0, k, t))
                    put(fup, 2 * n + k, t, up_z)
                    put(dp, 2 * n + k, t, drop_z)
                    flux_z = here(fld, ZB + k, t) * up_z * drop_z
                    net = net + flux_z
                below, kept = form.carry(kept, k, flux_z)
                if k >= first_down:
                    net = net - below
                finish(here(sat, sat_base + k, t) - time_step * net / here(fld, VB + k, t), k, t)

    tiles = range(1, 5)
    relax(q0, fld, PB, fld, PB, SRC0, range(1, 6))
    relax(p1, q0, 0, fld, PB, SRC0, tiles)
    for t in tiles:
        for k in range(n):
            put_mobility(here(fld, SB + k, t), k, t, f0, d0)

    def finish_first(moved, k, t):
        put(s1, k, t, moved)
        put_mobility(moved, k, t, f1, d1)

    transport(p1, fld, SB, f0, 0, fup0, dp1, finish_first)
    relax(q1, p1, 0, p1, 0, SRC1, tiles)
    relax(p2, q1, 0, p1, 0, SRC1, tiles)

    def finish_second(moved, k, t):
        miss = here(dense.at[CNT], k, t) * moved - here(dense.at[OS1], k, t)
        put(sig2, k, t, miss)
        put(psi2, k, t, time_step * miss / here(fld, VB + k, t))

    transport(p2, s1, 0, f1, 1, fup1, dp2, finish_second)

    for t in tiles:
        kept_h = kept_r = None
        for k in range(n):
            psi = here(psi2, k, t)
            phi_x = (down(psi2, k, t) - psi) * here(fld, XB + k, t)
            phi_y = (right(psi) - psi) * here(fld, YB + k, t)
            h_x = phi_x * here(fup1, k, t)
            h_y = phi_y * here(fup1, n + k, t)
            k_x = phi_x * here(dp2, k, t)
            k_y = phi_y * here(dp2, n + k, t)
            s_x = jnp.where(bit(k, t, 3), k_x, 0.0)
            s_y = jnp.where(bit(k, t, 4), k_y, 0.0)
            put(flux, k, t, h_x)
            put(rest, k, t, k_x - s_x)
            press = (h_x - above(flux, k, t)) + (h_y - left(h_y))
            satur = (s_x + above(rest, k, t)) + (s_y + left(k_y - s_y))
            h_z = r_z = None
            if k < last_up:
                phi_z = (up(psi2, 0, k, t) - psi) * here(fld, ZB + k, t)
                h_z = phi_z * here(fup1, 2 * n + k, t)
                k_z = phi_z * here(dp2, 2 * n + k, t)
                s_z = jnp.where(bit(k, t, 5), k_z, 0.0)
                r_z = k_z - s_z
                press = press + h_z
                satur = satur + s_z
            below_h, kept_h = form.carry(kept_h, k, h_z)
            below_r, kept_r = form.carry(kept_r, k, r_z)
            if k >= first_down:
                press = press - below_h
                satur = satur + below_r
            count = here(dense.at[CNT], k, t)
            press = press + (count * here(p2, k, t) - here(dense.at[OP1], k, t))
            put(mup2, k, t, press * here(rcp, k, t))
            sigma = here(sig2, k, t) + satur * here(d1, k, t)
            sigma = sigma + (count * here(s1, k, t) - here(dense.at[OS0], k, t))
            put(psi1, k, t, time_step * sigma / here(fld, VB + k, t))

    for t in tiles:
        for k in range(n):
            put(muq1, k, t, neighbours(mup2, 0, k, t) * here(rcp, k, t))

    for t in tiles:
        kept_h = None
        for k in range(n):
            psi = here(psi1, k, t)
            h_x = (down(psi1, k, t) - psi) * here(fld, XB + k, t) * here(fup0, k, t)
            h_y = (right(psi) - psi) * here(fld, YB + k, t) * here(fup0, n + k, t)
            put(flux, k, t, h_x)
            press = (h_x - above(flux, k, t)) + (h_y - left(h_y))
            h_z = None
            if k < last_up:
                h_z = (up(psi1, 0, k, t) - psi) * here(fld, ZB + k, t) * here(fup0, 2 * n + k, t)
                press = press + h_z
            below_h, kept_h = form.carry(kept_h, k, h_z)
            if k >= first_down:
                press = press - below_h
            count = here(dense.at[CNT], k, t)
            press = press + (count * here(p1, k, t) - here(dense.at[OP0], k, t))
            press = press + here(fld, VB + k, t) * (here(mup2, k, t) + here(muq1, k, t))
            press = press + neighbours(muq1, 0, k, t)
            put(mup1, k, t, press * here(rcp, k, t))

    for t in range(2, 5):
        for k in range(n):
            put(muq0, k, t, neighbours(mup1, 0, k, t) * here(rcp, k, t))

    stages = (
        (mup2, q1, 0, p2, 0),
        (muq1, p1, 0, q1, 0),
        (mup1, q0, 0, p1, 0),
        (muq0, fld, PB, q0, 0),
    )
    for t in range(2, 4):
        for k in range(n):
            sum_x = sum_y = sum_z = 0.0
            for psi, fup, dp in ((psi2, fup1, dp2), (psi1, fup0, dp1)):
                mid = here(psi, k, t)
                sum_x = sum_x + (down(psi, k, t) - mid) * here(fup, k, t) * here(dp, k, t)
                sum_y = sum_y + (right(mid) - mid) * here(fup, n + k, t) * here(dp, n + k, t)
                if k < last_up:
                    sum_z = sum_z + (up(psi, 0, k, t) - mid) * here(fup, 2 * n + k, t) * here(dp, 2 * n + k, t)
            for mu, value, base, out, out_base in stages:
                mu_c, v_c, o_c = here(mu, k, t), here(value, base + k, t), here(out, out_base + k, t)
                mu_d, v_d, o_d = down(mu, k, t), down(value, base + k, t), down(out, out_base + k, t)
                sum_x = sum_x + (mu_c * (v_d - o_c) + mu_d * (v_c - o_d))
                sum_y = sum_y + (mu_c * (right(v_c) - o_c) + right(mu_c) * (v_c - right(o_c)))
                if k < last_up:
                    mu_u = up(mu, 0, k, t)
                    v_u = up(value, base, k, t)
                    o_u = up(out, out_base, k, t)
                    sum_z = sum_z + (mu_c * (v_u - o_c) + mu_u * (v_c - o_u))
            emit_x(k, t, jnp.where(here(fld, XB + k, t) == 0.0, 0.0, sum_x))
            emit_y(k, t, jnp.where(here(fld, YB + k, t) == 0.0, 0.0, sum_y))
            if k < last_up:
                emit_z(k, t, sum_z)


PLACES = (
    (("p", 7), ("tx", 7)),
    (("p", 40), ("tx", 40)),
    (("ty", 40), ("tz", 40)),
    (("pv", 40), ("p", 41)),
)


def model_center(own, row_far, row_near, grads, edge, edge_dense, fld, dense, upi, *scratch):
    low, high = sorted_ends("gx", row_far, row_near)
    lane = lanes()

    low_half = (lane & 63) < HALO

    def edge_of(one, two):
        first = jnp.where(low_half, pltpu.roll(one, HALO, 1), pltpu.roll(one, HALO + 2 * SLOT, 1))
        second = jnp.where(low_half, pltpu.roll(two, HALO + 64, 1), pltpu.roll(two, HALO + 2 * SLOT + 64, 1))
        return jnp.where(lane < 64, first, second)

    def blocks_of(g):
        return [low(g), own[g, 0:8, :], own[g, 8:16, :], high(g)]

    for name in ORDER:
        first, layers = GROUPS[name]
        for pair in range(2):
            one = blocks_of(first + 2 * pair)
            there = 2 * pair + 1 < layers
            two = blocks_of(first + 2 * pair + 1) if there else [jnp.zeros((8, 128), jnp.float32)] * 4
            for k in range(4):
                rows = slice(8 + 8 * k, 16 + 8 * k)
                edge[Paired.first[name] + pair, rows, :] = edge_of(one[k], two[k])
                for layer, value in ((2 * pair, one[k]), (2 * pair + 1, two[k])):
                    if layer < layers:
                        fld[first + layer, rows, :] = value
                    if name == "up":
                        upi[layer, rows, :] = value.astype(jnp.int32)
    extras = [low(COUNT)] + [high(COUNT + k) for k in range(3)]
    for value, places in zip(extras, PLACES):
        for block, (name, row) in enumerate(places):
            first, layers = GROUPS[name]
            for layer in range(layers):
                k = 4 * (layer & 1) + 2 * block + layer // 2
                fld[first + layer, row : row + 1, :] = value[k : k + 1]
    for half in range(2):
        value = edge_of(*extra_pair(*extras[2 * half : 2 * half + 2]))
        for number, places in enumerate(PLACES[2 * half : 2 * half + 2]):
            for block, (name, row) in enumerate(places):
                for pair in range(2):
                    k = 4 * number + 2 * block + pair
                    edge[Paired.first[name] + pair, row : row + 1, :] = value[k : k + 1]

    info = jnp.concatenate(
        [own[COUNT, 0:8, 0:64], low(COUNT + 3)[:, 0:64], high(COUNT + 3)[:, 0:64]], axis=1
    )
    block = list_block(info)
    base = jnp.where(block == 0, 16, jnp.where(block == 1, 0, 32))

    def write_center(number, total):
        for k in range(4):
            dense[number, k, 8:48, :] = total[40 * k : 40 * k + 40]

    def write_edge(number, total):
        for pair in range(2):
            edge_dense[number, pair, 8:48, :] = total[40 * pair : 40 * pair + 40]

    def edge_lane(layer, col):
        start = 64 * (layer & 1)
        late = jnp.where(col >= 128 - HALO, start + col - (128 - HALO), -1)
        return jnp.where(col < 64 - HALO - 2 * SLOT, start + HALO + 2 * SLOT + col, late)

    spread_wells(info, base, lambda layer, col: col, lambda layer: layer, 160, write_center)
    spread_wells(info, base, edge_lane, lambda layer: layer >> 1, 80, write_edge)

    def emit(first):
        def write(k, t, value):
            grads[first + k, 8 * t - 16 : 8 * t - 8, :] = value

        return write

    simulate(Single(), fld, dense, upi, scratch, emit(0), emit(4), emit(8))


def model_edge(
    col_far, col_near, edge, edge_dense, center, grad_x, grad_y, grad_z, fld, dense, upi, *scratch
):
    before, after = sorted_ends("gy", col_far, col_near)
    odd = lax.axis_index("gy") & 1
    lane = lanes()
    lower = lane < 64
    far_cols = [in_slot(lane, SLOT * (j + 1 - odd)) for j in range(SLOTS)]
    beside = ((lane - HALO) & 63) < 2 * SLOT

    def unpack(at, piece):
        at, j = at + piece // SLOTS, piece % SLOTS
        both = jnp.where(far_cols[j], col_far[at], col_near[at])
        return pltpu.roll(both, (HALO - SLOT * j) % 128, 1)

    for name in ORDER:
        for pair in range(2):
            g = Paired.first[name] + pair
            places = ((PACKED, g), (0, g), (0, PAIRS + g), (PACKED, PAIRS + g))
            for k, place in enumerate(places):
                rows = slice(8 + 8 * k, 16 + 8 * k)
                block = jnp.where(beside, unpack(*place), edge[g, rows, :])
                if name == "up":
                    upi[pair, rows, :] = block.astype(jnp.int32)
                else:
                    fld[g, rows, :] = block
    for half in range(2):
        value = unpack(PACKED, 2 * PAIRS + half)
        for number, places in enumerate(PLACES[2 * half : 2 * half + 2]):
            for block, (name, row) in enumerate(places):
                for pair in range(2):
                    k = 4 * number + 2 * block + pair
                    at = (Paired.first[name] + pair, slice(row, row + 1), slice(None))
                    fld[at] = jnp.where(beside[0:1], value[k : k + 1], edge[at])
    first, second = 2 * PACKED, 2 * PACKED + 1
    own_lists = [before(first)[:, 0:64], after(first)[:, 0:64]]
    low_lists = [before(first)[:, 64:128], after(first)[:, 64:128]]
    high_lists = [before(second)[:, 0:64], after(second)[:, 0:64]]
    info = jnp.concatenate(own_lists + low_lists + high_lists, axis=1)
    block = list_block(info)
    base = jnp.where(block < 2, 16, jnp.where(block < 4, 0, 32))
    ahead = (block & 1) == 1

    def beside_lane(layer, col):
        start = 64 * (layer & 1) + HALO
        return jnp.where(
            ahead,
            jnp.where(col < SLOT, start + col, -1),
            jnp.where(col >= 128 - SLOT, start + col - 128 + 2 * SLOT, -1),
        )

    def write_beside(number, total):
        for pair in range(2):
            dense[number, pair, 8:48, :] = total[40 * pair : 40 * pair + 40] + edge_dense[number, pair, 8:48, :]

    spread_wells(info, base, beside_lane, lambda layer: layer >> 1, 80, write_beside)

    def emit(out, group):
        def write(k, t, value):
            rows = slice(8 * t - 16, 8 * t - 8)
            for half in range(2):
                layer = 2 * k + half
                if layer < out.shape[0]:
                    firsts = pltpu.roll(value, 128 - (HALO + 2 * SLOT) - 64 * half, 1)
                    lasts = pltpu.roll(value, 128 - HALO - 64 * half, 1)
                    inner = jnp.where(lane < SLOT - 1, firsts, center[group + layer, rows, :])
                    out[layer, rows, :] = jnp.where(lane >= 128 - SLOT, lasts, inner)

        return write

    simulate(Paired(lower), fld, dense, upi, scratch, emit(grad_x, 0), emit(grad_y, 4), emit(grad_z, 8))


def swapped(value, axis, first):
    count = lax.axis_size(axis)
    pairs = []
    for i in range(first, count - 1, 2):
        pairs += [(i, i + 1), (i + 1, i)]
    return lax.ppermute(value, axis, pairs)


def on_device(p, s, tx, ty, tz, pv, up, cell, rate, plan, observed):
    f32 = jnp.float32

    def shape(*dims):
        return jax.ShapeDtypeStruct(dims, f32)

    limit = pltpu.CompilerParams(vmem_limit_bytes=24 * 1024 * 1024)
    inputs = (p, s, tx, ty, tz, pv, up, cell, rate, plan, observed)
    inputs = [pltpu.with_memory_space_constraint(value, pltpu.HBM) for value in inputs]
    strip = shape(COUNT + 4, 8, 128)
    own, far, near = pl.pallas_call(
        pack_rows,
        out_shape=(shape(COUNT + 1, 16, 128), strip, strip),
        in_specs=[pl.BlockSpec(memory_space=pltpu.HBM)] * len(inputs),
        scratch_shapes=[pltpu.VMEM(value.shape, value.dtype) for value in inputs[6:]]
        + [pltpu.SemaphoreType.DMA((len(inputs),))],
        compiler_params=limit,
        name="pack_rows",
    )(*inputs)
    row_far = swapped(far, "gx", 1)
    row_near = swapped(near, "gx", 0)
    hide = pl.CostEstimate(flops=10**11, bytes_accessed=1 << 28, transcendentals=0)
    strip = shape(PACKED, 8, 128)
    own_far, own_near = pl.pallas_call(
        pack_own,
        out_shape=(strip, strip),
        compiler_params=limit,
        cost_estimate=hide,
        name="pack_own",
    )(own)
    strip = shape(2 * PACKED + 2, 8, 128)
    far, near = pl.pallas_call(
        pack_cols,
        out_shape=(strip, strip),
        compiler_params=limit,
        name="pack_cols",
    )(own, own_far, own_near, row_far, row_near)
    col_far = swapped(far, "gy", 1)
    col_near = swapped(near, "gy", 0)
    center, edge, edge_dense = pl.pallas_call(
        model_center,
        out_shape=(shape(11, 16, 128), shape(PAIRS, ROWS, 128), shape(7, 2, ROWS, 128)),
        scratch_shapes=scratch_of(4, COUNT),
        compiler_params=limit,
        cost_estimate=hide,
        name="model_center",
    )(own, row_far, row_near)
    return pl.pallas_call(
        model_edge,
        out_shape=(shape(*tx.shape), shape(*ty.shape), shape(*tz.shape)),
        scratch_shapes=scratch_of(2, PAIRS),
        compiler_params=limit,
        name="model_edge",
    )(col_far, col_near, edge, edge_dense, center)


def solution(mesh):
    cells = P(None, "gx", "gy")
    in_specs = (cells,) * 7 + (
        P("gx", "gy", None),
        P("gx", "gy", None),
        P(None, "gx", "gy", None),
        P(None, None, "gx", "gy", None),
    )
    return jax.shard_map(
        on_device, mesh=mesh, in_specs=in_specs, out_specs=(cells,) * 3, check_vma=False
    )
```

```python
import jax
import jax.numpy as jnp
from jax import lax
from jax.experimental import pallas as pl
from jax.experimental.pallas import tpu as pltpu
from jax.sharding import PartitionSpec as P

time_step = 0.05

GROUPS = {"p": (0, 4), "s": (4, 4), "tx": (8, 4), "ty": (12, 4), "tz": (16, 3), "pv": (19, 4), "up": (23, 4)}
ORDER = ("p", "s", "tx", "ty", "tz", "pv", "up")
COUNT = 27
SLOT = 10
PAIRS = 14
SLOTS = {"p": (0, 10), "tx": (10, 9), "ty": (19, 9), "tz": (28, 9), "pv": (37, 9), "s": (46, 7), "up": (53, 6)}
PACKED = 4
ROWS = 56
HALO = 19


FIELDS = 11


def pack_rows(*refs):
    p, s, tx, ty, tz, pv, up, cell, rate, plan, observed = refs[:FIELDS]
    own, far, near, upi, cells, rates, plans, seen, sems = refs[FIELDS:]
    targets = [own.at[pl.ds(*GROUPS[name])] for name in ORDER[:6]] + [upi, cells, rates, plans, seen]
    copies = [
        pltpu.make_async_copy(source, target, sems.at[k])
        for k, (source, target) in enumerate(zip(refs[:FIELDS], targets))
    ]
    for copy in copies:
        copy.start()
    for copy in copies:
        copy.wait()
    first = GROUPS["up"][0]
    for layer in range(4):
        own[first + layer] = upi[layer].astype(jnp.float32)
    own[COUNT] = jnp.zeros((16, 128), jnp.float32)
    own[COUNT, 0:1, 0:64] = cells[0].astype(jnp.float32)
    own[COUNT, 1:2, 0:64] = rates[0]
    for n in range(2):
        own[COUNT, 2 + n : 3 + n, 0:64] = plans[n, 0].astype(jnp.float32)
        for k in range(2):
            row = 4 + 2 * n + k
            own[COUNT, row : row + 1, 0:64] = seen[n, k, 0]
    odd = lax.axis_index("gx") & 1
    for g in range(COUNT):
        far[g] = own[g, pl.ds(pl.multiple_of(8 * odd, 8), 8), :]
        near[g] = own[g, pl.ds(pl.multiple_of(8 - 8 * odd, 8), 8), :]
    base = {name: GROUPS[name][0] for name in ORDER}

    blank = jnp.zeros((1, 128), jnp.float32)

    def gathered(*places):
        rows = []
        for layer in (0, 2, 1, 3):
            for name, row in places:
                there = layer < GROUPS[name][1]
                rows.append(own[base[name] + layer, row : row + 1, :] if there else blank)
        return jnp.concatenate([rows[k] for k in (0, 2, 1, 3, 4, 6, 5, 7)], axis=0)

    for_next = [gathered(("p", 7), ("tx", 7))]
    for_next += [jnp.zeros((8, 128), jnp.float32)] * 2
    for_prev = [
        gathered(("p", 8), ("tx", 8)),
        gathered(("ty", 8), ("tz", 8)),
        gathered(("pv", 8), ("p", 9)),
    ]
    for k in range(3):
        far[COUNT + k] = jnp.where(odd == 1, for_next[k], for_prev[k])
        near[COUNT + k] = jnp.where(odd == 1, for_prev[k], for_next[k])
    far[COUNT + 3] = own[COUNT, 0:8, :]
    near[COUNT + 3] = own[COUNT, 0:8, :]


def lanes():
    return lax.broadcasted_iota(jnp.int32, (8, 128), 1)


def in_slot(lane, start, ends, width):
    return ((lane - start - ends * (2 * SLOT - width)) & 63) < width


def sorted_ends(axis, far, near):
    odd = (lax.axis_index(axis) & 1) == 1

    def before(g):
        return jnp.where(odd, near[g], far[g])

    def after(g):
        return jnp.where(odd, far[g], near[g])

    return before, after


def pack_pairs(block, far, near, at):
    odd = lax.axis_index("gy") & 1
    lane = lanes()
    zero = jnp.zeros((8, 128), jnp.float32)
    for pair in range(2):
        ones, twos = {}, {}
        for name in SLOTS:
            first, layers = GROUPS[name]
            ones[name] = block(first + 2 * pair)
            there = 2 * pair + 1 < layers
            twos[name] = pltpu.roll(block(first + 2 * pair + 1), 64, 1) if there else zero
        for out, ends in ((far, odd), (near, 1 - odd)):
            straight = ((lane >> 6) ^ ends) == 0
            part = zero
            for name, (start, width) in SLOTS.items():
                both = jnp.where(straight, ones[name], twos[name])
                both = pltpu.roll(both, start + 2 * SLOT * ends, 1)
                part = jnp.where(in_slot(lane, start, ends, width), both, part)
            out[at + pair] = part


def extra_pair(one, two):
    row = lax.broadcasted_iota(jnp.int32, (8, 128), 0)
    return jnp.where(row < 4, one, pltpu.roll(two, 4, 0)), jnp.where(row < 4, pltpu.roll(one, 4, 0), two)


def pack_own(own, far, near):
    for tile in range(2):
        rows = slice(8 * tile, 8 * tile + 8)
        pack_pairs(lambda g: own[g, rows, :], far, near, 2 * tile)


def pack_cols(own, own_far, own_near, row_far, row_near, far, near):
    low, high = sorted_ends("gx", row_far, row_near)
    for out, part in ((far, own_far), (near, own_near)):
        for at in range(PACKED):
            out[at] = part[at]
    pack_pairs(low, far, near, PACKED)
    pack_pairs(high, far, near, PACKED + 2)
    odd = lax.axis_index("gy") & 1
    lane = lanes()
    both = jnp.where(lane < 64, own[COUNT, 0:8, :], pltpu.roll(low(COUNT + 3), 64, 1))
    extras = extra_pair(low(COUNT), high(COUNT)) + extra_pair(high(COUNT + 1), high(COUNT + 2))
    for out, ends in ((far, odd), (near, 1 - odd)):
        out[2 * PACKED] = both
        part = high(COUNT + 3)
        for k, value in enumerate(extras):
            start = 64 + SLOT * k
            mask = ((lane - start - SLOT * ends) & 127) < SLOT
            part = jnp.where(mask, pltpu.roll(value, start + 2 * SLOT * ends, 1), part)
        out[2 * PACKED + 1] = part


def split3(value):
    hi = value.astype(jnp.bfloat16).astype(jnp.float32)
    rest = value - hi
    mid = rest.astype(jnp.bfloat16).astype(jnp.float32)
    return hi, mid, rest - mid


SRC0, SRC1, OP0, OS0, OP1, OS1, CNT = range(7)


def spread_wells(info, base, to_spot, rows_of, count, write):
    width = info.shape[1]
    cell = info[0:1].astype(jnp.int32)
    layer = lax.shift_right_logical(cell, 11)
    place = (lax.shift_right_logical(cell, 7) & 15) + base
    target = jnp.where(place >= 8, rows_of(layer) * 40 + place - 8, -1)
    spot = to_spot(layer, cell & 127)
    hit = lax.broadcasted_iota(jnp.int32, (count, width), 0) == target
    hit = jnp.where(hit, 1.0, 0.0).astype(jnp.bfloat16)
    lane = lax.broadcasted_iota(jnp.int32, (128, width), 0)
    to_lane = jnp.where(lane == spot, 1.0, 0.0).astype(jnp.bfloat16)
    rate = info[1:2] * 0.5
    values = [rate * info[2:3], rate * info[3:4]] + [info[k : k + 1] for k in range(4, 8)]
    for number, value in enumerate(values):
        total = None
        for part in split3(value):
            part = jnp.broadcast_to(part, (16, width)).astype(jnp.bfloat16)
            left = hit * jnp.concatenate([part] * (count // 16), axis=0)
            term = dot(left, to_lane)
            total = term if total is None else total + term
        write(number, total)
    write(CNT, dot(hit, to_lane))


def dot(left, right):
    return lax.dot_general(left, right, (((1,), (1,)), ((), ())), preferred_element_type=jnp.float32)


def list_block(info):
    return lax.shift_right_logical(lax.broadcasted_iota(jnp.int32, (1, info.shape[1]), 1), 6)


def scratch_of(slabs, groups):
    counts = (slabs,) * 12 + (3 * slabs,) * 4 + (slabs,) * 9
    f32 = jnp.float32
    shapes = [pltpu.VMEM((groups, ROWS, 128), f32), pltpu.VMEM((7, slabs, ROWS, 128), f32)]
    shapes += [pltpu.VMEM((slabs, ROWS, 128), jnp.int32)]
    return shapes + [pltpu.VMEM((count, ROWS, 128), f32) for count in counts]


class Single:
    slabs = 4
    paired = False
    first = {name: GROUPS[name][0] for name in ORDER}

    def carry(self, kept, k, value):
        return kept, value


class Paired:
    slabs = 2
    paired = True
    first = {name: 2 * k for k, name in enumerate(ORDER)}

    def __init__(self, lower):
        self.lower = lower

    def carry(self, kept, k, value):
        turned = pltpu.roll(value, 64, 1)
        return jnp.where(self.lower, kept if k else 0.0, turned), turned


def simulate(form, fld, dense, upi, scratch, emit_x, emit_y, emit_z):
    (rcp, tym, tzd, q0, p1, q1, p2, f0, d0, s1, f1, d1, fup0, fup1, dp1, dp2,
     sig2, psi2, psi1, mup2, muq1, mup1, muq0, flux, rest) = scratch
    n = form.slabs
    last_up = n if form.paired else n - 1
    first_down = 0 if form.paired else 1
    PB, SB, XB, YB, ZB, VB = (form.first[name] for name in ORDER[:6])

    def here(ref, k, t):
        return ref[k, 8 * t : 8 * t + 8, :]

    def down(ref, k, t):
        return ref[k, 8 * t + 1 : 8 * t + 9, :]

    def above(ref, k, t):
        return ref[k, 8 * t - 1 : 8 * t + 7, :]

    def put(ref, k, t, value):
        ref[k, 8 * t : 8 * t + 8, :] = value

    def right(value):
        return pltpu.roll(value, 127, 1)

    def left(value):
        return pltpu.roll(value, 1, 1)

    def up(ref, base, k, t):
        if not form.paired:
            return here(ref, base + k + 1, t)
        turned = pltpu.roll(here(ref, base + 1, t), 64, 1)
        return turned if k else jnp.where(form.lower, pltpu.roll(here(ref, base, t), 64, 1), turned)

    def under(ref, base, k, t):
        if not form.paired:
            return here(ref, base + k - 1, t)
        turned = pltpu.roll(here(ref, base, t), 64, 1)
        return jnp.where(form.lower, turned, pltpu.roll(here(ref, base + 1, t), 64, 1)) if k else turned

    def z_under(k, t):
        return here(tzd, k, t) if form.paired else here(fld, ZB + k - 1, t)

    for k in range(n):
        for t in range(1, 6):
            beyond = right(here(fld, VB + k, t))
            put(fld, YB + k, t, jnp.where(beyond == 0.0, 0.0, here(fld, YB + k, t)))
        last = slice(31, 32)
        fld[XB + k, last, :] = jnp.where(fld[VB + k, 32:33, :] == 0.0, 0.0, fld[XB + k, last, :])
    for t in range(1, 6):
        for k in range(n):
            volume = here(fld, VB + k, t)
            volume = jnp.where(volume == 0.0, 1.0, volume)
            put(fld, VB + k, t, volume)
            if form.paired:
                below = under(fld, ZB, k, t)
                put(tzd, k, t, below if k else jnp.where(form.lower, 0.0, below))
            west = left(here(fld, YB + k, t))
            put(tym, k, t, west)
            total = volume + (here(fld, XB + k, t) + above(fld, XB + k, t)) + (here(fld, YB + k, t) + west)
            if k < last_up:
                total = total + here(fld, ZB + k, t)
            if k >= first_down:
                total = total + z_under(k, t)
            put(rcp, k, t, 1.0 / total)

    def neighbours(ref, base, k, t):
        value = here(ref, base + k, t)
        total = here(fld, XB + k, t) * down(ref, base + k, t) + above(fld, XB + k, t) * above(ref, base + k, t)
        total = total + (here(fld, YB + k, t) * right(value) + here(tym, k, t) * left(value))
        if k < last_up:
            total = total + here(fld, ZB + k, t) * up(ref, base, k, t)
        if k >= first_down:
            total = total + z_under(k, t) * under(ref, base, k, t)
        return total

    def relax(out, ref, base, old, old_base, source, tiles):
        for t in tiles:
            for k in range(n):
                total = here(fld, VB + k, t) * here(old, old_base + k, t) + here(dense.at[source], k, t)
                put(out, k, t, (total + neighbours(ref, base, k, t)) * here(rcp, k, t))

    def put_mobility(value, k, t, mobile, slope):
        rest_of = 1.0 - value
        wetted = value * value
        inverse = 1.0 / (wetted + 0.5 * rest_of * rest_of)
        put(mobile, k, t, wetted * inverse)
        put(slope, k, t, value * rest_of * (inverse * inverse))

    def bit(k, t, number):
        return (here(upi, k, t) & (1 << number)) != 0

    def transport(pressure, sat, sat_base, mobile, number, fup, dp, finish):
        for t in range(1, 5):
            kept = None
            for k in range(n):
                mob = here(mobile, k, t)
                pres = here(pressure, k, t)
                drop_x = pres - down(pressure, k, t)
                drop_y = pres - right(pres)
                up_x = jnp.where(bit(k, t, 3 * number), mob, down(mobile, k, t))
                up_y = jnp.where(bit(k, t, 3 * number + 1), mob, right(mob))
                put(fup, k, t, up_x)
                put(fup, n + k, t, up_y)
                put(dp, k, t, drop_x)
                put(dp, n + k, t, drop_y)
                flux_x = here(fld, XB + k, t) * up_x * drop_x
                flux_y = here(fld, YB + k, t) * up_y * drop_y
                put(flux, k, t, flux_x)
                net = (flux_x - above(flux, k, t)) + (flux_y - left(flux_y))
                flux_z = None
                if k < last_up:
                    drop_z = pres - up(pressure, 0, k, t)
                    up_z = jnp.where(bit(k, t, 3 * number + 2), mob, up(mobile, 0, k, t))
                    put(fup, 2 * n + k, t, up_z)
                    put(dp, 2 * n + k, t, drop_z)
                    flux_z = here(fld, ZB + k, t) * up_z * drop_z
                    net = net + flux_z
                below, kept = form.carry(kept, k, flux_z)
                if k >= first_down:
                    net = net - below
                finish(here(sat, sat_base + k, t) - time_step * net / here(fld, VB + k, t), k, t)

    tiles = range(1, 5)
    relax(q0, fld, PB, fld, PB, SRC0, range(1, 6))
    relax(p1, q0, 0, fld, PB, SRC0, tiles)
    for t in tiles:
        for k in range(n):
            put_mobility(here(fld, SB + k, t), k, t, f0, d0)

    def finish_first(moved, k, t):
        put(s1, k, t, moved)
        put_mobility(moved, k, t, f1, d1)

    transport(p1, fld, SB, f0, 0, fup0, dp1, finish_first)
    relax(q1, p1, 0, p1, 0, SRC1, tiles)
    relax(p2, q1, 0, p1, 0, SRC1, tiles)

    def finish_second(moved, k, t):
        miss = here(dense.at[CNT], k, t) * moved - here(dense.at[OS1], k, t)
        put(sig2, k, t, miss)
        put(psi2, k, t, time_step * miss / here(fld, VB + k, t))

    transport(p2, s1, 0, f1, 1, fup1, dp2, finish_second)

    for t in tiles:
        kept_h = kept_r = None
        for k in range(n):
            psi = here(psi2, k, t)
            phi_x = (down(psi2, k, t) - psi) * here(fld, XB + k, t)
            phi_y = (right(psi) - psi) * here(fld, YB + k, t)
            h_x = phi_x * here(fup1, k, t)
            h_y = phi_y * here(fup1, n + k, t)
            k_x = phi_x * here(dp2, k, t)
            k_y = phi_y * here(dp2, n + k, t)
            s_x = jnp.where(bit(k, t, 3), k_x, 0.0)
            s_y = jnp.where(bit(k, t, 4), k_y, 0.0)
            put(flux, k, t, h_x)
            put(rest, k, t, k_x - s_x)
            press = (h_x - above(flux, k, t)) + (h_y - left(h_y))
            satur = (s_x + above(rest, k, t)) + (s_y + left(k_y - s_y))
            h_z = r_z = None
            if k < last_up:
                phi_z = (up(psi2, 0, k, t) - psi) * here(fld, ZB + k, t)
                h_z = phi_z * here(fup1, 2 * n + k, t)
                k_z = phi_z * here(dp2, 2 * n + k, t)
                s_z = jnp.where(bit(k, t, 5), k_z, 0.0)
                r_z = k_z - s_z
                press = press + h_z
                satur = satur + s_z
            below_h, kept_h = form.carry(kept_h, k, h_z)
            below_r, kept_r = form.carry(kept_r, k, r_z)
            if k >= first_down:
                press = press - below_h
                satur = satur + below_r
            count = here(dense.at[CNT], k, t)
            press = press + (count * here(p2, k, t) - here(dense.at[OP1], k, t))
            put(mup2, k, t, press * here(rcp, k, t))
            sigma = here(sig2, k, t) + satur * here(d1, k, t)
            sigma = sigma + (count * here(s1, k, t) - here(dense.at[OS0], k, t))
            put(psi1, k, t, time_step * sigma / here(fld, VB + k, t))

    for t in tiles:
        for k in range(n):
            put(muq1, k, t, neighbours(mup2, 0, k, t) * here(rcp, k, t))

    for t in tiles:
        kept_h = None
        for k in range(n):
            psi = here(psi1, k, t)
            h_x = (down(psi1, k, t) - psi) * here(fld, XB + k, t) * here(fup0, k, t)
            h_y = (right(psi) - psi) * here(fld, YB + k, t) * here(fup0, n + k, t)
            put(flux, k, t, h_x)
            press = (h_x - above(flux, k, t)) + (h_y - left(h_y))
            h_z = None
            if k < last_up:
                h_z = (up(psi1, 0, k, t) - psi) * here(fld, ZB + k, t) * here(fup0, 2 * n + k, t)
                press = press + h_z
            below_h, kept_h = form.carry(kept_h, k, h_z)
            if k >= first_down:
                press = press - below_h
            count = here(dense.at[CNT], k, t)
            press = press + (count * here(p1, k, t) - here(dense.at[OP0], k, t))
            press = press + here(fld, VB + k, t) * (here(mup2, k, t) + here(muq1, k, t))
            press = press + neighbours(muq1, 0, k, t)
            put(mup1, k, t, press * here(rcp, k, t))

    for t in range(2, 5):
        for k in range(n):
            put(muq0, k, t, neighbours(mup1, 0, k, t) * here(rcp, k, t))

    stages = (
        (mup2, q1, 0, p2, 0),
        (muq1, p1, 0, q1, 0),
        (mup1, q0, 0, p1, 0),
        (muq0, fld, PB, q0, 0),
    )
    for t in range(2, 4):
        for k in range(n):
            sum_x = sum_y = sum_z = 0.0
            for psi, fup, dp in ((psi2, fup1, dp2), (psi1, fup0, dp1)):
                mid = here(psi, k, t)
                sum_x = sum_x + (down(psi, k, t) - mid) * here(fup, k, t) * here(dp, k, t)
                sum_y = sum_y + (right(mid) - mid) * here(fup, n + k, t) * here(dp, n + k, t)
                if k < last_up:
                    sum_z = sum_z + (up(psi, 0, k, t) - mid) * here(fup, 2 * n + k, t) * here(dp, 2 * n + k, t)
            for mu, value, base, out, out_base in stages:
                mu_c, v_c, o_c = here(mu, k, t), here(value, base + k, t), here(out, out_base + k, t)
                mu_d, v_d, o_d = down(mu, k, t), down(value, base + k, t), down(out, out_base + k, t)
                sum_x = sum_x + (mu_c * (v_d - o_c) + mu_d * (v_c - o_d))
                sum_y = sum_y + (mu_c * (right(v_c) - o_c) + right(mu_c) * (v_c - right(o_c)))
                if k < last_up:
                    mu_u = up(mu, 0, k, t)
                    v_u = up(value, base, k, t)
                    o_u = up(out, out_base, k, t)
                    sum_z = sum_z + (mu_c * (v_u - o_c) + mu_u * (v_c - o_u))
            emit_x(k, t, jnp.where(here(fld, XB + k, t) == 0.0, 0.0, sum_x))
            emit_y(k, t, jnp.where(here(fld, YB + k, t) == 0.0, 0.0, sum_y))
            if k < last_up:
                emit_z(k, t, sum_z)


PLACES = (
    (("p", 7), ("tx", 7)),
    (("p", 40), ("tx", 40)),
    (("ty", 40), ("tz", 40)),
    (("pv", 40), ("p", 41)),
)


def model_center(own, row_far, row_near, grads, edge, edge_dense, fld, dense, upi, *scratch):
    low, high = sorted_ends("gx", row_far, row_near)
    lane = lanes()

    low_half = (lane & 63) < HALO

    def edge_of(one, two):
        first = jnp.where(low_half, pltpu.roll(one, HALO, 1), pltpu.roll(one, HALO + 2 * SLOT, 1))
        second = jnp.where(low_half, pltpu.roll(two, HALO + 64, 1), pltpu.roll(two, HALO + 2 * SLOT + 64, 1))
        return jnp.where(lane < 64, first, second)

    def blocks_of(g):
        return [low(g), own[g, 0:8, :], own[g, 8:16, :], high(g)]

    for name in ORDER:
        first, layers = GROUPS[name]
        for pair in range(2):
            one = blocks_of(first + 2 * pair)
            there = 2 * pair + 1 < layers
            two = blocks_of(first + 2 * pair + 1) if there else [jnp.zeros((8, 128), jnp.float32)] * 4
            for k in range(4):
                rows = slice(8 + 8 * k, 16 + 8 * k)
                edge[Paired.first[name] + pair, rows, :] = edge_of(one[k], two[k])
                for layer, value in ((2 * pair, one[k]), (2 * pair + 1, two[k])):
                    if layer < layers:
                        fld[first + layer, rows, :] = value
                    if name == "up":
                        upi[layer, rows, :] = value.astype(jnp.int32)
    extras = [low(COUNT)] + [high(COUNT + k) for k in range(3)]
    for value, places in zip(extras, PLACES):
        for block, (name, row) in enumerate(places):
            first, layers = GROUPS[name]
            for layer in range(layers):
                k = 4 * (layer & 1) + 2 * block + layer // 2
                fld[first + layer, row : row + 1, :] = value[k : k + 1]
    for half in range(2):
        value = edge_of(*extra_pair(*extras[2 * half : 2 * half + 2]))
        for number, places in enumerate(PLACES[2 * half : 2 * half + 2]):
            for block, (name, row) in enumerate(places):
                for pair in range(2):
                    k = 4 * number + 2 * block + pair
                    edge[Paired.first[name] + pair, row : row + 1, :] = value[k : k + 1]

    info = jnp.concatenate(
        [own[COUNT, 0:8, 0:64], low(COUNT + 3)[:, 0:64], high(COUNT + 3)[:, 0:64]], axis=1
    )
    block = list_block(info)
    base = jnp.where(block == 0, 16, jnp.where(block == 1, 0, 32))

    def write_center(number, total):
        for k in range(4):
            dense[number, k, 8:48, :] = total[40 * k : 40 * k + 40]

    def write_edge(number, total):
        for pair in range(2):
            edge_dense[number, pair, 8:48, :] = total[40 * pair : 40 * pair + 40]

    def edge_lane(layer, col):
        start = 64 * (layer & 1)
        late = jnp.where(col >= 128 - HALO, start + col - (128 - HALO), -1)
        return jnp.where(col < 64 - HALO - 2 * SLOT, start + HALO + 2 * SLOT + col, late)

    spread_wells(info, base, lambda layer, col: col, lambda layer: layer, 160, write_center)
    spread_wells(info, base, edge_lane, lambda layer: layer >> 1, 80, write_edge)

    def emit(first):
        def write(k, t, value):
            grads[first + k, 8 * t - 16 : 8 * t - 8, :] = value

        return write

    simulate(Single(), fld, dense, upi, scratch, emit(0), emit(4), emit(8))


def model_edge(
    col_far, col_near, edge, edge_dense, center, grad_x, grad_y, grad_z, fld, dense, upi, *scratch
):
    before, after = sorted_ends("gy", col_far, col_near)
    odd = lax.axis_index("gy") & 1
    lane = lanes()
    lower = lane < 64
    beside = ((lane - HALO) & 63) < 2 * SLOT

    for name, (start, width) in SLOTS.items():
        far_cols = in_slot(lane, start, 1 - odd, width)
        for pair in range(2):
            g = Paired.first[name] + pair
            for k, at in enumerate((PACKED, 0, 2, PACKED + 2)):
                rows = slice(8 + 8 * k, 16 + 8 * k)
                both = jnp.where(far_cols, col_far[at + pair], col_near[at + pair])
                both = pltpu.roll(both, (HALO - start) % 128, 1)
                block = jnp.where(beside, both, edge[g, rows, :])
                if name == "up":
                    upi[pair, rows, :] = block.astype(jnp.int32)
                else:
                    fld[g, rows, :] = block
    for half in range(2):
        values = []
        for k in (2 * half, 2 * half + 1):
            start = 64 + SLOT * k
            mask = ((lane - start - SLOT * (1 - odd)) & 127) < SLOT
            both = jnp.where(mask, col_far[2 * PACKED + 1], col_near[2 * PACKED + 1])
            values.append(pltpu.roll(both, (HALO + 64 * (k & 1) - start) % 128, 1))
        value = jnp.where(lower, *values)
        for number, places in enumerate(PLACES[2 * half : 2 * half + 2]):
            for block, (name, row) in enumerate(places):
                for pair in range(2):
                    k = 4 * number + 2 * block + pair
                    at = (Paired.first[name] + pair, slice(row, row + 1), slice(None))
                    fld[at] = jnp.where(beside[0:1], value[k : k + 1], edge[at])
    first, second = 2 * PACKED, 2 * PACKED + 1
    own_lists = [before(first)[:, 0:64], after(first)[:, 0:64]]
    low_lists = [before(first)[:, 64:128], after(first)[:, 64:128]]
    high_lists = [before(second)[:, 0:64], after(second)[:, 0:64]]
    info = jnp.concatenate(own_lists + low_lists + high_lists, axis=1)
    block = list_block(info)
    base = jnp.where(block < 2, 16, jnp.where(block < 4, 0, 32))
    ahead = (block & 1) == 1

    def beside_lane(layer, col):
        start = 64 * (layer & 1) + HALO
        return jnp.where(
            ahead,
            jnp.where(col < SLOT, start + col, -1),
            jnp.where(col >= 128 - SLOT, start + col - 128 + 2 * SLOT, -1),
        )

    def write_beside(number, total):
        for pair in range(2):
            dense[number, pair, 8:48, :] = total[40 * pair : 40 * pair + 40] + edge_dense[number, pair, 8:48, :]

    spread_wells(info, base, beside_lane, lambda layer: layer >> 1, 80, write_beside)

    def emit(out, group):
        def write(k, t, value):
            rows = slice(8 * t - 16, 8 * t - 8)
            for half in range(2):
                layer = 2 * k + half
                if layer < out.shape[0]:
                    firsts = pltpu.roll(value, 128 - (HALO + 2 * SLOT) - 64 * half, 1)
                    lasts = pltpu.roll(value, 128 - HALO - 64 * half, 1)
                    inner = jnp.where(lane < SLOT - 1, firsts, center[group + layer, rows, :])
                    out[layer, rows, :] = jnp.where(lane >= 128 - SLOT, lasts, inner)

        return write

    simulate(Paired(lower), fld, dense, upi, scratch, emit(grad_x, 0), emit(grad_y, 4), emit(grad_z, 8))


def swapped(value, axis, first):
    count = lax.axis_size(axis)
    pairs = []
    for i in range(first, count - 1, 2):
        pairs += [(i, i + 1), (i + 1, i)]
    return lax.ppermute(value, axis, pairs)


def on_device(p, s, tx, ty, tz, pv, up, cell, rate, plan, observed):
    f32 = jnp.float32

    def shape(*dims):
        return jax.ShapeDtypeStruct(dims, f32)

    limit = pltpu.CompilerParams(vmem_limit_bytes=24 * 1024 * 1024)
    inputs = (p, s, tx, ty, tz, pv, up, cell, rate, plan, observed)
    inputs = [pltpu.with_memory_space_constraint(value, pltpu.HBM) for value in inputs]
    strip = shape(COUNT + 4, 8, 128)
    own, far, near = pl.pallas_call(
        pack_rows,
        out_shape=(shape(COUNT + 1, 16, 128), strip, strip),
        in_specs=[pl.BlockSpec(memory_space=pltpu.HBM)] * len(inputs),
        scratch_shapes=[pltpu.VMEM(value.shape, value.dtype) for value in inputs[6:]]
        + [pltpu.SemaphoreType.DMA((len(inputs),))],
        compiler_params=limit,
        name="pack_rows",
    )(*inputs)
    row_far = swapped(far, "gx", 1)
    row_near = swapped(near, "gx", 0)
    hide = pl.CostEstimate(flops=10**11, bytes_accessed=1 << 28, transcendentals=0)
    strip = shape(PACKED, 8, 128)
    own_far, own_near = pl.pallas_call(
        pack_own,
        out_shape=(strip, strip),
        compiler_params=limit,
        cost_estimate=hide,
        name="pack_own",
    )(own)
    strip = shape(2 * PACKED + 2, 8, 128)
    far, near = pl.pallas_call(
        pack_cols,
        out_shape=(strip, strip),
        compiler_params=limit,
        name="pack_cols",
    )(own, own_far, own_near, row_far, row_near)
    col_far = swapped(far, "gy", 1)
    col_near = swapped(near, "gy", 0)
    center, edge, edge_dense = pl.pallas_call(
        model_center,
        out_shape=(shape(11, 16, 128), shape(PAIRS, ROWS, 128), shape(7, 2, ROWS, 128)),
        scratch_shapes=scratch_of(4, COUNT),
        compiler_params=limit,
        cost_estimate=hide,
        name="model_center",
    )(own, row_far, row_near)
    return pl.pallas_call(
        model_edge,
        out_shape=(shape(*tx.shape), shape(*ty.shape), shape(*tz.shape)),
        scratch_shapes=scratch_of(2, PAIRS),
        compiler_params=limit,
        name="model_edge",
    )(col_far, col_near, edge, edge_dense, center)


def solution(mesh):
    cells = P(None, "gx", "gy")
    in_specs = (cells,) * 7 + (
        P("gx", "gy", None),
        P("gx", "gy", None),
        P(None, "gx", "gy", None),
        P(None, None, "gx", "gy", None),
    )
    return jax.shard_map(
        on_device, mesh=mesh, in_specs=in_specs, out_specs=(cells,) * 3, check_vma=False
    )
```

```python
import jax
import jax.numpy as jnp
from jax import lax
from jax.experimental import pallas as pl
from jax.experimental.pallas import tpu as pltpu
from jax.sharding import PartitionSpec as P

time_step = 0.05

GROUPS = {"p": (0, 4), "s": (4, 4), "tx": (8, 4), "ty": (12, 4), "tz": (16, 3), "pv": (19, 4), "up": (23, 4)}
ORDER = ("p", "s", "tx", "ty", "tz", "pv", "up")
COUNT = 27
SLOT = 10
SLOTS = {"p": (0, 10), "tx": (10, 9), "ty": (19, 9), "tz": (28, 9), "pv": (37, 9), "s": (46, 7), "up": (53, 6)}
PACKED = 4
ROWS = 56
HALO = 2 * SLOT
LATE = 99


FIELDS = 11


def pack_rows(*refs):
    p, s, tx, ty, tz, pv, up, cell, rate, plan, observed = refs[:FIELDS]
    own, far, near, upi, cells, rates, plans, seen, sems = refs[FIELDS:]
    targets = [own.at[pl.ds(*GROUPS[name])] for name in ORDER[:6]] + [upi, cells, rates, plans, seen]
    copies = [
        pltpu.make_async_copy(source, target, sems.at[k])
        for k, (source, target) in enumerate(zip(refs[:FIELDS], targets))
    ]
    for copy in copies:
        copy.start()
    for copy in copies:
        copy.wait()
    first = GROUPS["up"][0]
    for layer in range(4):
        own[first + layer] = upi[layer].astype(jnp.float32)
    own[COUNT] = jnp.zeros((16, 128), jnp.float32)
    own[COUNT, 0:1, 0:64] = cells[0].astype(jnp.float32)
    own[COUNT, 1:2, 0:64] = rates[0]
    for n in range(2):
        own[COUNT, 2 + n : 3 + n, 0:64] = plans[n, 0].astype(jnp.float32)
        for k in range(2):
            row = 4 + 2 * n + k
            own[COUNT, row : row + 1, 0:64] = seen[n, k, 0]
    odd = lax.axis_index("gx") & 1
    for g in range(COUNT):
        far[g] = own[g, pl.ds(pl.multiple_of(8 * odd, 8), 8), :]
        near[g] = own[g, pl.ds(pl.multiple_of(8 - 8 * odd, 8), 8), :]
    base = {name: GROUPS[name][0] for name in ORDER}

    blank = jnp.zeros((1, 128), jnp.float32)

    def gathered(*places):
        rows = []
        for layer in (0, 2, 1, 3):
            for name, row in places:
                there = layer < GROUPS[name][1]
                rows.append(own[base[name] + layer, row : row + 1, :] if there else blank)
        return jnp.concatenate([rows[k] for k in (0, 2, 1, 3, 4, 6, 5, 7)], axis=0)

    for_next = [gathered(("p", 7), ("tx", 7))]
    for_next += [jnp.zeros((8, 128), jnp.float32)] * 2
    for_prev = [
        gathered(("p", 8), ("tx", 8)),
        gathered(("ty", 8), ("tz", 8)),
        gathered(("pv", 8), ("p", 9)),
    ]
    for k in range(3):
        far[COUNT + k] = jnp.where(odd == 1, for_next[k], for_prev[k])
        near[COUNT + k] = jnp.where(odd == 1, for_prev[k], for_next[k])
    far[COUNT + 3] = own[COUNT, 0:8, :]
    near[COUNT + 3] = own[COUNT, 0:8, :]


def lanes():
    return lax.broadcasted_iota(jnp.int32, (8, 128), 1)


def in_slot(lane, start, ends, width):
    return ((lane - start - ends * (2 * SLOT - width)) & 63) < width


def sorted_ends(axis, far, near):
    odd = (lax.axis_index(axis) & 1) == 1

    def before(g):
        return jnp.where(odd, near[g], far[g])

    def after(g):
        return jnp.where(odd, far[g], near[g])

    return before, after


def pack_pairs(block, far, near, at):
    odd = lax.axis_index("gy") & 1
    lane = lanes()
    zero = jnp.zeros((8, 128), jnp.float32)
    for pair in range(2):
        ones, twos = {}, {}
        for name in SLOTS:
            first, layers = GROUPS[name]
            ones[name] = block(first + 2 * pair)
            there = 2 * pair + 1 < layers
            twos[name] = pltpu.roll(block(first + 2 * pair + 1), 64, 1) if there else zero
        for out, ends in ((far, odd), (near, 1 - odd)):
            straight = ((lane >> 6) ^ ends) == 0
            part = zero
            for name, (start, width) in SLOTS.items():
                both = jnp.where(straight, ones[name], twos[name])
                both = pltpu.roll(both, start + 2 * SLOT * ends, 1)
                part = jnp.where(in_slot(lane, start, ends, width), both, part)
            out[at + pair] = part


def extra_pair(one, two):
    row = lax.broadcasted_iota(jnp.int32, (8, 128), 0)
    return jnp.where(row < 4, one, pltpu.roll(two, 4, 0)), jnp.where(row < 4, pltpu.roll(one, 4, 0), two)


def pack_own(own, far, near):
    for tile in range(2):
        rows = slice(8 * tile, 8 * tile + 8)
        pack_pairs(lambda g: own[g, rows, :], far, near, 2 * tile)


def pack_cols(own, own_far, own_near, row_far, row_near, far, near):
    low, high = sorted_ends("gx", row_far, row_near)
    for out, part in ((far, own_far), (near, own_near)):
        for at in range(PACKED):
            out[at] = part[at]
    pack_pairs(low, far, near, PACKED)
    pack_pairs(high, far, near, PACKED + 2)
    odd = lax.axis_index("gy") & 1
    lane = lanes()
    both = jnp.where(lane < 64, own[COUNT, 0:8, :], pltpu.roll(low(COUNT + 3), 64, 1))
    extras = extra_pair(low(COUNT), high(COUNT)) + extra_pair(high(COUNT + 1), high(COUNT + 2))
    for out, ends in ((far, odd), (near, 1 - odd)):
        out[2 * PACKED] = both
        part = high(COUNT + 3)
        for k, value in enumerate(extras):
            start = 64 + SLOT * k
            mask = ((lane - start - SLOT * ends) & 127) < SLOT
            part = jnp.where(mask, pltpu.roll(value, start + 2 * SLOT * ends, 1), part)
        out[2 * PACKED + 1] = part


def split3(value):
    hi = value.astype(jnp.bfloat16).astype(jnp.float32)
    rest = value - hi
    mid = rest.astype(jnp.bfloat16).astype(jnp.float32)
    return hi, mid, rest - mid


SRC0, SRC1, OP0, OS0, OP1, OS1, CNT = range(7)


def spread_wells(info, base, to_spot, write):
    width = info.shape[1]
    cell = info[0:1].astype(jnp.int32)
    layer = lax.shift_right_logical(cell, 11)
    place = (lax.shift_right_logical(cell, 7) & 15) + base
    target = jnp.where(place >= 8, layer * 40 + place - 8, -1)
    spot = to_spot(cell & 127)
    hit = lax.broadcasted_iota(jnp.int32, (160, width), 0) == target
    hit = jnp.where(hit, 1.0, 0.0).astype(jnp.bfloat16)
    lane = lax.broadcasted_iota(jnp.int32, (128, width), 0)
    to_lane = jnp.where(lane == spot, 1.0, 0.0).astype(jnp.bfloat16)
    rate = info[1:2] * 0.5
    values = [rate * info[2:3], rate * info[3:4]] + [info[k : k + 1] for k in range(4, 8)]
    for number, value in enumerate(values):
        total = None
        for part in split3(value):
            part = jnp.broadcast_to(part, (16, width)).astype(jnp.bfloat16)
            left = hit * jnp.concatenate([part] * 10, axis=0)
            term = dot(left, to_lane)
            total = term if total is None else total + term
        write(number, total)
    write(CNT, dot(hit, to_lane))


def dot(left, right):
    return lax.dot_general(left, right, (((1,), (1,)), ((), ())), preferred_element_type=jnp.float32)


def list_block(info):
    return lax.shift_right_logical(lax.broadcasted_iota(jnp.int32, (1, info.shape[1]), 1), 6)


SCRATCH = (4,) * 11 + (11,) * 4 + (4,) * 9


def simulate(fld, dense, upi, scratch, emit_x, emit_y, emit_z):
    (rcp, tym, q0, p1, q1, p2, f0, d0, s1, f1, d1, fup0, fup1, dp1, dp2,
     sig2, psi2, psi1, mup2, muq1, mup1, muq0, flux, rest) = scratch
    PB, SB, XB, YB, ZB, VB = (GROUPS[name][0] for name in ORDER[:6])

    def here(ref, k, t):
        return ref[k, 8 * t : 8 * t + 8, :]

    def down(ref, k, t):
        return ref[k, 8 * t + 1 : 8 * t + 9, :]

    def above(ref, k, t):
        return ref[k, 8 * t - 1 : 8 * t + 7, :]

    def put(ref, k, t, value):
        ref[k, 8 * t : 8 * t + 8, :] = value

    def right(value):
        return pltpu.roll(value, 127, 1)

    def left(value):
        return pltpu.roll(value, 1, 1)

    for k in range(4):
        for t in range(1, 6):
            beyond = right(here(fld, VB + k, t))
            put(fld, YB + k, t, jnp.where(beyond == 0.0, 0.0, here(fld, YB + k, t)))
        last = slice(31, 32)
        fld[XB + k, last, :] = jnp.where(fld[VB + k, 32:33, :] == 0.0, 0.0, fld[XB + k, last, :])
    for t in range(1, 6):
        for k in range(4):
            volume = here(fld, VB + k, t)
            volume = jnp.where(volume == 0.0, 1.0, volume)
            put(fld, VB + k, t, volume)
            west = left(here(fld, YB + k, t))
            put(tym, k, t, west)
            total = volume + (here(fld, XB + k, t) + above(fld, XB + k, t)) + (here(fld, YB + k, t) + west)
            if k < 3:
                total = total + here(fld, ZB + k, t)
            if k > 0:
                total = total + here(fld, ZB + k - 1, t)
            put(rcp, k, t, 1.0 / total)

    def neighbours(ref, base, k, t):
        value = here(ref, base + k, t)
        total = here(fld, XB + k, t) * down(ref, base + k, t) + above(fld, XB + k, t) * above(ref, base + k, t)
        total = total + (here(fld, YB + k, t) * right(value) + here(tym, k, t) * left(value))
        if k < 3:
            total = total + here(fld, ZB + k, t) * here(ref, base + k + 1, t)
        if k > 0:
            total = total + here(fld, ZB + k - 1, t) * here(ref, base + k - 1, t)
        return total

    def relax(out, ref, base, old, old_base, source, tiles):
        for t in tiles:
            for k in range(4):
                total = here(fld, VB + k, t) * here(old, old_base + k, t) + here(dense.at[source], k, t)
                put(out, k, t, (total + neighbours(ref, base, k, t)) * here(rcp, k, t))

    def put_mobility(value, k, t, mobile, slope):
        rest_of = 1.0 - value
        wetted = value * value
        inverse = 1.0 / (wetted + 0.5 * rest_of * rest_of)
        put(mobile, k, t, wetted * inverse)
        put(slope, k, t, value * rest_of * (inverse * inverse))

    def bit(k, t, number):
        return (here(upi, k, t) & (1 << number)) != 0

    def transport(pressure, sat, sat_base, mobile, n, fup, dp, finish):
        for t in range(1, 5):
            below = None
            for k in range(4):
                mob = here(mobile, k, t)
                pres = here(pressure, k, t)
                drop_x = pres - down(pressure, k, t)
                drop_y = pres - right(pres)
                up_x = jnp.where(bit(k, t, 3 * n), mob, down(mobile, k, t))
                up_y = jnp.where(bit(k, t, 3 * n + 1), mob, right(mob))
                put(fup, k, t, up_x)
                put(fup, 4 + k, t, up_y)
                put(dp, k, t, drop_x)
                put(dp, 4 + k, t, drop_y)
                flux_x = here(fld, XB + k, t) * up_x * drop_x
                flux_y = here(fld, YB + k, t) * up_y * drop_y
                put(flux, k, t, flux_x)
                net = (flux_x - above(flux, k, t)) + (flux_y - left(flux_y))
                if k > 0:
                    net = net - below
                if k < 3:
                    drop_z = pres - here(pressure, k + 1, t)
                    up_z = jnp.where(bit(k, t, 3 * n + 2), mob, here(mobile, k + 1, t))
                    put(fup, 8 + k, t, up_z)
                    put(dp, 8 + k, t, drop_z)
                    below = here(fld, ZB + k, t) * up_z * drop_z
                    net = net + below
                finish(here(sat, sat_base + k, t) - time_step * net / here(fld, VB + k, t), k, t)

    tiles = range(1, 5)
    relax(q0, fld, PB, fld, PB, SRC0, range(1, 6))
    relax(p1, q0, 0, fld, PB, SRC0, tiles)
    for t in tiles:
        for k in range(4):
            put_mobility(here(fld, SB + k, t), k, t, f0, d0)

    def finish_first(moved, k, t):
        put(s1, k, t, moved)
        put_mobility(moved, k, t, f1, d1)

    transport(p1, fld, SB, f0, 0, fup0, dp1, finish_first)
    relax(q1, p1, 0, p1, 0, SRC1, tiles)
    relax(p2, q1, 0, p1, 0, SRC1, tiles)

    def finish_second(moved, k, t):
        miss = here(dense.at[CNT], k, t) * moved - here(dense.at[OS1], k, t)
        put(sig2, k, t, miss)
        put(psi2, k, t, time_step * miss / here(fld, VB + k, t))

    transport(p2, s1, 0, f1, 1, fup1, dp2, finish_second)

    for t in tiles:
        below_h = below_r = None
        for k in range(4):
            psi = here(psi2, k, t)
            phi_x = (down(psi2, k, t) - psi) * here(fld, XB + k, t)
            phi_y = (right(psi) - psi) * here(fld, YB + k, t)
            h_x = phi_x * here(fup1, k, t)
            h_y = phi_y * here(fup1, 4 + k, t)
            k_x = phi_x * here(dp2, k, t)
            k_y = phi_y * here(dp2, 4 + k, t)
            s_x = jnp.where(bit(k, t, 3), k_x, 0.0)
            s_y = jnp.where(bit(k, t, 4), k_y, 0.0)
            put(flux, k, t, h_x)
            put(rest, k, t, k_x - s_x)
            press = (h_x - above(flux, k, t)) + (h_y - left(h_y))
            satur = (s_x + above(rest, k, t)) + (s_y + left(k_y - s_y))
            if k > 0:
                press = press - below_h
                satur = satur + below_r
            if k < 3:
                phi_z = (here(psi2, k + 1, t) - psi) * here(fld, ZB + k, t)
                below_h = phi_z * here(fup1, 8 + k, t)
                k_z = phi_z * here(dp2, 8 + k, t)
                s_z = jnp.where(bit(k, t, 5), k_z, 0.0)
                below_r = k_z - s_z
                press = press + below_h
                satur = satur + s_z
            count = here(dense.at[CNT], k, t)
            press = press + (count * here(p2, k, t) - here(dense.at[OP1], k, t))
            put(mup2, k, t, press * here(rcp, k, t))
            sigma = here(sig2, k, t) + satur * here(d1, k, t)
            sigma = sigma + (count * here(s1, k, t) - here(dense.at[OS0], k, t))
            put(psi1, k, t, time_step * sigma / here(fld, VB + k, t))

    for t in tiles:
        for k in range(4):
            put(muq1, k, t, neighbours(mup2, 0, k, t) * here(rcp, k, t))

    for t in tiles:
        below_h = None
        for k in range(4):
            psi = here(psi1, k, t)
            h_x = (down(psi1, k, t) - psi) * here(fld, XB + k, t) * here(fup0, k, t)
            h_y = (right(psi) - psi) * here(fld, YB + k, t) * here(fup0, 4 + k, t)
            put(flux, k, t, h_x)
            press = (h_x - above(flux, k, t)) + (h_y - left(h_y))
            if k > 0:
                press = press - below_h
            if k < 3:
                below_h = (here(psi1, k + 1, t) - psi) * here(fld, ZB + k, t) * here(fup0, 8 + k, t)
                press = press + below_h
            count = here(dense.at[CNT], k, t)
            press = press + (count * here(p1, k, t) - here(dense.at[OP0], k, t))
            press = press + here(fld, VB + k, t) * (here(mup2, k, t) + here(muq1, k, t))
            press = press + neighbours(muq1, 0, k, t)
            put(mup1, k, t, press * here(rcp, k, t))

    for t in range(2, 5):
        for k in range(4):
            put(muq0, k, t, neighbours(mup1, 0, k, t) * here(rcp, k, t))

    stages = (
        (mup2, q1, 0, p2, 0),
        (muq1, p1, 0, q1, 0),
        (mup1, q0, 0, p1, 0),
        (muq0, fld, PB, q0, 0),
    )
    for t in range(2, 4):
        for k in range(4):
            sum_x = sum_y = sum_z = 0.0
            for psi, fup, dp in ((psi2, fup1, dp2), (psi1, fup0, dp1)):
                mid = here(psi, k, t)
                sum_x = sum_x + (down(psi, k, t) - mid) * here(fup, k, t) * here(dp, k, t)
                sum_y = sum_y + (right(mid) - mid) * here(fup, 4 + k, t) * here(dp, 4 + k, t)
                if k < 3:
                    sum_z = sum_z + (here(psi, k + 1, t) - mid) * here(fup, 8 + k, t) * here(dp, 8 + k, t)
            for mu, value, base, out, out_base in stages:
                mu_c, v_c, o_c = here(mu, k, t), here(value, base + k, t), here(out, out_base + k, t)
                mu_d, v_d, o_d = down(mu, k, t), down(value, base + k, t), down(out, out_base + k, t)
                sum_x = sum_x + (mu_c * (v_d - o_c) + mu_d * (v_c - o_d))
                sum_y = sum_y + (mu_c * (right(v_c) - o_c) + right(mu_c) * (v_c - right(o_c)))
                if k < 3:
                    mu_u = here(mu, k + 1, t)
                    v_u = here(value, base + k + 1, t)
                    o_u = here(out, out_base + k + 1, t)
                    sum_z = sum_z + (mu_c * (v_u - o_c) + mu_u * (v_c - o_u))
            emit_x(k, t, jnp.where(here(fld, XB + k, t) == 0.0, 0.0, sum_x))
            emit_y(k, t, jnp.where(here(fld, YB + k, t) == 0.0, 0.0, sum_y))
            if k < 3:
                emit_z(k, t, sum_z)


PLACES = (
    (("p", 7), ("tx", 7)),
    (("p", 40), ("tx", 40)),
    (("ty", 40), ("tz", 40)),
    (("pv", 40), ("p", 41)),
)


def put_beyond(fld, value, places):
    for block, (name, row) in enumerate(places):
        first, layers = GROUPS[name]
        for layer in range(layers):
            k = 4 * (layer & 1) + 2 * block + layer // 2
            fld[first + layer, row : row + 1, :] = value[k : k + 1]


def model_center(own, row_far, row_near, grads, edge, edge_dense, fld, dense, upi, *scratch):
    low, high = sorted_ends("gx", row_far, row_near)
    lane = lanes()

    early = lane < LATE

    def edge_of(value):
        return jnp.where(early, pltpu.roll(value, HALO, 1), value)

    for g in range(COUNT):
        for k, block in enumerate((low(g), own[g, 0:8, :], own[g, 8:16, :], high(g))):
            rows = slice(8 + 8 * k, 16 + 8 * k)
            fld[g, rows, :] = block
            edge[g, rows, :] = edge_of(block)
            if g >= GROUPS["up"][0]:
                upi[g - GROUPS["up"][0], rows, :] = block.astype(jnp.int32)
    for value, places in zip([low(COUNT)] + [high(COUNT + k) for k in range(3)], PLACES):
        for out, rows in ((fld, value), (edge, edge_of(value))):
            put_beyond(out, rows, places)

    info = jnp.concatenate(
        [own[COUNT, 0:8, 0:64], low(COUNT + 3)[:, 0:64], high(COUNT + 3)[:, 0:64]], axis=1
    )
    block = list_block(info)
    base = jnp.where(block == 0, 16, jnp.where(block == 1, 0, 32))

    def write_center(number, total):
        for k in range(4):
            dense[number, k, 8:48, :] = total[40 * k : 40 * k + 40]

    def write_edge(number, total):
        for k in range(4):
            edge_dense[number, k, 8:48, :] = total[40 * k : 40 * k + 40]

    def edge_lane(col):
        return jnp.where(col < LATE - HALO, col + HALO, jnp.where(col >= LATE, col, -1))

    spread_wells(info, base, lambda col: col, write_center)
    spread_wells(info, base, edge_lane, write_edge)

    def emit(first):
        def write(k, t, value):
            grads[first + k, 8 * t - 16 : 8 * t - 8, :] = value

        return write

    simulate(fld, dense, upi, scratch, emit(0), emit(4), emit(8))


def model_edge(
    col_far, col_near, edge, edge_dense, center, grad_x, grad_y, grad_z, fld, dense, upi, *scratch
):
    before, after = sorted_ends("gy", col_far, col_near)
    odd = lax.axis_index("gy") & 1
    lane = lanes()
    beside = lane < HALO
    for name, (start, width) in SLOTS.items():
        far_cols = in_slot(lane, start, 1 - odd, width)
        first, layers = GROUPS[name]
        for layer in range(layers):
            for k, at in enumerate((PACKED, 0, 2, PACKED + 2)):
                rows = slice(8 + 8 * k, 16 + 8 * k)
                both = jnp.where(far_cols, col_far[at + layer // 2], col_near[at + layer // 2])
                both = pltpu.roll(both, (64 * (layer & 1) - start) % 128, 1)
                block = jnp.where(beside, both, edge[first + layer, rows, :])
                if name == "up":
                    upi[layer, rows, :] = block.astype(jnp.int32)
                else:
                    fld[first + layer, rows, :] = block
    for number, places in enumerate(PLACES):
        for half in range(2):
            start = 64 + SLOT * (2 * (number // 2) + half)
            mask = ((lane - start - SLOT * (1 - odd)) & 127) < SLOT
            both = jnp.where(mask, col_far[2 * PACKED + 1], col_near[2 * PACKED + 1])
            value = pltpu.roll(both, 128 - start, 1)
            for block, (name, row) in enumerate(places):
                for pair in range(2):
                    layer = 2 * pair + half
                    if layer < GROUPS[name][1]:
                        k = 4 * (number & 1) + 2 * block + pair
                        at = (GROUPS[name][0] + layer, slice(row, row + 1), slice(None))
                        fld[at] = jnp.where(beside[0:1], value[k : k + 1], edge[at])
    first, second = 2 * PACKED, 2 * PACKED + 1
    own_lists = [before(first)[:, 0:64], after(first)[:, 0:64]]
    low_lists = [before(first)[:, 64:128], after(first)[:, 64:128]]
    high_lists = [before(second)[:, 0:64], after(second)[:, 0:64]]
    info = jnp.concatenate(own_lists + low_lists + high_lists, axis=1)
    block = list_block(info)
    base = jnp.where(block < 2, 16, jnp.where(block < 4, 0, 32))
    ahead = (block & 1) == 1

    def beside_lane(col):
        last = jnp.where(col >= 128 - SLOT, col - 128 + 2 * SLOT, -1)
        return jnp.where(ahead, jnp.where(col < SLOT, col, -1), last)

    def write_beside(number, total):
        for k in range(4):
            dense[number, k, 8:48, :] = total[40 * k : 40 * k + 40] + edge_dense[number, k, 8:48, :]

    spread_wells(info, base, beside_lane, write_beside)

    def emit(out, group):
        def write(k, t, value):
            rows = slice(8 * t - 16, 8 * t - 8)
            value = jnp.where(lane < 64, pltpu.roll(value, 128 - HALO, 1), value)
            inner = (lane >= SLOT - 1) & (lane < 128 - SLOT)
            out[k, rows, :] = jnp.where(inner, center[group + k, rows, :], value)

        return write

    simulate(fld, dense, upi, scratch, emit(grad_x, 0), emit(grad_y, 4), emit(grad_z, 8))


def swapped(value, axis, first):
    count = lax.axis_size(axis)
    pairs = []
    for i in range(first, count - 1, 2):
        pairs += [(i, i + 1), (i + 1, i)]
    return lax.ppermute(value, axis, pairs)


def on_device(p, s, tx, ty, tz, pv, up, cell, rate, plan, observed):
    f32 = jnp.float32

    def shape(*dims):
        return jax.ShapeDtypeStruct(dims, f32)

    limit = pltpu.CompilerParams(vmem_limit_bytes=24 * 1024 * 1024)
    inputs = (p, s, tx, ty, tz, pv, up, cell, rate, plan, observed)
    inputs = [pltpu.with_memory_space_constraint(value, pltpu.HBM) for value in inputs]
    strip = shape(COUNT + 4, 8, 128)
    own, far, near = pl.pallas_call(
        pack_rows,
        out_shape=(shape(COUNT + 1, 16, 128), strip, strip),
        in_specs=[pl.BlockSpec(memory_space=pltpu.HBM)] * len(inputs),
        scratch_shapes=[pltpu.VMEM(value.shape, value.dtype) for value in inputs[6:]]
        + [pltpu.SemaphoreType.DMA((len(inputs),))],
        compiler_params=limit,
        name="pack_rows",
    )(*inputs)
    row_far = swapped(far, "gx", 1)
    row_near = swapped(near, "gx", 0)
    hide = pl.CostEstimate(flops=10**11, bytes_accessed=1 << 28, transcendentals=0)
    strip = shape(PACKED, 8, 128)
    own_far, own_near = pl.pallas_call(
        pack_own,
        out_shape=(strip, strip),
        compiler_params=limit,
        cost_estimate=hide,
        name="pack_own",
    )(own)
    strip = shape(2 * PACKED + 2, 8, 128)
    far, near = pl.pallas_call(
        pack_cols,
        out_shape=(strip, strip),
        compiler_params=limit,
        name="pack_cols",
    )(own, own_far, own_near, row_far, row_near)
    col_far = swapped(far, "gy", 1)
    col_near = swapped(near, "gy", 0)
    scratch = [pltpu.VMEM((COUNT, ROWS, 128), f32), pltpu.VMEM((7, 4, ROWS, 128), f32)]
    scratch += [pltpu.VMEM((4, ROWS, 128), jnp.int32)]
    scratch += [pltpu.VMEM((count, ROWS, 128), f32) for count in SCRATCH]
    center, edge, edge_dense = pl.pallas_call(
        model_center,
        out_shape=(shape(11, 16, 128), shape(COUNT, ROWS, 128), shape(7, 4, ROWS, 128)),
        scratch_shapes=scratch,
        compiler_params=limit,
        cost_estimate=hide,
        name="model_center",
    )(own, row_far, row_near)
    return pl.pallas_call(
        model_edge,
        out_shape=(shape(*tx.shape), shape(*ty.shape), shape(*tz.shape)),
        scratch_shapes=scratch,
        compiler_params=limit,
        name="model_edge",
    )(col_far, col_near, edge, edge_dense, center)


def solution(mesh):
    cells = P(None, "gx", "gy")
    in_specs = (cells,) * 7 + (
        P("gx", "gy", None),
        P("gx", "gy", None),
        P(None, "gx", "gy", None),
        P(None, None, "gx", "gy", None),
    )
    return jax.shard_map(
        on_device, mesh=mesh, in_specs=in_specs, out_specs=(cells,) * 3, check_vma=False
    )
```

```python
import jax
import jax.numpy as jnp
from jax import lax
from jax.experimental import pallas as pl
from jax.experimental.pallas import tpu as pltpu
from jax.sharding import PartitionSpec as P

time_step = 0.05

GROUPS = {"p": (0, 4), "s": (4, 4), "tx": (8, 4), "ty": (12, 4), "tz": (16, 3), "pv": (19, 4), "up": (23, 4)}
ORDER = ("p", "s", "tx", "ty", "tz", "pv", "up")
COUNT = 27
SLOT = 10
SLOTS = {"p": (0, 10), "tx": (10, 9), "ty": (19, 9), "tz": (28, 9), "pv": (37, 9), "s": (46, 7), "up": (53, 6)}
PACKED = 4
ROWS = 56
HALO = 2 * SLOT
LATE = 99


FIELDS = 11


def pack_rows(*refs):
    p, s, tx, ty, tz, pv, up, cell, rate, plan, observed = refs[:FIELDS]
    own, far, near, upi, cells, rates, plans, seen, sems = refs[FIELDS:]
    targets = [own.at[pl.ds(*GROUPS[name])] for name in ORDER[:6]] + [upi, cells, rates, plans, seen]
    copies = [
        pltpu.make_async_copy(source, target, sems.at[k])
        for k, (source, target) in enumerate(zip(refs[:FIELDS], targets))
    ]
    for copy in copies:
        copy.start()
    for copy in copies:
        copy.wait()
    first = GROUPS["up"][0]
    for layer in range(4):
        own[first + layer] = upi[layer].astype(jnp.float32)
    own[COUNT] = jnp.zeros((16, 128), jnp.float32)
    own[COUNT, 0:1, 0:64] = cells[0].astype(jnp.float32)
    own[COUNT, 1:2, 0:64] = rates[0]
    for n in range(2):
        own[COUNT, 2 + n : 3 + n, 0:64] = plans[n, 0].astype(jnp.float32)
        for k in range(2):
            row = 4 + 2 * n + k
            own[COUNT, row : row + 1, 0:64] = seen[n, k, 0]
    odd = lax.axis_index("gx") & 1
    for g in range(COUNT):
        far[g] = own[g, pl.ds(pl.multiple_of(8 * odd, 8), 8), :]
        near[g] = own[g, pl.ds(pl.multiple_of(8 - 8 * odd, 8), 8), :]
    base = {name: GROUPS[name][0] for name in ORDER}

    blank = jnp.zeros((1, 128), jnp.float32)

    def gathered(*places):
        rows = []
        for layer in (0, 2, 1, 3):
            for name, row in places:
                there = layer < GROUPS[name][1]
                rows.append(own[base[name] + layer, row : row + 1, :] if there else blank)
        return jnp.concatenate([rows[k] for k in (0, 2, 1, 3, 4, 6, 5, 7)], axis=0)

    for_next = [gathered(("p", 7), ("tx", 7))]
    for_next += [jnp.zeros((8, 128), jnp.float32)] * 2
    for_prev = [
        gathered(("p", 8), ("tx", 8)),
        gathered(("ty", 8), ("tz", 8)),
        gathered(("pv", 8), ("p", 9)),
    ]
    for k in range(3):
        far[COUNT + k] = jnp.where(odd == 1, for_next[k], for_prev[k])
        near[COUNT + k] = jnp.where(odd == 1, for_prev[k], for_next[k])
    far[COUNT + 3] = own[COUNT, 0:8, :]
    near[COUNT + 3] = own[COUNT, 0:8, :]


def lanes():
    return lax.broadcasted_iota(jnp.int32, (8, 128), 1)


def in_slot(lane, start, ends, width):
    return ((lane - start - ends * (2 * SLOT - width)) & 63) < width


def sorted_ends(axis, far, near):
    odd = (lax.axis_index(axis) & 1) == 1

    def before(g):
        return jnp.where(odd, near[g], far[g])

    def after(g):
        return jnp.where(odd, far[g], near[g])

    return before, after


def pack_pairs(block, far, near, at):
    odd = lax.axis_index("gy") & 1
    lane = lanes()
    zero = jnp.zeros((8, 128), jnp.float32)
    for pair in range(2):
        ones, twos = {}, {}
        for name in SLOTS:
            first, layers = GROUPS[name]
            ones[name] = block(first + 2 * pair)
            there = 2 * pair + 1 < layers
            twos[name] = pltpu.roll(block(first + 2 * pair + 1), 64, 1) if there else zero
        for out, ends in ((far, odd), (near, 1 - odd)):
            straight = ((lane >> 6) ^ ends) == 0
            part = zero
            for name, (start, width) in SLOTS.items():
                both = jnp.where(straight, ones[name], twos[name])
                both = pltpu.roll(both, start + 2 * SLOT * ends, 1)
                part = jnp.where(in_slot(lane, start, ends, width), both, part)
            out[at + pair] = part


def extra_pair(one, two):
    row = lax.broadcasted_iota(jnp.int32, (8, 128), 0)
    return jnp.where(row < 4, one, pltpu.roll(two, 4, 0)), jnp.where(row < 4, pltpu.roll(one, 4, 0), two)


def pack_own(own, far, near):
    for tile in range(2):
        rows = slice(8 * tile, 8 * tile + 8)
        pack_pairs(lambda g: own[g, rows, :], far, near, 2 * tile)


def pack_cols(own, own_far, own_near, row_far, row_near, far, near):
    low, high = sorted_ends("gx", row_far, row_near)
    for out, part in ((far, own_far), (near, own_near)):
        for at in range(PACKED):
            out[at] = part[at]
    pack_pairs(low, far, near, PACKED)
    pack_pairs(high, far, near, PACKED + 2)
    odd = lax.axis_index("gy") & 1
    lane = lanes()
    both = jnp.where(lane < 64, own[COUNT, 0:8, :], pltpu.roll(low(COUNT + 3), 64, 1))
    extras = extra_pair(low(COUNT), high(COUNT)) + extra_pair(high(COUNT + 1), high(COUNT + 2))
    for out, ends in ((far, odd), (near, 1 - odd)):
        out[2 * PACKED] = both
        part = high(COUNT + 3)
        for k, value in enumerate(extras):
            start = 64 + SLOT * k
            mask = ((lane - start - SLOT * ends) & 127) < SLOT
            part = jnp.where(mask, pltpu.roll(value, start + 2 * SLOT * ends, 1), part)
        out[2 * PACKED + 1] = part


def split3(value):
    hi = value.astype(jnp.bfloat16).astype(jnp.float32)
    rest = value - hi
    mid = rest.astype(jnp.bfloat16).astype(jnp.float32)
    return hi, mid, rest - mid


SRC0, SRC1, OP0, OS0, OP1, OS1, CNT = range(7)


def spread_wells(info, base, to_spot, write):
    width = info.shape[1]
    cell = info[0:1].astype(jnp.int32)
    layer = lax.shift_right_logical(cell, 11)
    place = (lax.shift_right_logical(cell, 7) & 15) + base
    target = jnp.where(place >= 8, layer * 40 + place - 8, -1)
    spot = to_spot(cell & 127)
    hit = lax.broadcasted_iota(jnp.int32, (160, width), 0) == target
    hit = jnp.where(hit, 1.0, 0.0).astype(jnp.bfloat16)
    lane = lax.broadcasted_iota(jnp.int32, (128, width), 0)
    to_lane = jnp.where(lane == spot, 1.0, 0.0).astype(jnp.bfloat16)
    rate = info[1:2] * 0.5
    values = [rate * info[2:3], rate * info[3:4]] + [info[k : k + 1] for k in range(4, 8)]
    for number, value in enumerate(values):
        total = None
        for part in split3(value):
            part = jnp.broadcast_to(part, (16, width)).astype(jnp.bfloat16)
            left = hit * jnp.concatenate([part] * 10, axis=0)
            term = dot(left, to_lane)
            total = term if total is None else total + term
        write(number, total)
    write(CNT, dot(hit, to_lane))


def dot(left, right):
    return lax.dot_general(left, right, (((1,), (1,)), ((), ())), preferred_element_type=jnp.float32)


def list_block(info):
    return lax.shift_right_logical(lax.broadcasted_iota(jnp.int32, (1, info.shape[1]), 1), 6)


SCRATCH = (4,) * 11 + (11,) * 4 + (4,) * 9


def simulate(fld, dense, upi, scratch, emit_x, emit_y, emit_z, tile_done=None):
    (rcp, tym, q0, p1, q1, p2, f0, d0, s1, f1, d1, fup0, fup1, dp1, dp2,
     sig2, psi2, psi1, mup2, muq1, mup1, muq0, flux, rest) = scratch
    PB, SB, XB, YB, ZB, VB = (GROUPS[name][0] for name in ORDER[:6])

    def here(ref, k, t):
        return ref[k, 8 * t : 8 * t + 8, :]

    def down(ref, k, t):
        return ref[k, 8 * t + 1 : 8 * t + 9, :]

    def above(ref, k, t):
        return ref[k, 8 * t - 1 : 8 * t + 7, :]

    def put(ref, k, t, value):
        ref[k, 8 * t : 8 * t + 8, :] = value

    def right(value):
        return pltpu.roll(value, 127, 1)

    def left(value):
        return pltpu.roll(value, 1, 1)

    for k in range(4):
        for t in range(1, 6):
            beyond = right(here(fld, VB + k, t))
            put(fld, YB + k, t, jnp.where(beyond == 0.0, 0.0, here(fld, YB + k, t)))
        last = slice(31, 32)
        fld[XB + k, last, :] = jnp.where(fld[VB + k, 32:33, :] == 0.0, 0.0, fld[XB + k, last, :])
    for t in range(1, 6):
        for k in range(4):
            volume = here(fld, VB + k, t)
            volume = jnp.where(volume == 0.0, 1.0, volume)
            put(fld, VB + k, t, volume)
            west = left(here(fld, YB + k, t))
            put(tym, k, t, west)
            total = volume + (here(fld, XB + k, t) + above(fld, XB + k, t)) + (here(fld, YB + k, t) + west)
            if k < 3:
                total = total + here(fld, ZB + k, t)
            if k > 0:
                total = total + here(fld, ZB + k - 1, t)
            put(rcp, k, t, 1.0 / total)

    def neighbours(ref, base, k, t):
        value = here(ref, base + k, t)
        total = here(fld, XB + k, t) * down(ref, base + k, t) + above(fld, XB + k, t) * above(ref, base + k, t)
        total = total + (here(fld, YB + k, t) * right(value) + here(tym, k, t) * left(value))
        if k < 3:
            total = total + here(fld, ZB + k, t) * here(ref, base + k + 1, t)
        if k > 0:
            total = total + here(fld, ZB + k - 1, t) * here(ref, base + k - 1, t)
        return total

    def relax(out, ref, base, old, old_base, source, tiles):
        for t in tiles:
            for k in range(4):
                total = here(fld, VB + k, t) * here(old, old_base + k, t) + here(dense.at[source], k, t)
                put(out, k, t, (total + neighbours(ref, base, k, t)) * here(rcp, k, t))

    def put_mobility(value, k, t, mobile, slope):
        rest_of = 1.0 - value
        wetted = value * value
        inverse = 1.0 / (wetted + 0.5 * rest_of * rest_of)
        put(mobile, k, t, wetted * inverse)
        put(slope, k, t, value * rest_of * (inverse * inverse))

    def bit(k, t, number):
        return (here(upi, k, t) & (1 << number)) != 0

    def transport(pressure, sat, sat_base, mobile, n, fup, dp, finish):
        for t in range(1, 5):
            below = None
            for k in range(4):
                mob = here(mobile, k, t)
                pres = here(pressure, k, t)
                drop_x = pres - down(pressure, k, t)
                drop_y = pres - right(pres)
                up_x = jnp.where(bit(k, t, 3 * n), mob, down(mobile, k, t))
                up_y = jnp.where(bit(k, t, 3 * n + 1), mob, right(mob))
                put(fup, k, t, up_x)
                put(fup, 4 + k, t, up_y)
                put(dp, k, t, drop_x)
                put(dp, 4 + k, t, drop_y)
                flux_x = here(fld, XB + k, t) * up_x * drop_x
                flux_y = here(fld, YB + k, t) * up_y * drop_y
                put(flux, k, t, flux_x)
                net = (flux_x - above(flux, k, t)) + (flux_y - left(flux_y))
                if k > 0:
                    net = net - below
                if k < 3:
                    drop_z = pres - here(pressure, k + 1, t)
                    up_z = jnp.where(bit(k, t, 3 * n + 2), mob, here(mobile, k + 1, t))
                    put(fup, 8 + k, t, up_z)
                    put(dp, 8 + k, t, drop_z)
                    below = here(fld, ZB + k, t) * up_z * drop_z
                    net = net + below
                finish(here(sat, sat_base + k, t) - time_step * net / here(fld, VB + k, t), k, t)

    tiles = range(1, 5)
    relax(q0, fld, PB, fld, PB, SRC0, range(1, 6))
    relax(p1, q0, 0, fld, PB, SRC0, tiles)
    for t in tiles:
        for k in range(4):
            put_mobility(here(fld, SB + k, t), k, t, f0, d0)

    def finish_first(moved, k, t):
        put(s1, k, t, moved)
        put_mobility(moved, k, t, f1, d1)

    transport(p1, fld, SB, f0, 0, fup0, dp1, finish_first)
    relax(q1, p1, 0, p1, 0, SRC1, tiles)
    relax(p2, q1, 0, p1, 0, SRC1, tiles)

    def finish_second(moved, k, t):
        miss = here(dense.at[CNT], k, t) * moved - here(dense.at[OS1], k, t)
        put(sig2, k, t, miss)
        put(psi2, k, t, time_step * miss / here(fld, VB + k, t))

    transport(p2, s1, 0, f1, 1, fup1, dp2, finish_second)

    for t in tiles:
        below_h = below_r = None
        for k in range(4):
            psi = here(psi2, k, t)
            phi_x = (down(psi2, k, t) - psi) * here(fld, XB + k, t)
            phi_y = (right(psi) - psi) * here(fld, YB + k, t)
            h_x = phi_x * here(fup1, k, t)
            h_y = phi_y * here(fup1, 4 + k, t)
            k_x = phi_x * here(dp2, k, t)
            k_y = phi_y * here(dp2, 4 + k, t)
            s_x = jnp.where(bit(k, t, 3), k_x, 0.0)
            s_y = jnp.where(bit(k, t, 4), k_y, 0.0)
            put(flux, k, t, h_x)
            put(rest, k, t, k_x - s_x)
            press = (h_x - above(flux, k, t)) + (h_y - left(h_y))
            satur = (s_x + above(rest, k, t)) + (s_y + left(k_y - s_y))
            if k > 0:
                press = press - below_h
                satur = satur + below_r
            if k < 3:
                phi_z = (here(psi2, k + 1, t) - psi) * here(fld, ZB + k, t)
                below_h = phi_z * here(fup1, 8 + k, t)
                k_z = phi_z * here(dp2, 8 + k, t)
                s_z = jnp.where(bit(k, t, 5), k_z, 0.0)
                below_r = k_z - s_z
                press = press + below_h
                satur = satur + s_z
            count = here(dense.at[CNT], k, t)
            press = press + (count * here(p2, k, t) - here(dense.at[OP1], k, t))
            put(mup2, k, t, press * here(rcp, k, t))
            sigma = here(sig2, k, t) + satur * here(d1, k, t)
            sigma = sigma + (count * here(s1, k, t) - here(dense.at[OS0], k, t))
            put(psi1, k, t, time_step * sigma / here(fld, VB + k, t))

    for t in tiles:
        for k in range(4):
            put(muq1, k, t, neighbours(mup2, 0, k, t) * here(rcp, k, t))

    for t in tiles:
        below_h = None
        for k in range(4):
            psi = here(psi1, k, t)
            h_x = (down(psi1, k, t) - psi) * here(fld, XB + k, t) * here(fup0, k, t)
            h_y = (right(psi) - psi) * here(fld, YB + k, t) * here(fup0, 4 + k, t)
            put(flux, k, t, h_x)
            press = (h_x - above(flux, k, t)) + (h_y - left(h_y))
            if k > 0:
                press = press - below_h
            if k < 3:
                below_h = (here(psi1, k + 1, t) - psi) * here(fld, ZB + k, t) * here(fup0, 8 + k, t)
                press = press + below_h
            count = here(dense.at[CNT], k, t)
            press = press + (count * here(p1, k, t) - here(dense.at[OP0], k, t))
            press = press + here(fld, VB + k, t) * (here(mup2, k, t) + here(muq1, k, t))
            press = press + neighbours(muq1, 0, k, t)
            put(mup1, k, t, press * here(rcp, k, t))

    for t in range(2, 5):
        for k in range(4):
            put(muq0, k, t, neighbours(mup1, 0, k, t) * here(rcp, k, t))

    stages = (
        (mup2, q1, 0, p2, 0),
        (muq1, p1, 0, q1, 0),
        (mup1, q0, 0, p1, 0),
        (muq0, fld, PB, q0, 0),
    )
    for t in range(2, 4):
        for k in range(4):
            sum_x = sum_y = sum_z = 0.0
            for psi, fup, dp in ((psi2, fup1, dp2), (psi1, fup0, dp1)):
                mid = here(psi, k, t)
                sum_x = sum_x + (down(psi, k, t) - mid) * here(fup, k, t) * here(dp, k, t)
                sum_y = sum_y + (right(mid) - mid) * here(fup, 4 + k, t) * here(dp, 4 + k, t)
                if k < 3:
                    sum_z = sum_z + (here(psi, k + 1, t) - mid) * here(fup, 8 + k, t) * here(dp, 8 + k, t)
            for mu, value, base, out, out_base in stages:
                mu_c, v_c, o_c = here(mu, k, t), here(value, base + k, t), here(out, out_base + k, t)
                mu_d, v_d, o_d = down(mu, k, t), down(value, base + k, t), down(out, out_base + k, t)
                sum_x = sum_x + (mu_c * (v_d - o_c) + mu_d * (v_c - o_d))
                sum_y = sum_y + (mu_c * (right(v_c) - o_c) + right(mu_c) * (v_c - right(o_c)))
                if k < 3:
                    mu_u = here(mu, k + 1, t)
                    v_u = here(value, base + k + 1, t)
                    o_u = here(out, out_base + k + 1, t)
                    sum_z = sum_z + (mu_c * (v_u - o_c) + mu_u * (v_c - o_u))
            emit_x(k, t, jnp.where(here(fld, XB + k, t) == 0.0, 0.0, sum_x))
            emit_y(k, t, jnp.where(here(fld, YB + k, t) == 0.0, 0.0, sum_y))
            if k < 3:
                emit_z(k, t, sum_z)
        if tile_done is not None:
            tile_done(t)


PLACES = (
    (("p", 7), ("tx", 7)),
    (("p", 40), ("tx", 40)),
    (("ty", 40), ("tz", 40)),
    (("pv", 40), ("p", 41)),
)


def put_beyond(fld, value, places):
    for block, (name, row) in enumerate(places):
        first, layers = GROUPS[name]
        for layer in range(layers):
            k = 4 * (layer & 1) + 2 * block + layer // 2
            fld[first + layer, row : row + 1, :] = value[k : k + 1]


def model_center(own, row_far, row_near, grads, edge, edge_dense, fld, dense, upi, *scratch):
    low, high = sorted_ends("gx", row_far, row_near)
    lane = lanes()

    early = lane < LATE

    def edge_of(value):
        return jnp.where(early, pltpu.roll(value, HALO, 1), value)

    for g in range(COUNT):
        for k, block in enumerate((low(g), own[g, 0:8, :], own[g, 8:16, :], high(g))):
            rows = slice(8 + 8 * k, 16 + 8 * k)
            fld[g, rows, :] = block
            edge[g, rows, :] = edge_of(block)
            if g >= GROUPS["up"][0]:
                upi[g - GROUPS["up"][0], rows, :] = block.astype(jnp.int32)
    for value, places in zip([low(COUNT)] + [high(COUNT + k) for k in range(3)], PLACES):
        for out, rows in ((fld, value), (edge, edge_of(value))):
            put_beyond(out, rows, places)

    info = jnp.concatenate(
        [own[COUNT, 0:8, 0:64], low(COUNT + 3)[:, 0:64], high(COUNT + 3)[:, 0:64]], axis=1
    )
    block = list_block(info)
    base = jnp.where(block == 0, 16, jnp.where(block == 1, 0, 32))

    def write_center(number, total):
        for k in range(4):
            dense[number, k, 8:48, :] = total[40 * k : 40 * k + 40]

    def write_edge(number, total):
        for k in range(4):
            edge_dense[number, k, 8:48, :] = total[40 * k : 40 * k + 40]

    def edge_lane(col):
        return jnp.where(col < LATE - HALO, col + HALO, jnp.where(col >= LATE, col, -1))

    spread_wells(info, base, lambda col: col, write_center)
    spread_wells(info, base, edge_lane, write_edge)

    def emit(first):
        def write(k, t, value):
            grads[first + k, 8 * t - 16 : 8 * t - 8, :] = value

        return write

    simulate(fld, dense, upi, scratch, emit(0), emit(4), emit(8))


def model_edge(
    col_far, col_near, edge, edge_dense, center, grad_x, grad_y, grad_z, first_rows, last_rows, sems, fld, dense, upi,
    *scratch
):
    before, after = sorted_ends("gy", col_far, col_near)
    odd = lax.axis_index("gy") & 1
    lane = lanes()
    beside = lane < HALO
    for name, (start, width) in SLOTS.items():
        far_cols = in_slot(lane, start, 1 - odd, width)
        first, layers = GROUPS[name]
        for layer in range(layers):
            for k, at in enumerate((PACKED, 0, 2, PACKED + 2)):
                rows = slice(8 + 8 * k, 16 + 8 * k)
                both = jnp.where(far_cols, col_far[at + layer // 2], col_near[at + layer // 2])
                both = pltpu.roll(both, (64 * (layer & 1) - start) % 128, 1)
                block = jnp.where(beside, both, edge[first + layer, rows, :])
                if name == "up":
                    upi[layer, rows, :] = block.astype(jnp.int32)
                else:
                    fld[first + layer, rows, :] = block
    for number, places in enumerate(PLACES):
        for half in range(2):
            start = 64 + SLOT * (2 * (number // 2) + half)
            mask = ((lane - start - SLOT * (1 - odd)) & 127) < SLOT
            both = jnp.where(mask, col_far[2 * PACKED + 1], col_near[2 * PACKED + 1])
            value = pltpu.roll(both, 128 - start, 1)
            for block, (name, row) in enumerate(places):
                for pair in range(2):
                    layer = 2 * pair + half
                    if layer < GROUPS[name][1]:
                        k = 4 * (number & 1) + 2 * block + pair
                        at = (GROUPS[name][0] + layer, slice(row, row + 1), slice(None))
                        fld[at] = jnp.where(beside[0:1], value[k : k + 1], edge[at])
    first, second = 2 * PACKED, 2 * PACKED + 1
    own_lists = [before(first)[:, 0:64], after(first)[:, 0:64]]
    low_lists = [before(first)[:, 64:128], after(first)[:, 64:128]]
    high_lists = [before(second)[:, 0:64], after(second)[:, 0:64]]
    info = jnp.concatenate(own_lists + low_lists + high_lists, axis=1)
    block = list_block(info)
    base = jnp.where(block < 2, 16, jnp.where(block < 4, 0, 32))
    ahead = (block & 1) == 1

    def beside_lane(col):
        last = jnp.where(col >= 128 - SLOT, col - 128 + 2 * SLOT, -1)
        return jnp.where(ahead, jnp.where(col < SLOT, col, -1), last)

    def write_beside(number, total):
        for k in range(4):
            dense[number, k, 8:48, :] = total[40 * k : 40 * k + 40] + edge_dense[number, k, 8:48, :]

    spread_wells(info, base, beside_lane, write_beside)

    def emit(group):
        def write(k, t, value):
            rows = slice(8 * t - 16, 8 * t - 8)
            value = jnp.where(lane < 64, pltpu.roll(value, 128 - HALO, 1), value)
            inner = (lane >= SLOT - 1) & (lane < 128 - SLOT)
            (first_rows, last_rows)[t - 2][group + k] = jnp.where(inner, center[group + k, rows, :], value)

        return write

    def send(t):
        copies = []
        for k, (out, group) in enumerate(((grad_x, 0), (grad_y, 4), (grad_z, 8))):
            source = (first_rows, last_rows)[t - 2].at[pl.ds(group, out.shape[0])]
            target = out.at[:, pl.ds(8 * t - 16, 8), :]
            copies.append(pltpu.make_async_copy(source, target, sems.at[3 * (t - 2) + k]))
            copies[-1].start()
        return copies

    copies = []
    simulate(fld, dense, upi, scratch, emit(0), emit(4), emit(8), lambda t: copies.extend(send(t)))
    for copy in copies:
        copy.wait()


def swapped(value, axis, first):
    count = lax.axis_size(axis)
    pairs = []
    for i in range(first, count - 1, 2):
        pairs += [(i, i + 1), (i + 1, i)]
    return lax.ppermute(value, axis, pairs)


def on_device(p, s, tx, ty, tz, pv, up, cell, rate, plan, observed):
    f32 = jnp.float32

    def shape(*dims):
        return jax.ShapeDtypeStruct(dims, f32)

    limit = pltpu.CompilerParams(vmem_limit_bytes=24 * 1024 * 1024)
    inputs = (p, s, tx, ty, tz, pv, up, cell, rate, plan, observed)
    inputs = [pltpu.with_memory_space_constraint(value, pltpu.HBM) for value in inputs]
    strip = shape(COUNT + 4, 8, 128)
    own, far, near = pl.pallas_call(
        pack_rows,
        out_shape=(shape(COUNT + 1, 16, 128), strip, strip),
        in_specs=[pl.BlockSpec(memory_space=pltpu.HBM)] * len(inputs),
        scratch_shapes=[pltpu.VMEM(value.shape, value.dtype) for value in inputs[6:]]
        + [pltpu.SemaphoreType.DMA((len(inputs),))],
        compiler_params=limit,
        name="pack_rows",
    )(*inputs)
    row_far = swapped(far, "gx", 1)
    row_near = swapped(near, "gx", 0)
    hide = pl.CostEstimate(flops=10**11, bytes_accessed=1 << 28, transcendentals=0)
    strip = shape(PACKED, 8, 128)
    own_far, own_near = pl.pallas_call(
        pack_own,
        out_shape=(strip, strip),
        compiler_params=limit,
        cost_estimate=hide,
        name="pack_own",
    )(own)
    strip = shape(2 * PACKED + 2, 8, 128)
    far, near = pl.pallas_call(
        pack_cols,
        out_shape=(strip, strip),
        compiler_params=limit,
        name="pack_cols",
    )(own, own_far, own_near, row_far, row_near)
    col_far = swapped(far, "gy", 1)
    col_near = swapped(near, "gy", 0)
    scratch = [pltpu.VMEM((COUNT, ROWS, 128), f32), pltpu.VMEM((7, 4, ROWS, 128), f32)]
    scratch += [pltpu.VMEM((4, ROWS, 128), jnp.int32)]
    scratch += [pltpu.VMEM((count, ROWS, 128), f32) for count in SCRATCH]
    center, edge, edge_dense = pl.pallas_call(
        model_center,
        out_shape=(shape(11, 16, 128), shape(COUNT, ROWS, 128), shape(7, 4, ROWS, 128)),
        scratch_shapes=scratch,
        compiler_params=limit,
        cost_estimate=hide,
        name="model_center",
    )(own, row_far, row_near)
    return pl.pallas_call(
        model_edge,
        out_shape=(shape(*tx.shape), shape(*ty.shape), shape(*tz.shape)),
        out_specs=(pl.BlockSpec(memory_space=pltpu.HBM),) * 3,
        scratch_shapes=[pltpu.VMEM((11, 8, 128), f32)] * 2 + [pltpu.SemaphoreType.DMA((6,))] + scratch,
        compiler_params=limit,
        name="model_edge",
    )(col_far, col_near, edge, edge_dense, center)


def solution(mesh):
    cells = P(None, "gx", "gy")
    in_specs = (cells,) * 7 + (
        P("gx", "gy", None),
        P("gx", "gy", None),
        P(None, "gx", "gy", None),
        P(None, None, "gx", "gy", None),
    )
    return jax.shard_map(
        on_device, mesh=mesh, in_specs=in_specs, out_specs=(cells,) * 3, check_vma=False
    )
```

```python
import jax
import jax.numpy as jnp
from jax import lax
from jax.experimental import pallas as pl
from jax.experimental.pallas import tpu as pltpu
from jax.sharding import PartitionSpec as P

time_step = 0.05

GROUPS = {"p": (0, 4), "s": (4, 4), "tx": (8, 4), "ty": (12, 4), "tz": (16, 3), "pv": (19, 4), "up": (23, 4)}
ORDER = ("p", "s", "tx", "ty", "tz", "pv", "up")
COUNT = 27
SLOT = 10
SLOTS = {"p": (0, 10), "tx": (10, 9), "ty": (19, 9), "tz": (28, 9), "pv": (37, 9), "s": (46, 7), "up": (53, 6)}
PACKED = 4
ROWS = 56
HALO = 2 * SLOT
LATE = 99


FIELDS = 11


def pack_rows(*refs):
    p, s, tx, ty, tz, pv, up, cell, rate, plan, observed = refs[:FIELDS]
    own, far, near, upi, cells, rates, plans, seen, sems = refs[FIELDS:]
    targets = [own.at[pl.ds(*GROUPS[name])] for name in ORDER[:6]] + [upi, cells, rates, plans, seen]
    copies = [
        pltpu.make_async_copy(source, target, sems.at[k])
        for k, (source, target) in enumerate(zip(refs[:FIELDS], targets))
    ]
    for copy in copies:
        copy.start()
    odd = lax.axis_index("gx") & 1
    for name, copy in zip(ORDER, copies):
        copy.wait()
        first, layers = GROUPS[name]
        for layer in range(layers):
            g = first + layer
            if name == "up":
                own[g] = upi[layer].astype(jnp.float32)
            far[g] = own[g, pl.ds(pl.multiple_of(8 * odd, 8), 8), :]
            near[g] = own[g, pl.ds(pl.multiple_of(8 - 8 * odd, 8), 8), :]
    for copy in copies[len(ORDER) :]:
        copy.wait()
    own[COUNT] = jnp.zeros((16, 128), jnp.float32)
    own[COUNT, 0:1, 0:64] = cells[0].astype(jnp.float32)
    own[COUNT, 1:2, 0:64] = rates[0]
    for n in range(2):
        own[COUNT, 2 + n : 3 + n, 0:64] = plans[n, 0].astype(jnp.float32)
        for k in range(2):
            row = 4 + 2 * n + k
            own[COUNT, row : row + 1, 0:64] = seen[n, k, 0]
    base = {name: GROUPS[name][0] for name in ORDER}

    blank = jnp.zeros((1, 128), jnp.float32)

    def gathered(*places):
        rows = []
        for layer in (0, 2, 1, 3):
            for name, row in places:
                there = layer < GROUPS[name][1]
                rows.append(own[base[name] + layer, row : row + 1, :] if there else blank)
        return jnp.concatenate([rows[k] for k in (0, 2, 1, 3, 4, 6, 5, 7)], axis=0)

    for_next = [gathered(("p", 7), ("tx", 7))]
    for_next += [jnp.zeros((8, 128), jnp.float32)] * 2
    for_prev = [
        gathered(("p", 8), ("tx", 8)),
        gathered(("ty", 8), ("tz", 8)),
        gathered(("pv", 8), ("p", 9)),
    ]
    for k in range(3):
        far[COUNT + k] = jnp.where(odd == 1, for_next[k], for_prev[k])
        near[COUNT + k] = jnp.where(odd == 1, for_prev[k], for_next[k])
    far[COUNT + 3] = own[COUNT, 0:8, :]
    near[COUNT + 3] = own[COUNT, 0:8, :]


def lanes():
    return lax.broadcasted_iota(jnp.int32, (8, 128), 1)


def in_slot(lane, start, ends, width):
    return ((lane - start - ends * (2 * SLOT - width)) & 63) < width


def sorted_ends(axis, far, near):
    odd = (lax.axis_index(axis) & 1) == 1

    def before(g):
        return jnp.where(odd, near[g], far[g])

    def after(g):
        return jnp.where(odd, far[g], near[g])

    return before, after


def pack_pairs(block, far, near, at):
    odd = lax.axis_index("gy") & 1
    lane = lanes()
    zero = jnp.zeros((8, 128), jnp.float32)
    for pair in range(2):
        ones, twos = {}, {}
        for name in SLOTS:
            first, layers = GROUPS[name]
            ones[name] = block(first + 2 * pair)
            there = 2 * pair + 1 < layers
            twos[name] = pltpu.roll(block(first + 2 * pair + 1), 64, 1) if there else zero
        for out, ends in ((far, odd), (near, 1 - odd)):
            straight = ((lane >> 6) ^ ends) == 0
            part = zero
            for name, (start, width) in SLOTS.items():
                both = jnp.where(straight, ones[name], twos[name])
                both = pltpu.roll(both, start + 2 * SLOT * ends, 1)
                part = jnp.where(in_slot(lane, start, ends, width), both, part)
            out[at + pair] = part


def extra_pair(one, two):
    row = lax.broadcasted_iota(jnp.int32, (8, 128), 0)
    return jnp.where(row < 4, one, pltpu.roll(two, 4, 0)), jnp.where(row < 4, pltpu.roll(one, 4, 0), two)


def pack_own(own, far, near):
    for tile in range(2):
        rows = slice(8 * tile, 8 * tile + 8)
        pack_pairs(lambda g: own[g, rows, :], far, near, 2 * tile)


def pack_cols(own, own_far, own_near, row_far, row_near, near, far):
    low, high = sorted_ends("gx", row_far, row_near)
    for out, part in ((far, own_far), (near, own_near)):
        for at in range(PACKED):
            out[at] = part[at]
    pack_pairs(low, far, near, PACKED)
    pack_pairs(high, far, near, PACKED + 2)
    odd = lax.axis_index("gy") & 1
    lane = lanes()
    both = jnp.where(lane < 64, own[COUNT, 0:8, :], pltpu.roll(low(COUNT + 3), 64, 1))
    extras = extra_pair(low(COUNT), high(COUNT)) + extra_pair(high(COUNT + 1), high(COUNT + 2))
    for out, ends in ((far, odd), (near, 1 - odd)):
        out[2 * PACKED] = both
        part = high(COUNT + 3)
        for k, value in enumerate(extras):
            start = 64 + SLOT * k
            mask = ((lane - start - SLOT * ends) & 127) < SLOT
            part = jnp.where(mask, pltpu.roll(value, start + 2 * SLOT * ends, 1), part)
        out[2 * PACKED + 1] = part


def split3(value):
    hi = value.astype(jnp.bfloat16).astype(jnp.float32)
    rest = value - hi
    mid = rest.astype(jnp.bfloat16).astype(jnp.float32)
    return hi, mid, rest - mid


SRC0, SRC1, OP0, OS0, OP1, OS1, CNT = range(7)


def spread_wells(info, base, rows_of, count, to_spot, write):
    width = info.shape[1]
    cell = info[0:1].astype(jnp.int32)
    layer = lax.shift_right_logical(cell, 11)
    place = (lax.shift_right_logical(cell, 7) & 15) + base
    target = jnp.where(place >= 8, rows_of(layer) + place - 8, -1)
    spot = to_spot(layer, cell & 127)
    hit = lax.broadcasted_iota(jnp.int32, (count, width), 0) == target
    hit = jnp.where(hit, 1.0, 0.0).astype(jnp.bfloat16)
    lane = lax.broadcasted_iota(jnp.int32, (128, width), 0)
    to_lane = jnp.where(lane == spot, 1.0, 0.0).astype(jnp.bfloat16)
    rate = info[1:2] * 0.5
    values = [rate * info[2:3], rate * info[3:4]] + [info[k : k + 1] for k in range(4, 8)]
    for number, value in enumerate(values):
        total = None
        for part in split3(value):
            part = jnp.broadcast_to(part, (16, width)).astype(jnp.bfloat16)
            left = hit * jnp.concatenate([part] * (count // 16), axis=0)
            term = dot(left, to_lane)
            total = term if total is None else total + term
        write(number, total)
    write(CNT, dot(hit, to_lane))


def dot(left, right):
    return lax.dot_general(left, right, (((1,), (1,)), ((), ())), preferred_element_type=jnp.float32)


def list_block(info):
    return lax.shift_right_logical(lax.broadcasted_iota(jnp.int32, (1, info.shape[1]), 1), 6)


SCRATCH = (4,) * 11 + (11,) * 4 + (4,) * 9


def simulate(fld, dense, upi, scratch, emit_x, emit_y, emit_z, tile_done=None):
    (rcp, tym, q0, p1, q1, p2, f0, d0, s1, f1, d1, fup0, fup1, dp1, dp2,
     sig2, psi2, psi1, mup2, muq1, mup1, muq0, flux, rest) = scratch
    PB, SB, XB, YB, ZB, VB = (GROUPS[name][0] for name in ORDER[:6])

    def here(ref, k, t):
        return ref[k, 8 * t : 8 * t + 8, :]

    def down(ref, k, t):
        return ref[k, 8 * t + 1 : 8 * t + 9, :]

    def above(ref, k, t):
        return ref[k, 8 * t - 1 : 8 * t + 7, :]

    def put(ref, k, t, value):
        ref[k, 8 * t : 8 * t + 8, :] = value

    def right(value):
        return pltpu.roll(value, 127, 1)

    def left(value):
        return pltpu.roll(value, 1, 1)

    for k in range(4):
        for t in range(1, 6):
            beyond = right(here(fld, VB + k, t))
            put(fld, YB + k, t, jnp.where(beyond == 0.0, 0.0, here(fld, YB + k, t)))
        last = slice(31, 32)
        fld[XB + k, last, :] = jnp.where(fld[VB + k, 32:33, :] == 0.0, 0.0, fld[XB + k, last, :])
    for t in range(1, 6):
        for k in range(4):
            volume = here(fld, VB + k, t)
            volume = jnp.where(volume == 0.0, 1.0, volume)
            put(fld, VB + k, t, volume)
            west = left(here(fld, YB + k, t))
            put(tym, k, t, west)
            total = volume + (here(fld, XB + k, t) + above(fld, XB + k, t)) + (here(fld, YB + k, t) + west)
            if k < 3:
                total = total + here(fld, ZB + k, t)
            if k > 0:
                total = total + here(fld, ZB + k - 1, t)
            put(rcp, k, t, 1.0 / total)

    def neighbours(ref, base, k, t):
        value = here(ref, base + k, t)
        total = here(fld, XB + k, t) * down(ref, base + k, t) + above(fld, XB + k, t) * above(ref, base + k, t)
        total = total + (here(fld, YB + k, t) * right(value) + here(tym, k, t) * left(value))
        if k < 3:
            total = total + here(fld, ZB + k, t) * here(ref, base + k + 1, t)
        if k > 0:
            total = total + here(fld, ZB + k - 1, t) * here(ref, base + k - 1, t)
        return total

    def relax(out, ref, base, old, old_base, source, tiles):
        for t in tiles:
            for k in range(4):
                total = here(fld, VB + k, t) * here(old, old_base + k, t) + here(dense.at[source], k, t)
                put(out, k, t, (total + neighbours(ref, base, k, t)) * here(rcp, k, t))

    def put_mobility(value, k, t, mobile, slope):
        rest_of = 1.0 - value
        wetted = value * value
        inverse = 1.0 / (wetted + 0.5 * rest_of * rest_of)
        put(mobile, k, t, wetted * inverse)
        put(slope, k, t, value * rest_of * (inverse * inverse))

    def bit(k, t, number):
        return (here(upi, k, t) & (1 << number)) != 0

    def transport(pressure, sat, sat_base, mobile, n, fup, dp, finish):
        for t in range(1, 5):
            below = None
            for k in range(4):
                mob = here(mobile, k, t)
                pres = here(pressure, k, t)
                drop_x = pres - down(pressure, k, t)
                drop_y = pres - right(pres)
                up_x = jnp.where(bit(k, t, 3 * n), mob, down(mobile, k, t))
                up_y = jnp.where(bit(k, t, 3 * n + 1), mob, right(mob))
                put(fup, k, t, up_x)
                put(fup, 4 + k, t, up_y)
                put(dp, k, t, drop_x)
                put(dp, 4 + k, t, drop_y)
                flux_x = here(fld, XB + k, t) * up_x * drop_x
                flux_y = here(fld, YB + k, t) * up_y * drop_y
                put(flux, k, t, flux_x)
                net = (flux_x - above(flux, k, t)) + (flux_y - left(flux_y))
                if k > 0:
                    net = net - below
                if k < 3:
                    drop_z = pres - here(pressure, k + 1, t)
                    up_z = jnp.where(bit(k, t, 3 * n + 2), mob, here(mobile, k + 1, t))
                    put(fup, 8 + k, t, up_z)
                    put(dp, 8 + k, t, drop_z)
                    below = here(fld, ZB + k, t) * up_z * drop_z
                    net = net + below
                finish(here(sat, sat_base + k, t) - time_step * net / here(fld, VB + k, t), k, t)

    tiles = range(1, 5)
    relax(q0, fld, PB, fld, PB, SRC0, range(1, 6))
    relax(p1, q0, 0, fld, PB, SRC0, tiles)
    for t in tiles:
        for k in range(4):
            put_mobility(here(fld, SB + k, t), k, t, f0, d0)

    def finish_first(moved, k, t):
        put(s1, k, t, moved)
        put_mobility(moved, k, t, f1, d1)

    transport(p1, fld, SB, f0, 0, fup0, dp1, finish_first)
    relax(q1, p1, 0, p1, 0, SRC1, tiles)
    relax(p2, q1, 0, p1, 0, SRC1, tiles)

    def finish_second(moved, k, t):
        miss = here(dense.at[CNT], k, t) * moved - here(dense.at[OS1], k, t)
        put(sig2, k, t, miss)
        put(psi2, k, t, time_step * miss / here(fld, VB + k, t))

    transport(p2, s1, 0, f1, 1, fup1, dp2, finish_second)

    for t in tiles:
        below_h = below_r = None
        for k in range(4):
            psi = here(psi2, k, t)
            phi_x = (down(psi2, k, t) - psi) * here(fld, XB + k, t)
            phi_y = (right(psi) - psi) * here(fld, YB + k, t)
            h_x = phi_x * here(fup1, k, t)
            h_y = phi_y * here(fup1, 4 + k, t)
            k_x = phi_x * here(dp2, k, t)
            k_y = phi_y * here(dp2, 4 + k, t)
            s_x = jnp.where(bit(k, t, 3), k_x, 0.0)
            s_y = jnp.where(bit(k, t, 4), k_y, 0.0)
            put(flux, k, t, h_x)
            put(rest, k, t, k_x - s_x)
            press = (h_x - above(flux, k, t)) + (h_y - left(h_y))
            satur = (s_x + above(rest, k, t)) + (s_y + left(k_y - s_y))
            if k > 0:
                press = press - below_h
                satur = satur + below_r
            if k < 3:
                phi_z = (here(psi2, k + 1, t) - psi) * here(fld, ZB + k, t)
                below_h = phi_z * here(fup1, 8 + k, t)
                k_z = phi_z * here(dp2, 8 + k, t)
                s_z = jnp.where(bit(k, t, 5), k_z, 0.0)
                below_r = k_z - s_z
                press = press + below_h
                satur = satur + s_z
            count = here(dense.at[CNT], k, t)
            press = press + (count * here(p2, k, t) - here(dense.at[OP1], k, t))
            put(mup2, k, t, press * here(rcp, k, t))
            sigma = here(sig2, k, t) + satur * here(d1, k, t)
            sigma = sigma + (count * here(s1, k, t) - here(dense.at[OS0], k, t))
            put(psi1, k, t, time_step * sigma / here(fld, VB + k, t))

    for t in tiles:
        for k in range(4):
            put(muq1, k, t, neighbours(mup2, 0, k, t) * here(rcp, k, t))

    for t in tiles:
        below_h = None
        for k in range(4):
            psi = here(psi1, k, t)
            h_x = (down(psi1, k, t) - psi) * here(fld, XB + k, t) * here(fup0, k, t)
            h_y = (right(psi) - psi) * here(fld, YB + k, t) * here(fup0, 4 + k, t)
            put(flux, k, t, h_x)
            press = (h_x - above(flux, k, t)) + (h_y - left(h_y))
            if k > 0:
                press = press - below_h
            if k < 3:
                below_h = (here(psi1, k + 1, t) - psi) * here(fld, ZB + k, t) * here(fup0, 8 + k, t)
                press = press + below_h
            count = here(dense.at[CNT], k, t)
            press = press + (count * here(p1, k, t) - here(dense.at[OP0], k, t))
            press = press + here(fld, VB + k, t) * (here(mup2, k, t) + here(muq1, k, t))
            press = press + neighbours(muq1, 0, k, t)
            put(mup1, k, t, press * here(rcp, k, t))

    for t in range(2, 5):
        for k in range(4):
            put(muq0, k, t, neighbours(mup1, 0, k, t) * here(rcp, k, t))

    stages = (
        (mup2, q1, 0, p2, 0),
        (muq1, p1, 0, q1, 0),
        (mup1, q0, 0, p1, 0),
        (muq0, fld, PB, q0, 0),
    )
    for t in range(2, 4):
        for k in range(4):
            sum_x = sum_y = sum_z = 0.0
            for psi, fup, dp in ((psi2, fup1, dp2), (psi1, fup0, dp1)):
                mid = here(psi, k, t)
                sum_x = sum_x + (down(psi, k, t) - mid) * here(fup, k, t) * here(dp, k, t)
                sum_y = sum_y + (right(mid) - mid) * here(fup, 4 + k, t) * here(dp, 4 + k, t)
                if k < 3:
                    sum_z = sum_z + (here(psi, k + 1, t) - mid) * here(fup, 8 + k, t) * here(dp, 8 + k, t)
            for mu, value, base, out, out_base in stages:
                mu_c, v_c, o_c = here(mu, k, t), here(value, base + k, t), here(out, out_base + k, t)
                mu_d, v_d, o_d = down(mu, k, t), down(value, base + k, t), down(out, out_base + k, t)
                sum_x = sum_x + (mu_c * (v_d - o_c) + mu_d * (v_c - o_d))
                sum_y = sum_y + (mu_c * (right(v_c) - o_c) + right(mu_c) * (v_c - right(o_c)))
                if k < 3:
                    mu_u = here(mu, k + 1, t)
                    v_u = here(value, base + k + 1, t)
                    o_u = here(out, out_base + k + 1, t)
                    sum_z = sum_z + (mu_c * (v_u - o_c) + mu_u * (v_c - o_u))
            emit_x(k, t, jnp.where(here(fld, XB + k, t) == 0.0, 0.0, sum_x))
            emit_y(k, t, jnp.where(here(fld, YB + k, t) == 0.0, 0.0, sum_y))
            if k < 3:
                emit_z(k, t, sum_z)
        if tile_done is not None:
            tile_done(t)


PLACES = (
    (("p", 7), ("tx", 7)),
    (("p", 40), ("tx", 40)),
    (("ty", 40), ("tz", 40)),
    (("pv", 40), ("p", 41)),
)


def put_beyond(fld, value, places):
    for block, (name, row) in enumerate(places):
        first, layers = GROUPS[name]
        for layer in range(layers):
            k = 4 * (layer & 1) + 2 * block + layer // 2
            fld[first + layer, row : row + 1, :] = value[k : k + 1]


def model_center(own, row_far, row_near, grads, edge, edge_dense, fld, dense, upi, *scratch):
    low, high = sorted_ends("gx", row_far, row_near)
    lane = lanes()

    early = lane < LATE

    def edge_of(value):
        return jnp.where(early, pltpu.roll(value, HALO, 1), value)

    for g in range(COUNT):
        for k, block in enumerate((low(g), own[g, 0:8, :], own[g, 8:16, :], high(g))):
            rows = slice(8 + 8 * k, 16 + 8 * k)
            fld[g, rows, :] = block
            edge[g, rows, :] = edge_of(block)
            if g >= GROUPS["up"][0]:
                upi[g - GROUPS["up"][0], rows, :] = block.astype(jnp.int32)
    for value, places in zip([low(COUNT)] + [high(COUNT + k) for k in range(3)], PLACES):
        for out, rows in ((fld, value), (edge, edge_of(value))):
            put_beyond(out, rows, places)

    info = jnp.concatenate(
        [own[COUNT, 0:8, 0:64], low(COUNT + 3)[:, 0:64], high(COUNT + 3)[:, 0:64]], axis=1
    )
    block = list_block(info)
    base = jnp.where(block == 0, 16, jnp.where(block == 1, 0, 32))

    def write_center(number, total):
        for k in range(4):
            dense[number, k, 8:48, :] = total[40 * k : 40 * k + 40]

    def write_edge(number, total):
        for k in range(4):
            edge_dense[number, k, 8:48, :] = total[40 * k : 40 * k + 40]

    def edge_lane(layer, col):
        return jnp.where(col < LATE - HALO, col + HALO, jnp.where(col >= LATE, col, -1))

    spread_wells(info, base, lambda layer: layer * 40, 160, lambda layer, col: col, write_center)
    spread_wells(info, base, lambda layer: layer * 40, 160, edge_lane, write_edge)

    def emit(first):
        def write(k, t, value):
            grads[first + k, 8 * t - 16 : 8 * t - 8, :] = value

        return write

    simulate(fld, dense, upi, scratch, emit(0), emit(4), emit(8))


def model_edge(
    col_near, col_far, edge, edge_dense, center, grad_x, grad_y, grad_z, first_rows, last_rows, sems, fld, dense, upi,
    *scratch
):
    before, after = sorted_ends("gy", col_far, col_near)
    odd = lax.axis_index("gy") & 1
    lane = lanes()
    beside = lane < HALO
    for name, (start, width) in SLOTS.items():
        far_cols = in_slot(lane, start, 1 - odd, width)
        first, layers = GROUPS[name]
        for layer in range(layers):
            for k, at in enumerate((PACKED, 0, 2, PACKED + 2)):
                rows = slice(8 + 8 * k, 16 + 8 * k)
                both = jnp.where(far_cols, col_far[at + layer // 2], col_near[at + layer // 2])
                both = pltpu.roll(both, (64 * (layer & 1) - start) % 128, 1)
                block = jnp.where(beside, both, edge[first + layer, rows, :])
                if name == "up":
                    upi[layer, rows, :] = block.astype(jnp.int32)
                else:
                    fld[first + layer, rows, :] = block
    for number, places in enumerate(PLACES):
        for half in range(2):
            start = 64 + SLOT * (2 * (number // 2) + half)
            mask = ((lane - start - SLOT * (1 - odd)) & 127) < SLOT
            both = jnp.where(mask, col_far[2 * PACKED + 1], col_near[2 * PACKED + 1])
            value = pltpu.roll(both, 128 - start, 1)
            for block, (name, row) in enumerate(places):
                for pair in range(2):
                    layer = 2 * pair + half
                    if layer < GROUPS[name][1]:
                        k = 4 * (number & 1) + 2 * block + pair
                        at = (GROUPS[name][0] + layer, slice(row, row + 1), slice(None))
                        fld[at] = jnp.where(beside[0:1], value[k : k + 1], edge[at])
    first, second = 2 * PACKED, 2 * PACKED + 1
    own_lists = [before(first)[:, 0:64], after(first)[:, 0:64]]
    low_lists = [before(first)[:, 64:128], after(first)[:, 64:128]]
    high_lists = [before(second)[:, 0:64], after(second)[:, 0:64]]
    info = jnp.concatenate(own_lists + low_lists + high_lists, axis=1)
    block = list_block(info)
    base = jnp.where(block < 2, 16, jnp.where(block < 4, 0, 32))
    ahead = (block & 1) == 1

    def beside_lane(layer, col):
        last = jnp.where(col >= 128 - SLOT, 32 * layer + col - 128 + 2 * SLOT, -1)
        return jnp.where(ahead, jnp.where(col < SLOT, 32 * layer + col, -1), last)

    def write_beside(number, total):
        for t in range(1, 6):
            rows = slice(8 * t, 8 * t + 8)
            for k in range(4):
                value = total[8 * t - 8 : 8 * t]
                value = pltpu.roll(value, 128 - 32 * k, 1) if k else value
                dense[number, k, rows, :] = jnp.where(beside, value, edge_dense[number, k, rows, :])

    spread_wells(info, base, lambda layer: 0, 48, beside_lane, write_beside)

    def emit(group):
        def write(k, t, value):
            rows = slice(8 * t - 16, 8 * t - 8)
            value = jnp.where(lane < 64, pltpu.roll(value, 128 - HALO, 1), value)
            inner = (lane >= SLOT - 1) & (lane < 128 - SLOT)
            (first_rows, last_rows)[t - 2][group + k] = jnp.where(inner, center[group + k, rows, :], value)

        return write

    def send(t):
        copies = []
        for k, (out, group) in enumerate(((grad_x, 0), (grad_y, 4), (grad_z, 8))):
            source = (first_rows, last_rows)[t - 2].at[pl.ds(group, out.shape[0])]
            target = out.at[:, pl.ds(8 * t - 16, 8), :]
            copies.append(pltpu.make_async_copy(source, target, sems.at[3 * (t - 2) + k]))
            copies[-1].start()
        return copies

    copies = []
    simulate(fld, dense, upi, scratch, emit(0), emit(4), emit(8), lambda t: copies.extend(send(t)))
    for copy in copies:
        copy.wait()


def swapped(value, axis, first):
    count = lax.axis_size(axis)
    pairs = []
    for i in range(first, count - 1, 2):
        pairs += [(i, i + 1), (i + 1, i)]
    return lax.ppermute(value, axis, pairs)


def on_device(p, s, tx, ty, tz, pv, up, cell, rate, plan, observed):
    f32 = jnp.float32

    def shape(*dims):
        return jax.ShapeDtypeStruct(dims, f32)

    limit = pltpu.CompilerParams(vmem_limit_bytes=24 * 1024 * 1024)
    inputs = (p, s, tx, ty, tz, pv, up, cell, rate, plan, observed)
    inputs = [pltpu.with_memory_space_constraint(value, pltpu.HBM) for value in inputs]
    strip = shape(COUNT + 4, 8, 128)
    own, far, near = pl.pallas_call(
        pack_rows,
        out_shape=(shape(COUNT + 1, 16, 128), strip, strip),
        in_specs=[pl.BlockSpec(memory_space=pltpu.HBM)] * len(inputs),
        scratch_shapes=[pltpu.VMEM(value.shape, value.dtype) for value in inputs[6:]]
        + [pltpu.SemaphoreType.DMA((len(inputs),))],
        compiler_params=limit,
        name="pack_rows",
    )(*inputs)
    row_far = swapped(far, "gx", 1)
    row_near = swapped(near, "gx", 0)
    hide = pl.CostEstimate(flops=10**11, bytes_accessed=1 << 28, transcendentals=0)
    strip = shape(PACKED, 8, 128)
    own_far, own_near = pl.pallas_call(
        pack_own,
        out_shape=(strip, strip),
        compiler_params=limit,
        cost_estimate=hide,
        name="pack_own",
    )(own)
    strip = shape(2 * PACKED + 2, 8, 128)
    near, far = pl.pallas_call(
        pack_cols,
        out_shape=(strip, strip),
        compiler_params=limit,
        name="pack_cols",
    )(own, own_far, own_near, row_far, row_near)
    col_near = swapped(near, "gy", 0)
    col_far = swapped(far, "gy", 1)
    scratch = [pltpu.VMEM((COUNT, ROWS, 128), f32), pltpu.VMEM((7, 4, ROWS, 128), f32)]
    scratch += [pltpu.VMEM((4, ROWS, 128), jnp.int32)]
    scratch += [pltpu.VMEM((count, ROWS, 128), f32) for count in SCRATCH]
    center, edge, edge_dense = pl.pallas_call(
        model_center,
        out_shape=(shape(11, 16, 128), shape(COUNT, ROWS, 128), shape(7, 4, ROWS, 128)),
        scratch_shapes=scratch,
        compiler_params=limit,
        cost_estimate=hide,
        name="model_center",
    )(own, row_far, row_near)
    return pl.pallas_call(
        model_edge,
        out_shape=(shape(*tx.shape), shape(*ty.shape), shape(*tz.shape)),
        out_specs=(pl.BlockSpec(memory_space=pltpu.HBM),) * 3,
        scratch_shapes=[pltpu.VMEM((11, 8, 128), f32)] * 2 + [pltpu.SemaphoreType.DMA((6,))] + scratch,
        compiler_params=limit,
        name="model_edge",
    )(col_near, col_far, edge, edge_dense, center)


def solution(mesh):
    cells = P(None, "gx", "gy")
    in_specs = (cells,) * 7 + (
        P("gx", "gy", None),
        P("gx", "gy", None),
        P(None, "gx", "gy", None),
        P(None, None, "gx", "gy", None),
    )
    return jax.shard_map(
        on_device, mesh=mesh, in_specs=in_specs, out_specs=(cells,) * 3, check_vma=False
    )
```

```python
import jax
import jax.numpy as jnp
from jax import lax
from jax.experimental import pallas as pl
from jax.experimental.pallas import tpu as pltpu
from jax.sharding import PartitionSpec as P

time_step = 0.05

GROUPS = {"p": (0, 4), "s": (4, 4), "tx": (8, 4), "ty": (12, 4), "tz": (16, 3), "pv": (19, 4), "up": (23, 4)}
ORDER = ("p", "s", "tx", "ty", "tz", "pv", "up")
COUNT = 27
SLOT = 10
SLOTS = {"p": (0, 10), "tx": (10, 9), "ty": (19, 9), "tz": (28, 9), "pv": (37, 9), "s": (46, 7), "up": (53, 6)}
PACKED = 4
ROWS = 56
HALO = 2 * SLOT
LATE = 99


FIELDS = 11


def pack_rows(*refs):
    p, s, tx, ty, tz, pv, up, cell, rate, plan, observed = refs[:FIELDS]
    own, far, near, upi, cells, rates, plans, seen, sems = refs[FIELDS:]
    targets = [own.at[pl.ds(*GROUPS[name])] for name in ORDER[:6]] + [upi, cells, rates, plans, seen]
    copies = [
        pltpu.make_async_copy(source, target, sems.at[k])
        for k, (source, target) in enumerate(zip(refs[:FIELDS], targets))
    ]
    for copy in copies:
        copy.start()
    odd = lax.axis_index("gx") & 1
    for name, copy in zip(ORDER, copies):
        copy.wait()
        first, layers = GROUPS[name]
        for layer in range(layers):
            g = first + layer
            if name == "up":
                own[g] = upi[layer].astype(jnp.float32)
            far[g] = own[g, pl.ds(pl.multiple_of(8 * odd, 8), 8), :]
            near[g] = own[g, pl.ds(pl.multiple_of(8 - 8 * odd, 8), 8), :]
    for copy in copies[len(ORDER) :]:
        copy.wait()
    own[COUNT] = jnp.zeros((16, 128), jnp.float32)
    own[COUNT, 0:1, 0:64] = cells[0].astype(jnp.float32)
    own[COUNT, 1:2, 0:64] = rates[0]
    for n in range(2):
        own[COUNT, 2 + n : 3 + n, 0:64] = plans[n, 0].astype(jnp.float32)
        for k in range(2):
            row = 4 + 2 * n + k
            own[COUNT, row : row + 1, 0:64] = seen[n, k, 0]
    base = {name: GROUPS[name][0] for name in ORDER}

    blank = jnp.zeros((1, 128), jnp.float32)

    def gathered(*places):
        rows = []
        for layer in (0, 2, 1, 3):
            for name, row in places:
                there = layer < GROUPS[name][1]
                rows.append(own[base[name] + layer, row : row + 1, :] if there else blank)
        return jnp.concatenate([rows[k] for k in (0, 2, 1, 3, 4, 6, 5, 7)], axis=0)

    for_next = [gathered(("p", 7), ("tx", 7))]
    for_next += [jnp.zeros((8, 128), jnp.float32)] * 2
    for_prev = [
        gathered(("p", 8), ("tx", 8)),
        gathered(("ty", 8), ("tz", 8)),
        gathered(("pv", 8), ("p", 9)),
    ]
    for k in range(3):
        far[COUNT + k] = jnp.where(odd == 1, for_next[k], for_prev[k])
        near[COUNT + k] = jnp.where(odd == 1, for_prev[k], for_next[k])
    far[COUNT + 3] = own[COUNT, 0:8, :]
    near[COUNT + 3] = own[COUNT, 0:8, :]


def lanes():
    return lax.broadcasted_iota(jnp.int32, (8, 128), 1)


def in_slot(lane, start, ends, width):
    return ((lane - start - ends * (2 * SLOT - width)) & 63) < width


def sorted_ends(axis, far, near):
    odd = (lax.axis_index(axis) & 1) == 1

    def before(g):
        return jnp.where(odd, near[g], far[g])

    def after(g):
        return jnp.where(odd, far[g], near[g])

    return before, after


def pack_pairs(block, far, near, at):
    odd = lax.axis_index("gy") & 1
    lane = lanes()
    zero = jnp.zeros((8, 128), jnp.float32)
    for pair in range(2):
        ones, twos = {}, {}
        for name in SLOTS:
            first, layers = GROUPS[name]
            ones[name] = block(first + 2 * pair)
            there = 2 * pair + 1 < layers
            twos[name] = pltpu.roll(block(first + 2 * pair + 1), 64, 1) if there else zero
        for out, ends in ((far, odd), (near, 1 - odd)):
            straight = ((lane >> 6) ^ ends) == 0
            part = zero
            for name, (start, width) in SLOTS.items():
                both = jnp.where(straight, ones[name], twos[name])
                both = pltpu.roll(both, start + 2 * SLOT * ends, 1)
                part = jnp.where(in_slot(lane, start, ends, width), both, part)
            out[at + pair] = part


def extra_pair(one, two):
    row = lax.broadcasted_iota(jnp.int32, (8, 128), 0)
    return jnp.where(row < 4, one, pltpu.roll(two, 4, 0)), jnp.where(row < 4, pltpu.roll(one, 4, 0), two)


def pack_own(own, far, near):
    for tile in range(2):
        rows = slice(8 * tile, 8 * tile + 8)
        pack_pairs(lambda g: own[g, rows, :], far, near, 2 * tile)


def pack_cols(own, own_far, own_near, row_far, row_near, far, near):
    low, high = sorted_ends("gx", row_far, row_near)
    for out, part in ((far, own_far), (near, own_near)):
        for at in range(PACKED):
            out[at] = part[at]
    pack_pairs(low, far, near, PACKED)
    pack_pairs(high, far, near, PACKED + 2)
    odd = lax.axis_index("gy") & 1
    lane = lanes()
    both = jnp.where(lane < 64, own[COUNT, 0:8, :], pltpu.roll(low(COUNT + 3), 64, 1))
    extras = extra_pair(low(COUNT), high(COUNT)) + extra_pair(high(COUNT + 1), high(COUNT + 2))
    for out, ends in ((far, odd), (near, 1 - odd)):
        out[2 * PACKED] = both
        part = high(COUNT + 3)
        for k, value in enumerate(extras):
            start = 64 + SLOT * k
            mask = ((lane - start - SLOT * ends) & 127) < SLOT
            part = jnp.where(mask, pltpu.roll(value, start + 2 * SLOT * ends, 1), part)
        out[2 * PACKED + 1] = part


def split3(value):
    hi = value.astype(jnp.bfloat16).astype(jnp.float32)
    rest = value - hi
    mid = rest.astype(jnp.bfloat16).astype(jnp.float32)
    return hi, mid, rest - mid


SRC0, SRC1, OP0, OS0, OP1, OS1, CNT = range(7)


def spread_wells(info, base, rows_of, count, to_spot, write):
    width = info.shape[1]
    cell = info[0:1].astype(jnp.int32)
    layer = lax.shift_right_logical(cell, 11)
    place = (lax.shift_right_logical(cell, 7) & 15) + base
    target = jnp.where(place >= 8, rows_of(layer) + place - 8, -1)
    spot = to_spot(layer, cell & 127)
    hit = lax.broadcasted_iota(jnp.int32, (count, width), 0) == target
    hit = jnp.where(hit, 1.0, 0.0).astype(jnp.bfloat16)
    lane = lax.broadcasted_iota(jnp.int32, (128, width), 0)
    to_lane = jnp.where(lane == spot, 1.0, 0.0).astype(jnp.bfloat16)
    rate = info[1:2] * 0.5
    values = [rate * info[2:3], rate * info[3:4]] + [info[k : k + 1] for k in range(4, 8)]
    for number, value in enumerate(values):
        total = None
        for part in split3(value):
            part = jnp.broadcast_to(part, (16, width)).astype(jnp.bfloat16)
            left = hit * jnp.concatenate([part] * (count // 16), axis=0)
            term = dot(left, to_lane)
            total = term if total is None else total + term
        write(number, total)
    write(CNT, dot(hit, to_lane))


def dot(left, right):
    return lax.dot_general(left, right, (((1,), (1,)), ((), ())), preferred_element_type=jnp.float32)


def list_block(info):
    return lax.shift_right_logical(lax.broadcasted_iota(jnp.int32, (1, info.shape[1]), 1), 6)


SCRATCH = (4,) * 12 + (11,) * 4 + (4,) * 9


def simulate(fld, dense, upi, scratch, emit_x, emit_y, emit_z, tile_done=None):
    (rcp, tym, per, q0, p1, q1, p2, f0, d0, s1, f1, d1, fup0, fup1, dp1, dp2,
     sig2, psi2, psi1, mup2, muq1, mup1, muq0, flux, rest) = scratch
    PB, SB, XB, YB, ZB, VB = (GROUPS[name][0] for name in ORDER[:6])

    def here(ref, k, t):
        return ref[k, 8 * t : 8 * t + 8, :]

    def down(ref, k, t):
        return ref[k, 8 * t + 1 : 8 * t + 9, :]

    def above(ref, k, t):
        return ref[k, 8 * t - 1 : 8 * t + 7, :]

    def put(ref, k, t, value):
        ref[k, 8 * t : 8 * t + 8, :] = value

    def right(value):
        return pltpu.roll(value, 127, 1)

    def left(value):
        return pltpu.roll(value, 1, 1)

    for k in range(4):
        for t in range(1, 6):
            beyond = right(here(fld, VB + k, t))
            put(fld, YB + k, t, jnp.where(beyond == 0.0, 0.0, here(fld, YB + k, t)))
        last = slice(31, 32)
        fld[XB + k, last, :] = jnp.where(fld[VB + k, 32:33, :] == 0.0, 0.0, fld[XB + k, last, :])
    for t in range(1, 6):
        for k in range(4):
            volume = here(fld, VB + k, t)
            volume = jnp.where(volume == 0.0, 1.0, volume)
            put(fld, VB + k, t, volume)
            put(per, k, t, time_step * pl.reciprocal(volume))
            west = left(here(fld, YB + k, t))
            put(tym, k, t, west)
            total = volume + (here(fld, XB + k, t) + above(fld, XB + k, t)) + (here(fld, YB + k, t) + west)
            if k < 3:
                total = total + here(fld, ZB + k, t)
            if k > 0:
                total = total + here(fld, ZB + k - 1, t)
            put(rcp, k, t, pl.reciprocal(total))

    def neighbours(ref, base, k, t):
        value = here(ref, base + k, t)
        total = here(fld, XB + k, t) * down(ref, base + k, t) + above(fld, XB + k, t) * above(ref, base + k, t)
        total = total + (here(fld, YB + k, t) * right(value) + here(tym, k, t) * left(value))
        if k < 3:
            total = total + here(fld, ZB + k, t) * here(ref, base + k + 1, t)
        if k > 0:
            total = total + here(fld, ZB + k - 1, t) * here(ref, base + k - 1, t)
        return total

    def relax(out, ref, base, old, old_base, source, tiles):
        for t in tiles:
            for k in range(4):
                total = here(fld, VB + k, t) * here(old, old_base + k, t) + here(dense.at[source], k, t)
                put(out, k, t, (total + neighbours(ref, base, k, t)) * here(rcp, k, t))

    def put_mobility(value, k, t, mobile, slope):
        rest_of = 1.0 - value
        wetted = value * value
        inverse = pl.reciprocal(wetted + 0.5 * rest_of * rest_of)
        put(mobile, k, t, wetted * inverse)
        put(slope, k, t, value * rest_of * (inverse * inverse))

    def bit(k, t, number):
        return (here(upi, k, t) & (1 << number)) != 0

    def transport(pressure, sat, sat_base, mobile, n, fup, dp, finish):
        for t in range(1, 5):
            below = None
            for k in range(4):
                mob = here(mobile, k, t)
                pres = here(pressure, k, t)
                drop_x = pres - down(pressure, k, t)
                drop_y = pres - right(pres)
                up_x = jnp.where(bit(k, t, 3 * n), mob, down(mobile, k, t))
                up_y = jnp.where(bit(k, t, 3 * n + 1), mob, right(mob))
                put(fup, k, t, up_x)
                put(fup, 4 + k, t, up_y)
                put(dp, k, t, drop_x)
                put(dp, 4 + k, t, drop_y)
                flux_x = here(fld, XB + k, t) * up_x * drop_x
                flux_y = here(fld, YB + k, t) * up_y * drop_y
                put(flux, k, t, flux_x)
                net = (flux_x - above(flux, k, t)) + (flux_y - left(flux_y))
                if k > 0:
                    net = net - below
                if k < 3:
                    drop_z = pres - here(pressure, k + 1, t)
                    up_z = jnp.where(bit(k, t, 3 * n + 2), mob, here(mobile, k + 1, t))
                    put(fup, 8 + k, t, up_z)
                    put(dp, 8 + k, t, drop_z)
                    below = here(fld, ZB + k, t) * up_z * drop_z
                    net = net + below
                finish(here(sat, sat_base + k, t) - net * here(per, k, t), k, t)

    tiles = range(1, 5)
    relax(q0, fld, PB, fld, PB, SRC0, range(1, 6))
    relax(p1, q0, 0, fld, PB, SRC0, tiles)
    for t in tiles:
        for k in range(4):
            put_mobility(here(fld, SB + k, t), k, t, f0, d0)

    def finish_first(moved, k, t):
        put(s1, k, t, moved)
        put_mobility(moved, k, t, f1, d1)

    transport(p1, fld, SB, f0, 0, fup0, dp1, finish_first)
    relax(q1, p1, 0, p1, 0, SRC1, tiles)
    relax(p2, q1, 0, p1, 0, SRC1, tiles)

    def finish_second(moved, k, t):
        miss = here(dense.at[CNT], k, t) * moved - here(dense.at[OS1], k, t)
        put(sig2, k, t, miss)
        put(psi2, k, t, miss * here(per, k, t))

    transport(p2, s1, 0, f1, 1, fup1, dp2, finish_second)

    for t in tiles:
        below_h = below_r = None
        for k in range(4):
            psi = here(psi2, k, t)
            phi_x = (down(psi2, k, t) - psi) * here(fld, XB + k, t)
            phi_y = (right(psi) - psi) * here(fld, YB + k, t)
            h_x = phi_x * here(fup1, k, t)
            h_y = phi_y * here(fup1, 4 + k, t)
            k_x = phi_x * here(dp2, k, t)
            k_y = phi_y * here(dp2, 4 + k, t)
            s_x = jnp.where(bit(k, t, 3), k_x, 0.0)
            s_y = jnp.where(bit(k, t, 4), k_y, 0.0)
            put(flux, k, t, h_x)
            put(rest, k, t, k_x - s_x)
            press = (h_x - above(flux, k, t)) + (h_y - left(h_y))
            satur = (s_x + above(rest, k, t)) + (s_y + left(k_y - s_y))
            if k > 0:
                press = press - below_h
                satur = satur + below_r
            if k < 3:
                phi_z = (here(psi2, k + 1, t) - psi) * here(fld, ZB + k, t)
                below_h = phi_z * here(fup1, 8 + k, t)
                k_z = phi_z * here(dp2, 8 + k, t)
                s_z = jnp.where(bit(k, t, 5), k_z, 0.0)
                below_r = k_z - s_z
                press = press + below_h
                satur = satur + s_z
            count = here(dense.at[CNT], k, t)
            press = press + (count * here(p2, k, t) - here(dense.at[OP1], k, t))
            put(mup2, k, t, press * here(rcp, k, t))
            sigma = here(sig2, k, t) + satur * here(d1, k, t)
            sigma = sigma + (count * here(s1, k, t) - here(dense.at[OS0], k, t))
            put(psi1, k, t, sigma * here(per, k, t))

    for t in tiles:
        for k in range(4):
            put(muq1, k, t, neighbours(mup2, 0, k, t) * here(rcp, k, t))

    for t in tiles:
        below_h = None
        for k in range(4):
            psi = here(psi1, k, t)
            h_x = (down(psi1, k, t) - psi) * here(fld, XB + k, t) * here(fup0, k, t)
            h_y = (right(psi) - psi) * here(fld, YB + k, t) * here(fup0, 4 + k, t)
            put(flux, k, t, h_x)
            press = (h_x - above(flux, k, t)) + (h_y - left(h_y))
            if k > 0:
                press = press - below_h
            if k < 3:
                below_h = (here(psi1, k + 1, t) - psi) * here(fld, ZB + k, t) * here(fup0, 8 + k, t)
                press = press + below_h
            count = here(dense.at[CNT], k, t)
            press = press + (count * here(p1, k, t) - here(dense.at[OP0], k, t))
            press = press + here(fld, VB + k, t) * (here(mup2, k, t) + here(muq1, k, t))
            press = press + neighbours(muq1, 0, k, t)
            put(mup1, k, t, press * here(rcp, k, t))

    for t in range(2, 5):
        for k in range(4):
            put(muq0, k, t, neighbours(mup1, 0, k, t) * here(rcp, k, t))

    stages = (
        (mup2, q1, 0, p2, 0),
        (muq1, p1, 0, q1, 0),
        (mup1, q0, 0, p1, 0),
        (muq0, fld, PB, q0, 0),
    )
    for t in range(2, 4):
        for k in range(4):
            sum_x = sum_y = sum_z = 0.0
            for psi, fup, dp in ((psi2, fup1, dp2), (psi1, fup0, dp1)):
                mid = here(psi, k, t)
                sum_x = sum_x + (down(psi, k, t) - mid) * here(fup, k, t) * here(dp, k, t)
                sum_y = sum_y + (right(mid) - mid) * here(fup, 4 + k, t) * here(dp, 4 + k, t)
                if k < 3:
                    sum_z = sum_z + (here(psi, k + 1, t) - mid) * here(fup, 8 + k, t) * here(dp, 8 + k, t)
            for mu, value, base, out, out_base in stages:
                mu_c, v_c, o_c = here(mu, k, t), here(value, base + k, t), here(out, out_base + k, t)
                mu_d, v_d, o_d = down(mu, k, t), down(value, base + k, t), down(out, out_base + k, t)
                sum_x = sum_x + (mu_c * (v_d - o_c) + mu_d * (v_c - o_d))
                sum_y = sum_y + (mu_c * (right(v_c) - o_c) + right(mu_c) * (v_c - right(o_c)))
                if k < 3:
                    mu_u = here(mu, k + 1, t)
                    v_u = here(value, base + k + 1, t)
                    o_u = here(out, out_base + k + 1, t)
                    sum_z = sum_z + (mu_c * (v_u - o_c) + mu_u * (v_c - o_u))
            emit_x(k, t, jnp.where(here(fld, XB + k, t) == 0.0, 0.0, sum_x))
            emit_y(k, t, jnp.where(here(fld, YB + k, t) == 0.0, 0.0, sum_y))
            if k < 3:
                emit_z(k, t, sum_z)
        if tile_done is not None:
            tile_done(t)


PLACES = (
    (("p", 7), ("tx", 7)),
    (("p", 40), ("tx", 40)),
    (("ty", 40), ("tz", 40)),
    (("pv", 40), ("p", 41)),
)


def put_beyond(fld, value, places):
    for block, (name, row) in enumerate(places):
        first, layers = GROUPS[name]
        for layer in range(layers):
            k = 4 * (layer & 1) + 2 * block + layer // 2
            fld[first + layer, row : row + 1, :] = value[k : k + 1]


def model_center(own, row_far, row_near, grads, edge, edge_dense, fld, dense, upi, *scratch):
    low, high = sorted_ends("gx", row_far, row_near)
    lane = lanes()

    early = lane < LATE

    def edge_of(value):
        return jnp.where(early, pltpu.roll(value, HALO, 1), value)

    for g in range(COUNT):
        for k, block in enumerate((low(g), own[g, 0:8, :], own[g, 8:16, :], high(g))):
            rows = slice(8 + 8 * k, 16 + 8 * k)
            fld[g, rows, :] = block
            edge[g, rows, :] = edge_of(block)
            if g >= GROUPS["up"][0]:
                upi[g - GROUPS["up"][0], rows, :] = block.astype(jnp.int32)
    for value, places in zip([low(COUNT)] + [high(COUNT + k) for k in range(3)], PLACES):
        for out, rows in ((fld, value), (edge, edge_of(value))):
            put_beyond(out, rows, places)

    info = jnp.concatenate(
        [own[COUNT, 0:8, 0:64], low(COUNT + 3)[:, 0:64], high(COUNT + 3)[:, 0:64]], axis=1
    )
    block = list_block(info)
    base = jnp.where(block == 0, 16, jnp.where(block == 1, 0, 32))

    def write_center(number, total):
        for k in range(4):
            dense[number, k, 8:48, :] = total[40 * k : 40 * k + 40]

    def write_edge(number, total):
        for k in range(4):
            edge_dense[number, k, 8:48, :] = total[40 * k : 40 * k + 40]

    def edge_lane(layer, col):
        return jnp.where(col < LATE - HALO, col + HALO, jnp.where(col >= LATE, col, -1))

    spread_wells(info, base, lambda layer: layer * 40, 160, lambda layer, col: col, write_center)
    spread_wells(info, base, lambda layer: layer * 40, 160, edge_lane, write_edge)

    def emit(first):
        def write(k, t, value):
            grads[first + k, 8 * t - 16 : 8 * t - 8, :] = value

        return write

    simulate(fld, dense, upi, scratch, emit(0), emit(4), emit(8))


def model_edge(
    col_far, col_near, edge, edge_dense, center, grad_x, grad_y, grad_z, first_rows, last_rows, sems, fld, dense, upi,
    *scratch
):
    before, after = sorted_ends("gy", col_far, col_near)
    odd = lax.axis_index("gy") & 1
    lane = lanes()
    beside = lane < HALO
    for name, (start, width) in SLOTS.items():
        far_cols = in_slot(lane, start, 1 - odd, width)
        first, layers = GROUPS[name]
        for layer in range(layers):
            for k, at in enumerate((PACKED, 0, 2, PACKED + 2)):
                rows = slice(8 + 8 * k, 16 + 8 * k)
                both = jnp.where(far_cols, col_far[at + layer // 2], col_near[at + layer // 2])
                both = pltpu.roll(both, (64 * (layer & 1) - start) % 128, 1)
                block = jnp.where(beside, both, edge[first + layer, rows, :])
                if name == "up":
                    upi[layer, rows, :] = block.astype(jnp.int32)
                else:
                    fld[first + layer, rows, :] = block
    for number, places in enumerate(PLACES):
        for half in range(2):
            start = 64 + SLOT * (2 * (number // 2) + half)
            mask = ((lane - start - SLOT * (1 - odd)) & 127) < SLOT
            both = jnp.where(mask, col_far[2 * PACKED + 1], col_near[2 * PACKED + 1])
            value = pltpu.roll(both, 128 - start, 1)
            for block, (name, row) in enumerate(places):
                for pair in range(2):
                    layer = 2 * pair + half
                    if layer < GROUPS[name][1]:
                        k = 4 * (number & 1) + 2 * block + pair
                        at = (GROUPS[name][0] + layer, slice(row, row + 1), slice(None))
                        fld[at] = jnp.where(beside[0:1], value[k : k + 1], edge[at])
    first, second = 2 * PACKED, 2 * PACKED + 1
    own_lists = [before(first)[:, 0:64], after(first)[:, 0:64]]
    low_lists = [before(first)[:, 64:128], after(first)[:, 64:128]]
    high_lists = [before(second)[:, 0:64], after(second)[:, 0:64]]
    info = jnp.concatenate(own_lists + low_lists + high_lists, axis=1)
    block = list_block(info)
    base = jnp.where(block < 2, 16, jnp.where(block < 4, 0, 32))
    ahead = (block & 1) == 1

    def beside_lane(layer, col):
        last = jnp.where(col >= 128 - SLOT, 32 * layer + col - 128 + 2 * SLOT, -1)
        return jnp.where(ahead, jnp.where(col < SLOT, 32 * layer + col, -1), last)

    def write_beside(number, total):
        for t in range(1, 6):
            rows = slice(8 * t, 8 * t + 8)
            for k in range(4):
                value = total[8 * t - 8 : 8 * t]
                value = pltpu.roll(value, 128 - 32 * k, 1) if k else value
                dense[number, k, rows, :] = jnp.where(beside, value, edge_dense[number, k, rows, :])

    spread_wells(info, base, lambda layer: 0, 48, beside_lane, write_beside)

    def emit(group):
        def write(k, t, value):
            rows = slice(8 * t - 16, 8 * t - 8)
            value = jnp.where(lane < 64, pltpu.roll(value, 128 - HALO, 1), value)
            inner = (lane >= SLOT - 1) & (lane < 128 - SLOT)
            (first_rows, last_rows)[t - 2][group + k] = jnp.where(inner, center[group + k, rows, :], value)

        return write

    def send(t):
        copies = []
        for k, (out, group) in enumerate(((grad_x, 0), (grad_y, 4), (grad_z, 8))):
            source = (first_rows, last_rows)[t - 2].at[pl.ds(group, out.shape[0])]
            target = out.at[:, pl.ds(8 * t - 16, 8), :]
            copies.append(pltpu.make_async_copy(source, target, sems.at[3 * (t - 2) + k]))
            copies[-1].start()
        return copies

    copies = []
    simulate(fld, dense, upi, scratch, emit(0), emit(4), emit(8), lambda t: copies.extend(send(t)))
    for copy in copies:
        copy.wait()


def swapped(value, axis, first):
    count = lax.axis_size(axis)
    pairs = []
    for i in range(first, count - 1, 2):
        pairs += [(i, i + 1), (i + 1, i)]
    return lax.ppermute(value, axis, pairs)


def on_device(p, s, tx, ty, tz, pv, up, cell, rate, plan, observed):
    f32 = jnp.float32

    def shape(*dims):
        return jax.ShapeDtypeStruct(dims, f32)

    limit = pltpu.CompilerParams(vmem_limit_bytes=24 * 1024 * 1024)
    inputs = (p, s, tx, ty, tz, pv, up, cell, rate, plan, observed)
    inputs = [pltpu.with_memory_space_constraint(value, pltpu.HBM) for value in inputs]
    strip = shape(COUNT + 4, 8, 128)
    own, far, near = pl.pallas_call(
        pack_rows,
        out_shape=(shape(COUNT + 1, 16, 128), strip, strip),
        in_specs=[pl.BlockSpec(memory_space=pltpu.HBM)] * len(inputs),
        scratch_shapes=[pltpu.VMEM(value.shape, value.dtype) for value in inputs[6:]]
        + [pltpu.SemaphoreType.DMA((len(inputs),))],
        compiler_params=limit,
        name="pack_rows",
    )(*inputs)
    row_far = swapped(far, "gx", 1)
    row_near = swapped(near, "gx", 0)
    hide = pl.CostEstimate(flops=10**11, bytes_accessed=1 << 28, transcendentals=0)
    strip = shape(PACKED, 8, 128)
    own_far, own_near = pl.pallas_call(
        pack_own,
        out_shape=(strip, strip),
        compiler_params=limit,
        cost_estimate=hide,
        name="pack_own",
    )(own)
    strip = shape(2 * PACKED + 2, 8, 128)
    far, near = pl.pallas_call(
        pack_cols,
        out_shape=(strip, strip),
        compiler_params=limit,
        name="pack_cols",
    )(own, own_far, own_near, row_far, row_near)
    col_far = swapped(far, "gy", 1)
    col_near = swapped(near, "gy", 0)
    scratch = [pltpu.VMEM((COUNT, ROWS, 128), f32), pltpu.VMEM((7, 4, ROWS, 128), f32)]
    scratch += [pltpu.VMEM((4, ROWS, 128), jnp.int32)]
    scratch += [pltpu.VMEM((count, ROWS, 128), f32) for count in SCRATCH]
    center, edge, edge_dense = pl.pallas_call(
        model_center,
        out_shape=(shape(11, 16, 128), shape(COUNT, ROWS, 128), shape(7, 4, ROWS, 128)),
        scratch_shapes=scratch,
        compiler_params=limit,
        cost_estimate=hide,
        name="model_center",
    )(own, row_far, row_near)
    return pl.pallas_call(
        model_edge,
        out_shape=(shape(*tx.shape), shape(*ty.shape), shape(*tz.shape)),
        out_specs=(pl.BlockSpec(memory_space=pltpu.HBM),) * 3,
        scratch_shapes=[pltpu.VMEM((11, 8, 128), f32)] * 2 + [pltpu.SemaphoreType.DMA((6,))] + scratch,
        compiler_params=limit,
        name="model_edge",
    )(col_far, col_near, edge, edge_dense, center)


def solution(mesh):
    cells = P(None, "gx", "gy")
    in_specs = (cells,) * 7 + (
        P("gx", "gy", None),
        P("gx", "gy", None),
        P(None, "gx", "gy", None),
        P(None, None, "gx", "gy", None),
    )
    return jax.shard_map(
        on_device, mesh=mesh, in_specs=in_specs, out_specs=(cells,) * 3, check_vma=False
    )
```

```python
import jax
import jax.numpy as jnp
from jax import lax
from jax.experimental import pallas as pl
from jax.experimental.pallas import tpu as pltpu
from jax.sharding import PartitionSpec as P

time_step = 0.05

GROUPS = {"p": (0, 4), "s": (4, 4), "tx": (8, 4), "ty": (12, 4), "tz": (16, 3), "pv": (19, 4), "up": (23, 4)}
ORDER = ("p", "s", "tx", "ty", "tz", "pv", "up")
COUNT = 27
SLOT = 10
SLOTS = {"p": (0, 10), "tx": (10, 9), "ty": (19, 9), "tz": (28, 9), "pv": (37, 9), "s": (46, 7), "up": (53, 6)}
PACKED = 4
ROWS = 56
HALO = 2 * SLOT
LATE = 99


FIELDS = 11


def pack_rows(*refs):
    p, s, tx, ty, tz, pv, up, cell, rate, plan, observed = refs[:FIELDS]
    own, far, near, upi, cells, rates, plans, seen, sems = refs[FIELDS:]
    targets = [own.at[pl.ds(*GROUPS[name])] for name in ORDER[:6]] + [upi, cells, rates, plans, seen]
    copies = [
        pltpu.make_async_copy(source, target, sems.at[k])
        for k, (source, target) in enumerate(zip(refs[:FIELDS], targets))
    ]
    for copy in copies:
        copy.start()
    odd = lax.axis_index("gx") & 1
    for name, copy in zip(ORDER, copies):
        copy.wait()
        first, layers = GROUPS[name]
        for layer in range(layers):
            g = first + layer
            if name == "up":
                own[g] = upi[layer].astype(jnp.float32)
            far[g] = own[g, pl.ds(pl.multiple_of(8 * odd, 8), 8), :]
            near[g] = own[g, pl.ds(pl.multiple_of(8 - 8 * odd, 8), 8), :]
    for copy in copies[len(ORDER) :]:
        copy.wait()
    own[COUNT] = jnp.zeros((16, 128), jnp.float32)
    own[COUNT, 0:1, 0:64] = cells[0].astype(jnp.float32)
    own[COUNT, 1:2, 0:64] = rates[0]
    for n in range(2):
        own[COUNT, 2 + n : 3 + n, 0:64] = plans[n, 0].astype(jnp.float32)
        for k in range(2):
            row = 4 + 2 * n + k
            own[COUNT, row : row + 1, 0:64] = seen[n, k, 0]
    base = {name: GROUPS[name][0] for name in ORDER}

    blank = jnp.zeros((1, 128), jnp.float32)

    def gathered(*places):
        rows = []
        for layer in (0, 2, 1, 3):
            for name, row in places:
                there = layer < GROUPS[name][1]
                rows.append(own[base[name] + layer, row : row + 1, :] if there else blank)
        return jnp.concatenate([rows[k] for k in (0, 2, 1, 3, 4, 6, 5, 7)], axis=0)

    for_next = [gathered(("p", 7), ("tx", 7))]
    for_next += [jnp.zeros((8, 128), jnp.float32)] * 2
    for_prev = [
        gathered(("p", 8), ("tx", 8)),
        gathered(("ty", 8), ("tz", 8)),
        gathered(("pv", 8), ("p", 9)),
    ]
    for k in range(3):
        far[COUNT + k] = jnp.where(odd == 1, for_next[k], for_prev[k])
        near[COUNT + k] = jnp.where(odd == 1, for_prev[k], for_next[k])
    far[COUNT + 3] = own[COUNT, 0:8, :]
    near[COUNT + 3] = own[COUNT, 0:8, :]


def lanes():
    return lax.broadcasted_iota(jnp.int32, (8, 128), 1)


def in_slot(lane, start, ends, width):
    return ((lane - start - ends * (2 * SLOT - width)) & 63) < width


def sorted_ends(axis, far, near):
    odd = (lax.axis_index(axis) & 1) == 1

    def before(g):
        return jnp.where(odd, near[g], far[g])

    def after(g):
        return jnp.where(odd, far[g], near[g])

    return before, after


def pack_pairs(block, far, near, at):
    odd = lax.axis_index("gy") & 1
    lane = lanes()
    zero = jnp.zeros((8, 128), jnp.float32)
    for pair in range(2):
        ones, twos = {}, {}
        for name in SLOTS:
            first, layers = GROUPS[name]
            ones[name] = block(first + 2 * pair)
            there = 2 * pair + 1 < layers
            twos[name] = pltpu.roll(block(first + 2 * pair + 1), 64, 1) if there else zero
        for out, ends in ((far, odd), (near, 1 - odd)):
            straight = ((lane >> 6) ^ ends) == 0
            part = zero
            for name, (start, width) in SLOTS.items():
                both = jnp.where(straight, ones[name], twos[name])
                both = pltpu.roll(both, start + 2 * SLOT * ends, 1)
                part = jnp.where(in_slot(lane, start, ends, width), both, part)
            out[at + pair] = part


def extra_pair(one, two):
    row = lax.broadcasted_iota(jnp.int32, (8, 128), 0)
    return jnp.where(row < 4, one, pltpu.roll(two, 4, 0)), jnp.where(row < 4, pltpu.roll(one, 4, 0), two)


def pack_own(own, far, near):
    for tile in range(2):
        rows = slice(8 * tile, 8 * tile + 8)
        pack_pairs(lambda g: own[g, rows, :], far, near, 2 * tile)


def pack_cols(own, own_far, own_near, row_far, row_near, far, near):
    low, high = sorted_ends("gx", row_far, row_near)
    for out, part in ((far, own_far), (near, own_near)):
        for at in range(PACKED):
            out[at] = part[at]
    pack_pairs(low, far, near, PACKED)
    pack_pairs(high, far, near, PACKED + 2)
    odd = lax.axis_index("gy") & 1
    lane = lanes()
    both = jnp.where(lane < 64, own[COUNT, 0:8, :], pltpu.roll(low(COUNT + 3), 64, 1))
    extras = extra_pair(low(COUNT), high(COUNT)) + extra_pair(high(COUNT + 1), high(COUNT + 2))
    for out, ends in ((far, odd), (near, 1 - odd)):
        out[2 * PACKED] = both
        part = high(COUNT + 3)
        for k, value in enumerate(extras):
            start = 64 + SLOT * k
            mask = ((lane - start - SLOT * ends) & 127) < SLOT
            part = jnp.where(mask, pltpu.roll(value, start + 2 * SLOT * ends, 1), part)
        out[2 * PACKED + 1] = part


def split3(value):
    hi = value.astype(jnp.bfloat16).astype(jnp.float32)
    rest = value - hi
    mid = rest.astype(jnp.bfloat16).astype(jnp.float32)
    return hi, mid, rest - mid


SRC0, SRC1, OP0, OS0, OP1, OS1, CNT = range(7)


def spread_wells(info, base, rows_of, count, to_spot, write):
    width = info.shape[1]
    cell = info[0:1].astype(jnp.int32)
    layer = lax.shift_right_logical(cell, 11)
    place = (lax.shift_right_logical(cell, 7) & 15) + base
    target = jnp.where(place >= 8, rows_of(layer) + place - 8, -1)
    spot = to_spot(layer, cell & 127)
    hit = lax.broadcasted_iota(jnp.int32, (count, width), 0) == target
    hit = jnp.where(hit, 1.0, 0.0).astype(jnp.bfloat16)
    lane = lax.broadcasted_iota(jnp.int32, (128, width), 0)
    to_lane = jnp.where(lane == spot, 1.0, 0.0).astype(jnp.bfloat16)
    rate = info[1:2] * 0.5
    values = [rate * info[2:3], rate * info[3:4]] + [info[k : k + 1] for k in range(4, 8)]
    for number, value in enumerate(values):
        total = None
        for part in split3(value):
            part = jnp.broadcast_to(part, (16, width)).astype(jnp.bfloat16)
            left = hit * jnp.concatenate([part] * (count // 16), axis=0)
            term = dot(left, to_lane)
            total = term if total is None else total + term
        write(number, total)
    write(CNT, dot(hit, to_lane))


def dot(left, right):
    return lax.dot_general(left, right, (((1,), (1,)), ((), ())), preferred_element_type=jnp.float32)


def list_block(info):
    return lax.shift_right_logical(lax.broadcasted_iota(jnp.int32, (1, info.shape[1]), 1), 6)


SCRATCH = (4,) * 12 + (11,) * 4 + (4,) * 9


def simulate(fld, dense, upi, scratch, emit_x, emit_y, emit_z, tile_done=None, looped=False):
    (rcp, tym, per, q0, p1, q1, p2, f0, d0, s1, f1, d1, fup0, fup1, dp1, dp2,
     sig2, psi2, psi1, mup2, muq1, mup1, muq0, flux, rest) = scratch
    PB, SB, XB, YB, ZB, VB = (GROUPS[name][0] for name in ORDER[:6])

    def whole(t):
        return 8 * t if isinstance(t, int) else pl.multiple_of(8 * t, 8)

    def over(tiles, body):
        if looped:
            lax.fori_loop(tiles.start, tiles.stop, lambda t, none: (body(t), none)[1], 0)
        else:
            for t in tiles:
                body(t)

    def here(ref, k, t):
        return ref[k, pl.ds(whole(t), 8), :]

    def down(ref, k, t):
        return ref[k, pl.ds(8 * t + 1, 8), :]

    def above(ref, k, t):
        return ref[k, pl.ds(8 * t - 1, 8), :]

    def put(ref, k, t, value):
        ref[k, pl.ds(whole(t), 8), :] = value

    def right(value):
        return pltpu.roll(value, 127, 1)

    def left(value):
        return pltpu.roll(value, 1, 1)

    for k in range(4):
        for t in range(1, 6):
            beyond = right(here(fld, VB + k, t))
            put(fld, YB + k, t, jnp.where(beyond == 0.0, 0.0, here(fld, YB + k, t)))
        last = slice(31, 32)
        fld[XB + k, last, :] = jnp.where(fld[VB + k, 32:33, :] == 0.0, 0.0, fld[XB + k, last, :])

    def pass_2(t):
        for k in range(4):
            volume = here(fld, VB + k, t)
            volume = jnp.where(volume == 0.0, 1.0, volume)
            put(fld, VB + k, t, volume)
            put(per, k, t, time_step * pl.reciprocal(volume))
            west = left(here(fld, YB + k, t))
            put(tym, k, t, west)
            total = volume + (here(fld, XB + k, t) + above(fld, XB + k, t)) + (here(fld, YB + k, t) + west)
            if k < 3:
                total = total + here(fld, ZB + k, t)
            if k > 0:
                total = total + here(fld, ZB + k - 1, t)
            put(rcp, k, t, pl.reciprocal(total))

    over(range(1, 6), pass_2)

    def neighbours(ref, base, k, t):
        value = here(ref, base + k, t)
        total = here(fld, XB + k, t) * down(ref, base + k, t) + above(fld, XB + k, t) * above(ref, base + k, t)
        total = total + (here(fld, YB + k, t) * right(value) + here(tym, k, t) * left(value))
        if k < 3:
            total = total + here(fld, ZB + k, t) * here(ref, base + k + 1, t)
        if k > 0:
            total = total + here(fld, ZB + k - 1, t) * here(ref, base + k - 1, t)
        return total

    def relax(out, ref, base, old, old_base, source, tiles):
        def pass_3(t):
            for k in range(4):
                total = here(fld, VB + k, t) * here(old, old_base + k, t) + here(dense.at[source], k, t)
                put(out, k, t, (total + neighbours(ref, base, k, t)) * here(rcp, k, t))

        over(tiles, pass_3)

    def put_mobility(value, k, t, mobile, slope):
        rest_of = 1.0 - value
        wetted = value * value
        inverse = pl.reciprocal(wetted + 0.5 * rest_of * rest_of)
        put(mobile, k, t, wetted * inverse)
        put(slope, k, t, value * rest_of * (inverse * inverse))

    def bit(k, t, number):
        return (here(upi, k, t) & (1 << number)) != 0

    def transport(pressure, sat, sat_base, mobile, n, fup, dp, finish):
        def pass_4(t):
            below = None
            for k in range(4):
                mob = here(mobile, k, t)
                pres = here(pressure, k, t)
                drop_x = pres - down(pressure, k, t)
                drop_y = pres - right(pres)
                up_x = jnp.where(bit(k, t, 3 * n), mob, down(mobile, k, t))
                up_y = jnp.where(bit(k, t, 3 * n + 1), mob, right(mob))
                put(fup, k, t, up_x)
                put(fup, 4 + k, t, up_y)
                put(dp, k, t, drop_x)
                put(dp, 4 + k, t, drop_y)
                flux_x = here(fld, XB + k, t) * up_x * drop_x
                flux_y = here(fld, YB + k, t) * up_y * drop_y
                put(flux, k, t, flux_x)
                net = (flux_x - above(flux, k, t)) + (flux_y - left(flux_y))
                if k > 0:
                    net = net - below
                if k < 3:
                    drop_z = pres - here(pressure, k + 1, t)
                    up_z = jnp.where(bit(k, t, 3 * n + 2), mob, here(mobile, k + 1, t))
                    put(fup, 8 + k, t, up_z)
                    put(dp, 8 + k, t, drop_z)
                    below = here(fld, ZB + k, t) * up_z * drop_z
                    net = net + below
                finish(here(sat, sat_base + k, t) - net * here(per, k, t), k, t)

        over(range(1, 5), pass_4)

    tiles = range(1, 5)
    relax(q0, fld, PB, fld, PB, SRC0, range(1, 6))
    relax(p1, q0, 0, fld, PB, SRC0, tiles)
    def pass_5(t):
        for k in range(4):
            put_mobility(here(fld, SB + k, t), k, t, f0, d0)

    over(tiles, pass_5)

    def finish_first(moved, k, t):
        put(s1, k, t, moved)
        put_mobility(moved, k, t, f1, d1)

    transport(p1, fld, SB, f0, 0, fup0, dp1, finish_first)
    relax(q1, p1, 0, p1, 0, SRC1, tiles)
    relax(p2, q1, 0, p1, 0, SRC1, tiles)

    def finish_second(moved, k, t):
        miss = here(dense.at[CNT], k, t) * moved - here(dense.at[OS1], k, t)
        put(sig2, k, t, miss)
        put(psi2, k, t, miss * here(per, k, t))

    transport(p2, s1, 0, f1, 1, fup1, dp2, finish_second)

    def pass_6(t):
        below_h = below_r = None
        for k in range(4):
            psi = here(psi2, k, t)
            phi_x = (down(psi2, k, t) - psi) * here(fld, XB + k, t)
            phi_y = (right(psi) - psi) * here(fld, YB + k, t)
            h_x = phi_x * here(fup1, k, t)
            h_y = phi_y * here(fup1, 4 + k, t)
            k_x = phi_x * here(dp2, k, t)
            k_y = phi_y * here(dp2, 4 + k, t)
            s_x = jnp.where(bit(k, t, 3), k_x, 0.0)
            s_y = jnp.where(bit(k, t, 4), k_y, 0.0)
            put(flux, k, t, h_x)
            put(rest, k, t, k_x - s_x)
            press = (h_x - above(flux, k, t)) + (h_y - left(h_y))
            satur = (s_x + above(rest, k, t)) + (s_y + left(k_y - s_y))
            if k > 0:
                press = press - below_h
                satur = satur + below_r
            if k < 3:
                phi_z = (here(psi2, k + 1, t) - psi) * here(fld, ZB + k, t)
                below_h = phi_z * here(fup1, 8 + k, t)
                k_z = phi_z * here(dp2, 8 + k, t)
                s_z = jnp.where(bit(k, t, 5), k_z, 0.0)
                below_r = k_z - s_z
                press = press + below_h
                satur = satur + s_z
            count = here(dense.at[CNT], k, t)
            press = press + (count * here(p2, k, t) - here(dense.at[OP1], k, t))
            put(mup2, k, t, press * here(rcp, k, t))
            sigma = here(sig2, k, t) + satur * here(d1, k, t)
            sigma = sigma + (count * here(s1, k, t) - here(dense.at[OS0], k, t))
            put(psi1, k, t, sigma * here(per, k, t))

    over(tiles, pass_6)

    def pass_7(t):
        for k in range(4):
            put(muq1, k, t, neighbours(mup2, 0, k, t) * here(rcp, k, t))

    over(tiles, pass_7)

    def pass_8(t):
        below_h = None
        for k in range(4):
            psi = here(psi1, k, t)
            h_x = (down(psi1, k, t) - psi) * here(fld, XB + k, t) * here(fup0, k, t)
            h_y = (right(psi) - psi) * here(fld, YB + k, t) * here(fup0, 4 + k, t)
            put(flux, k, t, h_x)
            press = (h_x - above(flux, k, t)) + (h_y - left(h_y))
            if k > 0:
                press = press - below_h
            if k < 3:
                below_h = (here(psi1, k + 1, t) - psi) * here(fld, ZB + k, t) * here(fup0, 8 + k, t)
                press = press + below_h
            count = here(dense.at[CNT], k, t)
            press = press + (count * here(p1, k, t) - here(dense.at[OP0], k, t))
            press = press + here(fld, VB + k, t) * (here(mup2, k, t) + here(muq1, k, t))
            press = press + neighbours(muq1, 0, k, t)
            put(mup1, k, t, press * here(rcp, k, t))

    over(tiles, pass_8)

    def pass_9(t):
        for k in range(4):
            put(muq0, k, t, neighbours(mup1, 0, k, t) * here(rcp, k, t))

    over(range(2, 5), pass_9)

    stages = (
        (mup2, q1, 0, p2, 0),
        (muq1, p1, 0, q1, 0),
        (mup1, q0, 0, p1, 0),
        (muq0, fld, PB, q0, 0),
    )
    for t in range(2, 4):
        for k in range(4):
            sum_x = sum_y = sum_z = 0.0
            for psi, fup, dp in ((psi2, fup1, dp2), (psi1, fup0, dp1)):
                mid = here(psi, k, t)
                sum_x = sum_x + (down(psi, k, t) - mid) * here(fup, k, t) * here(dp, k, t)
                sum_y = sum_y + (right(mid) - mid) * here(fup, 4 + k, t) * here(dp, 4 + k, t)
                if k < 3:
                    sum_z = sum_z + (here(psi, k + 1, t) - mid) * here(fup, 8 + k, t) * here(dp, 8 + k, t)
            for mu, value, base, out, out_base in stages:
                mu_c, v_c, o_c = here(mu, k, t), here(value, base + k, t), here(out, out_base + k, t)
                mu_d, v_d, o_d = down(mu, k, t), down(value, base + k, t), down(out, out_base + k, t)
                sum_x = sum_x + (mu_c * (v_d - o_c) + mu_d * (v_c - o_d))
                sum_y = sum_y + (mu_c * (right(v_c) - o_c) + right(mu_c) * (v_c - right(o_c)))
                if k < 3:
                    mu_u = here(mu, k + 1, t)
                    v_u = here(value, base + k + 1, t)
                    o_u = here(out, out_base + k + 1, t)
                    sum_z = sum_z + (mu_c * (v_u - o_c) + mu_u * (v_c - o_u))
            emit_x(k, t, jnp.where(here(fld, XB + k, t) == 0.0, 0.0, sum_x))
            emit_y(k, t, jnp.where(here(fld, YB + k, t) == 0.0, 0.0, sum_y))
            if k < 3:
                emit_z(k, t, sum_z)
        if tile_done is not None:
            tile_done(t)


PLACES = (
    (("p", 7), ("tx", 7)),
    (("p", 40), ("tx", 40)),
    (("ty", 40), ("tz", 40)),
    (("pv", 40), ("p", 41)),
)


def put_beyond(fld, value, places):
    for block, (name, row) in enumerate(places):
        first, layers = GROUPS[name]
        for layer in range(layers):
            k = 4 * (layer & 1) + 2 * block + layer // 2
            fld[first + layer, row : row + 1, :] = value[k : k + 1]


def model_center(own, row_far, row_near, grads, edge, edge_dense, fld, dense, upi, *scratch):
    low, high = sorted_ends("gx", row_far, row_near)
    lane = lanes()

    early = lane < LATE

    def edge_of(value):
        return jnp.where(early, pltpu.roll(value, HALO, 1), value)

    for g in range(COUNT):
        for k, block in enumerate((low(g), own[g, 0:8, :], own[g, 8:16, :], high(g))):
            rows = slice(8 + 8 * k, 16 + 8 * k)
            fld[g, rows, :] = block
            edge[g, rows, :] = edge_of(block)
            if g >= GROUPS["up"][0]:
                upi[g - GROUPS["up"][0], rows, :] = block.astype(jnp.int32)
    for value, places in zip([low(COUNT)] + [high(COUNT + k) for k in range(3)], PLACES):
        for out, rows in ((fld, value), (edge, edge_of(value))):
            put_beyond(out, rows, places)

    info = jnp.concatenate(
        [own[COUNT, 0:8, 0:64], low(COUNT + 3)[:, 0:64], high(COUNT + 3)[:, 0:64]], axis=1
    )
    block = list_block(info)
    base = jnp.where(block == 0, 16, jnp.where(block == 1, 0, 32))

    def write_center(number, total):
        for k in range(4):
            dense[number, k, 8:48, :] = total[40 * k : 40 * k + 40]

    def write_edge(number, total):
        for k in range(4):
            edge_dense[number, k, 8:48, :] = total[40 * k : 40 * k + 40]

    def edge_lane(layer, col):
        return jnp.where(col < LATE - HALO, col + HALO, jnp.where(col >= LATE, col, -1))

    spread_wells(info, base, lambda layer: layer * 40, 160, lambda layer, col: col, write_center)
    spread_wells(info, base, lambda layer: layer * 40, 160, edge_lane, write_edge)

    def emit(first):
        def write(k, t, value):
            grads[first + k, 8 * t - 16 : 8 * t - 8, :] = value

        return write

    simulate(fld, dense, upi, scratch, emit(0), emit(4), emit(8))


def model_edge(
    col_far, col_near, edge, edge_dense, center, grad_x, grad_y, grad_z, first_rows, last_rows, sems, fld, dense, upi,
    *scratch
):
    before, after = sorted_ends("gy", col_far, col_near)
    odd = lax.axis_index("gy") & 1
    lane = lanes()
    beside = lane < HALO
    for name, (start, width) in SLOTS.items():
        far_cols = in_slot(lane, start, 1 - odd, width)
        first, layers = GROUPS[name]
        for layer in range(layers):
            for k, at in enumerate((PACKED, 0, 2, PACKED + 2)):
                rows = slice(8 + 8 * k, 16 + 8 * k)
                both = jnp.where(far_cols, col_far[at + layer // 2], col_near[at + layer // 2])
                both = pltpu.roll(both, (64 * (layer & 1) - start) % 128, 1)
                block = jnp.where(beside, both, edge[first + layer, rows, :])
                if name == "up":
                    upi[layer, rows, :] = block.astype(jnp.int32)
                else:
                    fld[first + layer, rows, :] = block
    for number, places in enumerate(PLACES):
        for half in range(2):
            start = 64 + SLOT * (2 * (number // 2) + half)
            mask = ((lane - start - SLOT * (1 - odd)) & 127) < SLOT
            both = jnp.where(mask, col_far[2 * PACKED + 1], col_near[2 * PACKED + 1])
            value = pltpu.roll(both, 128 - start, 1)
            for block, (name, row) in enumerate(places):
                for pair in range(2):
                    layer = 2 * pair + half
                    if layer < GROUPS[name][1]:
                        k = 4 * (number & 1) + 2 * block + pair
                        at = (GROUPS[name][0] + layer, slice(row, row + 1), slice(None))
                        fld[at] = jnp.where(beside[0:1], value[k : k + 1], edge[at])
    first, second = 2 * PACKED, 2 * PACKED + 1
    own_lists = [before(first)[:, 0:64], after(first)[:, 0:64]]
    low_lists = [before(first)[:, 64:128], after(first)[:, 64:128]]
    high_lists = [before(second)[:, 0:64], after(second)[:, 0:64]]
    info = jnp.concatenate(own_lists + low_lists + high_lists, axis=1)
    block = list_block(info)
    base = jnp.where(block < 2, 16, jnp.where(block < 4, 0, 32))
    ahead = (block & 1) == 1

    def beside_lane(layer, col):
        last = jnp.where(col >= 128 - SLOT, 32 * layer + col - 128 + 2 * SLOT, -1)
        return jnp.where(ahead, jnp.where(col < SLOT, 32 * layer + col, -1), last)

    def write_beside(number, total):
        for t in range(1, 6):
            rows = slice(8 * t, 8 * t + 8)
            for k in range(4):
                value = total[8 * t - 8 : 8 * t]
                value = pltpu.roll(value, 128 - 32 * k, 1) if k else value
                dense[number, k, rows, :] = jnp.where(beside, value, edge_dense[number, k, rows, :])

    spread_wells(info, base, lambda layer: 0, 48, beside_lane, write_beside)

    def emit(group):
        def write(k, t, value):
            rows = slice(8 * t - 16, 8 * t - 8)
            value = jnp.where(lane < 64, pltpu.roll(value, 128 - HALO, 1), value)
            inner = (lane >= SLOT - 1) & (lane < 128 - SLOT)
            (first_rows, last_rows)[t - 2][group + k] = jnp.where(inner, center[group + k, rows, :], value)

        return write

    def send(t):
        copies = []
        for k, (out, group) in enumerate(((grad_x, 0), (grad_y, 4), (grad_z, 8))):
            source = (first_rows, last_rows)[t - 2].at[pl.ds(group, out.shape[0])]
            target = out.at[:, pl.ds(8 * t - 16, 8), :]
            copies.append(pltpu.make_async_copy(source, target, sems.at[3 * (t - 2) + k]))
            copies[-1].start()
        return copies

    copies = []
    simulate(fld, dense, upi, scratch, emit(0), emit(4), emit(8), lambda t: copies.extend(send(t)), True)
    for copy in copies:
        copy.wait()


def swapped(value, axis, first):
    count = lax.axis_size(axis)
    pairs = []
    for i in range(first, count - 1, 2):
        pairs += [(i, i + 1), (i + 1, i)]
    return lax.ppermute(value, axis, pairs)


def on_device(p, s, tx, ty, tz, pv, up, cell, rate, plan, observed):
    f32 = jnp.float32

    def shape(*dims):
        return jax.ShapeDtypeStruct(dims, f32)

    limit = pltpu.CompilerParams(vmem_limit_bytes=24 * 1024 * 1024)
    inputs = (p, s, tx, ty, tz, pv, up, cell, rate, plan, observed)
    inputs = [pltpu.with_memory_space_constraint(value, pltpu.HBM) for value in inputs]
    strip = shape(COUNT + 4, 8, 128)
    own, far, near = pl.pallas_call(
        pack_rows,
        out_shape=(shape(COUNT + 1, 16, 128), strip, strip),
        in_specs=[pl.BlockSpec(memory_space=pltpu.HBM)] * len(inputs),
        scratch_shapes=[pltpu.VMEM(value.shape, value.dtype) for value in inputs[6:]]
        + [pltpu.SemaphoreType.DMA((len(inputs),))],
        compiler_params=limit,
        name="pack_rows",
    )(*inputs)
    row_far = swapped(far, "gx", 1)
    row_near = swapped(near, "gx", 0)
    hide = pl.CostEstimate(flops=10**11, bytes_accessed=1 << 28, transcendentals=0)
    strip = shape(PACKED, 8, 128)
    own_far, own_near = pl.pallas_call(
        pack_own,
        out_shape=(strip, strip),
        compiler_params=limit,
        cost_estimate=hide,
        name="pack_own",
    )(own)
    strip = shape(2 * PACKED + 2, 8, 128)
    far, near = pl.pallas_call(
        pack_cols,
        out_shape=(strip, strip),
        compiler_params=limit,
        name="pack_cols",
    )(own, own_far, own_near, row_far, row_near)
    col_far = swapped(far, "gy", 1)
    col_near = swapped(near, "gy", 0)
    scratch = [pltpu.VMEM((COUNT, ROWS, 128), f32), pltpu.VMEM((7, 4, ROWS, 128), f32)]
    scratch += [pltpu.VMEM((4, ROWS, 128), jnp.int32)]
    scratch += [pltpu.VMEM((count, ROWS, 128), f32) for count in SCRATCH]
    center, edge, edge_dense = pl.pallas_call(
        model_center,
        out_shape=(shape(11, 16, 128), shape(COUNT, ROWS, 128), shape(7, 4, ROWS, 128)),
        scratch_shapes=scratch,
        compiler_params=limit,
        cost_estimate=hide,
        name="model_center",
    )(own, row_far, row_near)
    return pl.pallas_call(
        model_edge,
        out_shape=(shape(*tx.shape), shape(*ty.shape), shape(*tz.shape)),
        out_specs=(pl.BlockSpec(memory_space=pltpu.HBM),) * 3,
        scratch_shapes=[pltpu.VMEM((11, 8, 128), f32)] * 2 + [pltpu.SemaphoreType.DMA((6,))] + scratch,
        compiler_params=limit,
        name="model_edge",
    )(col_far, col_near, edge, edge_dense, center)


def solution(mesh):
    cells = P(None, "gx", "gy")
    in_specs = (cells,) * 7 + (
        P("gx", "gy", None),
        P("gx", "gy", None),
        P(None, "gx", "gy", None),
        P(None, None, "gx", "gy", None),
    )
    return jax.shard_map(
        on_device, mesh=mesh, in_specs=in_specs, out_specs=(cells,) * 3, check_vma=False
    )
```

```python
import jax
import jax.numpy as jnp
from jax import lax
from jax.experimental import pallas as pl
from jax.experimental.pallas import tpu as pltpu
from jax.sharding import PartitionSpec as P

time_step = 0.05

GROUPS = {"p": (0, 4), "s": (4, 4), "tx": (8, 4), "ty": (12, 4), "tz": (16, 3), "pv": (19, 4), "up": (23, 4)}
ORDER = ("p", "s", "tx", "ty", "tz", "pv", "up")
COUNT = 27
SLOT = 10
SLOTS = {"p": (0, 10), "tx": (10, 9), "ty": (19, 9), "tz": (28, 9), "pv": (37, 9), "s": (46, 7), "up": (53, 6)}
PACKED = 4
ROWS = 56
HALO = 2 * SLOT
LATE = 99


FIELDS = 11


def pack_rows(*refs):
    p, s, tx, ty, tz, pv, up, cell, rate, plan, observed = refs[:FIELDS]
    own, far, near, upi, cells, rates, plans, seen, sems = refs[FIELDS:]
    targets = [own.at[pl.ds(*GROUPS[name])] for name in ORDER[:6]] + [upi, cells, rates, plans, seen]
    copies = [
        pltpu.make_async_copy(source, target, sems.at[k])
        for k, (source, target) in enumerate(zip(refs[:FIELDS], targets))
    ]
    for copy in copies:
        copy.start()
    odd = lax.axis_index("gx") & 1
    for name, copy in zip(ORDER, copies):
        copy.wait()
        first, layers = GROUPS[name]
        for layer in range(layers):
            g = first + layer
            if name == "up":
                own[g] = upi[layer].astype(jnp.float32)
            far[g] = own[g, pl.ds(pl.multiple_of(8 * odd, 8), 8), :]
            near[g] = own[g, pl.ds(pl.multiple_of(8 - 8 * odd, 8), 8), :]
    for copy in copies[len(ORDER) :]:
        copy.wait()
    own[COUNT] = jnp.zeros((16, 128), jnp.float32)
    own[COUNT, 0:1, 0:64] = cells[0].astype(jnp.float32)
    own[COUNT, 1:2, 0:64] = rates[0]
    for n in range(2):
        own[COUNT, 2 + n : 3 + n, 0:64] = plans[n, 0].astype(jnp.float32)
        for k in range(2):
            row = 4 + 2 * n + k
            own[COUNT, row : row + 1, 0:64] = seen[n, k, 0]
    base = {name: GROUPS[name][0] for name in ORDER}

    blank = jnp.zeros((1, 128), jnp.float32)

    def gathered(*places):
        rows = []
        for layer in (0, 2, 1, 3):
            for name, row in places:
                there = layer < GROUPS[name][1]
                rows.append(own[base[name] + layer, row : row + 1, :] if there else blank)
        return jnp.concatenate([rows[k] for k in (0, 2, 1, 3, 4, 6, 5, 7)], axis=0)

    for_next = [gathered(("p", 7), ("tx", 7))]
    for_next += [jnp.zeros((8, 128), jnp.float32)] * 2
    for_prev = [
        gathered(("p", 8), ("tx", 8)),
        gathered(("ty", 8), ("tz", 8)),
        gathered(("pv", 8), ("p", 9)),
    ]
    for k in range(3):
        far[COUNT + k] = jnp.where(odd == 1, for_next[k], for_prev[k])
        near[COUNT + k] = jnp.where(odd == 1, for_prev[k], for_next[k])
    far[COUNT + 3] = own[COUNT, 0:8, :]
    near[COUNT + 3] = own[COUNT, 0:8, :]


def lanes():
    return lax.broadcasted_iota(jnp.int32, (8, 128), 1)


def in_slot(lane, start, ends, width):
    return ((lane - start - ends * (2 * SLOT - width)) & 63) < width


def sorted_ends(axis, far, near):
    odd = (lax.axis_index(axis) & 1) == 1

    def before(g):
        return jnp.where(odd, near[g], far[g])

    def after(g):
        return jnp.where(odd, far[g], near[g])

    return before, after


def pack_pairs(block, far, near, at):
    odd = lax.axis_index("gy") & 1
    lane = lanes()
    zero = jnp.zeros((8, 128), jnp.float32)
    for pair in range(2):
        ones, twos = {}, {}
        for name in SLOTS:
            first, layers = GROUPS[name]
            ones[name] = block(first + 2 * pair)
            there = 2 * pair + 1 < layers
            twos[name] = pltpu.roll(block(first + 2 * pair + 1), 64, 1) if there else zero
        for out, ends in ((far, odd), (near, 1 - odd)):
            straight = ((lane >> 6) ^ ends) == 0
            part = zero
            for name, (start, width) in SLOTS.items():
                both = jnp.where(straight, ones[name], twos[name])
                both = pltpu.roll(both, start + 2 * SLOT * ends, 1)
                part = jnp.where(in_slot(lane, start, ends, width), both, part)
            out[at + pair] = part


def extra_pair(one, two):
    row = lax.broadcasted_iota(jnp.int32, (8, 128), 0)
    return jnp.where(row < 4, one, pltpu.roll(two, 4, 0)), jnp.where(row < 4, pltpu.roll(one, 4, 0), two)


def pack_own(own, far, near):
    for tile in range(2):
        rows = slice(8 * tile, 8 * tile + 8)
        pack_pairs(lambda g: own[g, rows, :], far, near, 2 * tile)


def pack_cols(own, own_far, own_near, row_far, row_near, far, near):
    low, high = sorted_ends("gx", row_far, row_near)
    for out, part in ((far, own_far), (near, own_near)):
        for at in range(PACKED):
            out[at] = part[at]
    pack_pairs(low, far, near, PACKED)
    pack_pairs(high, far, near, PACKED + 2)
    odd = lax.axis_index("gy") & 1
    lane = lanes()
    both = jnp.where(lane < 64, own[COUNT, 0:8, :], pltpu.roll(low(COUNT + 3), 64, 1))
    extras = extra_pair(low(COUNT), high(COUNT)) + extra_pair(high(COUNT + 1), high(COUNT + 2))
    for out, ends in ((far, odd), (near, 1 - odd)):
        out[2 * PACKED] = both
        part = high(COUNT + 3)
        for k, value in enumerate(extras):
            start = 64 + SLOT * k
            mask = ((lane - start - SLOT * ends) & 127) < SLOT
            part = jnp.where(mask, pltpu.roll(value, start + 2 * SLOT * ends, 1), part)
        out[2 * PACKED + 1] = part


def split3(value):
    hi = value.astype(jnp.bfloat16).astype(jnp.float32)
    rest = value - hi
    mid = rest.astype(jnp.bfloat16).astype(jnp.float32)
    return hi, mid, rest - mid


SRC0, SRC1, OP0, OS0, OP1, OS1, CNT = range(7)


def spread_wells(info, base, rows_of, count, to_spot, write):
    width = info.shape[1]
    cell = info[0:1].astype(jnp.int32)
    layer = lax.shift_right_logical(cell, 11)
    place = (lax.shift_right_logical(cell, 7) & 15) + base
    target = jnp.where(place >= 8, rows_of(layer) + place - 8, -1)
    spot = to_spot(layer, cell & 127)
    hit = lax.broadcasted_iota(jnp.int32, (count, width), 0) == target
    hit = jnp.where(hit, 1.0, 0.0).astype(jnp.bfloat16)
    lane = lax.broadcasted_iota(jnp.int32, (128, width), 0)
    to_lane = jnp.where(lane == spot, 1.0, 0.0).astype(jnp.bfloat16)
    rate = info[1:2] * 0.5
    values = [rate * info[2:3], rate * info[3:4]] + [info[k : k + 1] for k in range(4, 8)]
    for number, value in enumerate(values):
        total = None
        for part in split3(value):
            part = jnp.broadcast_to(part, (16, width)).astype(jnp.bfloat16)
            left = hit * jnp.concatenate([part] * (count // 16), axis=0)
            term = dot(left, to_lane)
            total = term if total is None else total + term
        write(number, total)
    write(CNT, dot(hit, to_lane))


def dot(left, right):
    return lax.dot_general(left, right, (((1,), (1,)), ((), ())), preferred_element_type=jnp.float32)


def list_block(info):
    return lax.shift_right_logical(lax.broadcasted_iota(jnp.int32, (1, info.shape[1]), 1), 6)


SCRATCH = (4,) * 12 + (11,) * 4 + (4,) * 13


def simulate(fld, dense, upi, scratch, emit_x, emit_y, emit_z, tile_done=None):
    (rcp, tym, per, q0, p1, q1, p2, f0, d0, s1, f1, d1, fup0, fup1, dp1, dp2,
     sig2, psi2, psi1, mup2, muq1, mup1, muq0, flux, rest,
     west0, west1, drop1, drop2, upl) = scratch
    PB, SB, XB, YB, ZB, VB = (GROUPS[name][0] for name in ORDER[:6])

    def here(ref, k, t):
        return ref[k, 8 * t : 8 * t + 8, :]

    def down(ref, k, t):
        return ref[k, 8 * t + 1 : 8 * t + 9, :]

    def above(ref, k, t):
        return ref[k, 8 * t - 1 : 8 * t + 7, :]

    def put(ref, k, t, value):
        ref[k, 8 * t : 8 * t + 8, :] = value

    def right(value):
        return pltpu.roll(value, 127, 1)

    def left(value):
        return pltpu.roll(value, 1, 1)

    for k in range(4):
        for t in range(1, 6):
            beyond = right(here(fld, VB + k, t))
            put(fld, YB + k, t, jnp.where(beyond == 0.0, 0.0, here(fld, YB + k, t)))
        last = slice(31, 32)
        fld[XB + k, last, :] = jnp.where(fld[VB + k, 32:33, :] == 0.0, 0.0, fld[XB + k, last, :])
    for t in range(1, 6):
        for k in range(4):
            volume = here(fld, VB + k, t)
            volume = jnp.where(volume == 0.0, 1.0, volume)
            put(fld, VB + k, t, volume)
            put(per, k, t, time_step * pl.reciprocal(volume))
            west = left(here(fld, YB + k, t))
            put(tym, k, t, west)
            put(upl, k, t, left(here(upi, k, t)))
            total = volume + (here(fld, XB + k, t) + above(fld, XB + k, t)) + (here(fld, YB + k, t) + west)
            if k < 3:
                total = total + here(fld, ZB + k, t)
            if k > 0:
                total = total + here(fld, ZB + k - 1, t)
            put(rcp, k, t, pl.reciprocal(total))

    def neighbours(ref, base, k, t):
        value = here(ref, base + k, t)
        total = here(fld, XB + k, t) * down(ref, base + k, t) + above(fld, XB + k, t) * above(ref, base + k, t)
        total = total + (here(fld, YB + k, t) * right(value) + here(tym, k, t) * left(value))
        if k < 3:
            total = total + here(fld, ZB + k, t) * here(ref, base + k + 1, t)
        if k > 0:
            total = total + here(fld, ZB + k - 1, t) * here(ref, base + k - 1, t)
        return total

    def relax(out, ref, base, old, old_base, source, tiles):
        for t in tiles:
            for k in range(4):
                total = here(fld, VB + k, t) * here(old, old_base + k, t) + here(dense.at[source], k, t)
                put(out, k, t, (total + neighbours(ref, base, k, t)) * here(rcp, k, t))

    def put_mobility(value, k, t, mobile, slope):
        rest_of = 1.0 - value
        wetted = value * value
        inverse = pl.reciprocal(wetted + 0.5 * rest_of * rest_of)
        put(mobile, k, t, wetted * inverse)
        put(slope, k, t, value * rest_of * (inverse * inverse))

    def bit(k, t, number):
        return (here(upi, k, t) & (1 << number)) != 0

    def bit_left(k, t, number):
        return (here(upl, k, t) & (1 << number)) != 0

    def transport(pressure, sat, sat_base, mobile, n, fup, dp, wests, drops, finish):
        for t in range(1, 5):
            below = None
            for k in range(4):
                mob = here(mobile, k, t)
                pres = here(pressure, k, t)
                drop_x = pres - down(pressure, k, t)
                drop_y = pres - right(pres)
                up_x = jnp.where(bit(k, t, 3 * n), mob, down(mobile, k, t))
                up_y = jnp.where(bit(k, t, 3 * n + 1), mob, right(mob))
                put(fup, k, t, up_x)
                put(fup, 4 + k, t, up_y)
                put(dp, k, t, drop_x)
                put(dp, 4 + k, t, drop_y)
                flux_x = here(fld, XB + k, t) * up_x * drop_x
                flux_y = here(fld, YB + k, t) * up_y * drop_y
                put(flux, k, t, flux_x)
                west = jnp.where(bit_left(k, t, 3 * n + 1), left(mob), mob)
                drop_w = left(pres) - pres
                put(wests, k, t, west)
                put(drops, k, t, drop_w)
                net = (flux_x - above(flux, k, t)) + (flux_y - here(tym, k, t) * west * drop_w)
                if k > 0:
                    net = net - below
                if k < 3:
                    drop_z = pres - here(pressure, k + 1, t)
                    up_z = jnp.where(bit(k, t, 3 * n + 2), mob, here(mobile, k + 1, t))
                    put(fup, 8 + k, t, up_z)
                    put(dp, 8 + k, t, drop_z)
                    below = here(fld, ZB + k, t) * up_z * drop_z
                    net = net + below
                finish(here(sat, sat_base + k, t) - net * here(per, k, t), k, t)

    tiles = range(1, 5)
    relax(q0, fld, PB, fld, PB, SRC0, range(1, 6))
    relax(p1, q0, 0, fld, PB, SRC0, tiles)
    for t in tiles:
        for k in range(4):
            put_mobility(here(fld, SB + k, t), k, t, f0, d0)

    def finish_first(moved, k, t):
        put(s1, k, t, moved)
        put_mobility(moved, k, t, f1, d1)

    transport(p1, fld, SB, f0, 0, fup0, dp1, west0, drop1, finish_first)
    relax(q1, p1, 0, p1, 0, SRC1, tiles)
    relax(p2, q1, 0, p1, 0, SRC1, tiles)

    def finish_second(moved, k, t):
        miss = here(dense.at[CNT], k, t) * moved - here(dense.at[OS1], k, t)
        put(sig2, k, t, miss)
        put(psi2, k, t, miss * here(per, k, t))

    transport(p2, s1, 0, f1, 1, fup1, dp2, west1, drop2, finish_second)

    for t in tiles:
        below_h = below_r = None
        for k in range(4):
            psi = here(psi2, k, t)
            phi_x = (down(psi2, k, t) - psi) * here(fld, XB + k, t)
            phi_y = (right(psi) - psi) * here(fld, YB + k, t)
            h_x = phi_x * here(fup1, k, t)
            h_y = phi_y * here(fup1, 4 + k, t)
            k_x = phi_x * here(dp2, k, t)
            k_y = phi_y * here(dp2, 4 + k, t)
            s_x = jnp.where(bit(k, t, 3), k_x, 0.0)
            s_y = jnp.where(bit(k, t, 4), k_y, 0.0)
            put(flux, k, t, h_x)
            put(rest, k, t, k_x - s_x)
            phi_w = (psi - left(psi)) * here(tym, k, t)
            r_w = jnp.where(bit_left(k, t, 4), 0.0, phi_w * here(drop2, k, t))
            press = (h_x - above(flux, k, t)) + (h_y - phi_w * here(west1, k, t))
            satur = (s_x + above(rest, k, t)) + (s_y + r_w)
            if k > 0:
                press = press - below_h
                satur = satur + below_r
            if k < 3:
                phi_z = (here(psi2, k + 1, t) - psi) * here(fld, ZB + k, t)
                below_h = phi_z * here(fup1, 8 + k, t)
                k_z = phi_z * here(dp2, 8 + k, t)
                s_z = jnp.where(bit(k, t, 5), k_z, 0.0)
                below_r = k_z - s_z
                press = press + below_h
                satur = satur + s_z
            count = here(dense.at[CNT], k, t)
            press = press + (count * here(p2, k, t) - here(dense.at[OP1], k, t))
            put(mup2, k, t, press * here(rcp, k, t))
            sigma = here(sig2, k, t) + satur * here(d1, k, t)
            sigma = sigma + (count * here(s1, k, t) - here(dense.at[OS0], k, t))
            put(psi1, k, t, sigma * here(per, k, t))

    for t in tiles:
        for k in range(4):
            put(muq1, k, t, neighbours(mup2, 0, k, t) * here(rcp, k, t))

    for t in tiles:
        below_h = None
        for k in range(4):
            psi = here(psi1, k, t)
            h_x = (down(psi1, k, t) - psi) * here(fld, XB + k, t) * here(fup0, k, t)
            h_y = (right(psi) - psi) * here(fld, YB + k, t) * here(fup0, 4 + k, t)
            put(flux, k, t, h_x)
            h_w = (psi - left(psi)) * here(tym, k, t) * here(west0, k, t)
            press = (h_x - above(flux, k, t)) + (h_y - h_w)
            if k > 0:
                press = press - below_h
            if k < 3:
                below_h = (here(psi1, k + 1, t) - psi) * here(fld, ZB + k, t) * here(fup0, 8 + k, t)
                press = press + below_h
            count = here(dense.at[CNT], k, t)
            press = press + (count * here(p1, k, t) - here(dense.at[OP0], k, t))
            press = press + here(fld, VB + k, t) * (here(mup2, k, t) + here(muq1, k, t))
            press = press + neighbours(muq1, 0, k, t)
            put(mup1, k, t, press * here(rcp, k, t))

    for t in range(2, 5):
        for k in range(4):
            put(muq0, k, t, neighbours(mup1, 0, k, t) * here(rcp, k, t))

    stages = (
        (mup2, q1, 0, p2, 0),
        (muq1, p1, 0, q1, 0),
        (mup1, q0, 0, p1, 0),
        (muq0, fld, PB, q0, 0),
    )
    for t in range(2, 4):
        for k in range(4):
            sum_x = sum_y = sum_z = 0.0
            for psi, fup, dp in ((psi2, fup1, dp2), (psi1, fup0, dp1)):
                mid = here(psi, k, t)
                sum_x = sum_x + (down(psi, k, t) - mid) * here(fup, k, t) * here(dp, k, t)
                sum_y = sum_y + (right(mid) - mid) * here(fup, 4 + k, t) * here(dp, 4 + k, t)
                if k < 3:
                    sum_z = sum_z + (here(psi, k + 1, t) - mid) * here(fup, 8 + k, t) * here(dp, 8 + k, t)
            for mu, value, base, out, out_base in stages:
                mu_c, v_c, o_c = here(mu, k, t), here(value, base + k, t), here(out, out_base + k, t)
                mu_d, v_d, o_d = down(mu, k, t), down(value, base + k, t), down(out, out_base + k, t)
                sum_x = sum_x + (mu_c * (v_d - o_c) + mu_d * (v_c - o_d))
                sum_y = sum_y + (mu_c * (right(v_c) - o_c) + right(mu_c) * (v_c - right(o_c)))
                if k < 3:
                    mu_u = here(mu, k + 1, t)
                    v_u = here(value, base + k + 1, t)
                    o_u = here(out, out_base + k + 1, t)
                    sum_z = sum_z + (mu_c * (v_u - o_c) + mu_u * (v_c - o_u))
            emit_x(k, t, jnp.where(here(fld, XB + k, t) == 0.0, 0.0, sum_x))
            emit_y(k, t, jnp.where(here(fld, YB + k, t) == 0.0, 0.0, sum_y))
            if k < 3:
                emit_z(k, t, sum_z)
        if tile_done is not None:
            tile_done(t)


PLACES = (
    (("p", 7), ("tx", 7)),
    (("p", 40), ("tx", 40)),
    (("ty", 40), ("tz", 40)),
    (("pv", 40), ("p", 41)),
)


def put_beyond(fld, value, places):
    for block, (name, row) in enumerate(places):
        first, layers = GROUPS[name]
        for layer in range(layers):
            k = 4 * (layer & 1) + 2 * block + layer // 2
            fld[first + layer, row : row + 1, :] = value[k : k + 1]


def model_center(own, row_far, row_near, grads, edge, edge_dense, fld, dense, upi, *scratch):
    low, high = sorted_ends("gx", row_far, row_near)
    lane = lanes()

    early = lane < LATE

    def edge_of(value):
        return jnp.where(early, pltpu.roll(value, HALO, 1), value)

    for g in range(COUNT):
        for k, block in enumerate((low(g), own[g, 0:8, :], own[g, 8:16, :], high(g))):
            rows = slice(8 + 8 * k, 16 + 8 * k)
            fld[g, rows, :] = block
            edge[g, rows, :] = edge_of(block)
            if g >= GROUPS["up"][0]:
                upi[g - GROUPS["up"][0], rows, :] = block.astype(jnp.int32)
    for value, places in zip([low(COUNT)] + [high(COUNT + k) for k in range(3)], PLACES):
        for out, rows in ((fld, value), (edge, edge_of(value))):
            put_beyond(out, rows, places)

    info = jnp.concatenate(
        [own[COUNT, 0:8, 0:64], low(COUNT + 3)[:, 0:64], high(COUNT + 3)[:, 0:64]], axis=1
    )
    block = list_block(info)
    base = jnp.where(block == 0, 16, jnp.where(block == 1, 0, 32))

    def write_center(number, total):
        for k in range(4):
            dense[number, k, 8:48, :] = total[40 * k : 40 * k + 40]

    def write_edge(number, total):
        for k in range(4):
            edge_dense[number, k, 8:48, :] = total[40 * k : 40 * k + 40]

    def edge_lane(layer, col):
        return jnp.where(col < LATE - HALO, col + HALO, jnp.where(col >= LATE, col, -1))

    spread_wells(info, base, lambda layer: layer * 40, 160, lambda layer, col: col, write_center)
    spread_wells(info, base, lambda layer: layer * 40, 160, edge_lane, write_edge)

    def emit(first):
        def write(k, t, value):
            grads[first + k, 8 * t - 16 : 8 * t - 8, :] = value

        return write

    simulate(fld, dense, upi, scratch, emit(0), emit(4), emit(8))


def model_edge(
    col_far, col_near, edge, edge_dense, center, grad_x, grad_y, grad_z, first_rows, last_rows, sems, fld, dense, upi,
    *scratch
):
    before, after = sorted_ends("gy", col_far, col_near)
    odd = lax.axis_index("gy") & 1
    lane = lanes()
    beside = lane < HALO
    for name, (start, width) in SLOTS.items():
        far_cols = in_slot(lane, start, 1 - odd, width)
        first, layers = GROUPS[name]
        for layer in range(layers):
            for k, at in enumerate((PACKED, 0, 2, PACKED + 2)):
                rows = slice(8 + 8 * k, 16 + 8 * k)
                both = jnp.where(far_cols, col_far[at + layer // 2], col_near[at + layer // 2])
                both = pltpu.roll(both, (64 * (layer & 1) - start) % 128, 1)
                block = jnp.where(beside, both, edge[first + layer, rows, :])
                if name == "up":
                    upi[layer, rows, :] = block.astype(jnp.int32)
                else:
                    fld[first + layer, rows, :] = block
    for number, places in enumerate(PLACES):
        for half in range(2):
            start = 64 + SLOT * (2 * (number // 2) + half)
            mask = ((lane - start - SLOT * (1 - odd)) & 127) < SLOT
            both = jnp.where(mask, col_far[2 * PACKED + 1], col_near[2 * PACKED + 1])
            value = pltpu.roll(both, 128 - start, 1)
            for block, (name, row) in enumerate(places):
                for pair in range(2):
                    layer = 2 * pair + half
                    if layer < GROUPS[name][1]:
                        k = 4 * (number & 1) + 2 * block + pair
                        at = (GROUPS[name][0] + layer, slice(row, row + 1), slice(None))
                        fld[at] = jnp.where(beside[0:1], value[k : k + 1], edge[at])
    first, second = 2 * PACKED, 2 * PACKED + 1
    own_lists = [before(first)[:, 0:64], after(first)[:, 0:64]]
    low_lists = [before(first)[:, 64:128], after(first)[:, 64:128]]
    high_lists = [before(second)[:, 0:64], after(second)[:, 0:64]]
    info = jnp.concatenate(own_lists + low_lists + high_lists, axis=1)
    block = list_block(info)
    base = jnp.where(block < 2, 16, jnp.where(block < 4, 0, 32))
    ahead = (block & 1) == 1

    def beside_lane(layer, col):
        last = jnp.where(col >= 128 - SLOT, 32 * layer + col - 128 + 2 * SLOT, -1)
        return jnp.where(ahead, jnp.where(col < SLOT, 32 * layer + col, -1), last)

    def write_beside(number, total):
        for t in range(1, 6):
            rows = slice(8 * t, 8 * t + 8)
            for k in range(4):
                value = total[8 * t - 8 : 8 * t]
                value = pltpu.roll(value, 128 - 32 * k, 1) if k else value
                dense[number, k, rows, :] = jnp.where(beside, value, edge_dense[number, k, rows, :])

    spread_wells(info, base, lambda layer: 0, 48, beside_lane, write_beside)

    def emit(group):
        def write(k, t, value):
            rows = slice(8 * t - 16, 8 * t - 8)
            value = jnp.where(lane < 64, pltpu.roll(value, 128 - HALO, 1), value)
            inner = (lane >= SLOT - 1) & (lane < 128 - SLOT)
            (first_rows, last_rows)[t - 2][group + k] = jnp.where(inner, center[group + k, rows, :], value)

        return write

    def send(t):
        copies = []
        for k, (out, group) in enumerate(((grad_x, 0), (grad_y, 4), (grad_z, 8))):
            source = (first_rows, last_rows)[t - 2].at[pl.ds(group, out.shape[0])]
            target = out.at[:, pl.ds(8 * t - 16, 8), :]
            copies.append(pltpu.make_async_copy(source, target, sems.at[3 * (t - 2) + k]))
            copies[-1].start()
        return copies

    copies = []
    simulate(fld, dense, upi, scratch, emit(0), emit(4), emit(8), lambda t: copies.extend(send(t)))
    for copy in copies:
        copy.wait()


def swapped(value, axis, first):
    count = lax.axis_size(axis)
    pairs = []
    for i in range(first, count - 1, 2):
        pairs += [(i, i + 1), (i + 1, i)]
    return lax.ppermute(value, axis, pairs)


def on_device(p, s, tx, ty, tz, pv, up, cell, rate, plan, observed):
    f32 = jnp.float32

    def shape(*dims):
        return jax.ShapeDtypeStruct(dims, f32)

    limit = pltpu.CompilerParams(vmem_limit_bytes=24 * 1024 * 1024)
    inputs = (p, s, tx, ty, tz, pv, up, cell, rate, plan, observed)
    inputs = [pltpu.with_memory_space_constraint(value, pltpu.HBM) for value in inputs]
    strip = shape(COUNT + 4, 8, 128)
    own, far, near = pl.pallas_call(
        pack_rows,
        out_shape=(shape(COUNT + 1, 16, 128), strip, strip),
        in_specs=[pl.BlockSpec(memory_space=pltpu.HBM)] * len(inputs),
        scratch_shapes=[pltpu.VMEM(value.shape, value.dtype) for value in inputs[6:]]
        + [pltpu.SemaphoreType.DMA((len(inputs),))],
        compiler_params=limit,
        name="pack_rows",
    )(*inputs)
    row_far = swapped(far, "gx", 1)
    row_near = swapped(near, "gx", 0)
    hide = pl.CostEstimate(flops=10**11, bytes_accessed=1 << 28, transcendentals=0)
    strip = shape(PACKED, 8, 128)
    own_far, own_near = pl.pallas_call(
        pack_own,
        out_shape=(strip, strip),
        compiler_params=limit,
        cost_estimate=hide,
        name="pack_own",
    )(own)
    strip = shape(2 * PACKED + 2, 8, 128)
    far, near = pl.pallas_call(
        pack_cols,
        out_shape=(strip, strip),
        compiler_params=limit,
        name="pack_cols",
    )(own, own_far, own_near, row_far, row_near)
    col_far = swapped(far, "gy", 1)
    col_near = swapped(near, "gy", 0)
    scratch = [pltpu.VMEM((COUNT, ROWS, 128), f32), pltpu.VMEM((7, 4, ROWS, 128), f32)]
    scratch += [pltpu.VMEM((4, ROWS, 128), jnp.int32)]
    scratch += [pltpu.VMEM((count, ROWS, 128), f32) for count in SCRATCH]
    scratch += [pltpu.VMEM((4, ROWS, 128), jnp.int32)]
    center, edge, edge_dense = pl.pallas_call(
        model_center,
        out_shape=(shape(11, 16, 128), shape(COUNT, ROWS, 128), shape(7, 4, ROWS, 128)),
        scratch_shapes=scratch,
        compiler_params=limit,
        cost_estimate=hide,
        name="model_center",
    )(own, row_far, row_near)
    return pl.pallas_call(
        model_edge,
        out_shape=(shape(*tx.shape), shape(*ty.shape), shape(*tz.shape)),
        out_specs=(pl.BlockSpec(memory_space=pltpu.HBM),) * 3,
        scratch_shapes=[pltpu.VMEM((11, 8, 128), f32)] * 2 + [pltpu.SemaphoreType.DMA((6,))] + scratch,
        compiler_params=limit,
        name="model_edge",
    )(col_far, col_near, edge, edge_dense, center)


def solution(mesh):
    cells = P(None, "gx", "gy")
    in_specs = (cells,) * 7 + (
        P("gx", "gy", None),
        P("gx", "gy", None),
        P(None, "gx", "gy", None),
        P(None, None, "gx", "gy", None),
    )
    return jax.shard_map(
        on_device, mesh=mesh, in_specs=in_specs, out_specs=(cells,) * 3, check_vma=False
    )
```
